32 devices in a mesh: event: 2 (over x), cuts: 16 (over z, y, core).
Axes of the slice: x: 2, y: 2, z: 4, core: 2. Of those that a mesh axis runs over, the one named last changes fastest.
Arguments:
- forward_displacement: float32 [2, 278784], P('event', 'cuts'), may hold values from -6 to 6
- forward_velocity: float32 [2, 278784], P('event', 'cuts'), may hold values from -6 to 6
- adjoint_displacement: float32 [2, 278784], P('event', 'cuts'), may hold values from -6 to 6
- adjoint_velocity: float32 [2, 278784], P('event', 'cuts'), may hold values from -6 to 6
- inverse_mass: float32 [278784], P('cuts'), may hold values from 0.3 to 3
- shear_modulus: float32 [125, 4096], P(None, 'cuts'), may hold values from 0.5 to 4
- connectivity: int32 [125, 4096], P(None, 'cuts'), may hold values from 0 to 18512, as said below
- face_points: int32 [16, 1152], P('cuts'), may hold values from 0 to 1088, as said below
- element_count: int32 [16], P('cuts'), may hold values from 128 to 256, as said below
Outputs:
- forward_displacement_next: float32 [2, 278784], P('event', 'cuts')
- forward_velocity_next: float32 [2, 278784], P('event', 'cuts')
- adjoint_displacement_next: float32 [2, 278784], P('event', 'cuts')
- adjoint_velocity_next: float32 [2, 278784], P('event', 'cuts')
- shear_kernel: float32 [256, 1089], P('cuts')
The draws below stay inside these ranges and needn't reach their ends.
Inputs may be any that keep to these rules, and one draw needn't show every extreme that they name: `connectivity`: slot n of slice s is the element (ex, ey, ez) of a structured block of 4 x 8 x 8 elements, in an order drawn per slice; its point (i, j, k) has coordinates x = 4 ex + i, y = 4 ey + j, z = 4 ez + k and index x 1089 + y * 33 + z for x < 16; points with x = 16 lie on the next slice's first plane and have index 17424 + g, where g is their slot in the next slice's face list. `face_points`: row s lists in slots 0 to 1088 each point of slice s with x = 0 once; slots 1089 to 1151 hold 0. `element_count`: some slice has all 256 slots live in every draw.
All inputs are finite; a program needn't handle non-finite values.
Results may differ from the reference program's by a relative error of at most 0.0001.
Values sent between devices are 32-bit elements; how exact they have to be, the bound alone decides.
No kernel may reach another device: no remote copies, remote signals or barrier semaphores. Data moves between devices by JAX's collectives and lax.ppermute only.
A program may use at most 128 MiB of HBM per device.

```python
import math
import jax
import jax.numpy as jnp
import numpy as np
from jax import lax

NGLL = 5
NGLL3 = 125
EY = 8
EZ = 8
NEL = 256
PXU = 16
PY = 33
PZ = 33
PYZ = 1089
NPTS = 17424
NBUF = 1152
SLICES = 16
EVENTS = 2


def slice_tables(key):
    face_key = jax.random.fold_in(key, 101)
    order_key = jax.random.fold_in(key, 202)

    def face_order(subkey):
        return jax.random.permutation(subkey, PYZ).astype(jnp.int32)

    def element_order(subkey):
        return jax.random.permutation(subkey, NEL).astype(jnp.int32)

    def slot_lookup(permuted):
        return jnp.zeros((PYZ,), jnp.int32).at[permuted].set(jnp.arange(PYZ, dtype=jnp.int32))
    face_perm = jax.vmap(face_order)(jax.random.split(face_key, SLICES))
    slot_of = jax.vmap(slot_lookup)(face_perm)
    orders = jax.vmap(element_order)(jax.random.split(order_key, SLICES))
    return (face_perm, slot_of, orders)


def draw_connectivity(key, part):
    face_perm, slot_of, orders = slice_tables(key)
    element = jnp.arange(NEL, dtype=jnp.int32)
    node = jnp.arange(NGLL3, dtype=jnp.int32)
    coord_x = (NGLL - 1) * (element // (EY * EZ))[None, :] + (node // (NGLL * NGLL))[:, None]
    coord_y = (NGLL - 1) * (element // EZ % EY)[None, :] + (node // NGLL % NGLL)[:, None]
    coord_z = (NGLL - 1) * (element % EZ)[None, :] + (node % NGLL)[:, None]
    column = coord_y * PZ + coord_z
    owned = coord_x * PYZ + column
    next_slots = jnp.roll(slot_of, -1, axis=0)
    ghost = NPTS + next_slots[:, column]
    point_table = jnp.where((coord_x < PXU)[None, :, :], owned[None, :, :], ghost)
    point_table = jnp.take_along_axis(point_table, orders[:, None, :], axis=2)
    return point_table.transpose(1, 0, 2).reshape(NGLL3, SLICES * NEL).astype(jnp.int32)


def draw_face_points(key, part):
    face_perm, slot_of, orders = slice_tables(key)
    return jnp.pad(face_perm, ((0, 0), (0, NBUF - PYZ))).astype(jnp.int32)


def draw_element_count(key, part):
    counts = jax.random.randint(jax.random.fold_in(key, 303), (SLICES,), NEL // 2, NEL + 1, dtype=jnp.int32)
    fullest = jax.random.randint(jax.random.fold_in(key, 404), (), 0, SLICES, dtype=jnp.int32)
    return counts.at[fullest].set(NEL).astype(jnp.int32)


def level_of(key, dims, cuts, least, high):
    factor_of, own = 1.0, jax.random.fold_in(key, 6)
    for position, blocks in cuts:
        steps = jnp.exp(jax.random.uniform(jax.random.fold_in(own, position), (blocks,), jnp.float32, least / len(cuts), high / len(cuts)))
        factor_of = factor_of * jnp.repeat(steps, dims[position] // blocks).reshape([-1 if axis == position else 1 for axis in range(len(dims))])
    return factor_of


def noise(rng, extent, width, reach, cuts=(), kind=jnp.bfloat16):
    entries = jax.random.normal(rng, extent, jnp.float32) * width
    if len(cuts) > 0:
        entries = level_of(rng, extent, cuts, -0.22, 0.18) * entries
    return jnp.clip(entries, min=-reach, max=reach).astype(kind)


def setup_inputs(seed: int = 0) -> dict:
    keys = jax.random.split(jax.random.key(seed), 10)
    forward_displacement = noise(keys[0], (EVENTS, SLICES * NPTS), 1.0, 6.0, ((0, 2), (1, 16)), jnp.float32)
    forward_velocity = noise(keys[1], (EVENTS, SLICES * NPTS), 1.0, 6.0, ((0, 2), (1, 16)), jnp.float32)
    adjoint_displacement = noise(keys[2], (EVENTS, SLICES * NPTS), 1.0, 6.0, ((0, 2), (1, 16)), jnp.float32)
    adjoint_velocity = noise(keys[3], (EVENTS, SLICES * NPTS), 1.0, 6.0, ((0, 2), (1, 16)), jnp.float32)
    inverse_mass = jnp.clip(jnp.exp(math.log(3.0) - 2.3025851 * jax.random.uniform(keys[4], (SLICES * NPTS,), jnp.float32) ** level_of(keys[4], (SLICES * NPTS,), ((0, 16),), -0.2, 0.2)), 0.3, 3.0)
    shear_modulus = jnp.clip(jnp.exp(math.log(4.0) - 2.0794415 * jax.random.uniform(keys[5], (NGLL3, SLICES * NEL), jnp.float32) ** level_of(keys[5], (NGLL3, SLICES * NEL), ((1, 16),), -0.2, 0.2)), 0.5, 4.0)
    connectivity = draw_connectivity(jax.random.fold_in(keys[9], 71), 0)
    face_points = draw_face_points(jax.random.fold_in(keys[9], 71), 0)
    element_count = draw_element_count(jax.random.fold_in(keys[9], 71), 0)
    return {"forward_displacement": forward_displacement, "forward_velocity": forward_velocity, "adjoint_displacement": adjoint_displacement, "adjoint_velocity": adjoint_velocity, "inverse_mass": inverse_mass, "shear_modulus": shear_modulus, "connectivity": connectivity, "face_points": face_points, "element_count": element_count}


time_step = 0.02
cross_sigma = 1.5
cross_reach = 4

def gll_tables():
    nodes = np.array([-1.0, -np.sqrt(3.0 / 7.0), 0.0, np.sqrt(3.0 / 7.0), 1.0])
    quad_weights = np.array([0.1, 49.0 / 90.0, 32.0 / 45.0, 49.0 / 90.0, 0.1])
    barycentric = np.array([1.0 / np.prod([nodes[node_row] - nodes[node_column] for node_column in range(5) if node_column != node_row]) for node_row in range(5)])
    derivative = np.zeros((5, 5))
    for node_row in range(5):
        for node_column in range(5):
            if node_column != node_row:
                derivative[node_row, node_column] = barycentric[node_column] / barycentric[node_row] / (nodes[node_row] - nodes[node_column])
        derivative[node_row, node_row] = -np.sum(derivative[node_row])
    weights_cube = (quad_weights[:, None, None] * quad_weights[None, :, None] * quad_weights[None, None, :]).reshape(125)
    return (jnp.asarray(derivative, dtype=jnp.float32), jnp.asarray(weights_cube, dtype=jnp.float32))

def gradients(cube, derivative):
    grad_x = jnp.einsum('il,ljkn->ijkn', derivative, cube, precision=lax.Precision.HIGHEST)
    grad_y = jnp.einsum('jl,ilkn->ijkn', derivative, cube, precision=lax.Precision.HIGHEST)
    grad_z = jnp.einsum('kl,ijln->ijkn', derivative, cube, precision=lax.Precision.HIGHEST)
    return (grad_x, grad_y, grad_z)

def stiffness(grads, flux_cube, derivative):
    term_x = jnp.einsum('li,ljkn->ijkn', derivative, flux_cube * grads[0], precision=lax.Precision.HIGHEST)
    term_y = jnp.einsum('lj,ilkn->ijkn', derivative, flux_cube * grads[1], precision=lax.Precision.HIGHEST)
    term_z = jnp.einsum('lk,ijln->ijkn', derivative, flux_cube * grads[2], precision=lax.Precision.HIGHEST)
    return -(term_x + term_y + term_z)

def slice_terms(forward_ext, adjoint_ext, connect_slice, flux_slice, derivative):
    elements = connect_slice.shape[1]
    forward_grads = gradients(forward_ext[connect_slice].reshape(NGLL, NGLL, NGLL, elements), derivative)
    adjoint_grads = gradients(adjoint_ext[connect_slice].reshape(NGLL, NGLL, NGLL, elements), derivative)
    flux_cube = flux_slice.reshape(NGLL, NGLL, NGLL, elements)
    point_ids = connect_slice.reshape(-1)
    total = NPTS + NBUF
    forward_force = jax.ops.segment_sum(stiffness(forward_grads, flux_cube, derivative).reshape(-1), point_ids, num_segments=total)
    adjoint_force = jax.ops.segment_sum(stiffness(adjoint_grads, flux_cube, derivative).reshape(-1), point_ids, num_segments=total)
    product = forward_grads[0] * adjoint_grads[0] + forward_grads[1] * adjoint_grads[1] + forward_grads[2] * adjoint_grads[2]
    kernel_ext = jax.ops.segment_sum((-flux_cube * product).reshape(-1), point_ids, num_segments=total)
    return (forward_force, adjoint_force, kernel_ext)

def along_weight(offset):
    sigma = PXU / 4.0
    return jnp.exp(-offset * offset / (2.0 * sigma * sigma))

def cross_matrix(count):
    point_index = jnp.arange(count, dtype=jnp.int32)
    offset = (point_index[:, None] - point_index[None, :]).astype(jnp.float32)
    kept = jnp.exp(-offset * offset / (2.0 * cross_sigma * cross_sigma)) * (jnp.abs(offset) <= cross_reach).astype(jnp.float32)
    return kept / lax.optimization_barrier(jnp.sum(kept, axis=1, keepdims=True))

def cross_table():
    return jnp.kron(cross_matrix(PY), cross_matrix(PZ))

def along_norm():
    offsets = jnp.arange(-PXU, PXU + 1, dtype=jnp.int32).astype(jnp.float32)
    return jnp.sum(along_weight(offsets))

def cycle_matrix():
    count_rows = SLICES * PXU
    row_index = jnp.arange(count_rows, dtype=jnp.int32)
    spread = (row_index[None, :] - row_index[:, None]) % count_rows
    spread = jnp.where(spread > count_rows // 2, spread - count_rows, spread)
    inside = (jnp.abs(spread) <= PXU).astype(jnp.float32)
    return along_weight(spread.astype(jnp.float32)) * inside / along_norm()

def add_faces(owned, indices, received):
    return owned.at[indices].add(received)

def reference(forward_displacement, forward_velocity, adjoint_displacement, adjoint_velocity, inverse_mass, shear_modulus, connectivity, face_points, element_count):
    derivative, weights_cube = gll_tables()
    slice_connect = connectivity.reshape(NGLL3, SLICES, NEL).transpose(1, 0, 2)
    slice_shear = shear_modulus.reshape(NGLL3, SLICES, NEL).transpose(1, 0, 2)
    active = (jnp.arange(NEL, dtype=jnp.int32)[None, :] < element_count[:, None]).astype(jnp.float32)
    slice_flux = weights_cube[None, :, None] * slice_shear * active[:, None, :]
    mass_rows = inverse_mass.reshape(SLICES, NPTS)

    def extend(points):
        face_values = jnp.take_along_axis(points, face_points, axis=1)
        return jnp.concatenate([points, jnp.roll(face_values, -1, axis=0)], axis=1)

    def finish(extended):
        received = jnp.roll(extended[:, NPTS:], 1, axis=0)
        return jax.vmap(add_faces)(extended[:, :NPTS], face_points, received)

    def one_event(fields):
        forward_now = fields[0].reshape(SLICES, NPTS)
        forward_speed = fields[1].reshape(SLICES, NPTS)
        adjoint_now = fields[2].reshape(SLICES, NPTS)
        adjoint_speed = fields[3].reshape(SLICES, NPTS)
        forward_force, adjoint_force, kernel_ext = jax.vmap(slice_terms, in_axes=(0, 0, 0, 0, None))(extend(forward_now), extend(adjoint_now), slice_connect, slice_flux, derivative)
        forward_force = finish(forward_force)
        adjoint_force = finish(adjoint_force)
        kernel_points = finish(kernel_ext)
        forward_speed_next = forward_speed - time_step * mass_rows * forward_force
        forward_now_next = forward_now - time_step * forward_speed_next
        adjoint_speed_next = adjoint_speed + time_step * mass_rows * adjoint_force
        adjoint_now_next = adjoint_now + time_step * adjoint_speed_next
        return (forward_now_next.reshape(-1), forward_speed_next.reshape(-1), adjoint_now_next.reshape(-1), adjoint_speed_next.reshape(-1), kernel_points)
    results = lax.map(one_event, (forward_displacement, forward_velocity, adjoint_displacement, adjoint_velocity))
    kernel_total = lax.optimization_barrier(jnp.sum(results[4], axis=0)).reshape(SLICES * PXU, PYZ)
    smoothed_along = jnp.dot(cycle_matrix(), kernel_total, precision=lax.Precision.HIGHEST)
    shear_kernel = jnp.dot(smoothed_along, cross_table().T, precision=lax.Precision.HIGHEST)
    return (results[0], results[1], results[2], results[3], shear_kernel)
```

```python
import numpy as np
import jax
import jax.numpy as jnp
import ml_dtypes
from jax import lax
from jax.experimental import pallas as pl
from jax.experimental.pallas import tpu as pltpu
from jax.sharding import PartitionSpec as P

NGLL = 5
EX, EY, EZ = 4, 8, 8
PXU = 16
PY = 33
PZ = 33
PYZ = 1089
NPTS = 17424
LANES = 128
ROWS = 144
TIME_STEP = 0.02
F32 = jnp.float32
BF16 = jnp.bfloat16


def gll():
    nodes = np.array([-1.0, -np.sqrt(3.0 / 7.0), 0.0, np.sqrt(3.0 / 7.0), 1.0])
    bary = np.array([1.0 / np.prod([nodes[r] - nodes[c] for c in range(5) if c != r]) for r in range(5)])
    d = np.zeros((5, 5))
    for r in range(5):
        for c in range(5):
            if c != r:
                d[r, c] = bary[c] / bary[r] / (nodes[r] - nodes[c])
        d[r, r] = -np.sum(d[r])
    return d


DERIV = gll()


def split_np(x):
    x = np.asarray(x, np.float32)
    parts = []
    for _ in range(3):
        p = x.astype(ml_dtypes.bfloat16)
        parts.append(p)
        x = x - p.astype(np.float32)
    return parts


def band_table():
    offsets = np.arange(-PXU, PXU + 1)
    w = lambda d: np.exp(-d * d / (2.0 * (PXU / 4.0) ** 2))
    total = w(offsets.astype(np.float64)).sum()
    target = np.arange(-PXU, 2 * PXU + 1)
    source = np.zeros(24, np.int64)
    for r, i in ((0, 1), (4, 0), (8, 3), (12, 2), (20, 4)):
        source[r : r + 4] = 4 * np.arange(4) + i
    spread = target[:, None] - source[None, :]
    band = np.zeros((64, 24))
    band[:49] = w(spread.astype(np.float64)) * (np.abs(spread) <= PXU) / total
    band[:, 16:20] = 0.0
    b1, b2, b3 = split_np(band)
    return np.concatenate([b1, b1, b1, b2, b2, b3], axis=1)


def cross_table():
    off = np.arange(-4, 5)
    k = np.exp(-off * off / (2.0 * 1.5 * 1.5))
    point = np.arange(33)
    inside = ((point[None, :] + off[:, None]) >= 0) & ((point[None, :] + off[:, None]) < 33)
    taps = k[:, None] * inside
    taps = taps / taps.sum(axis=0, keepdims=True)
    out = np.zeros((24, 1152), np.float32)
    out[0:9, :PYZ] = np.tile(taps, (1, PY))
    out[9:18, :PYZ] = np.repeat(taps, PZ, axis=1)
    return out


def split3(x):
    hi = x.astype(BF16)
    rest = x - hi.astype(F32)
    mid = rest.astype(BF16)
    low = (rest - mid.astype(F32)).astype(BF16)
    return hi, mid, low


def dot_nt(a, b):
    return lax.dot_general(a, b, (((1,), (1,)), ((), ())), preferred_element_type=F32)


def dot_tn(a, b):
    return lax.dot_general(a, b, (((0,), (0,)), ((), ())), preferred_element_type=F32)


def selector():
    column = lax.broadcasted_iota(jnp.int32, (8, 256), 1)
    row = lax.broadcasted_iota(jnp.int32, (8, 256), 0)
    base = column - 4 * row
    blocks = [jnp.where(base == j * PZ + k, 1.0, 0.0) for j in range(5) for k in range(5)]
    return jnp.concatenate(blocks, axis=0).astype(BF16)


def flux_kernel(count_ref, conn_ref, shear_ref, flux_ref):
    point = conn_ref[0:1, :].astype(F32)
    x = jnp.floor((point + 0.5) * (1.0 / PYZ))
    rest = point - x * PYZ
    y = jnp.floor((rest + 0.5) * (1.0 / PZ))
    z = rest - y * PZ
    code = (8.0 * z + y + 0.25 * x).astype(jnp.int32)
    slot = lax.broadcasted_iota(jnp.int32, (1, 256), 1)
    code = jnp.where(slot < count_ref[0], code, -1)
    row = lax.broadcasted_iota(jnp.int32, (LANES, 256), 0)
    member = ((row >> 3) & 7) * 4 + (row & 3)
    picks = [jnp.where(code - member == ez * 32, 1.0, 0.0).astype(BF16) for ez in range(EZ)]
    pick = jnp.concatenate(picks, axis=0)
    q = lax.broadcasted_iota(jnp.int32, (125, 256), 0)
    weight = None
    for digit in (q // 25, (q // 5) % 5, q % 5):
        w = jnp.where(digit == 2, 32.0 / 45.0, jnp.where((digit == 0) | (digit == 4), 0.1, 49.0 / 90.0))
        weight = w if weight is None else weight * w
    hi, mid, low = split3(shear_ref[...] * weight)
    moved = dot_nt(hi, pick) + (dot_nt(mid, pick) + dot_nt(low, pick))
    for ez in range(EZ):
        flux_ref[pl.ds(ez, 125, stride=8), :] = moved[:, ez * LANES : (ez + 1) * LANES]


def derive(e):
    d = DERIV
    s0, s1 = e[0] + e[4], e[1] + e[3]
    d0, d1 = e[0] - e[4], e[1] - e[3]
    out = [None] * 5
    for i in (0, 1):
        even = float((d[i, 0] - d[i, 4]) / 2) * d0 + float((d[i, 1] - d[i, 3]) / 2) * d1
        odd = float((d[i, 0] + d[i, 4]) / 2) * s0 + float((d[i, 1] + d[i, 3]) / 2) * s1 + float(d[i, 2]) * e[2]
        out[i] = odd + even
        out[4 - i] = even - odd
    out[2] = float(d[2, 0]) * d0 + float(d[2, 1]) * d1
    return out


def derive_back(t):
    d = DERIV
    s0, s1 = t[0] + t[4], t[1] + t[3]
    d0, d1 = t[0] - t[4], t[1] - t[3]
    out = [None] * 5
    for i in (0, 1):
        even = float((d[0, i] - d[4, i]) / 2) * d0 + float((d[1, i] - d[3, i]) / 2) * d1
        odd = float((d[0, i] + d[4, i]) / 2) * s0 + float((d[1, i] + d[3, i]) / 2) * s1 + float(d[2, i]) * t[2]
        out[i] = odd + even
        out[4 - i] = even - odd
    out[2] = float(d[0, 2]) * d0 + float(d[1, 2]) * d1
    return out


def shifted(tiles, distance, lane):
    skip, part = divmod(distance, LANES)
    if part == 0:
        moved = tiles
        pick = None
    else:
        moved = [pltpu.roll(t, LANES - part, 1) for t in tiles]
        pick = lane < LANES - part
    n = len(tiles)
    out = []
    for i in range(n):
        a = moved[(i + skip) % n]
        b = moved[(i + skip + 1) % n]
        out.append(a if pick is None else jnp.where(pick, a, b))
    return out


def main_kernel(
    own_ref, ghost_ref, flux_ref, band_ref, cross_ref,
    force_ref, face_ref, before_ref, here_ref, after_ref, far_ref,
    plane_ref, win_ref, elem_ref, term_ref, kern_ref,
):
    lane = lax.broadcasted_iota(jnp.int32, (8, LANES), 1)
    lane9 = lax.broadcasted_iota(jnp.int32, (9, LANES), 1)
    for x in range(PXU + 1):
        for f in range(2):
            if x < PXU:
                r0, off = divmod(PYZ * x, LANES)
                flat = own_ref[f, r0 : r0 + 9, :]
                if off:
                    flat = jnp.where(
                        lane9 < LANES - off,
                        pltpu.roll(flat, LANES - off, 1),
                        pltpu.roll(own_ref[f, r0 + 1 : r0 + 10, :], LANES - off, 1),
                    )
            else:
                flat = ghost_ref[f, 0:9, :]
            if x < PXU:
                plane_ref[pl.ds((x % 4) * 72 + f * 4 + x // 4, 9, stride=8), :] = flat
            if x % 4 == 0 and x > 0:
                plane_ref[pl.ds(4 * 72 + f * 4 + x // 4 - 1, 9, stride=8), :] = flat
    for i in range(NGLL):
        tiles = [plane_ref[i * 72 + t * 8 : i * 72 + t * 8 + 8, :] for t in range(9)]
        for ey in range(EY):
            near = [tiles[ey], tiles[ey + 1], tiles[min(ey + 2, 8)]]
            if ey:
                near = [pltpu.roll(t, LANES - 4 * ey, 1) for t in near]
                keep = lane < LANES - 4 * ey
                near = [jnp.where(keep, near[0], near[1]), jnp.where(keep, near[1], near[2])]
            for copy in range(2):
                r = i * LANES + copy * 64 + ey * 8
                win_ref[r : r + 8, 0:LANES] = near[0]
                win_ref[r : r + 8, LANES:] = near[1]
    select = selector()
    hi, mid, low = split3(win_ref[...])
    elem_ref[...] = dot_nt(select, hi) + (dot_nt(select, mid) + dot_nt(select, low))

    def at(ref, i, j, k):
        r = (j * 5 + k) * 8
        return ref[r : r + 8, i * LANES : (i + 1) * LANES]

    def put(ref, i, j, k, value):
        r = (j * 5 + k) * 8
        ref[r : r + 8, i * LANES : (i + 1) * LANES] = value

    def flux_at(i, j, k):
        r = ((i * 5 + j) * 5 + k) * 8
        return flux_ref[r : r + 8, :]

    upper = lane >= 64
    for axis in range(3):
        for p in range(5):
            for q in range(5):
                line = [((l, p, q), (p, l, q), (p, q, l))[axis] for l in range(5)]
                grads = derive([at(elem_ref, *c) for c in line])
                flux = [flux_at(*c) for c in line]
                back = derive_back([g * m for g, m in zip(grads, flux)])
                for n, c in enumerate(line):
                    prod = grads[n] * pltpu.roll(grads[n], 4, 1)
                    if axis == 0:
                        put(term_ref, *c, back[n])
                        put(kern_ref, *c, prod)
                    elif axis == 1:
                        put(term_ref, *c, at(term_ref, *c) + back[n])
                        put(kern_ref, *c, at(kern_ref, *c) + prod)
                    else:
                        total = at(term_ref, *c) + back[n]
                        kern = flux[n] * (at(kern_ref, *c) + prod)
                        put(term_ref, *c, -jnp.where(upper, kern, total))
    hi, mid, low = split3(term_ref[...])
    win_ref[...] = dot_tn(hi, select) + (dot_tn(mid, select) + dot_tn(low, select))

    def gathered(i, copy):
        tiles = [None] * 9
        for ey in range(EY):
            r = i * LANES + copy * 64 + ey * 8
            a, b = win_ref[r : r + 8, 0:LANES], win_ref[r : r + 8, LANES:]
            if ey:
                a, b = pltpu.roll(a, 4 * ey, 1), pltpu.roll(b, 4 * ey, 1)
                keep = lane >= 4 * ey
                a, b = jnp.where(keep, a, 0.0), jnp.where(keep, b, a)
            tiles[ey] = a if ey == 0 else tiles[ey] + a
            tiles[ey + 1] = b
        return tiles

    row = lax.broadcasted_iota(jnp.int32, (8, LANES), 0)
    force = [gathered(i, 0) for i in range(NGLL)]
    inner = (row != 0) & (row != 4)
    for t in range(9):
        force[0][t] = force[0][t] + jnp.where(inner, pltpu.roll(force[4][t], 1, 0), 0.0)
    for i in range(NGLL):
        for t in range(9):
            plane_ref[i * 72 + t * 8 : i * 72 + t * 8 + 8, :] = force[i][t]
    force_ref[...] = jnp.zeros(force_ref.shape, F32)
    for f in range(2):
        for x in range(PXU):
            r0, off = divmod(PYZ * x, LANES)
            flat = plane_ref[pl.ds((x % 4) * 72 + f * 4 + x // 4, 9, stride=8), :]
            if off:
                flat = pltpu.roll(flat, off, 1)
                spill = jnp.where(lane9 < off, flat, 0.0)
                flat = jnp.where(lane9 < off, 0.0, flat)
            force_ref[f, r0 : r0 + 9, :] = force_ref[f, r0 : r0 + 9, :] + flat
            if off:
                force_ref[f, r0 + 1 : r0 + 10, :] = force_ref[f, r0 + 1 : r0 + 10, :] + spill
        face_ref[f] = jnp.zeros((16, LANES), F32)
        face_ref[f, 0:9, :] = plane_ref[pl.ds(4 * 72 + f * 4 + 3, 9, stride=8), :]
    kern = [gathered(i, 1) for i in range(NGLL)]
    lower = row < 4
    rows = []
    for t in range(9):
        part = [jnp.where(lower, pltpu.roll(kern[i + 1][t], 4, 0), kern[i][t]) for i in (0, 2)]
        rows.append(jnp.concatenate(part + [jnp.where(lower, 0.0, kern[4][t])], axis=0))
    tiles = rows
    lane24 = lax.broadcasted_iota(jnp.int32, (24, LANES), 1)
    for base, step in ((0, 1), (9, PZ)):
        total = None
        for tap in range(9):
            moved = shifted(tiles, step * (tap - 4), lane24) if tap != 4 else tiles
            scaled = [m * cross_ref[base + tap : base + tap + 1, t * LANES : (t + 1) * LANES] for t, m in enumerate(moved)]
            total = scaled if total is None else [a + b for a, b in zip(total, scaled)]
        tiles = total
    flat = jnp.concatenate(tiles, axis=1)
    k1 = flat.astype(BF16).astype(F32)
    k2 = (flat - k1).astype(BF16).astype(F32)
    k3 = flat - k1 - k2
    stacked = jnp.concatenate([k1, k2, k3, k1, k2, k1], axis=0).astype(BF16)
    shares = jnp.dot(band_ref[...], stacked, preferred_element_type=F32)[:, :PYZ]
    before_ref[...] = shares[0:16]
    here_ref[...] = shares[16:32]
    after_ref[...] = shares[32:48]
    far_ref[...] = shares[48:56]


def on_device(
    forward_displacement,
    forward_velocity,
    adjoint_displacement,
    adjoint_velocity,
    inverse_mass,
    shear_modulus,
    connectivity,
    face_points,
    element_count,
):
    events = lax.axis_size("event")
    cuts = lax.axis_size("cuts")

    def from_cut(block, distance):
        return lax.ppermute(block, "cuts", [(i, (i + distance) % cuts) for i in range(cuts)])

    def from_both(block, turn, distance):
        pairs = [
            (e * cuts + i, ((e + turn) % events) * cuts + (i + distance) % cuts)
            for e in range(events)
            for i in range(cuts)
        ]
        return lax.ppermute(block, ("event", "cuts"), pairs)

    both = jnp.concatenate([forward_displacement, adjoint_displacement], axis=0)
    face = jnp.pad(both[:, :PYZ], ((0, 0), (0, 16 * LANES - PYZ))).reshape(2, 16, LANES)
    ghost = from_cut(face, -1)
    own = jnp.pad(both, ((0, 0), (0, ROWS * LANES - NPTS))).reshape(2, ROWS, LANES)

    flux = pl.pallas_call(
        flux_kernel,
        out_shape=jax.ShapeDtypeStruct((1000, LANES), F32),
        grid=(1,),
        in_specs=[
            pl.BlockSpec(memory_space=pltpu.SMEM),
            pl.BlockSpec((8, 256), lambda g: (0, 0)),
            pl.BlockSpec((125, 256), lambda g: (0, 0)),
        ],
        out_specs=pl.BlockSpec((1000, LANES), lambda g: (0, 0)),
        cost_estimate=pl.CostEstimate(flops=200000000, bytes_accessed=2000000, transcendentals=0),
        name="flux",
    )(element_count, connectivity, shear_modulus)

    share = jax.ShapeDtypeStruct((PXU, PYZ), F32)
    force, face_force, before, here, after, far = pl.pallas_call(
        main_kernel,
        out_shape=[
            jax.ShapeDtypeStruct((2, ROWS, LANES), F32),
            jax.ShapeDtypeStruct((2, 16, LANES), F32),
            share,
            share,
            share,
            jax.ShapeDtypeStruct((8, PYZ), F32),
        ],
        scratch_shapes=[
            pltpu.VMEM((5 * 72, LANES), F32),
            pltpu.VMEM((5 * LANES, 256), F32),
            pltpu.VMEM((200, 5 * LANES), F32),
            pltpu.VMEM((200, 5 * LANES), F32),
            pltpu.VMEM((200, 5 * LANES), F32),
        ],
        cost_estimate=pl.CostEstimate(flops=400000000, bytes_accessed=4000000, transcendentals=0),
        name="elements",
    )(own, ghost, flux, jnp.asarray(band_table()), jnp.asarray(cross_table()))

    face_back = from_cut(face_force, 1)
    far = far[0:1]
    if events <= 2:
        turns = range(events)
    else:
        before, here, after, far = lax.psum((before, here, after, far), "event")
        turns = range(1)
    total = None
    first = None
    for turn in turns:
        mine = here if turn == 0 else from_both(here, turn, 0)
        block = mine + from_both(before, turn, -1) + from_both(after, turn, 1)
        edge = from_both(far, turn, 2)
        total = block if total is None else total + block
        first = edge if first is None else first + edge
    shear_kernel = total + jnp.pad(first, ((0, PXU - 1), (0, 0)))

    back = jnp.pad(face_back.reshape(2, 16 * LANES)[:, :PYZ], ((0, 0), (0, NPTS - PYZ)))
    force = force.reshape(2, ROWS * LANES)[:, :NPTS] + back
    mass = inverse_mass[None, :]
    forward_velocity_next = forward_velocity - TIME_STEP * mass * force[0:1]
    forward_next = forward_displacement - TIME_STEP * forward_velocity_next
    adjoint_velocity_next = adjoint_velocity + TIME_STEP * mass * force[1:2]
    adjoint_next = adjoint_displacement + TIME_STEP * adjoint_velocity_next
    return (forward_next, forward_velocity_next, adjoint_next, adjoint_velocity_next, shear_kernel)


def solution(mesh):
    in_specs = (
        P("event", "cuts"),
        P("event", "cuts"),
        P("event", "cuts"),
        P("event", "cuts"),
        P("cuts"),
        P(None, "cuts"),
        P(None, "cuts"),
        P("cuts", None),
        P("cuts"),
    )
    out_specs = (
        P("event", "cuts"),
        P("event", "cuts"),
        P("event", "cuts"),
        P("event", "cuts"),
        P("cuts", None),
    )
    return jax.shard_map(on_device, mesh=mesh, in_specs=in_specs, out_specs=out_specs, check_vma=False)
```

```python
import numpy as np
import jax
import jax.numpy as jnp
import ml_dtypes
from jax import lax
from jax.experimental import pallas as pl
from jax.experimental.pallas import tpu as pltpu
from jax.sharding import PartitionSpec as P

NGLL = 5
EX, EY, EZ = 4, 8, 8
PXU = 16
PY = 33
PZ = 33
PYZ = 1089
NPTS = 17424
LANES = 128
ROWS = 144
TIME_STEP = 0.02
F32 = jnp.float32
BF16 = jnp.bfloat16


def gll():
    nodes = np.array([-1.0, -np.sqrt(3.0 / 7.0), 0.0, np.sqrt(3.0 / 7.0), 1.0])
    bary = np.array([1.0 / np.prod([nodes[r] - nodes[c] for c in range(5) if c != r]) for r in range(5)])
    d = np.zeros((5, 5))
    for r in range(5):
        for c in range(5):
            if c != r:
                d[r, c] = bary[c] / bary[r] / (nodes[r] - nodes[c])
        d[r, r] = -np.sum(d[r])
    return d


DERIV = gll()


def split_np(x):
    x = np.asarray(x, np.float32)
    parts = []
    for _ in range(3):
        p = x.astype(ml_dtypes.bfloat16)
        parts.append(p)
        x = x - p.astype(np.float32)
    return parts


ROW_PLANE = np.array([5, 9, 13, 0, 4, 8, 12, 1, 7, 11, 15, 2, 6, 10, 14, 3])


def band_table():
    offsets = np.arange(-PXU, PXU + 1)
    w = lambda d: np.exp(-d * d / (2.0 * (PXU / 4.0) ** 2))
    total = w(offsets.astype(np.float64)).sum()
    out = []
    for first in (-PXU, PXU):
        source = np.concatenate([ROW_PLANE, ROW_PLANE + first, ROW_PLANE - first])
        spread = np.arange(PXU)[:, None] - source[None, :]
        band = w(spread.astype(np.float64)) * (np.abs(spread) <= PXU) / total
        b1, b2, b3 = split_np(band)
        out.append(np.concatenate([b1, b1, b1, b2, b2, b3], axis=1))
    return np.stack(out)


def cross_table():
    off = np.arange(-4, 5)
    k = np.exp(-off * off / (2.0 * 1.5 * 1.5))
    point = np.arange(33)
    inside = ((point[None, :] + off[:, None]) >= 0) & ((point[None, :] + off[:, None]) < 33)
    taps = k[:, None] * inside
    taps = taps / taps.sum(axis=0, keepdims=True)
    out = np.zeros((24, 1152), np.float32)
    out[0:9, :PYZ] = np.tile(taps, (1, PY))
    out[9:18, :PYZ] = np.repeat(taps, PZ, axis=1)
    return out


def split3(x):
    hi = x.astype(BF16)
    rest = x - hi.astype(F32)
    mid = rest.astype(BF16)
    low = (rest - mid.astype(F32)).astype(BF16)
    return hi, mid, low


def dot_nt(a, b):
    return lax.dot_general(a, b, (((1,), (1,)), ((), ())), preferred_element_type=F32)


def dot_tn(a, b):
    return lax.dot_general(a, b, (((0,), (0,)), ((), ())), preferred_element_type=F32)


def selector():
    column = lax.broadcasted_iota(jnp.int32, (8, 256), 1)
    row = lax.broadcasted_iota(jnp.int32, (8, 256), 0)
    base = column - 4 * row
    blocks = [jnp.where(base == j * PZ + k, 1.0, 0.0) for j in range(5) for k in range(5)]
    return jnp.concatenate(blocks, axis=0).astype(BF16)


def slot_elements(conn_ref, count_ref):
    point = conn_ref[0:1, :].astype(F32)
    x = jnp.floor((point + 0.5) * (1.0 / PYZ))
    rest = point - x * PYZ
    y = jnp.floor((rest + 0.5) * (1.0 / PZ))
    z = rest - y * PZ
    code = (8.0 * z + y + 0.25 * x).astype(jnp.int32)
    slot = lax.broadcasted_iota(jnp.int32, (1, 256), 1)
    return jnp.where(slot < count_ref[0], code, -1000)


def weighted(shear_ref):
    q = lax.broadcasted_iota(jnp.int32, (125, 256), 0)
    weight = None
    for digit in (q // 25, (q // 5) % 5, q % 5):
        w = jnp.where(digit == 2, 32.0 / 45.0, jnp.where((digit == 0) | (digit == 4), 0.1, 49.0 / 90.0))
        weight = w if weight is None else weight * w
    return split3(shear_ref[...] * weight)


def moved_by(parts, pick):
    hi, mid, low = parts
    return dot_nt(hi, pick) + (dot_nt(mid, pick) + dot_nt(low, pick))


def pack_kernel(parity_ref, count_ref, conn_ref, shear_ref, fwd_ref, adj_ref, first_ref, second_ref, line_ref):
    code = slot_elements(conn_ref, count_ref)
    lane = lax.broadcasted_iota(jnp.int32, (LANES, 256), 0) & 63
    pick = jnp.where(code == (lane >> 3) * 32 + (lane & 7) * 4 + 3, 1.0, 0.0).astype(BF16)
    flux = moved_by(weighted(shear_ref), pick)
    flux = jnp.concatenate([flux, jnp.zeros((3, LANES), F32)], axis=0)
    low = lax.broadcasted_iota(jnp.int32, (64, LANES), 1) < 64
    flux = jnp.where(low, flux[0:64], flux[64:128])
    for f, ref in enumerate((fwd_ref, adj_ref)):
        for r in (0, 8, 16, 24, 32):
            line_ref[f, r : r + 8, :] = ref[0:1, r * LANES : (r + 8) * LANES].reshape(8, LANES)
        base = 102 * LANES
        for r in (0, 8, 16, 24):
            at = base + r * LANES
            line_ref[f, 40 + r : 48 + r, :] = ref[0:1, at : at + 8 * LANES].reshape(8, LANES)
        at = base + 32 * LANES
        line_ref[f, 72:74, :] = ref[0:1, at : at + 2 * LANES].reshape(2, LANES)
        line_ref[f, 74:80, :] = jnp.zeros((6, LANES), F32)
        line_ref[f, 74:75, 0:16] = ref[0:1, at + 2 * LANES : at + 2 * LANES + 16]
    odd = parity_ref[0] == 1
    for ref, flip in ((first_ref, odd), (second_ref, jnp.logical_not(odd))):
        for f in range(2):
            ref[40 * f : 40 * f + 40, :] = jnp.where(flip, line_ref[f, 40:80, :], line_ref[f, 0:40, :])
        ref[80:144, :] = flux


def flux_kernel(count_ref, conn_ref, shear_ref, flux_ref):
    code = slot_elements(conn_ref, count_ref)
    lane = lax.broadcasted_iota(jnp.int32, (LANES, 256), 0)
    layer = lane >> 3
    layer = jnp.where(layer >= 10, layer - 10, jnp.where(layer >= 5, layer - 5, layer)) - 1
    member = jnp.where((layer >= 0) & (layer < 4), (lane & 7) * 4 + layer, -1)
    member = jnp.where(member >= 0, member, 5000)
    pick = jnp.concatenate([jnp.where(code - member == ez * 32, 1.0, 0.0).astype(BF16) for ez in range(EZ)], axis=0)
    moved = moved_by(weighted(shear_ref), pick)
    for ez in range(EZ):
        flux_ref[pl.ds(ez, 125, stride=8), :] = moved[:, ez * LANES : (ez + 1) * LANES]


def derive(e):
    d = DERIV
    s0, s1 = e[0] + e[4], e[1] + e[3]
    d0, d1 = e[0] - e[4], e[1] - e[3]
    out = [None] * 5
    for i in (0, 1):
        even = float((d[i, 0] - d[i, 4]) / 2) * d0 + float((d[i, 1] - d[i, 3]) / 2) * d1
        odd = float((d[i, 0] + d[i, 4]) / 2) * s0 + float((d[i, 1] + d[i, 3]) / 2) * s1 + float(d[i, 2]) * e[2]
        out[i] = odd + even
        out[4 - i] = even - odd
    out[2] = float(d[2, 0]) * d0 + float(d[2, 1]) * d1
    return out


def derive_back(t):
    d = DERIV
    s0, s1 = t[0] + t[4], t[1] + t[3]
    d0, d1 = t[0] - t[4], t[1] - t[3]
    out = [None] * 5
    for i in (0, 1):
        even = float((d[0, i] - d[4, i]) / 2) * d0 + float((d[1, i] - d[3, i]) / 2) * d1
        odd = float((d[0, i] + d[4, i]) / 2) * s0 + float((d[1, i] + d[3, i]) / 2) * s1 + float(d[2, i]) * t[2]
        out[i] = odd + even
        out[4 - i] = even - odd
    out[2] = float(d[0, 2]) * d0 + float(d[1, 2]) * d1
    return out


def shifted(tiles, distance, lane):
    skip, part = divmod(distance, LANES)
    if part == 0:
        moved = tiles
        pick = None
    else:
        moved = [pltpu.roll(t, LANES - part, 1) for t in tiles]
        pick = lane < LANES - part
    n = len(tiles)
    out = []
    for i in range(n):
        a = moved[(i + skip) % n]
        b = moved[(i + skip + 1) % n]
        out.append(a if pick is None else jnp.where(pick, a, b))
    return out


def at(ref, i, j, k):
    r = (j * 5 + k) * 8
    return ref[r : r + 8, i * LANES : (i + 1) * LANES]


def put(ref, i, j, k, value):
    r = (j * 5 + k) * 8
    ref[r : r + 8, i * LANES : (i + 1) * LANES] = value


def flux_at(ref, i, j, k):
    r = ((i * 5 + j) * 5 + k) * 8
    return ref[r : r + 8, :]


def lines():
    for axis in range(3):
        for p in range(5):
            for q in range(5):
                yield axis, [((l, p, q), (p, l, q), (p, q, l))[axis] for l in range(5)]


def plane_of(ref, start, row):
    r0, off = divmod(start, LANES)
    lane9 = lax.broadcasted_iota(jnp.int32, (9, LANES), 1)
    flat = ref[row + r0 : row + r0 + 9, :]
    if off:
        flat = jnp.where(
            lane9 < LANES - off,
            pltpu.roll(flat, LANES - off, 1),
            pltpu.roll(ref[row + r0 + 1 : row + r0 + 10, :], LANES - off, 1),
        )
    return flat


def kernel_kernel(
    parity_ref, fwd_ref, adj_ref, first_ref, second_ref, flux_in_ref, cross_ref,
    kern_out_ref, elem_ref, flux_ref,
    own_ref, near_ref, plane_ref, win0_ref, win1_ref, kern_ref,
):
    lane = lax.broadcasted_iota(jnp.int32, (8, LANES), 1)
    even = parity_ref[0] == 0
    for f, ref in enumerate((fwd_ref, adj_ref)):
        for r in range(0, 136, 8):
            own_ref[ROWS * f + r : ROWS * f + r + 8, :] = ref[0:1, r * LANES : (r + 8) * LANES].reshape(8, LANES)
        own_ref[ROWS * f + 136 : ROWS * f + 144, :] = jnp.zeros((8, LANES), F32)
        own_ref[ROWS * f + 136 : ROWS * f + 137, 0:16] = ref[0:1, NPTS - 16 : NPTS]
    near_ref[0:144, :] = jnp.where(even, first_ref[...], second_ref[...])
    near_ref[144:224, :] = jnp.where(even, second_ref[0:80, :], first_ref[0:80, :])

    m = lax.broadcasted_iota(jnp.int32, (LANES, LANES), 0)
    n = lax.broadcasted_iota(jnp.int32, (LANES, LANES), 1) & 63
    layer = m >> 3
    base = jnp.where((layer == 0) | (layer == 5) | (layer == 10), n - (m & 7), -1)
    pick = jnp.concatenate([jnp.where(base == ez * 8, 1.0, 0.0).astype(BF16) for ez in range(EZ)], axis=0)
    low = lax.broadcasted_iota(jnp.int32, (64, LANES), 1) < 64
    packed = near_ref[80:144, :]
    packed = jnp.concatenate([jnp.where(low, packed, 0.0), jnp.where(low, 0.0, packed)], axis=0)
    extra = moved_by(split3(packed), pick)
    for ez in range(EZ):
        rows = pl.ds(ez, 125, stride=8)
        flux_ref[rows, :] = flux_in_ref[rows, :] + extra[0:125, ez * LANES : (ez + 1) * LANES]

    plane_ref[...] = jnp.zeros(plane_ref.shape, F32)
    for x in range(-4, PXU + 1):
        for f in range(2):
            if x < 0:
                flat = plane_of(near_ref, 12 + PYZ * (x + 4), 40 * f)
            elif x < PXU:
                flat = plane_of(own_ref, PYZ * x, ROWS * f)
            else:
                flat = plane_of(near_ref, 0, 144 + 40 * f)
            places = []
            if x < PXU:
                places.append((x % 4, x // 4 + 1))
            if x % 4 == 0 and x >= 0:
                places.append((4, x // 4))
            for i, layer in places:
                for r in (layer, 10 + layer) if f == 0 else (5 + layer,):
                    plane_ref[pl.ds(i * 144 + r, 9, stride=16), :] = flat
    for i in range(NGLL):
        for h in range(2):
            tiles = [plane_ref[i * 144 + t * 16 + 8 * h : i * 144 + t * 16 + 8 * h + 8, :] for t in range(9)]
            for ey in range(EY):
                near = [tiles[ey], tiles[ey + 1], tiles[min(ey + 2, 8)]]
                if ey:
                    near = [pltpu.roll(t, LANES - 4 * ey, 1) for t in near]
                    keep = lane < LANES - 4 * ey
                    near = [jnp.where(keep, near[0], near[1]), jnp.where(keep, near[1], near[2])]
                rows = pl.ds(i * LANES + h * 64 + ey, 8, stride=8)
                win0_ref[rows, :] = near[0]
                win1_ref[rows, :] = near[1]
    select = selector()
    hi, mid, low = split3(jnp.concatenate([win0_ref[...], win1_ref[...]], axis=1))
    elem_ref[...] = dot_nt(select, hi) + (dot_nt(select, mid) + dot_nt(select, low))

    for axis, line in lines():
        grads = derive([at(elem_ref, *c) for c in line])
        for n, c in enumerate(line):
            prod = grads[n] * pltpu.roll(grads[n], 40, 1)
            if axis > 0:
                prod = at(kern_ref, *c) + prod
            if axis == 2:
                prod = -prod * flux_at(flux_ref, *c)
            put(kern_ref, *c, prod)
    hi, mid, low = split3(kern_ref[...])
    back = dot_tn(hi, select) + (dot_tn(mid, select) + dot_tn(low, select))
    win0_ref[...] = back[:, :LANES]
    win1_ref[...] = back[:, LANES:]
    kern = [gathered(win0_ref, win1_ref, i, 1) for i in range(NGLL)]
    row = lax.broadcasted_iota(jnp.int32, (8, LANES), 0)
    inner = (row >= 3) & (row < 7)
    tiles = []
    for t in range(9):
        kern[0][t] = kern[0][t] + pltpu.roll(kern[4][t], 1, 0)
        tiles.append(
            jnp.concatenate([jnp.where(inner, kern[i][t], pltpu.roll(kern[i + 1][t], 4, 0)) for i in (0, 2)], axis=0)
        )
    lane16 = lax.broadcasted_iota(jnp.int32, (16, LANES), 1)
    for base, step in ((0, 1), (9, PZ)):
        total = None
        for tap in range(9):
            moved = shifted(tiles, step * (tap - 4), lane16) if tap != 4 else tiles
            scaled = [v * cross_ref[base + tap : base + tap + 1, t * LANES : (t + 1) * LANES] for t, v in enumerate(moved)]
            total = scaled if total is None else [a + b for a, b in zip(total, scaled)]
        tiles = total
    for t in range(9):
        kern_out_ref[:, t * LANES : (t + 1) * LANES] = tiles[t]


def gathered(win0_ref, win1_ref, i, h):
    lane = lax.broadcasted_iota(jnp.int32, (8, LANES), 1)
    tiles = [None] * 9
    for ey in range(EY):
        rows = pl.ds(i * LANES + h * 64 + ey, 8, stride=8)
        a, b = win0_ref[rows, :], win1_ref[rows, :]
        if ey:
            a, b = pltpu.roll(a, 4 * ey, 1), pltpu.roll(b, 4 * ey, 1)
            keep = lane >= 4 * ey
            a, b = jnp.where(keep, a, 0.0), jnp.where(keep, b, a)
        tiles[ey] = a if ey == 0 else tiles[ey] + a
        tiles[ey + 1] = b
    return tiles


def force_kernel(
    elem_ref, flux_ref, fwd_ref, fwd_speed_ref, adj_ref, adj_speed_ref, mass_ref, after_ref,
    fwd_out_ref, fwd_speed_out_ref, adj_out_ref, adj_speed_out_ref,
    term_ref, win0_ref, win1_ref, plane_ref, line_ref,
):
    for axis, line in lines():
        grads = derive([at(elem_ref, *c) for c in line])
        back = derive_back([g * flux_at(flux_ref, *c) for g, c in zip(grads, line)])
        for n, c in enumerate(line):
            put(term_ref, *c, back[n] if axis == 0 else at(term_ref, *c) + back[n])
    select = selector()
    hi, mid, low = split3(term_ref[...])
    back = dot_tn(hi, select) + (dot_tn(mid, select) + dot_tn(low, select))
    win0_ref[...] = back[:, :LANES]
    win1_ref[...] = back[:, LANES:]
    lane9 = lax.broadcasted_iota(jnp.int32, (9, LANES), 1)
    for i in range(NGLL):
        for h in range(2):
            for t, tile in enumerate(gathered(win0_ref, win1_ref, i, h)):
                plane_ref[i * 144 + t * 16 + 8 * h : i * 144 + t * 16 + 8 * h + 8, :] = tile
    line_ref[...] = jnp.zeros(line_ref.shape, F32)
    for f in range(2):
        for x in range(PXU):
            r0, off = divmod(PYZ * x, LANES)
            flat = plane_ref[pl.ds((x % 4) * 144 + 5 * f + x // 4 + 1, 9, stride=16), :]
            if x % 4 == 0:
                flat = flat + plane_ref[pl.ds(4 * 144 + 5 * f + x // 4, 9, stride=16), :]
            if off:
                flat = pltpu.roll(flat, off, 1)
                spill = jnp.where(lane9 < off, flat, 0.0)
                flat = jnp.where(lane9 < off, 0.0, flat)
            line_ref[f, r0 : r0 + 9, :] = line_ref[f, r0 : r0 + 9, :] + flat
            if off:
                line_ref[f, r0 + 1 : r0 + 10, :] = line_ref[f, r0 + 1 : r0 + 10, :] + spill

    def step(lo, hi, force):
        shape = (hi - lo) // force[0].shape[1], force[0].shape[1]
        take = lambda ref: ref[0:1, lo:hi].reshape(shape)
        scale = TIME_STEP * mass_ref[0:1, lo:hi].reshape(shape)
        speed = take(fwd_speed_ref) + scale * force[0]
        fwd_speed_out_ref[0:1, lo:hi] = speed.reshape(1, hi - lo)
        fwd_out_ref[0:1, lo:hi] = (take(fwd_ref) - TIME_STEP * speed).reshape(1, hi - lo)
        speed = take(adj_speed_ref) - scale * force[1]
        adj_speed_out_ref[0:1, lo:hi] = speed.reshape(1, hi - lo)
        adj_out_ref[0:1, lo:hi] = (take(adj_ref) + TIME_STEP * speed).reshape(1, hi - lo)

    for r in range(0, 136, 8):
        step(r * LANES, (r + 8) * LANES, [line_ref[f, r : r + 8, :] for f in range(2)])
    step(NPTS - 16, NPTS, [line_ref[f, 136:137, 0:16] for f in range(2)])


def band_kernel(parity_ref, own_ref, first_ref, second_ref, band_ref, out_ref):
    flat = jnp.concatenate([own_ref[...], first_ref[...], second_ref[...]], axis=0)
    k1 = flat.astype(BF16)
    rest = flat - k1.astype(F32)
    k2 = rest.astype(BF16)
    k3 = (rest - k2.astype(F32)).astype(BF16)
    stacked = jnp.concatenate([k1, k2, k3, k1, k2, k1], axis=0)
    band = band_ref[parity_ref[0]]
    out_ref[...] = jnp.dot(band, stacked, preferred_element_type=F32)[:, :PYZ]


def on_device(
    forward_displacement,
    forward_velocity,
    adjoint_displacement,
    adjoint_velocity,
    inverse_mass,
    shear_modulus,
    connectivity,
    face_points,
    element_count,
):
    events = lax.axis_size("event")
    cuts = lax.axis_size("cuts")
    parity = (lax.axis_index("cuts") % 2).astype(jnp.int32).reshape(1)
    pairs_first = [(i, (i - 1 if i % 2 == 0 else i + 1) % cuts) for i in range(cuts)]
    pairs_second = [(i, (i + 1 if i % 2 == 0 else i - 1) % cuts) for i in range(cuts)]

    vmem = pl.BlockSpec(memory_space=pltpu.VMEM)
    smem = pl.BlockSpec(memory_space=pltpu.SMEM)
    anywhere = pl.BlockSpec(memory_space=pl.ANY)
    message = jax.ShapeDtypeStruct((144, LANES), F32)
    conn = connectivity[0:8]
    first, second = pl.pallas_call(
        pack_kernel,
        out_shape=[message, message],
        in_specs=[smem, smem, vmem, vmem, vmem, vmem],
        scratch_shapes=[pltpu.VMEM((2, 80, LANES), F32)],
        cost_estimate=pl.CostEstimate(flops=100000000, bytes_accessed=1000000, transcendentals=0),
        name="pack",
    )(parity, element_count, conn, shear_modulus, forward_displacement, adjoint_displacement)
    first = lax.ppermute(first, "cuts", pairs_first)
    second = lax.ppermute(second, "cuts", pairs_second)

    flux = pl.pallas_call(
        flux_kernel,
        out_shape=jax.ShapeDtypeStruct((1000, LANES), F32),
        in_specs=[smem, vmem, vmem],
        cost_estimate=pl.CostEstimate(flops=200000000, bytes_accessed=2000000, transcendentals=0),
        name="flux",
    )(element_count, conn, shear_modulus)

    elem_shape = (200, 5 * LANES)
    kern, elem, flux = pl.pallas_call(
        kernel_kernel,
        out_shape=[
            jax.ShapeDtypeStruct((16, 9 * LANES), F32),
            jax.ShapeDtypeStruct(elem_shape, F32),
            jax.ShapeDtypeStruct((1000, LANES), F32),
        ],
        in_specs=[smem] + [vmem] * 6,
        scratch_shapes=[
            pltpu.VMEM((2 * ROWS, LANES), F32),
            pltpu.VMEM((224, LANES), F32),
            pltpu.VMEM((5 * 144, LANES), F32),
            pltpu.VMEM((5 * LANES, LANES), F32),
            pltpu.VMEM((5 * LANES, LANES), F32),
            pltpu.VMEM(elem_shape, F32),
        ],
        cost_estimate=pl.CostEstimate(flops=400000000, bytes_accessed=4000000, transcendentals=0),
        name="kernel_term",
    )(parity, forward_displacement, adjoint_displacement, first, second, flux, jnp.asarray(cross_table()))

    if events == 2:
        kern = kern + lax.ppermute(kern, "event", [(0, 1), (1, 0)])
    elif events > 2:
        kern = lax.psum(kern, "event")
    kern_first = lax.ppermute(kern, "cuts", pairs_first)
    kern_second = lax.ppermute(kern, "cuts", pairs_second)

    points = jax.ShapeDtypeStruct((1, NPTS), F32)
    outs = pl.pallas_call(
        force_kernel,
        out_shape=[points] * 4,
        in_specs=[vmem] * 7 + [anywhere],
        scratch_shapes=[
            pltpu.VMEM(elem_shape, F32),
            pltpu.VMEM((5 * LANES, LANES), F32),
            pltpu.VMEM((5 * LANES, LANES), F32),
            pltpu.VMEM((5 * 144, LANES), F32),
            pltpu.VMEM((2, ROWS, LANES), F32),
        ],
        cost_estimate=pl.CostEstimate(flops=400000000, bytes_accessed=4000000, transcendentals=0),
        name="forces",
    )(
        elem,
        flux,
        forward_displacement,
        forward_velocity,
        adjoint_displacement,
        adjoint_velocity,
        inverse_mass[None, :],
        kern,
    )
    shear_kernel = pl.pallas_call(
        band_kernel,
        out_shape=jax.ShapeDtypeStruct((PXU, PYZ), F32),
        in_specs=[smem] + [vmem] * 4,
        cost_estimate=pl.CostEstimate(flops=20000000, bytes_accessed=400000, transcendentals=0),
        name="band",
    )(parity, kern, kern_first, kern_second, jnp.asarray(band_table()))
    return (*outs, shear_kernel)


def solution(mesh):
    in_specs = (
        P("event", "cuts"),
        P("event", "cuts"),
        P("event", "cuts"),
        P("event", "cuts"),
        P("cuts"),
        P(None, "cuts"),
        P(None, "cuts"),
        P("cuts", None),
        P("cuts"),
    )
    out_specs = (
        P("event", "cuts"),
        P("event", "cuts"),
        P("event", "cuts"),
        P("event", "cuts"),
        P("cuts", None),
    )
    return jax.shard_map(on_device, mesh=mesh, in_specs=in_specs, out_specs=out_specs, check_vma=False)
```

```python
import numpy as np
import jax
import jax.numpy as jnp
import ml_dtypes
from jax import lax
from jax.experimental import pallas as pl
from jax.experimental.pallas import tpu as pltpu
from jax.sharding import PartitionSpec as P

NGLL = 5
EX, EY, EZ = 4, 8, 8
PXU = 16
PY = 33
PZ = 33
PYZ = 1089
NPTS = 17424
LANES = 128
ROWS = 144
TIME_STEP = 0.02
F32 = jnp.float32
BF16 = jnp.bfloat16


def gll():
    nodes = np.array([-1.0, -np.sqrt(3.0 / 7.0), 0.0, np.sqrt(3.0 / 7.0), 1.0])
    bary = np.array([1.0 / np.prod([nodes[r] - nodes[c] for c in range(5) if c != r]) for r in range(5)])
    d = np.zeros((5, 5))
    for r in range(5):
        for c in range(5):
            if c != r:
                d[r, c] = bary[c] / bary[r] / (nodes[r] - nodes[c])
        d[r, r] = -np.sum(d[r])
    return d


DERIV = gll()


def split_np(x):
    x = np.asarray(x, np.float32)
    parts = []
    for _ in range(3):
        p = x.astype(ml_dtypes.bfloat16)
        parts.append(p)
        x = x - p.astype(np.float32)
    return parts


ROW_PLANE = np.array([5, 9, 13, 0, 4, 8, 12, 1, 7, 11, 15, 2, 6, 10, 14, 3])


def band_table():
    offsets = np.arange(-PXU, PXU + 1)
    w = lambda d: np.exp(-d * d / (2.0 * (PXU / 4.0) ** 2))
    total = w(offsets.astype(np.float64)).sum()
    out = []
    for first in (-PXU, PXU):
        source = np.concatenate([ROW_PLANE, ROW_PLANE + first, ROW_PLANE - first])
        spread = np.arange(PXU)[:, None] - source[None, :]
        band = w(spread.astype(np.float64)) * (np.abs(spread) <= PXU) / total
        b1, b2, b3 = split_np(band)
        out.append(np.concatenate([b1, b1, b1, b2, b2, b3], axis=1))
    return np.stack(out)


def cross_table():
    off = np.arange(-4, 5)
    k = np.exp(-off * off / (2.0 * 1.5 * 1.5))
    point = np.arange(33)
    inside = ((point[None, :] + off[:, None]) >= 0) & ((point[None, :] + off[:, None]) < 33)
    taps = k[:, None] * inside
    taps = taps / taps.sum(axis=0, keepdims=True)
    out = np.zeros((24, 1152), np.float32)
    out[0:9, :PYZ] = np.tile(taps, (1, PY))
    out[9:18, :PYZ] = np.repeat(taps, PZ, axis=1)
    return out


def split3(x):
    hi = x.astype(BF16)
    rest = x - hi.astype(F32)
    mid = rest.astype(BF16)
    low = (rest - mid.astype(F32)).astype(BF16)
    return hi, mid, low


def dot_nt(a, b):
    return lax.dot_general(a, b, (((1,), (1,)), ((), ())), preferred_element_type=F32)


def dot_tn(a, b):
    return lax.dot_general(a, b, (((0,), (0,)), ((), ())), preferred_element_type=F32)


def selector():
    column = lax.broadcasted_iota(jnp.int32, (8, 256), 1)
    row = lax.broadcasted_iota(jnp.int32, (8, 256), 0)
    base = column - 4 * row
    blocks = [jnp.where(base == j * PZ + k, 1.0, 0.0) for j in range(5) for k in range(5)]
    return jnp.concatenate(blocks, axis=0).astype(BF16)


def slot_elements(conn_ref, count_ref):
    point = conn_ref[0:1, :].astype(F32)
    x = jnp.floor((point + 0.5) * (1.0 / PYZ))
    rest = point - x * PYZ
    y = jnp.floor((rest + 0.5) * (1.0 / PZ))
    z = rest - y * PZ
    code = (8.0 * z + y + 0.25 * x).astype(jnp.int32)
    slot = lax.broadcasted_iota(jnp.int32, (1, 256), 1)
    return jnp.where(slot < count_ref[0], code, -1000)


def weighted(shear_ref):
    q = lax.broadcasted_iota(jnp.int32, (125, 256), 0)
    weight = None
    for digit in (q // 25, (q // 5) % 5, q % 5):
        w = jnp.where(digit == 2, 32.0 / 45.0, jnp.where((digit == 0) | (digit == 4), 0.1, 49.0 / 90.0))
        weight = w if weight is None else weight * w
    return split3(shear_ref[...] * weight)


def moved_by(parts, pick):
    hi, mid, low = parts
    return dot_nt(hi, pick) + (dot_nt(mid, pick) + dot_nt(low, pick))


def fetch(sem, *pairs):
    copies = [pltpu.make_async_copy(src, dst, sem.at[n]) for n, (src, dst) in enumerate(pairs)]
    for c in copies:
        c.start()
    return copies


def pack_kernel(
    parity_ref, count_ref, conn_hbm, shear_hbm, fwd_hbm, adj_hbm,
    first_ref, second_ref,
    conn_ref, shear_ref, fwd_ref, adj_ref, line_ref, sem,
):
    copies = fetch(
        sem, (conn_hbm.at[0:8], conn_ref), (shear_hbm, shear_ref), (fwd_hbm, fwd_ref), (adj_hbm, adj_ref)
    )
    copies[0].wait()
    code = slot_elements(conn_ref, count_ref)
    lane = lax.broadcasted_iota(jnp.int32, (LANES, 256), 0) & 63
    pick = jnp.where(code == (lane >> 3) * 32 + (lane & 7) * 4 + 3, 1.0, 0.0).astype(BF16)
    copies[1].wait()
    flux = moved_by(weighted(shear_ref), pick)
    flux = jnp.concatenate([flux, jnp.zeros((3, LANES), F32)], axis=0)
    low = lax.broadcasted_iota(jnp.int32, (64, LANES), 1) < 64
    flux = jnp.where(low, flux[0:64], flux[64:128])
    for f, ref in enumerate((fwd_ref, adj_ref)):
        copies[2 + f].wait()
        for r in (0, 8, 16, 24, 32):
            line_ref[f, r : r + 8, :] = ref[0:1, r * LANES : (r + 8) * LANES].reshape(8, LANES)
        base = 102 * LANES
        for r in (0, 8, 16, 24):
            at = base + r * LANES
            line_ref[f, 40 + r : 48 + r, :] = ref[0:1, at : at + 8 * LANES].reshape(8, LANES)
        at = base + 32 * LANES
        line_ref[f, 72:74, :] = ref[0:1, at : at + 2 * LANES].reshape(2, LANES)
        line_ref[f, 74:80, :] = jnp.zeros((6, LANES), F32)
        line_ref[f, 74:75, 0:16] = ref[0:1, at + 2 * LANES : at + 2 * LANES + 16]
    odd = parity_ref[0] == 1
    for ref, flip in ((first_ref, odd), (second_ref, jnp.logical_not(odd))):
        for f in range(2):
            ref[40 * f : 40 * f + 40, :] = jnp.where(flip, line_ref[f, 40:80, :], line_ref[f, 0:40, :])
        ref[80:144, :] = flux


def flux_kernel(count_ref, conn_hbm, shear_hbm, flux_ref, conn_ref, shear_ref, sem):
    copies = fetch(sem, (conn_hbm.at[0:8], conn_ref), (shear_hbm, shear_ref))
    copies[0].wait()
    code = slot_elements(conn_ref, count_ref)
    lane = lax.broadcasted_iota(jnp.int32, (LANES, 256), 0)
    layer = lane >> 3
    layer = jnp.where(layer >= 10, layer - 10, jnp.where(layer >= 5, layer - 5, layer)) - 1
    member = jnp.where((layer >= 0) & (layer < 4), (lane & 7) * 4 + layer, -1)
    member = jnp.where(member >= 0, member, 5000)
    pick = jnp.concatenate([jnp.where(code - member == ez * 32, 1.0, 0.0).astype(BF16) for ez in range(EZ)], axis=0)
    copies[1].wait()
    moved = moved_by(weighted(shear_ref), pick)
    for ez in range(EZ):
        flux_ref[pl.ds(ez, 125, stride=8), :] = moved[:, ez * LANES : (ez + 1) * LANES]


def derive(e):
    d = DERIV
    s0, s1 = e[0] + e[4], e[1] + e[3]
    d0, d1 = e[0] - e[4], e[1] - e[3]
    out = [None] * 5
    for i in (0, 1):
        even = float((d[i, 0] - d[i, 4]) / 2) * d0 + float((d[i, 1] - d[i, 3]) / 2) * d1
        odd = float((d[i, 0] + d[i, 4]) / 2) * s0 + float((d[i, 1] + d[i, 3]) / 2) * s1 + float(d[i, 2]) * e[2]
        out[i] = odd + even
        out[4 - i] = even - odd
    out[2] = float(d[2, 0]) * d0 + float(d[2, 1]) * d1
    return out


def derive_back(t):
    d = DERIV
    s0, s1 = t[0] + t[4], t[1] + t[3]
    d0, d1 = t[0] - t[4], t[1] - t[3]
    out = [None] * 5
    for i in (0, 1):
        even = float((d[0, i] - d[4, i]) / 2) * d0 + float((d[1, i] - d[3, i]) / 2) * d1
        odd = float((d[0, i] + d[4, i]) / 2) * s0 + float((d[1, i] + d[3, i]) / 2) * s1 + float(d[2, i]) * t[2]
        out[i] = odd + even
        out[4 - i] = even - odd
    out[2] = float(d[0, 2]) * d0 + float(d[1, 2]) * d1
    return out


def shifted(tiles, distance, lane):
    skip, part = divmod(distance, LANES)
    if part == 0:
        moved = tiles
        pick = None
    else:
        moved = [pltpu.roll(t, LANES - part, 1) for t in tiles]
        pick = lane < LANES - part
    n = len(tiles)
    out = []
    for i in range(n):
        a = moved[(i + skip) % n]
        b = moved[(i + skip + 1) % n]
        out.append(a if pick is None else jnp.where(pick, a, b))
    return out


def at(ref, i, j, k):
    r = (j * 5 + k) * 8
    return ref[r : r + 8, i * LANES : (i + 1) * LANES]


def put(ref, i, j, k, value):
    r = (j * 5 + k) * 8
    ref[r : r + 8, i * LANES : (i + 1) * LANES] = value


def flux_at(ref, i, j, k):
    r = ((i * 5 + j) * 5 + k) * 8
    return ref[r : r + 8, :]


def lines():
    for axis in range(3):
        for p in range(5):
            for q in range(5):
                yield axis, [((l, p, q), (p, l, q), (p, q, l))[axis] for l in range(5)]


def plane_of(ref, start, row):
    r0, off = divmod(start, LANES)
    lane9 = lax.broadcasted_iota(jnp.int32, (9, LANES), 1)
    flat = ref[row + r0 : row + r0 + 9, :]
    if off:
        flat = jnp.where(
            lane9 < LANES - off,
            pltpu.roll(flat, LANES - off, 1),
            pltpu.roll(ref[row + r0 + 1 : row + r0 + 10, :], LANES - off, 1),
        )
    return flat


def kernel_kernel(
    parity_ref, fwd_hbm, adj_hbm, first_ref, second_ref, flux_in_ref, cross_hbm,
    kern_out_ref, elem_ref, flux_ref,
    fwd_ref, adj_ref, cross_ref, own_ref, near_ref, plane_ref, win0_ref, win1_ref, kern_ref, sem,
):
    copies = fetch(sem, (fwd_hbm, fwd_ref), (adj_hbm, adj_ref), (cross_hbm, cross_ref))
    lane = lax.broadcasted_iota(jnp.int32, (8, LANES), 1)
    even = parity_ref[0] == 0
    for f, ref in enumerate((fwd_ref, adj_ref)):
        copies[f].wait()
        for r in range(0, 136, 8):
            own_ref[ROWS * f + r : ROWS * f + r + 8, :] = ref[0:1, r * LANES : (r + 8) * LANES].reshape(8, LANES)
        own_ref[ROWS * f + 136 : ROWS * f + 144, :] = jnp.zeros((8, LANES), F32)
        own_ref[ROWS * f + 136 : ROWS * f + 137, 0:16] = ref[0:1, NPTS - 16 : NPTS]
    near_ref[0:144, :] = jnp.where(even, first_ref[...], second_ref[...])
    near_ref[144:224, :] = jnp.where(even, second_ref[0:80, :], first_ref[0:80, :])

    m = lax.broadcasted_iota(jnp.int32, (LANES, LANES), 0)
    n = lax.broadcasted_iota(jnp.int32, (LANES, LANES), 1) & 63
    layer = m >> 3
    base = jnp.where((layer == 0) | (layer == 5) | (layer == 10), n - (m & 7), -1)
    pick = jnp.concatenate([jnp.where(base == ez * 8, 1.0, 0.0).astype(BF16) for ez in range(EZ)], axis=0)
    low = lax.broadcasted_iota(jnp.int32, (64, LANES), 1) < 64
    packed = near_ref[80:144, :]
    packed = jnp.concatenate([jnp.where(low, packed, 0.0), jnp.where(low, 0.0, packed)], axis=0)
    extra = moved_by(split3(packed), pick)
    for ez in range(EZ):
        rows = pl.ds(ez, 125, stride=8)
        flux_ref[rows, :] = flux_in_ref[rows, :] + extra[0:125, ez * LANES : (ez + 1) * LANES]

    plane_ref[...] = jnp.zeros(plane_ref.shape, F32)
    for x in range(-4, PXU + 1):
        for f in range(2):
            if x < 0:
                flat = plane_of(near_ref, 12 + PYZ * (x + 4), 40 * f)
            elif x < PXU:
                flat = plane_of(own_ref, PYZ * x, ROWS * f)
            else:
                flat = plane_of(near_ref, 0, 144 + 40 * f)
            places = []
            if x < PXU:
                places.append((x % 4, x // 4 + 1))
            if x % 4 == 0 and x >= 0:
                places.append((4, x // 4))
            for i, layer in places:
                for r in (layer, 10 + layer) if f == 0 else (5 + layer,):
                    plane_ref[pl.ds(i * 144 + r, 9, stride=16), :] = flat
    for i in range(NGLL):
        for h in range(2):
            tiles = [plane_ref[i * 144 + t * 16 + 8 * h : i * 144 + t * 16 + 8 * h + 8, :] for t in range(9)]
            for ey in range(EY):
                near = [tiles[ey], tiles[ey + 1], tiles[min(ey + 2, 8)]]
                if ey:
                    near = [pltpu.roll(t, LANES - 4 * ey, 1) for t in near]
                    keep = lane < LANES - 4 * ey
                    near = [jnp.where(keep, near[0], near[1]), jnp.where(keep, near[1], near[2])]
                rows = pl.ds(i * LANES + h * 64 + ey, 8, stride=8)
                win0_ref[rows, :] = near[0]
                win1_ref[rows, :] = near[1]
    select = selector()
    hi, mid, low = split3(jnp.concatenate([win0_ref[...], win1_ref[...]], axis=1))
    elem_ref[...] = dot_nt(select, hi) + (dot_nt(select, mid) + dot_nt(select, low))

    for axis, line in lines():
        grads = derive([at(elem_ref, *c) for c in line])
        for n, c in enumerate(line):
            prod = grads[n] * pltpu.roll(grads[n], 40, 1)
            if axis > 0:
                prod = at(kern_ref, *c) + prod
            if axis == 2:
                prod = -prod * flux_at(flux_ref, *c)
            put(kern_ref, *c, prod)
    hi, mid, low = split3(kern_ref[...])
    back = dot_tn(hi, select) + (dot_tn(mid, select) + dot_tn(low, select))
    win0_ref[...] = back[:, :LANES]
    win1_ref[...] = back[:, LANES:]
    kern = [gathered(win0_ref, win1_ref, i, 1) for i in range(NGLL)]
    row = lax.broadcasted_iota(jnp.int32, (8, LANES), 0)
    inner = (row >= 3) & (row < 7)
    tiles = []
    for t in range(9):
        kern[0][t] = kern[0][t] + pltpu.roll(kern[4][t], 1, 0)
        tiles.append(
            jnp.concatenate([jnp.where(inner, kern[i][t], pltpu.roll(kern[i + 1][t], 4, 0)) for i in (0, 2)], axis=0)
        )
    lane16 = lax.broadcasted_iota(jnp.int32, (16, LANES), 1)
    copies[2].wait()
    for base, step in ((0, 1), (9, PZ)):
        total = None
        for tap in range(9):
            moved = shifted(tiles, step * (tap - 4), lane16) if tap != 4 else tiles
            scaled = [v * cross_ref[base + tap : base + tap + 1, t * LANES : (t + 1) * LANES] for t, v in enumerate(moved)]
            total = scaled if total is None else [a + b for a, b in zip(total, scaled)]
        tiles = total
    for t in range(9):
        kern_out_ref[:, t * LANES : (t + 1) * LANES] = tiles[t]


def gathered(win0_ref, win1_ref, i, h):
    lane = lax.broadcasted_iota(jnp.int32, (8, LANES), 1)
    tiles = [None] * 9
    for ey in range(EY):
        rows = pl.ds(i * LANES + h * 64 + ey, 8, stride=8)
        a, b = win0_ref[rows, :], win1_ref[rows, :]
        if ey:
            a, b = pltpu.roll(a, 4 * ey, 1), pltpu.roll(b, 4 * ey, 1)
            keep = lane >= 4 * ey
            a, b = jnp.where(keep, a, 0.0), jnp.where(keep, b, a)
        tiles[ey] = a if ey == 0 else tiles[ey] + a
        tiles[ey + 1] = b
    return tiles


def force_kernel(elem_ref, flux_ref, win0_ref, win1_ref, term_ref):
    for axis, line in lines():
        grads = derive([at(elem_ref, *c) for c in line])
        back = derive_back([g * flux_at(flux_ref, *c) for g, c in zip(grads, line)])
        for n, c in enumerate(line):
            put(term_ref, *c, back[n] if axis == 0 else at(term_ref, *c) + back[n])
    select = selector()
    hi, mid, low = split3(term_ref[...])
    back = dot_tn(hi, select) + (dot_tn(mid, select) + dot_tn(low, select))
    win0_ref[...] = back[:, :LANES]
    win1_ref[...] = back[:, LANES:]


def step_kernel(
    win0_ref, win1_ref, fwd_hbm, fwd_speed_hbm, adj_hbm, adj_speed_hbm, mass_hbm, after_ref,
    fwd_out_ref, fwd_speed_out_ref, adj_out_ref, adj_speed_out_ref,
    fwd_ref, fwd_speed_ref, adj_ref, adj_speed_ref, mass_ref, plane_ref, line_ref, sem,
):
    copies = fetch(
        sem,
        (fwd_hbm, fwd_ref),
        (fwd_speed_hbm, fwd_speed_ref),
        (adj_hbm, adj_ref),
        (adj_speed_hbm, adj_speed_ref),
        (mass_hbm, mass_ref),
    )
    lane9 = lax.broadcasted_iota(jnp.int32, (9, LANES), 1)
    for i in range(NGLL):
        for h in range(2):
            for t, tile in enumerate(gathered(win0_ref, win1_ref, i, h)):
                plane_ref[i * 144 + t * 16 + 8 * h : i * 144 + t * 16 + 8 * h + 8, :] = tile
    line_ref[...] = jnp.zeros(line_ref.shape, F32)
    for f in range(2):
        for x in range(PXU):
            r0, off = divmod(PYZ * x, LANES)
            flat = plane_ref[pl.ds((x % 4) * 144 + 5 * f + x // 4 + 1, 9, stride=16), :]
            if x % 4 == 0:
                flat = flat + plane_ref[pl.ds(4 * 144 + 5 * f + x // 4, 9, stride=16), :]
            if off:
                flat = pltpu.roll(flat, off, 1)
                spill = jnp.where(lane9 < off, flat, 0.0)
                flat = jnp.where(lane9 < off, 0.0, flat)
            line_ref[f, r0 : r0 + 9, :] = line_ref[f, r0 : r0 + 9, :] + flat
            if off:
                line_ref[f, r0 + 1 : r0 + 10, :] = line_ref[f, r0 + 1 : r0 + 10, :] + spill

    def step(lo, hi, force):
        shape = (hi - lo) // force[0].shape[1], force[0].shape[1]
        take = lambda ref: ref[0:1, lo:hi].reshape(shape)
        scale = TIME_STEP * mass_ref[lo:hi].reshape(shape)
        speed = take(fwd_speed_ref) + scale * force[0]
        fwd_speed_out_ref[0:1, lo:hi] = speed.reshape(1, hi - lo)
        fwd_out_ref[0:1, lo:hi] = (take(fwd_ref) - TIME_STEP * speed).reshape(1, hi - lo)
        speed = take(adj_speed_ref) - scale * force[1]
        adj_speed_out_ref[0:1, lo:hi] = speed.reshape(1, hi - lo)
        adj_out_ref[0:1, lo:hi] = (take(adj_ref) + TIME_STEP * speed).reshape(1, hi - lo)

    for c in copies:
        c.wait()
    for r in range(0, 136, 8):
        step(r * LANES, (r + 8) * LANES, [line_ref[f, r : r + 8, :] for f in range(2)])
    step(NPTS - 16, NPTS, [line_ref[f, 136:137, 0:16] for f in range(2)])


def band_kernel(parity_ref, own_ref, first_ref, second_ref, band_ref, out_ref):
    flat = jnp.concatenate([own_ref[...], first_ref[...], second_ref[...]], axis=0)
    k1 = flat.astype(BF16)
    rest = flat - k1.astype(F32)
    k2 = rest.astype(BF16)
    k3 = (rest - k2.astype(F32)).astype(BF16)
    stacked = jnp.concatenate([k1, k2, k3, k1, k2, k1], axis=0)
    band = band_ref[parity_ref[0]]
    out_ref[...] = jnp.dot(band, stacked, preferred_element_type=F32)[:, :PYZ]


def on_device(
    forward_displacement,
    forward_velocity,
    adjoint_displacement,
    adjoint_velocity,
    inverse_mass,
    shear_modulus,
    connectivity,
    face_points,
    element_count,
):
    events = lax.axis_size("event")
    cuts = lax.axis_size("cuts")
    parity = (lax.axis_index("cuts") % 2).astype(jnp.int32).reshape(1)
    pairs_first = [(i, (i - 1 if i % 2 == 0 else i + 1) % cuts) for i in range(cuts)]
    pairs_second = [(i, (i + 1 if i % 2 == 0 else i - 1) % cuts) for i in range(cuts)]

    vmem = pl.BlockSpec(memory_space=pltpu.VMEM)
    smem = pl.BlockSpec(memory_space=pltpu.SMEM)
    anywhere = pl.BlockSpec(memory_space=pl.ANY)

    def held(block):
        return pltpu.with_memory_space_constraint(block, pltpu.VMEM)

    def in_hbm(block):
        return pltpu.with_memory_space_constraint(block, pltpu.HBM)

    def cost(flops):
        return pl.CostEstimate(flops=flops, bytes_accessed=1000000, transcendentals=0)

    dma = pltpu.SemaphoreType.DMA
    point_row = pltpu.VMEM((1, NPTS), F32)
    conn_rows = pltpu.VMEM((8, 256), jnp.int32)
    shear_block = pltpu.VMEM((125, 256), F32)
    elem_block = pltpu.VMEM((200, 5 * LANES), F32)
    flux_block = pltpu.VMEM((1000, LANES), F32)
    window = pltpu.VMEM((5 * LANES, LANES), F32)
    message = pltpu.VMEM((144, LANES), F32)
    fields = (in_hbm(forward_displacement), in_hbm(adjoint_displacement))
    conn, shear = in_hbm(connectivity), in_hbm(shear_modulus)
    first, second = pl.pallas_call(
        pack_kernel,
        out_shape=[message, message],
        in_specs=[smem, smem] + [anywhere] * 4,
        scratch_shapes=[conn_rows, shear_block, point_row, point_row, pltpu.VMEM((2, 80, LANES), F32), dma((4,))],
        cost_estimate=cost(100000000),
        name="pack",
    )(parity, element_count, conn, shear, *fields)
    first = lax.ppermute(first, "cuts", pairs_first)
    second = lax.ppermute(second, "cuts", pairs_second)

    flux = pl.pallas_call(
        flux_kernel,
        out_shape=flux_block,
        in_specs=[smem] + [anywhere] * 2,
        scratch_shapes=[conn_rows, shear_block, dma((2,))],
        cost_estimate=cost(200000000),
        name="flux",
    )(element_count, conn, shear)

    kern, elem, flux = pl.pallas_call(
        kernel_kernel,
        out_shape=[pltpu.VMEM((16, 9 * LANES), F32), elem_block, flux_block],
        in_specs=[smem, anywhere, anywhere, vmem, vmem, vmem, anywhere],
        scratch_shapes=[
            point_row,
            point_row,
            pltpu.VMEM((24, 9 * LANES), F32),
            pltpu.VMEM((2 * ROWS, LANES), F32),
            pltpu.VMEM((224, LANES), F32),
            pltpu.VMEM((5 * 144, LANES), F32),
            window,
            window,
            elem_block,
            dma((3,)),
        ],
        cost_estimate=cost(400000000),
        name="kernel_term",
    )(parity, *fields, held(first), held(second), held(flux), in_hbm(jnp.asarray(cross_table())))

    win0, win1 = pl.pallas_call(
        force_kernel,
        out_shape=[window, window],
        in_specs=[vmem, vmem],
        scratch_shapes=[elem_block],
        cost_estimate=cost(200000000),
        name="forces",
    )(held(elem), held(flux))

    if events == 2:
        kern = kern + lax.ppermute(kern, "event", [(0, 1), (1, 0)])
    elif events > 2:
        kern = lax.psum(kern, "event")
    kern_first = lax.ppermute(kern, "cuts", pairs_first)
    kern_second = lax.ppermute(kern, "cuts", pairs_second)

    points = jax.ShapeDtypeStruct((1, NPTS), F32)
    outs = pl.pallas_call(
        step_kernel,
        out_shape=[points] * 4,
        in_specs=[vmem] * 2 + [anywhere] * 5 + [vmem],
        scratch_shapes=[point_row] * 4
        + [pltpu.VMEM((NPTS,), F32), pltpu.VMEM((5 * 144, LANES), F32), pltpu.VMEM((2, ROWS, LANES), F32), dma((5,))],
        cost_estimate=cost(200000000),
        name="step",
    )(
        held(win0),
        held(win1),
        fields[0],
        in_hbm(forward_velocity),
        fields[1],
        in_hbm(adjoint_velocity),
        in_hbm(inverse_mass),
        held(kern),
    )
    shear_kernel = pl.pallas_call(
        band_kernel,
        out_shape=jax.ShapeDtypeStruct((PXU, PYZ), F32),
        in_specs=[smem] + [vmem] * 4,
        cost_estimate=cost(20000000),
        name="band",
    )(parity, held(kern), held(kern_first), held(kern_second), held(jnp.asarray(band_table())))
    return (*outs, shear_kernel)


def solution(mesh):
    in_specs = (
        P("event", "cuts"),
        P("event", "cuts"),
        P("event", "cuts"),
        P("event", "cuts"),
        P("cuts"),
        P(None, "cuts"),
        P(None, "cuts"),
        P("cuts", None),
        P("cuts"),
    )
    out_specs = (
        P("event", "cuts"),
        P("event", "cuts"),
        P("event", "cuts"),
        P("event", "cuts"),
        P("cuts", None),
    )
    return jax.shard_map(on_device, mesh=mesh, in_specs=in_specs, out_specs=out_specs, check_vma=False)
```

```python
import numpy as np
import jax
import jax.numpy as jnp
import ml_dtypes
from jax import lax
from jax.experimental import pallas as pl
from jax.experimental.pallas import tpu as pltpu
from jax.sharding import PartitionSpec as P

NGLL = 5
EX, EY, EZ = 4, 8, 8
PXU = 16
PY = 33
PZ = 33
PYZ = 1089
NPTS = 17424
LANES = 128
ROWS = 144
TIME_STEP = 0.02
F32 = jnp.float32
BF16 = jnp.bfloat16


def gll():
    nodes = np.array([-1.0, -np.sqrt(3.0 / 7.0), 0.0, np.sqrt(3.0 / 7.0), 1.0])
    bary = np.array([1.0 / np.prod([nodes[r] - nodes[c] for c in range(5) if c != r]) for r in range(5)])
    d = np.zeros((5, 5))
    for r in range(5):
        for c in range(5):
            if c != r:
                d[r, c] = bary[c] / bary[r] / (nodes[r] - nodes[c])
        d[r, r] = -np.sum(d[r])
    return d


DERIV = gll()


def split_np(x):
    x = np.asarray(x, np.float32)
    parts = []
    for _ in range(3):
        p = x.astype(ml_dtypes.bfloat16)
        parts.append(p)
        x = x - p.astype(np.float32)
    return parts


ROW_PLANE = np.array([5, 9, 13, 0, 4, 8, 12, 1, 7, 11, 15, 2, 6, 10, 14, 3])


def band_table():
    offsets = np.arange(-PXU, PXU + 1)
    w = lambda d: np.exp(-d * d / (2.0 * (PXU / 4.0) ** 2))
    total = w(offsets.astype(np.float64)).sum()
    out = []
    for first in (-PXU, PXU):
        source = np.concatenate([ROW_PLANE, ROW_PLANE + first, ROW_PLANE - first])
        spread = np.arange(PXU)[:, None] - source[None, :]
        band = w(spread.astype(np.float64)) * (np.abs(spread) <= PXU) / total
        b1, b2, b3 = split_np(band)
        out.append(np.concatenate([b1, b1, b1, b2, b2, b3], axis=1))
    return np.stack(out)


def cross_table():
    off = np.arange(-4, 5)
    k = np.exp(-off * off / (2.0 * 1.5 * 1.5))
    point = np.arange(33)
    inside = ((point[None, :] + off[:, None]) >= 0) & ((point[None, :] + off[:, None]) < 33)
    taps = k[:, None] * inside
    taps = taps / taps.sum(axis=0, keepdims=True)
    out = np.zeros((24, 1152), np.float32)
    out[0:9, :PYZ] = np.tile(taps, (1, PY))
    out[9:18, :PYZ] = np.repeat(taps, PZ, axis=1)
    return out


def split3(x):
    hi = x.astype(BF16)
    rest = x - hi.astype(F32)
    mid = rest.astype(BF16)
    low = (rest - mid.astype(F32)).astype(BF16)
    return hi, mid, low


def dot_nt(a, b):
    return lax.dot_general(a, b, (((1,), (1,)), ((), ())), preferred_element_type=F32)


def dot_tn(a, b):
    return lax.dot_general(a, b, (((0,), (0,)), ((), ())), preferred_element_type=F32)


def selector():
    column = lax.broadcasted_iota(jnp.int32, (8, 256), 1)
    row = lax.broadcasted_iota(jnp.int32, (8, 256), 0)
    base = column - 4 * row
    blocks = [jnp.where(base == j * PZ + k, 1.0, 0.0) for j in range(5) for k in range(5)]
    return jnp.concatenate(blocks, axis=0).astype(BF16)


def slot_elements(conn_ref, count_ref):
    point = conn_ref[0:1, :].astype(F32)
    x = jnp.floor((point + 0.5) * (1.0 / PYZ))
    rest = point - x * PYZ
    y = jnp.floor((rest + 0.5) * (1.0 / PZ))
    z = rest - y * PZ
    code = (8.0 * z + y + 0.25 * x).astype(jnp.int32)
    slot = lax.broadcasted_iota(jnp.int32, (1, 256), 1)
    return jnp.where(slot < count_ref[0], code, -1000)


def weighted(shear_ref):
    q = lax.broadcasted_iota(jnp.int32, (125, 256), 0)
    weight = None
    for digit in (q // 25, (q // 5) % 5, q % 5):
        w = jnp.where(digit == 2, 32.0 / 45.0, jnp.where((digit == 0) | (digit == 4), 0.1, 49.0 / 90.0))
        weight = w if weight is None else weight * w
    return split3(shear_ref[...] * weight)


def moved_by(parts, pick):
    hi, mid, low = parts
    return dot_nt(hi, pick) + (dot_nt(mid, pick) + dot_nt(low, pick))


def fetch(sem, *pairs):
    copies = [pltpu.make_async_copy(src, dst, sem.at[n]) for n, (src, dst) in enumerate(pairs)]
    for c in copies:
        c.start()
    return copies


def pack_kernel(
    count_ref, conn_hbm, shear_hbm, fwd_hbm, adj_hbm,
    right_ref, left_ref,
    conn_ref, shear_ref, fwd_ref, adj_ref, sem,
):
    copies = fetch(
        sem, (conn_hbm.at[0:8], conn_ref), (shear_hbm, shear_ref), (fwd_hbm, fwd_ref), (adj_hbm, adj_ref)
    )
    copies[0].wait()
    code = slot_elements(conn_ref, count_ref)
    lane = lax.broadcasted_iota(jnp.int32, (LANES, 256), 0) & 63
    pick = jnp.where(code == (lane >> 3) * 32 + (lane & 7) * 4 + 3, 1.0, 0.0).astype(BF16)
    copies[1].wait()
    flux = moved_by(weighted(shear_ref), pick)
    flux = jnp.concatenate([flux, jnp.zeros((3, LANES), F32)], axis=0)
    low = lax.broadcasted_iota(jnp.int32, (64, LANES), 1) < 64
    right_ref[80:144, :] = jnp.where(low, flux[0:64], flux[64:128])
    for f, ref in enumerate((fwd_ref, adj_ref)):
        copies[2 + f].wait()
        left_ref[16 * f : 16 * f + 8, :] = ref[0:1, 0 : 8 * LANES].reshape(8, LANES)
        left_ref[16 * f + 8 : 16 * f + 16, :] = ref[0:1, 8 * LANES : 16 * LANES].reshape(8, LANES)
        for r in (0, 8, 16, 24):
            at = (102 + r) * LANES
            right_ref[40 * f + r : 40 * f + r + 8, :] = ref[0:1, at : at + 8 * LANES].reshape(8, LANES)
        at = 134 * LANES
        right_ref[40 * f + 32 : 40 * f + 34, :] = ref[0:1, at : at + 2 * LANES].reshape(2, LANES)
        right_ref[40 * f + 34 : 40 * f + 40, :] = jnp.zeros((6, LANES), F32)
        right_ref[40 * f + 34 : 40 * f + 35, 0:16] = ref[0:1, NPTS - 16 : NPTS]


def flux_kernel(count_ref, conn_hbm, shear_hbm, flux_ref, conn_ref, shear_ref, sem):
    copies = fetch(sem, (conn_hbm.at[0:8], conn_ref), (shear_hbm, shear_ref))
    copies[0].wait()
    code = slot_elements(conn_ref, count_ref)
    lane = lax.broadcasted_iota(jnp.int32, (LANES, 256), 0)
    layer = lane >> 3
    layer = jnp.where(layer >= 10, layer - 10, jnp.where(layer >= 5, layer - 5, layer)) - 1
    member = jnp.where((layer >= 0) & (layer < 4), (lane & 7) * 4 + layer, -1)
    member = jnp.where(member >= 0, member, 5000)
    pick = jnp.concatenate([jnp.where(code - member == ez * 32, 1.0, 0.0).astype(BF16) for ez in range(EZ)], axis=0)
    copies[1].wait()
    moved = moved_by(weighted(shear_ref), pick)
    for ez in range(EZ):
        flux_ref[pl.ds(ez, 125, stride=8), :] = moved[:, ez * LANES : (ez + 1) * LANES]


def derive(e):
    d = DERIV
    s0, s1 = e[0] + e[4], e[1] + e[3]
    d0, d1 = e[0] - e[4], e[1] - e[3]
    out = [None] * 5
    for i in (0, 1):
        even = float((d[i, 0] - d[i, 4]) / 2) * d0 + float((d[i, 1] - d[i, 3]) / 2) * d1
        odd = float((d[i, 0] + d[i, 4]) / 2) * s0 + float((d[i, 1] + d[i, 3]) / 2) * s1 + float(d[i, 2]) * e[2]
        out[i] = odd + even
        out[4 - i] = even - odd
    out[2] = float(d[2, 0]) * d0 + float(d[2, 1]) * d1
    return out


def derive_back(t):
    d = DERIV
    s0, s1 = t[0] + t[4], t[1] + t[3]
    d0, d1 = t[0] - t[4], t[1] - t[3]
    out = [None] * 5
    for i in (0, 1):
        even = float((d[0, i] - d[4, i]) / 2) * d0 + float((d[1, i] - d[3, i]) / 2) * d1
        odd = float((d[0, i] + d[4, i]) / 2) * s0 + float((d[1, i] + d[3, i]) / 2) * s1 + float(d[2, i]) * t[2]
        out[i] = odd + even
        out[4 - i] = even - odd
    out[2] = float(d[0, 2]) * d0 + float(d[1, 2]) * d1
    return out


def shifted(tiles, distance, lane):
    skip, part = divmod(distance, LANES)
    if part == 0:
        moved = tiles
        pick = None
    else:
        moved = [pltpu.roll(t, LANES - part, 1) for t in tiles]
        pick = lane < LANES - part
    n = len(tiles)
    out = []
    for i in range(n):
        a = moved[(i + skip) % n]
        b = moved[(i + skip + 1) % n]
        out.append(a if pick is None else jnp.where(pick, a, b))
    return out


def at(ref, i, j, k):
    r = (j * 5 + k) * 8
    return ref[r : r + 8, i * LANES : (i + 1) * LANES]


def put(ref, i, j, k, value):
    r = (j * 5 + k) * 8
    ref[r : r + 8, i * LANES : (i + 1) * LANES] = value


def flux_at(ref, i, j, k):
    r = ((i * 5 + j) * 5 + k) * 8
    return ref[r : r + 8, :]


def lines():
    for axis in range(3):
        for p in range(5):
            for q in range(5):
                yield axis, [((l, p, q), (p, l, q), (p, q, l))[axis] for l in range(5)]


def plane_of(ref, start, row):
    r0, off = divmod(start, LANES)
    lane9 = lax.broadcasted_iota(jnp.int32, (9, LANES), 1)
    flat = ref[row + r0 : row + r0 + 9, :]
    if off:
        flat = jnp.where(
            lane9 < LANES - off,
            pltpu.roll(flat, LANES - off, 1),
            pltpu.roll(ref[row + r0 + 1 : row + r0 + 10, :], LANES - off, 1),
        )
    return flat


def kernel_kernel(
    fwd_hbm, adj_hbm, prev_ref, next_ref, flux_in_ref, cross_hbm,
    kern_out_ref, elem_ref, flux_ref,
    fwd_ref, adj_ref, cross_ref, own_ref, plane_ref, win0_ref, win1_ref, kern_ref, sem,
):
    copies = fetch(sem, (fwd_hbm, fwd_ref), (adj_hbm, adj_ref), (cross_hbm, cross_ref))
    lane = lax.broadcasted_iota(jnp.int32, (8, LANES), 1)
    for f, ref in enumerate((fwd_ref, adj_ref)):
        copies[f].wait()
        for r in range(0, 136, 8):
            own_ref[ROWS * f + r : ROWS * f + r + 8, :] = ref[0:1, r * LANES : (r + 8) * LANES].reshape(8, LANES)
        own_ref[ROWS * f + 136 : ROWS * f + 144, :] = jnp.zeros((8, LANES), F32)
        own_ref[ROWS * f + 136 : ROWS * f + 137, 0:16] = ref[0:1, NPTS - 16 : NPTS]
    m = lax.broadcasted_iota(jnp.int32, (LANES, LANES), 0)
    n = lax.broadcasted_iota(jnp.int32, (LANES, LANES), 1) & 63
    layer = m >> 3
    base = jnp.where((layer == 0) | (layer == 5) | (layer == 10), n - (m & 7), -1)
    pick = jnp.concatenate([jnp.where(base == ez * 8, 1.0, 0.0).astype(BF16) for ez in range(EZ)], axis=0)
    low = lax.broadcasted_iota(jnp.int32, (64, LANES), 1) < 64
    packed = prev_ref[80:144, :]
    packed = jnp.concatenate([jnp.where(low, packed, 0.0), jnp.where(low, 0.0, packed)], axis=0)
    extra = moved_by(split3(packed), pick)
    for ez in range(EZ):
        rows = pl.ds(ez, 125, stride=8)
        flux_ref[rows, :] = flux_in_ref[rows, :] + extra[0:125, ez * LANES : (ez + 1) * LANES]

    plane_ref[...] = jnp.zeros(plane_ref.shape, F32)
    for x in range(-4, PXU + 1):
        for f in range(2):
            if x < 0:
                flat = plane_of(prev_ref, 12 + PYZ * (x + 4), 40 * f)
            elif x < PXU:
                flat = plane_of(own_ref, PYZ * x, ROWS * f)
            else:
                flat = plane_of(next_ref, 0, 16 * f)
            places = []
            if x < PXU:
                places.append((x % 4, x // 4 + 1))
            if x % 4 == 0 and x >= 0:
                places.append((4, x // 4))
            for i, layer in places:
                for r in (layer, 10 + layer) if f == 0 else (5 + layer,):
                    plane_ref[pl.ds(i * 144 + r, 9, stride=16), :] = flat
    for i in range(NGLL):
        for h in range(2):
            tiles = [plane_ref[i * 144 + t * 16 + 8 * h : i * 144 + t * 16 + 8 * h + 8, :] for t in range(9)]
            for ey in range(EY):
                near = [tiles[ey], tiles[ey + 1], tiles[min(ey + 2, 8)]]
                if ey:
                    near = [pltpu.roll(t, LANES - 4 * ey, 1) for t in near]
                    keep = lane < LANES - 4 * ey
                    near = [jnp.where(keep, near[0], near[1]), jnp.where(keep, near[1], near[2])]
                rows = pl.ds(i * LANES + h * 64 + ey, 8, stride=8)
                win0_ref[rows, :] = near[0]
                win1_ref[rows, :] = near[1]
    select = selector()
    hi, mid, low = split3(jnp.concatenate([win0_ref[...], win1_ref[...]], axis=1))
    elem_ref[...] = dot_nt(select, hi) + (dot_nt(select, mid) + dot_nt(select, low))

    for axis, line in lines():
        grads = derive([at(elem_ref, *c) for c in line])
        for n, c in enumerate(line):
            prod = grads[n] * pltpu.roll(grads[n], 40, 1)
            if axis > 0:
                prod = at(kern_ref, *c) + prod
            if axis == 2:
                prod = -prod * flux_at(flux_ref, *c)
            put(kern_ref, *c, prod)
    hi, mid, low = split3(kern_ref[...])
    back = dot_tn(hi, select) + (dot_tn(mid, select) + dot_tn(low, select))
    win0_ref[...] = back[:, :LANES]
    win1_ref[...] = back[:, LANES:]
    kern = [gathered(win0_ref, win1_ref, i, 1) for i in range(NGLL)]
    row = lax.broadcasted_iota(jnp.int32, (8, LANES), 0)
    inner = (row >= 3) & (row < 7)
    tiles = []
    for t in range(9):
        kern[0][t] = kern[0][t] + pltpu.roll(kern[4][t], 1, 0)
        tiles.append(
            jnp.concatenate([jnp.where(inner, kern[i][t], pltpu.roll(kern[i + 1][t], 4, 0)) for i in (0, 2)], axis=0)
        )
    lane16 = lax.broadcasted_iota(jnp.int32, (16, LANES), 1)
    copies[2].wait()
    for base, step in ((0, 1), (9, PZ)):
        total = None
        for tap in range(9):
            moved = shifted(tiles, step * (tap - 4), lane16) if tap != 4 else tiles
            scaled = [v * cross_ref[base + tap : base + tap + 1, t * LANES : (t + 1) * LANES] for t, v in enumerate(moved)]
            total = scaled if total is None else [a + b for a, b in zip(total, scaled)]
        tiles = total
    for t in range(9):
        kern_out_ref[:, t * LANES : (t + 1) * LANES] = tiles[t]


def gathered(win0_ref, win1_ref, i, h):
    lane = lax.broadcasted_iota(jnp.int32, (8, LANES), 1)
    tiles = [None] * 9
    for ey in range(EY):
        rows = pl.ds(i * LANES + h * 64 + ey, 8, stride=8)
        a, b = win0_ref[rows, :], win1_ref[rows, :]
        if ey:
            a, b = pltpu.roll(a, 4 * ey, 1), pltpu.roll(b, 4 * ey, 1)
            keep = lane >= 4 * ey
            a, b = jnp.where(keep, a, 0.0), jnp.where(keep, b, a)
        tiles[ey] = a if ey == 0 else tiles[ey] + a
        tiles[ey + 1] = b
    return tiles


def force_kernel(elem_ref, flux_ref, win0_ref, win1_ref, term_ref):
    for axis, line in lines():
        grads = derive([at(elem_ref, *c) for c in line])
        back = derive_back([g * flux_at(flux_ref, *c) for g, c in zip(grads, line)])
        for n, c in enumerate(line):
            put(term_ref, *c, back[n] if axis == 0 else at(term_ref, *c) + back[n])
    select = selector()
    hi, mid, low = split3(term_ref[...])
    back = dot_tn(hi, select) + (dot_tn(mid, select) + dot_tn(low, select))
    win0_ref[...] = back[:, :LANES]
    win1_ref[...] = back[:, LANES:]


def step_kernel(
    win0_ref, win1_ref, fwd_hbm, fwd_speed_hbm, adj_hbm, adj_speed_hbm, mass_hbm, after_ref,
    fwd_out_ref, fwd_speed_out_ref, adj_out_ref, adj_speed_out_ref,
    fwd_ref, fwd_speed_ref, adj_ref, adj_speed_ref, mass_ref, plane_ref, line_ref, sem,
):
    copies = fetch(
        sem,
        (fwd_hbm, fwd_ref),
        (fwd_speed_hbm, fwd_speed_ref),
        (adj_hbm, adj_ref),
        (adj_speed_hbm, adj_speed_ref),
        (mass_hbm, mass_ref),
    )
    lane9 = lax.broadcasted_iota(jnp.int32, (9, LANES), 1)
    for i in range(NGLL):
        for h in range(2):
            for t, tile in enumerate(gathered(win0_ref, win1_ref, i, h)):
                plane_ref[i * 144 + t * 16 + 8 * h : i * 144 + t * 16 + 8 * h + 8, :] = tile
    line_ref[...] = jnp.zeros(line_ref.shape, F32)
    for f in range(2):
        for x in range(PXU):
            r0, off = divmod(PYZ * x, LANES)
            flat = plane_ref[pl.ds((x % 4) * 144 + 5 * f + x // 4 + 1, 9, stride=16), :]
            if x % 4 == 0:
                flat = flat + plane_ref[pl.ds(4 * 144 + 5 * f + x // 4, 9, stride=16), :]
            if off:
                flat = pltpu.roll(flat, off, 1)
                spill = jnp.where(lane9 < off, flat, 0.0)
                flat = jnp.where(lane9 < off, 0.0, flat)
            line_ref[f, r0 : r0 + 9, :] = line_ref[f, r0 : r0 + 9, :] + flat
            if off:
                line_ref[f, r0 + 1 : r0 + 10, :] = line_ref[f, r0 + 1 : r0 + 10, :] + spill

    def step(lo, hi, force):
        shape = (hi - lo) // force[0].shape[1], force[0].shape[1]
        take = lambda ref: ref[0:1, lo:hi].reshape(shape)
        scale = TIME_STEP * mass_ref[lo:hi].reshape(shape)
        speed = take(fwd_speed_ref) + scale * force[0]
        fwd_speed_out_ref[0:1, lo:hi] = speed.reshape(1, hi - lo)
        fwd_out_ref[0:1, lo:hi] = (take(fwd_ref) - TIME_STEP * speed).reshape(1, hi - lo)
        speed = take(adj_speed_ref) - scale * force[1]
        adj_speed_out_ref[0:1, lo:hi] = speed.reshape(1, hi - lo)
        adj_out_ref[0:1, lo:hi] = (take(adj_ref) + TIME_STEP * speed).reshape(1, hi - lo)

    for c in copies:
        c.wait()
    for r in range(0, 136, 8):
        step(r * LANES, (r + 8) * LANES, [line_ref[f, r : r + 8, :] for f in range(2)])
    step(NPTS - 16, NPTS, [line_ref[f, 136:137, 0:16] for f in range(2)])


def band_kernel(parity_ref, own_ref, first_ref, second_ref, band_ref, out_ref):
    flat = jnp.concatenate([own_ref[...], first_ref[...], second_ref[...]], axis=0)
    k1 = flat.astype(BF16)
    rest = flat - k1.astype(F32)
    k2 = rest.astype(BF16)
    k3 = (rest - k2.astype(F32)).astype(BF16)
    stacked = jnp.concatenate([k1, k2, k3, k1, k2, k1], axis=0)
    band = band_ref[parity_ref[0]]
    out_ref[...] = jnp.dot(band, stacked, preferred_element_type=F32)[:, :PYZ]


def on_device(
    forward_displacement,
    forward_velocity,
    adjoint_displacement,
    adjoint_velocity,
    inverse_mass,
    shear_modulus,
    connectivity,
    face_points,
    element_count,
):
    events = lax.axis_size("event")
    cuts = lax.axis_size("cuts")
    parity = (lax.axis_index("cuts") % 2).astype(jnp.int32).reshape(1)
    pairs_first = [(i, (i - 1 if i % 2 == 0 else i + 1) % cuts) for i in range(cuts)]
    pairs_second = [(i, (i + 1 if i % 2 == 0 else i - 1) % cuts) for i in range(cuts)]

    vmem = pl.BlockSpec(memory_space=pltpu.VMEM)
    smem = pl.BlockSpec(memory_space=pltpu.SMEM)
    anywhere = pl.BlockSpec(memory_space=pl.ANY)

    def held(block):
        return pltpu.with_memory_space_constraint(block, pltpu.VMEM)

    def in_hbm(block):
        return pltpu.with_memory_space_constraint(block, pltpu.HBM)

    def cost(flops):
        return pl.CostEstimate(flops=flops, bytes_accessed=1000000, transcendentals=0)

    dma = pltpu.SemaphoreType.DMA
    point_row = pltpu.VMEM((1, NPTS), F32)
    conn_rows = pltpu.VMEM((8, 256), jnp.int32)
    shear_block = pltpu.VMEM((125, 256), F32)
    elem_block = pltpu.VMEM((200, 5 * LANES), F32)
    flux_block = pltpu.VMEM((1000, LANES), F32)
    window = pltpu.VMEM((5 * LANES, LANES), F32)
    fields = (in_hbm(forward_displacement), in_hbm(adjoint_displacement))
    conn, shear = in_hbm(connectivity), in_hbm(shear_modulus)
    right, left = pl.pallas_call(
        pack_kernel,
        out_shape=[pltpu.VMEM((144, LANES), F32), pltpu.VMEM((32, LANES), F32)],
        in_specs=[smem] + [anywhere] * 4,
        scratch_shapes=[conn_rows, shear_block, point_row, point_row, dma((4,))],
        cost_estimate=cost(100000000),
        name="pack",
    )(element_count, conn, shear, *fields)
    prev = lax.ppermute(right, "cuts", [(i, (i + 1) % cuts) for i in range(cuts)])
    left, right = lax.optimization_barrier((left, right))
    after = lax.ppermute(left, "cuts", [((i + 1) % cuts, i) for i in range(cuts)])

    flux = pl.pallas_call(
        flux_kernel,
        out_shape=flux_block,
        in_specs=[smem] + [anywhere] * 2,
        scratch_shapes=[conn_rows, shear_block, dma((2,))],
        cost_estimate=cost(200000000),
        name="flux",
    )(element_count, conn, shear)

    kern, elem, flux = pl.pallas_call(
        kernel_kernel,
        out_shape=[pltpu.VMEM((16, 9 * LANES), F32), elem_block, flux_block],
        in_specs=[anywhere, anywhere, vmem, vmem, vmem, anywhere],
        scratch_shapes=[
            point_row,
            point_row,
            pltpu.VMEM((24, 9 * LANES), F32),
            pltpu.VMEM((2 * ROWS, LANES), F32),
            pltpu.VMEM((5 * 144, LANES), F32),
            window,
            window,
            elem_block,
            dma((3,)),
        ],
        cost_estimate=cost(400000000),
        name="kernel_term",
    )(*fields, held(prev), held(after), held(flux), in_hbm(jnp.asarray(cross_table())))

    win0, win1 = pl.pallas_call(
        force_kernel,
        out_shape=[window, window],
        in_specs=[vmem, vmem],
        scratch_shapes=[elem_block],
        cost_estimate=cost(200000000),
        name="forces",
    )(held(elem), held(flux))

    if events == 2:
        other = lax.ppermute(kern, "event", [(0, 1), (1, 0)])
        other, win0, win1 = lax.optimization_barrier((other, win0, win1))
        kern = kern + other
    elif events > 2:
        kern = lax.psum(kern, "event")
    kern_first = lax.ppermute(kern, "cuts", pairs_first)
    kern_second = lax.ppermute(kern, "cuts", pairs_second)

    points = jax.ShapeDtypeStruct((1, NPTS), F32)
    outs = pl.pallas_call(
        step_kernel,
        out_shape=[points] * 4,
        in_specs=[vmem] * 2 + [anywhere] * 5 + [vmem],
        scratch_shapes=[point_row] * 4
        + [pltpu.VMEM((NPTS,), F32), pltpu.VMEM((5 * 144, LANES), F32), pltpu.VMEM((2, ROWS, LANES), F32), dma((5,))],
        cost_estimate=cost(200000000),
        name="step",
    )(
        held(win0),
        held(win1),
        fields[0],
        in_hbm(forward_velocity),
        fields[1],
        in_hbm(adjoint_velocity),
        in_hbm(inverse_mass),
        held(kern),
    )
    shear_kernel = pl.pallas_call(
        band_kernel,
        out_shape=jax.ShapeDtypeStruct((PXU, PYZ), F32),
        in_specs=[smem] + [vmem] * 4,
        cost_estimate=cost(20000000),
        name="band",
    )(parity, held(kern), held(kern_first), held(kern_second), held(jnp.asarray(band_table())))
    return (*outs, shear_kernel)


def solution(mesh):
    in_specs = (
        P("event", "cuts"),
        P("event", "cuts"),
        P("event", "cuts"),
        P("event", "cuts"),
        P("cuts"),
        P(None, "cuts"),
        P(None, "cuts"),
        P("cuts", None),
        P("cuts"),
    )
    out_specs = (
        P("event", "cuts"),
        P("event", "cuts"),
        P("event", "cuts"),
        P("event", "cuts"),
        P("cuts", None),
    )
    return jax.shard_map(on_device, mesh=mesh, in_specs=in_specs, out_specs=out_specs, check_vma=False)
```

```python
import numpy as np
import jax
import jax.numpy as jnp
import ml_dtypes
from jax import lax
from jax.experimental import pallas as pl
from jax.experimental.pallas import tpu as pltpu
from jax.sharding import PartitionSpec as P

NGLL = 5
EX, EY, EZ = 4, 8, 8
PXU = 16
PY = 33
PZ = 33
PYZ = 1089
NPTS = 17424
LANES = 128
ROWS = 144
TIME_STEP = 0.02
F32 = jnp.float32
BF16 = jnp.bfloat16


def gll():
    nodes = np.array([-1.0, -np.sqrt(3.0 / 7.0), 0.0, np.sqrt(3.0 / 7.0), 1.0])
    bary = np.array([1.0 / np.prod([nodes[r] - nodes[c] for c in range(5) if c != r]) for r in range(5)])
    d = np.zeros((5, 5))
    for r in range(5):
        for c in range(5):
            if c != r:
                d[r, c] = bary[c] / bary[r] / (nodes[r] - nodes[c])
        d[r, r] = -np.sum(d[r])
    return d


DERIV = gll()


def split_np(x):
    x = np.asarray(x, np.float32)
    parts = []
    for _ in range(3):
        p = x.astype(ml_dtypes.bfloat16)
        parts.append(p)
        x = x - p.astype(np.float32)
    return parts


ROW_PLANE = np.array([4 * (r % 3) + r // 3 for r in range(12)] + [12, 13, 14, 15])
OWN_AT = [[3 * i + m for i in range(5)] for m in range(3)]
NEAR_AT = [[1, 2, 3, 8, 0], [4, 5, 6, 7, 9]]


def band_table():
    offsets = np.arange(-PXU, PXU + 1)
    w = lambda d: np.exp(-d * d / (2.0 * (PXU / 4.0) ** 2))
    total = w(offsets.astype(np.float64)).sum()
    out = []
    for first in (-PXU, PXU):
        source = np.concatenate([ROW_PLANE, ROW_PLANE + first, ROW_PLANE - first])
        spread = np.arange(PXU)[:, None] - source[None, :]
        band = w(spread.astype(np.float64)) * (np.abs(spread) <= PXU) / total
        b1, b2, b3 = split_np(band)
        out.append(np.concatenate([b1, b1, b1, b2, b2, b3], axis=1))
    return np.stack(out)


def cross_table():
    off = np.arange(-4, 5)
    k = np.exp(-off * off / (2.0 * 1.5 * 1.5))
    point = np.arange(33)
    inside = ((point[None, :] + off[:, None]) >= 0) & ((point[None, :] + off[:, None]) < 33)
    taps = k[:, None] * inside
    taps = taps / taps.sum(axis=0, keepdims=True)
    out = np.zeros((24, 1152), np.float32)
    out[0:9, :PYZ] = np.tile(taps, (1, PY))
    out[9:18, :PYZ] = np.repeat(taps, PZ, axis=1)
    return out


def split3(x):
    hi = x.astype(BF16)
    rest = x - hi.astype(F32)
    mid = rest.astype(BF16)
    low = (rest - mid.astype(F32)).astype(BF16)
    return hi, mid, low


def dot_nt(a, b):
    return lax.dot_general(a, b, (((1,), (1,)), ((), ())), preferred_element_type=F32)


def dot_tn(a, b):
    return lax.dot_general(a, b, (((0,), (0,)), ((), ())), preferred_element_type=F32)


def selector():
    column = lax.broadcasted_iota(jnp.int32, (8, 256), 1)
    row = lax.broadcasted_iota(jnp.int32, (8, 256), 0)
    base = column - 4 * row
    blocks = [jnp.where(base == j * PZ + k, 1.0, 0.0) for j in range(5) for k in range(5)]
    return jnp.concatenate(blocks, axis=0).astype(BF16)


def fetch(sem, *pairs):
    copies = [pltpu.make_async_copy(src, dst, sem.at[n]) for n, (src, dst) in enumerate(pairs)]
    for c in copies:
        c.start()
    return copies


def add_parts(stacked):
    n = stacked.shape[0] // 3
    return stacked[0:n] + (stacked[n : 2 * n] + stacked[2 * n : 3 * n])


def pack_kernel(
    count_ref, conn_hbm, shear_hbm, fwd_hbm, adj_hbm,
    right_ref, left_ref, own_ref, code_ref, parts_ref,
    conn_ref, shear_ref, fwd_ref, adj_ref, block_ref, sem,
):
    copies = fetch(
        sem, (conn_hbm.at[0:8], conn_ref), (fwd_hbm, fwd_ref), (adj_hbm, adj_ref), (shear_hbm, shear_ref)
    )
    copies[0].wait()
    point = conn_ref[0:1, :].astype(F32)
    x = jnp.floor((point + 0.5) * (1.0 / PYZ))
    rest = point - x * PYZ
    y = jnp.floor((rest + 0.5) * (1.0 / PZ))
    z = rest - y * PZ
    code = (8.0 * z + 2.0 * x + 0.25 * y).astype(jnp.int32)
    slot = lax.broadcasted_iota(jnp.int32, (1, 256), 1)
    code = jnp.where(slot < count_ref[0], code, -1)
    code_ref[...] = jnp.broadcast_to(code, (8, 256))
    lane = lax.broadcasted_iota(jnp.int32, (LANES, 256), 0)
    pick = jnp.where(code == ((lane >> 3) & 7) * 32 + 24 + (lane & 7), 1.0, 0.0).astype(BF16)
    for f, ref in enumerate((fwd_ref, adj_ref)):
        copies[1 + f].wait()
        for r in range(0, 136, 8):
            own_ref[ROWS * f + r : ROWS * f + r + 8, :] = ref[0:1, r * LANES : (r + 8) * LANES].reshape(8, LANES)
        own_ref[ROWS * f + 136 : ROWS * f + 144, :] = jnp.zeros((8, LANES), F32)
        own_ref[ROWS * f + 136 : ROWS * f + 137, 0:16] = ref[0:1, NPTS - 16 : NPTS]
        right_ref[40 * f : 40 * f + 40, :] = own_ref[ROWS * f + 102 : ROWS * f + 142, :]
        left_ref[16 * f : 16 * f + 16, :] = own_ref[ROWS * f : ROWS * f + 16, :]
    copies[3].wait()
    block_ref[...] = jnp.zeros(block_ref.shape, F32)
    for i in range(NGLL):
        block_ref[32 * i : 32 * i + 25, :] = shear_ref[25 * i : 25 * i + 25, :]
    parts = jnp.concatenate(split3(block_ref[...]), axis=0)
    parts_ref[...] = parts
    flux = add_parts(dot_nt(parts, pick))
    low = lax.broadcasted_iota(jnp.int32, (80, LANES), 1) < 64
    right_ref[80:160, :] = jnp.where(low, flux[0:80], flux[80:160])


def gll_weight(i):
    return (0.1, 49.0 / 90.0, 32.0 / 45.0, 49.0 / 90.0, 0.1)[i]


def lane_weight(places):
    chunk = lax.broadcasted_iota(jnp.int32, (8, LANES), 1) >> 3
    weight = jnp.zeros((8, LANES), F32)
    for row in places:
        for i, place in enumerate(row):
            weight = jnp.where(chunk == place, gll_weight(i), weight)
    return weight


def scaled(ref, weight):
    for j in range(5):
        for k in range(5):
            r = (j * 5 + k) * 8
            ref[r : r + 8, :] = ref[r : r + 8, :] * (weight * (gll_weight(j) * gll_weight(k)))


def place_flux(ref, tile_of, moves):
    lane = lax.broadcasted_iota(jnp.int32, (32, LANES), 1)
    for ez in range(EZ):
        total = jnp.zeros((32, LANES), F32)
        for i in range(NGLL):
            tile, start = tile_of(i, ez)
            for source, target, width in moves(i):
                shift = (target - source - start) % LANES
                moved = pltpu.roll(tile, shift, 1) if shift else tile
                total = jnp.where((lane >= target) & (lane < target + width), moved, total)
        ref[pl.ds(ez, 25, stride=8), :] = total[0:25]


def derive(e):
    d = DERIV
    s0, s1 = e[0] + e[4], e[1] + e[3]
    d0, d1 = e[0] - e[4], e[1] - e[3]
    out = [None] * 5
    for i in (0, 1):
        even = float((d[i, 0] - d[i, 4]) / 2) * d0 + float((d[i, 1] - d[i, 3]) / 2) * d1
        odd = float((d[i, 0] + d[i, 4]) / 2) * s0 + float((d[i, 1] + d[i, 3]) / 2) * s1 + float(d[i, 2]) * e[2]
        out[i] = odd + even
        out[4 - i] = even - odd
    out[2] = float(d[2, 0]) * d0 + float(d[2, 1]) * d1
    return out


def derive_back(t):
    d = DERIV
    s0, s1 = t[0] + t[4], t[1] + t[3]
    d0, d1 = t[0] - t[4], t[1] - t[3]
    out = [None] * 5
    for i in (0, 1):
        even = float((d[0, i] - d[4, i]) / 2) * d0 + float((d[1, i] - d[3, i]) / 2) * d1
        odd = float((d[0, i] + d[4, i]) / 2) * s0 + float((d[1, i] + d[3, i]) / 2) * s1 + float(d[2, i]) * t[2]
        out[i] = odd + even
        out[4 - i] = even - odd
    out[2] = float(d[0, 2]) * d0 + float(d[1, 2]) * d1
    return out


def shifted(tiles, distance, lane):
    skip, part = divmod(distance, LANES)
    if part == 0:
        moved = tiles
        pick = None
    else:
        moved = [pltpu.roll(t, LANES - part, 1) for t in tiles]
        pick = lane < LANES - part
    n = len(tiles)
    out = []
    for i in range(n):
        a = moved[(i + skip) % n]
        b = moved[(i + skip + 1) % n]
        out.append(a if pick is None else jnp.where(pick, a, b))
    return out


def plane_of(ref, start, row):
    r0, off = divmod(start, LANES)
    lane9 = lax.broadcasted_iota(jnp.int32, (9, LANES), 1)
    flat = ref[row + r0 : row + r0 + 9, :]
    if off:
        flat = jnp.where(
            lane9 < LANES - off,
            pltpu.roll(flat, LANES - off, 1),
            pltpu.roll(ref[row + r0 + 1 : row + r0 + 10, :], LANES - off, 1),
        )
    return flat


def store_plane(ref, row, flat):
    ref[pl.ds(row, 9, stride=16), :] = flat


def make_windows(plane_ref, base, win_ref, row):
    lane = lax.broadcasted_iota(jnp.int32, (8, LANES), 1)
    for h in range(2):
        tiles = [plane_ref[base + t * 16 + 8 * h : base + t * 16 + 8 * h + 8, :] for t in range(9)]
        for ey in range(EY):
            near = [tiles[ey], tiles[ey + 1], tiles[min(ey + 2, 8)]]
            if ey:
                near = [pltpu.roll(t, LANES - 4 * ey, 1) for t in near]
                keep = lane < LANES - 4 * ey
                near = [jnp.where(keep, near[0], near[1]), jnp.where(keep, near[1], near[2])]
            for w in range(2):
                win_ref[w, pl.ds(row + 64 * h + ey, 8, stride=8), :] = near[w]


def along_x(win_ref, source, target, places, combine):
    for row in places:
        for w in range(2):
            values = combine([win_ref[w, source + 8 * c : source + 8 * c + 8, :] for c in row])
            for c, v in zip(row, values):
                yield w, target + 8 * c, v


def gather_elements(win_ref, elem_ref, places):
    win_ref[:, 256:512, :] = jnp.zeros((2, 256, LANES), F32)
    for f in range(2):
        for w, row, value in along_x(win_ref, 128 * f, 256 + 128 * f, places, derive):
            win_ref[w, row : row + 8, :] = value
    select = selector()
    hi, mid, low = split3(jnp.concatenate([win_ref[0], win_ref[1]], axis=1))
    elem_ref[...] = dot_nt(select, hi) + (dot_nt(select, mid) + dot_nt(select, low))


def part(ref, column, j, k):
    r = (j * 5 + k) * 8
    return ref[r : r + 8, column * LANES : (column + 1) * LANES]


def kernel_rows(elem_ref, flux_ref, win_ref, halves):
    kern = [[None] * 5 for _ in range(5)]
    for k in range(5):
        fwd = derive([part(elem_ref, 0, j, k) for j in range(5)])
        adj = derive([part(elem_ref, 1, j, k) for j in range(5)])
        for j in range(5):
            kern[j][k] = fwd[j] * adj[j] + part(elem_ref, 2, j, k) * part(elem_ref, 3, j, k)
    for j in range(5):
        fwd = derive([part(elem_ref, 0, j, k) for k in range(5)])
        adj = derive([part(elem_ref, 1, j, k) for k in range(5)])
        for k in range(5):
            kern[j][k] = -(kern[j][k] + fwd[k] * adj[k]) * part(flux_ref, 0, j, k)
    hi, mid, low = split3(jnp.concatenate([v for row in kern for v in row], axis=0))
    select = selector()
    back = dot_tn(hi, select) + (dot_tn(mid, select) + dot_tn(low, select))
    win_ref[0, 0:LANES, :] = back[:, :LANES]
    win_ref[1, 0:LANES, :] = back[:, LANES:]
    return [gathered(win_ref, 0, h) for h in range(halves)]


def cross_smoothed(tiles, cross_ref):
    lane = lax.broadcasted_iota(jnp.int32, tiles[0].shape, 1)
    for base, step in ((0, 1), (9, PZ)):
        total = None
        for tap in range(9):
            moved = shifted(tiles, step * (tap - 4), lane) if tap != 4 else tiles
            terms = [v * cross_ref[base + tap : base + tap + 1, t * LANES : (t + 1) * LANES] for t, v in enumerate(moved)]
            total = terms if total is None else [a + b for a, b in zip(total, terms)]
        tiles = total
    return tiles


def own_kernel(
    own_ref, code_ref, parts_ref, cross_hbm,
    elem_ref, flux_ref, near_flux_ref, kern_ref,
    cross_ref, plane_ref, win_ref, sem,
):
    copies = fetch(sem, (cross_hbm, cross_ref))
    element = lax.broadcasted_iota(jnp.int32, (256, 256), 0)
    pick = jnp.where(code_ref[0:1, :] == element, 1.0, 0.0).astype(BF16)
    moved = add_parts(dot_nt(parts_ref[...], pick))

    def tile_of(i, ez):
        t = ez // 4
        return moved[32 * i : 32 * i + 32, t * LANES : (t + 1) * LANES], 32 * (ez % 4)

    place_flux(flux_ref, tile_of, lambda i: [(0, 24 * i, 24)])
    place_flux(near_flux_ref, tile_of, lambda i: [(24, 8 * NEAR_AT[1][i], 8)])
    scaled(flux_ref, lane_weight(OWN_AT))
    scaled(near_flux_ref, lane_weight(NEAR_AT))
    plane_ref[...] = jnp.zeros(plane_ref.shape, F32)
    for f in range(2):
        for x in range(13):
            flat = plane_of(own_ref, PYZ * x, ROWS * f)
            if x < 12:
                store_plane(plane_ref, 144 * f + OWN_AT[x // 4][x % 4], flat)
            if x % 4 == 0 and x > 0:
                store_plane(plane_ref, 144 * f + OWN_AT[x // 4 - 1][4], flat)
        make_windows(plane_ref, 144 * f, win_ref, 128 * f)
    gather_elements(win_ref, elem_ref, OWN_AT)
    low, high = kernel_rows(elem_ref, flux_ref, win_ref, 2)
    row = lax.broadcasted_iota(jnp.int32, (8, LANES), 0)
    tiles = []
    for t in range(9):
        first = low[t] + jnp.where((row == 1) | (row == 2), pltpu.roll(high[t], 5, 0), 0.0)
        second = jnp.where(row < 4, high[t], jnp.where(row == 4, pltpu.roll(high[t], 6, 0), 0.0))
        tiles.append(jnp.concatenate([first, second], axis=0))
    copies[0].wait()
    for t, tile in enumerate(cross_smoothed(tiles, cross_ref)):
        kern_ref[:, t * LANES : (t + 1) * LANES] = tile


def near_kernel(
    own_ref, prev_ref, next_ref, flux_in_ref, kern_in_ref, cross_hbm,
    elem_ref, flux_ref, kern_ref,
    cross_ref, plane_ref, win_ref, sem,
):
    copies = fetch(sem, (cross_hbm, cross_ref))
    plane_ref[...] = jnp.zeros(plane_ref.shape, F32)
    for f in range(2):
        for i in range(5):
            flat = plane_of(prev_ref, 12 + PYZ * i, 40 * f) if i < 4 else plane_of(own_ref, 0, ROWS * f)
            store_plane(plane_ref, 144 * f + NEAR_AT[0][i], flat)
            flat = plane_of(own_ref, PYZ * (12 + i), ROWS * f) if i < 4 else plane_of(next_ref, 0, 16 * f)
            store_plane(plane_ref, 144 * f + NEAR_AT[1][i], flat)
        make_windows(plane_ref, 144 * f, win_ref, 128 * f)
    gather_elements(win_ref, elem_ref, NEAR_AT)

    def tile_of(i, ez):
        blocks = []
        for r in range(32 * i, 32 * i + 32, 16):
            at = 80 + r % 80
            blocks.append((prev_ref[at : at + 16, :], 64 * (r // 80)))
        (a, p), (b, q) = blocks
        if p != q:
            b = pltpu.roll(b, 64, 1)
        return jnp.concatenate([a, b], axis=0), 8 * ez + p

    place_flux(flux_ref, tile_of, lambda i: [(0, 8 * NEAR_AT[0][i], 8)])
    scaled(flux_ref, lane_weight(NEAR_AT))
    flux_ref[...] = flux_ref[...] + flux_in_ref[...]
    (tiles,) = kernel_rows(elem_ref, flux_ref, win_ref, 1)
    row = lax.broadcasted_iota(jnp.int32, (8, LANES), 0)
    tiles = [jnp.where((row == 0) | (row >= 4), v, 0.0) for v in tiles]
    copies[0].wait()
    for t, tile in enumerate(cross_smoothed(tiles, cross_ref)):
        columns = slice(t * LANES, (t + 1) * LANES)
        kern_ref[0:8, columns] = kern_in_ref[0:8, columns] + jnp.where(row == 0, tile, 0.0)
        kern_ref[8:16, columns] = kern_in_ref[8:16, columns] + jnp.where(row >= 4, tile, 0.0)


def gathered(win_ref, base, h):
    lane = lax.broadcasted_iota(jnp.int32, (8, LANES), 1)
    tiles = [None] * 9
    for ey in range(EY):
        rows = pl.ds(base + h * 64 + ey, 8, stride=8)
        a, b = win_ref[0, rows, :], win_ref[1, rows, :]
        if ey:
            a, b = pltpu.roll(a, 4 * ey, 1), pltpu.roll(b, 4 * ey, 1)
            keep = lane >= 4 * ey
            a, b = jnp.where(keep, a, 0.0), jnp.where(keep, b, a)
        tiles[ey] = a if ey == 0 else tiles[ey] + a
        tiles[ey + 1] = b
    return tiles


def force_kernel(elem_ref, flux_ref, near_elem_ref, near_flux_ref, out_ref, term_ref, win_ref):
    select = selector()
    for kind, (elem, flux, places) in enumerate(((elem_ref, flux_ref, OWN_AT), (near_elem_ref, near_flux_ref, NEAR_AT))):
        for f in range(2):
            term = [[None] * 5 for _ in range(5)]
            for k in range(5):
                grads = derive([part(elem, f, j, k) for j in range(5)])
                for j, v in enumerate(derive_back([g * part(flux, 0, j, k) for j, g in enumerate(grads)])):
                    term[j][k] = v
            for j in range(5):
                grads = derive([part(elem, f, j, k) for k in range(5)])
                for k, v in enumerate(derive_back([g * part(flux, 0, j, k) for k, g in enumerate(grads)])):
                    r = (j * 5 + k) * 8
                    term_ref[r : r + 8, f * LANES : (f + 1) * LANES] = term[j][k] + v
                    term_ref[r : r + 8, (2 + f) * LANES : (3 + f) * LANES] = part(elem, 2 + f, j, k) * part(flux, 0, j, k)
        hi, mid, low = split3(term_ref[...])
        back = dot_tn(hi, select) + (dot_tn(mid, select) + dot_tn(low, select))
        for w in range(2):
            win_ref[w] = back[:, w * LANES : (w + 1) * LANES]
        for f in range(2):
            to = 256 * kind + 128 * f
            for w, row, value in along_x(win_ref, 256 + 128 * f, 0, places, derive_back):
                out_ref[w, to + row : to + row + 8, :] = win_ref[w, 128 * f + row : 128 * f + row + 8, :] + value


def step_kernel(
    force_ref, fwd_hbm, fwd_speed_hbm, adj_hbm, adj_speed_hbm, mass_hbm, after_ref,
    fwd_out_ref, fwd_speed_out_ref, adj_out_ref, adj_speed_out_ref,
    fwd_ref, fwd_speed_ref, adj_ref, adj_speed_ref, mass_ref, plane_ref, line_ref, sem,
):
    copies = fetch(
        sem,
        (fwd_hbm, fwd_ref),
        (fwd_speed_hbm, fwd_speed_ref),
        (adj_hbm, adj_ref),
        (adj_speed_hbm, adj_speed_ref),
        (mass_hbm, mass_ref),
    )
    lane9 = lax.broadcasted_iota(jnp.int32, (9, LANES), 1)
    for n in range(4):
        for h in range(2):
            for t, tile in enumerate(gathered(force_ref, 128 * n, h)):
                plane_ref[n * 144 + t * 16 + 8 * h : n * 144 + t * 16 + 8 * h + 8, :] = tile
    line_ref[...] = jnp.zeros(line_ref.shape, F32)
    for f in range(2):
        for x in range(PXU):
            r0, off = divmod(PYZ * x, LANES)
            i, m = x % 4, x // 4
            rows = [144 * f + OWN_AT[m][i] if m < 3 else 288 + 144 * f + NEAR_AT[1][i]]
            if i == 0:
                rows.append(144 * f + OWN_AT[m - 1][4] if m > 0 else 288 + 144 * f + NEAR_AT[0][4])
            flat = plane_ref[pl.ds(rows[0], 9, stride=16), :]
            if i == 0:
                flat = flat + plane_ref[pl.ds(rows[1], 9, stride=16), :]
            if off:
                flat = pltpu.roll(flat, off, 1)
                spill = jnp.where(lane9 < off, flat, 0.0)
                flat = jnp.where(lane9 < off, 0.0, flat)
            line_ref[f, r0 : r0 + 9, :] = line_ref[f, r0 : r0 + 9, :] + flat
            if off:
                line_ref[f, r0 + 1 : r0 + 10, :] = line_ref[f, r0 + 1 : r0 + 10, :] + spill

    def step(lo, hi, force):
        shape = (hi - lo) // force[0].shape[1], force[0].shape[1]
        take = lambda ref: ref[0:1, lo:hi].reshape(shape)
        scale = TIME_STEP * mass_ref[lo:hi].reshape(shape)
        speed = take(fwd_speed_ref) + scale * force[0]
        fwd_speed_out_ref[0:1, lo:hi] = speed.reshape(1, hi - lo)
        fwd_out_ref[0:1, lo:hi] = (take(fwd_ref) - TIME_STEP * speed).reshape(1, hi - lo)
        speed = take(adj_speed_ref) - scale * force[1]
        adj_speed_out_ref[0:1, lo:hi] = speed.reshape(1, hi - lo)
        adj_out_ref[0:1, lo:hi] = (take(adj_ref) + TIME_STEP * speed).reshape(1, hi - lo)

    for c in copies:
        c.wait()
    for r in range(0, 136, 8):
        step(r * LANES, (r + 8) * LANES, [line_ref[f, r : r + 8, :] for f in range(2)])
    step(NPTS - 16, NPTS, [line_ref[f, 136:137, 0:16] for f in range(2)])


def band_kernel(parity_ref, own_ref, first_ref, second_ref, band_ref, out_ref):
    flat = jnp.concatenate([own_ref[...], first_ref[...], second_ref[...]], axis=0)
    k1 = flat.astype(BF16)
    rest = flat - k1.astype(F32)
    k2 = rest.astype(BF16)
    k3 = (rest - k2.astype(F32)).astype(BF16)
    stacked = jnp.concatenate([k1, k2, k3, k1, k2, k1], axis=0)
    band = band_ref[parity_ref[0]]
    out_ref[...] = jnp.dot(band, stacked, preferred_element_type=F32)[:, :PYZ]


def on_device(
    forward_displacement,
    forward_velocity,
    adjoint_displacement,
    adjoint_velocity,
    inverse_mass,
    shear_modulus,
    connectivity,
    face_points,
    element_count,
):
    events = lax.axis_size("event")
    cuts = lax.axis_size("cuts")
    parity = (lax.axis_index("cuts") % 2).astype(jnp.int32).reshape(1)
    pairs_first = [(i, (i - 1 if i % 2 == 0 else i + 1) % cuts) for i in range(cuts)]
    pairs_second = [(i, (i + 1 if i % 2 == 0 else i - 1) % cuts) for i in range(cuts)]

    vmem = pl.BlockSpec(memory_space=pltpu.VMEM)
    smem = pl.BlockSpec(memory_space=pltpu.SMEM)
    anywhere = pl.BlockSpec(memory_space=pl.ANY)

    def held(block):
        return pltpu.with_memory_space_constraint(block, pltpu.VMEM)

    def in_hbm(block):
        return pltpu.with_memory_space_constraint(block, pltpu.HBM)

    def cost(flops):
        return pl.CostEstimate(flops=flops, bytes_accessed=1000000, transcendentals=0)

    dma = pltpu.SemaphoreType.DMA
    point_row = pltpu.VMEM((1, NPTS), F32)
    elem_block = pltpu.VMEM((200, 4 * LANES), F32)
    flux_block = pltpu.VMEM((200, LANES), F32)
    kern_block = pltpu.VMEM((16, 9 * LANES), F32)
    cross_block = pltpu.VMEM((24, 9 * LANES), F32)
    plane_block = pltpu.VMEM((2 * 144, LANES), F32)
    window = pltpu.VMEM((2, 512, LANES), F32)
    fields = (in_hbm(forward_displacement), in_hbm(adjoint_displacement))
    cross = in_hbm(jnp.asarray(cross_table()))
    right, left, own, code, parts = pl.pallas_call(
        pack_kernel,
        out_shape=[
            pltpu.VMEM((160, LANES), F32),
            pltpu.VMEM((32, LANES), F32),
            pltpu.VMEM((2 * ROWS, LANES), F32),
            pltpu.VMEM((8, 256), jnp.int32),
            pltpu.VMEM((480, 256), BF16),
        ],
        in_specs=[smem] + [anywhere] * 4,
        scratch_shapes=[
            pltpu.VMEM((8, 256), jnp.int32),
            pltpu.VMEM((125, 256), F32),
            point_row,
            point_row,
            pltpu.VMEM((160, 256), F32),
            dma((4,)),
        ],
        cost_estimate=cost(100000000),
        name="pack",
    )(element_count, in_hbm(connectivity), in_hbm(shear_modulus), *fields)
    prev = lax.ppermute(right, "cuts", [(i, (i + 1) % cuts) for i in range(cuts)])
    left, right = lax.optimization_barrier((left, right))
    after = lax.ppermute(left, "cuts", [((i + 1) % cuts, i) for i in range(cuts)])

    elem, flux, near_flux, kern = pl.pallas_call(
        own_kernel,
        out_shape=[elem_block, flux_block, flux_block, kern_block],
        in_specs=[vmem] * 3 + [anywhere],
        scratch_shapes=[cross_block, plane_block, window, dma((1,))],
        cost_estimate=cost(300000000),
        name="own_layers",
    )(held(own), held(code), held(parts), cross)
    near_elem, near_flux, kern = pl.pallas_call(
        near_kernel,
        out_shape=[elem_block, flux_block, kern_block],
        in_specs=[vmem] * 5 + [anywhere],
        scratch_shapes=[cross_block, plane_block, window, dma((1,))],
        cost_estimate=cost(200000000),
        name="near_layers",
    )(held(own), held(prev), held(after), held(near_flux), held(kern), cross)

    (force,) = pl.pallas_call(
        force_kernel,
        out_shape=[window],
        in_specs=[vmem] * 4,
        scratch_shapes=[elem_block, window],
        cost_estimate=cost(200000000),
        name="forces",
    )(held(elem), held(flux), held(near_elem), held(near_flux))

    if events == 2:
        other = lax.ppermute(kern, "event", [(0, 1), (1, 0)])
        other, force = lax.optimization_barrier((other, force))
        kern = kern + other
    elif events > 2:
        kern = lax.psum(kern, "event")
    kern_first = lax.ppermute(kern, "cuts", pairs_first)
    kern_second = lax.ppermute(kern, "cuts", pairs_second)

    points = jax.ShapeDtypeStruct((1, NPTS), F32)
    outs = pl.pallas_call(
        step_kernel,
        out_shape=[points] * 4,
        in_specs=[vmem] + [anywhere] * 5 + [vmem],
        scratch_shapes=[point_row] * 4
        + [pltpu.VMEM((NPTS,), F32), pltpu.VMEM((4 * 144, LANES), F32), pltpu.VMEM((2, ROWS, LANES), F32), dma((5,))],
        cost_estimate=cost(200000000),
        name="step",
    )(
        held(force),
        fields[0],
        in_hbm(forward_velocity),
        fields[1],
        in_hbm(adjoint_velocity),
        in_hbm(inverse_mass),
        held(kern),
    )
    shear_kernel = pl.pallas_call(
        band_kernel,
        out_shape=jax.ShapeDtypeStruct((PXU, PYZ), F32),
        in_specs=[smem] + [vmem] * 4,
        cost_estimate=cost(20000000),
        name="band",
    )(parity, held(kern), held(kern_first), held(kern_second), held(jnp.asarray(band_table())))
    return (*outs, shear_kernel)


def solution(mesh):
    in_specs = (
        P("event", "cuts"),
        P("event", "cuts"),
        P("event", "cuts"),
        P("event", "cuts"),
        P("cuts"),
        P(None, "cuts"),
        P(None, "cuts"),
        P("cuts", None),
        P("cuts"),
    )
    out_specs = (
        P("event", "cuts"),
        P("event", "cuts"),
        P("event", "cuts"),
        P("event", "cuts"),
        P("cuts", None),
    )
    return jax.shard_map(on_device, mesh=mesh, in_specs=in_specs, out_specs=out_specs, check_vma=False)
```

```python
import numpy as np
import jax
import jax.numpy as jnp
import ml_dtypes
from jax import lax
from jax.experimental import pallas as pl
from jax.experimental.pallas import tpu as pltpu
from jax.sharding import PartitionSpec as P

NGLL = 5
EX, EY, EZ = 4, 8, 8
PXU = 16
PY = 33
PZ = 33
PYZ = 1089
NPTS = 17424
LANES = 128
ROWS = 144
TIME_STEP = 0.02
F32 = jnp.float32
BF16 = jnp.bfloat16


def gll():
    nodes = np.array([-1.0, -np.sqrt(3.0 / 7.0), 0.0, np.sqrt(3.0 / 7.0), 1.0])
    bary = np.array([1.0 / np.prod([nodes[r] - nodes[c] for c in range(5) if c != r]) for r in range(5)])
    d = np.zeros((5, 5))
    for r in range(5):
        for c in range(5):
            if c != r:
                d[r, c] = bary[c] / bary[r] / (nodes[r] - nodes[c])
        d[r, r] = -np.sum(d[r])
    return d


DERIV = gll()


def split_np(x):
    x = np.asarray(x, np.float32)
    parts = []
    for _ in range(3):
        p = x.astype(ml_dtypes.bfloat16)
        parts.append(p)
        x = x - p.astype(np.float32)
    return parts


ROW_PLANE = np.array([4 * (r % 3) + r // 3 for r in range(12)] + [12, 13, 14, 15])
OWN_AT = [[3 * i + m for i in range(5)] for m in range(3)]
NEAR_AT = [[8, 9, 10, 11, 0], [4, 5, 6, 7, 12]]


def band_table():
    offsets = np.arange(-PXU, PXU + 1)
    w = lambda d: np.exp(-d * d / (2.0 * (PXU / 4.0) ** 2))
    total = w(offsets.astype(np.float64)).sum()
    out = []
    for first in (-PXU, PXU):
        source = np.concatenate([ROW_PLANE, ROW_PLANE + first, ROW_PLANE - first])
        spread = np.arange(PXU)[:, None] - source[None, :]
        band = w(spread.astype(np.float64)) * (np.abs(spread) <= PXU) / total
        b1, b2, b3 = split_np(band)
        out.append(np.concatenate([b1, b1, b1, b2, b2, b3], axis=1))
    return np.stack(out)


def cross_table():
    off = np.arange(-4, 5)
    k = np.exp(-off * off / (2.0 * 1.5 * 1.5))
    point = np.arange(33)
    inside = ((point[None, :] + off[:, None]) >= 0) & ((point[None, :] + off[:, None]) < 33)
    taps = k[:, None] * inside
    taps = taps / taps.sum(axis=0, keepdims=True)
    out = np.zeros((24, 1152), np.float32)
    out[0:9, :PYZ] = np.tile(taps, (1, PY))
    out[9:18, :PYZ] = np.repeat(taps, PZ, axis=1)
    return out


def split3(x):
    hi = x.astype(BF16)
    rest = x - hi.astype(F32)
    mid = rest.astype(BF16)
    low = (rest - mid.astype(F32)).astype(BF16)
    return hi, mid, low


def dot_nt(a, b):
    return lax.dot_general(a, b, (((1,), (1,)), ((), ())), preferred_element_type=F32)


def fetch(sem, *pairs):
    copies = [pltpu.make_async_copy(src, dst, sem.at[n]) for n, (src, dst) in enumerate(pairs)]
    for c in copies:
        c.start()
    return copies


def add_parts(stacked):
    n = stacked.shape[0] // 3
    return stacked[0:n] + (stacked[n : 2 * n] + stacked[2 * n : 3 * n])


def pack_kernel(
    count_ref, conn_hbm, shear_hbm, fwd_hbm, adj_hbm,
    right_ref, left_ref, own_ref, code_ref, parts_ref,
    conn_ref, shear_ref, fwd_ref, adj_ref, block_ref, sem,
):
    copies = fetch(
        sem, (shear_hbm, shear_ref), (conn_hbm.at[0:8], conn_ref), (fwd_hbm, fwd_ref), (adj_hbm, adj_ref)
    )
    copies[1].wait()
    point = conn_ref[0:1, :].astype(F32)
    x = jnp.floor((point + 0.5) * (1.0 / PYZ))
    rest = point - x * PYZ
    y = jnp.floor((rest + 0.5) * (1.0 / PZ))
    z = rest - y * PZ
    code = (8.0 * z + 2.0 * x + 0.25 * y).astype(jnp.int32)
    slot = lax.broadcasted_iota(jnp.int32, (1, 256), 1)
    code = jnp.where(slot < count_ref[0], code, -1)
    code_ref[...] = jnp.broadcast_to(code, (8, 256))
    lane = lax.broadcasted_iota(jnp.int32, (LANES, 256), 0)
    pick = jnp.where(code == ((lane >> 3) & 7) * 32 + 24 + (lane & 7), 1.0, 0.0).astype(BF16)
    for f, ref in enumerate((fwd_ref, adj_ref)):
        copies[2 + f].wait()
        for r in range(0, 136, 8):
            own_ref[ROWS * f + r : ROWS * f + r + 8, :] = ref[0:1, r * LANES : (r + 8) * LANES].reshape(8, LANES)
        own_ref[ROWS * f + 136 : ROWS * f + 144, :] = jnp.zeros((8, LANES), F32)
        own_ref[ROWS * f + 136 : ROWS * f + 137, 0:16] = ref[0:1, NPTS - 16 : NPTS]
        right_ref[40 * f : 40 * f + 40, :] = own_ref[ROWS * f + 102 : ROWS * f + 142, :]
        left_ref[16 * f : 16 * f + 16, :] = own_ref[ROWS * f : ROWS * f + 16, :]
    copies[0].wait()
    block_ref[...] = jnp.zeros(block_ref.shape, F32)
    for i in range(NGLL):
        block_ref[32 * i : 32 * i + 25, :] = shear_ref[25 * i : 25 * i + 25, :]
    parts = jnp.concatenate(split3(block_ref[...]), axis=0)
    parts_ref[...] = parts
    flux = add_parts(dot_nt(parts, pick))
    low = lax.broadcasted_iota(jnp.int32, (80, LANES), 1) < 64
    right_ref[80:160, :] = jnp.where(low, flux[0:80], flux[80:160])


def gll_weight(i):
    return (0.1, 49.0 / 90.0, 32.0 / 45.0, 49.0 / 90.0, 0.1)[i]


def lane_weight(places):
    chunk = lax.broadcasted_iota(jnp.int32, (8, LANES), 1) >> 3
    weight = jnp.zeros((8, LANES), F32)
    for row in places:
        for i, place in enumerate(row):
            weight = jnp.where(chunk == place, gll_weight(i), weight)
    return weight


def scaled(ref, weight):
    for j in range(5):
        for k in range(5):
            r = (j * 5 + k) * 8
            ref[r : r + 8, :] = ref[r : r + 8, :] * (weight * (gll_weight(j) * gll_weight(k)))


def place_flux(ref, tile_of, moves, layers=range(NGLL)):
    lane = lax.broadcasted_iota(jnp.int32, (32, LANES), 1)
    for ez in range(EZ):
        total = jnp.zeros((32, LANES), F32)
        for i in layers:
            tile, start = tile_of(i, ez)
            for source, target, width in moves(i):
                shift = (target - source - start) % LANES
                moved = pltpu.roll(tile, shift, 1) if shift else tile
                total = jnp.where((lane >= target) & (lane < target + width), moved, total)
        ref[pl.ds(ez, 25, stride=8), :] = total[0:25]


def derive(e):
    d = DERIV
    s0, s1 = e[0] + e[4], e[1] + e[3]
    d0, d1 = e[0] - e[4], e[1] - e[3]
    out = [None] * 5
    for i in (0, 1):
        even = float((d[i, 0] - d[i, 4]) / 2) * d0 + float((d[i, 1] - d[i, 3]) / 2) * d1
        odd = float((d[i, 0] + d[i, 4]) / 2) * s0 + float((d[i, 1] + d[i, 3]) / 2) * s1 + float(d[i, 2]) * e[2]
        out[i] = odd + even
        out[4 - i] = even - odd
    out[2] = float(d[2, 0]) * d0 + float(d[2, 1]) * d1
    return out


def derive_back(t):
    d = DERIV
    s0, s1 = t[0] + t[4], t[1] + t[3]
    d0, d1 = t[0] - t[4], t[1] - t[3]
    out = [None] * 5
    for i in (0, 1):
        even = float((d[0, i] - d[4, i]) / 2) * d0 + float((d[1, i] - d[3, i]) / 2) * d1
        odd = float((d[0, i] + d[4, i]) / 2) * s0 + float((d[1, i] + d[3, i]) / 2) * s1 + float(d[2, i]) * t[2]
        out[i] = odd + even
        out[4 - i] = even - odd
    out[2] = float(d[0, 2]) * d0 + float(d[1, 2]) * d1
    return out


def shifted(tiles, distance, lane):
    skip, part = divmod(distance, LANES)
    if part == 0:
        moved = tiles
        pick = None
    else:
        moved = [pltpu.roll(t, LANES - part, 1) for t in tiles]
        pick = lane < LANES - part
    n = len(tiles)
    out = []
    for i in range(n):
        a = moved[(i + skip) % n]
        b = moved[(i + skip + 1) % n]
        out.append(a if pick is None else jnp.where(pick, a, b))
    return out


def plane_of(ref, start, row):
    r0, off = divmod(start, LANES)
    lane9 = lax.broadcasted_iota(jnp.int32, (9, LANES), 1)
    flat = ref[row + r0 : row + r0 + 9, :]
    if off:
        flat = jnp.where(
            lane9 < LANES - off,
            pltpu.roll(flat, LANES - off, 1),
            pltpu.roll(ref[row + r0 + 1 : row + r0 + 10, :], LANES - off, 1),
        )
    return flat


def store_plane(ref, row, flat):
    ref[pl.ds(row, 9, stride=16), :] = flat


def make_windows(plane_ref, base, pitch, win_ref, row):
    lane = lax.broadcasted_iota(jnp.int32, (8, LANES), 1)
    tiles = [plane_ref[base + t * pitch : base + t * pitch + 8, :] for t in range(9)]
    for ey in range(EY):
        near = [tiles[ey], tiles[ey + 1], tiles[min(ey + 2, 8)]]
        if ey:
            near = [pltpu.roll(t, LANES - 4 * ey, 1) for t in near]
            keep = lane < LANES - 4 * ey
            near = [jnp.where(keep, near[0], near[1]), jnp.where(keep, near[1], near[2])]
        for w in range(2):
            win_ref[w, pl.ds(row + ey, 8, stride=8), :] = near[w]


def along_x(win_ref, base, row, combine):
    for w in range(2):
        values = combine([win_ref[w, base + 8 * c : base + 8 * c + 8, :] for c in row])
        for i, v in enumerate(values):
            yield w, i, v


def turned(win_ref, base, elem_ref, column):
    elem_ref[column, 0:LANES, :] = win_ref[0, base : base + LANES, :].T
    elem_ref[column, LANES:168, :] = win_ref[1, base : base + LANES, :].T[0:40, :]


def part(ref, column, j, k):
    return ref[column, pl.ds(j * PZ + k, 8, stride=4), :]


def flux_part(ref, j, k):
    r = (j * 5 + k) * 8
    return ref[r : r + 8, :]


def folded(term, line_ref, win_ref, base):
    row = lax.broadcasted_iota(jnp.int32, (8, LANES), 0)
    line_ref[160:256, :] = jnp.zeros((96, LANES), F32)
    for j in range(5):
        for k in range(1, 4):
            line_ref[pl.ds(j * PZ + k, 8, stride=4), :] = term[j][k]
        last = term[j][4]
        line_ref[pl.ds(j * PZ, 8, stride=4), :] = term[j][0] + jnp.where(row == 0, 0.0, pltpu.roll(last, 1, 0))
        line_ref[j * PZ + 32 : j * PZ + 33, :] = last[7:8, :]
    for w in range(2):
        win_ref[w, base : base + LANES, :] = line_ref[w * LANES : (w + 1) * LANES, :].T


def force_terms(elem_ref, value, slope, flux_ref, line_ref, win_ref, row):
    term = [[None] * 5 for _ in range(5)]
    for k in range(5):
        grads = derive([part(elem_ref, value, j, k) for j in range(5)])
        for j, v in enumerate(derive_back([g * flux_part(flux_ref, j, k) for j, g in enumerate(grads)])):
            term[j][k] = v
    for j in range(5):
        grads = derive([part(elem_ref, value, j, k) for k in range(5)])
        for k, v in enumerate(derive_back([g * flux_part(flux_ref, j, k) for k, g in enumerate(grads)])):
            term[j][k] = term[j][k] + v
    folded(term, line_ref, win_ref, row)
    term = [[part(elem_ref, slope, j, k) * flux_part(flux_ref, j, k) for k in range(5)] for j in range(5)]
    folded(term, line_ref, win_ref, row + LANES)


def cross_smoothed(tiles, cross_ref):
    lane = lax.broadcasted_iota(jnp.int32, tiles[0].shape, 1)
    for base, step in ((0, 1), (9, PZ)):
        total = None
        for tap in range(9):
            moved = shifted(tiles, step * (tap - 4), lane) if tap != 4 else tiles
            terms = [v * cross_ref[base + tap : base + tap + 1, t * LANES : (t + 1) * LANES] for t, v in enumerate(moved)]
            total = terms if total is None else [a + b for a, b in zip(total, terms)]
        tiles = total
    return tiles


def own_kernel(
    own_ref, code_ref, parts_ref, cross_hbm,
    elem_ref, flux_ref, near_flux_ref, near_win_ref, near_kern_ref, kern_ref,
    cross_ref, plane_ref, win_ref, line_ref, near_elem_ref, sem,
):
    copies = fetch(sem, (cross_hbm, cross_ref))
    plane_ref[...] = jnp.zeros(plane_ref.shape, F32)
    for f in range(2):
        base = 24 * 9 * f
        for x in range(PXU):
            flat = plane_of(own_ref, PYZ * x, ROWS * f)
            rows = [OWN_AT[x // 4][x % 4]] if x < 12 else [16 + NEAR_AT[1][x - 12]]
            if x % 4 == 0:
                rows.append(OWN_AT[x // 4 - 1][4] if x else 16 + NEAR_AT[0][4])
            for r in rows:
                plane_ref[pl.ds(base + r, 9, stride=24), :] = flat
        for h in range(2):
            make_windows(plane_ref, base + 8 * h, 24, win_ref, 128 * f + 64 * h)
        make_windows(plane_ref, base + 16, 24, near_win_ref, 64 * f)
        win_ref[:, 256 + 128 * f : 384 + 128 * f, :] = jnp.zeros((2, LANES, LANES), F32)
        for row in OWN_AT:
            for w, i, v in along_x(win_ref, 128 * f, row, derive):
                r = 256 + 128 * f + 8 * row[i]
                win_ref[w, r : r + 8, :] = v
    for column in range(4):
        turned(win_ref, 128 * column, elem_ref, column)
    turned(near_win_ref, 0, near_elem_ref, 0)

    element = lax.broadcasted_iota(jnp.int32, (256, 256), 0)
    pick = jnp.where(code_ref[0:1, :] == element, 1.0, 0.0).astype(BF16)
    moved = add_parts(dot_nt(parts_ref[...], pick))

    def tile_of(i, ez):
        t = ez // 4
        return moved[32 * i : 32 * i + 32, t * LANES : (t + 1) * LANES], 32 * (ez % 4)

    place_flux(flux_ref, tile_of, lambda i: [(0, 24 * i, 24)])
    place_flux(near_flux_ref, tile_of, lambda i: [(24, 8 * NEAR_AT[1][i], 8)])
    scaled(flux_ref, lane_weight(OWN_AT))
    scaled(near_flux_ref, lane_weight(NEAR_AT))

    kern = [[None] * 5 for _ in range(5)]
    near = [[None] * 5 for _ in range(5)]
    for k in range(5):
        fwd, adj, both = [derive([part(ref, c, j, k) for j in range(5)]) for ref, c in ((elem_ref, 0), (elem_ref, 1), (near_elem_ref, 0))]
        for j in range(5):
            kern[j][k] = fwd[j] * adj[j] + part(elem_ref, 2, j, k) * part(elem_ref, 3, j, k)
            near[j][k] = both[j] * pltpu.roll(both[j], 64, 1)
    for j in range(5):
        fwd, adj, both = [derive([part(ref, c, j, k) for k in range(5)]) for ref, c in ((elem_ref, 0), (elem_ref, 1), (near_elem_ref, 0))]
        for k in range(5):
            kern[j][k] = -(kern[j][k] + fwd[k] * adj[k]) * flux_part(flux_ref, j, k)
            r = (j * 5 + k) * 8
            near_kern_ref[r : r + 8, :] = near[j][k] + both[k] * pltpu.roll(both[k], 64, 1)
    folded(kern, line_ref, win_ref, 0)
    low, high = [gathered(win_ref, 0, h) for h in range(2)]
    row = lax.broadcasted_iota(jnp.int32, (8, LANES), 0)
    tiles = []
    for t in range(9):
        first = low[t] + jnp.where((row == 1) | (row == 2), pltpu.roll(high[t], 5, 0), 0.0)
        second = jnp.where(row < 4, high[t], jnp.where(row == 4, pltpu.roll(high[t], 6, 0), 0.0))
        tiles.append(jnp.concatenate([first, second], axis=0))
    copies[0].wait()
    for t, tile in enumerate(cross_smoothed(tiles, cross_ref)):
        kern_ref[:, t * LANES : (t + 1) * LANES] = tile


def message_flux(prev_ref):
    def tile_of(i, ez):
        blocks = []
        for r in range(32 * i, 32 * i + 32, 16):
            at = 80 + r % 80
            blocks.append((prev_ref[at : at + 16, :], 64 * (r // 80)))
        (a, p), (b, q) = blocks
        if p != q:
            b = pltpu.roll(b, 64, 1)
        return jnp.concatenate([a, b], axis=0), 8 * ez + p

    return tile_of


def near_kernel(
    prev_ref, next_ref, flux_in_ref, near_in_ref, near_kern_ref, kern_in_ref, cross_hbm,
    near_win_ref, kern_ref,
    cross_ref, plane_ref, win_ref, elem_ref, flux_ref, line_ref, sem,
):
    copies = fetch(sem, (cross_hbm, cross_ref))
    plane_ref[...] = jnp.zeros(plane_ref.shape, F32)
    for f in range(2):
        for i in range(5):
            flat = plane_of(prev_ref, 12 + PYZ * i, 40 * f) if i < 4 else plane_of(next_ref, 0, 16 * f)
            plane_ref[pl.ds(72 * f + i, 9, stride=8), :] = flat
        near_win_ref[:, 128 * f : 128 * f + 64, :] = near_in_ref[:, 64 * f : 64 * f + 64, :]
        make_windows(plane_ref, 72 * f, 8, near_win_ref, 128 * f + 64)
        win_ref[:, 64 * f : 64 * f + 64, :] = jnp.zeros((2, 64, LANES), F32)
        for layer, row in enumerate(NEAR_AT):
            for w, i, v in along_x(near_win_ref, 128 * f, row, derive):
                if (layer == 0) == (i == 4):
                    r = 64 * f + 8 * row[i]
                    win_ref[w, r : r + 8, :] = v
    turned(win_ref, 0, elem_ref, 0)
    place_flux(flux_ref, message_flux(prev_ref), lambda i: [(0, 8 * NEAR_AT[0][i], 8)], (4,))
    scaled(flux_ref, lane_weight([NEAR_AT[0]]))
    kern = [[None] * 5 for _ in range(5)]
    for j in range(5):
        for k in range(5):
            slope = part(elem_ref, 0, j, k)
            total = flux_part(near_kern_ref, j, k) + slope * pltpu.roll(slope, 64, 1)
            kern[j][k] = -total * (flux_part(flux_ref, j, k) + flux_part(flux_in_ref, j, k))
    folded(kern, line_ref, win_ref, 0)
    row = lax.broadcasted_iota(jnp.int32, (8, LANES), 0)
    tiles = [jnp.where((row == 0) | (row >= 4), v, 0.0) for v in gathered(win_ref, 0, 0)]
    copies[0].wait()
    for t, tile in enumerate(cross_smoothed(tiles, cross_ref)):
        columns = slice(t * LANES, (t + 1) * LANES)
        kern_ref[0:8, columns] = kern_in_ref[0:8, columns] + jnp.where(row == 0, tile, 0.0)
        kern_ref[8:16, columns] = kern_in_ref[8:16, columns] + jnp.where(row >= 4, tile, 0.0)


def gathered(win_ref, base, h):
    lane = lax.broadcasted_iota(jnp.int32, (8, LANES), 1)
    tiles = [None] * 9
    for ey in range(EY):
        rows = pl.ds(base + h * 64 + ey, 8, stride=8)
        a, b = win_ref[0, rows, :], win_ref[1, rows, :]
        if ey:
            a, b = pltpu.roll(a, 4 * ey, 1), pltpu.roll(b, 4 * ey, 1)
            keep = lane >= 4 * ey
            a, b = jnp.where(keep, a, 0.0), jnp.where(keep, b, a)
        tiles[ey] = a if ey == 0 else tiles[ey] + a
        tiles[ey + 1] = b
    return tiles


def summed_along_x(win_ref, places, out_ref, row):
    for line in places:
        for w, i, v in along_x(win_ref, LANES, line, derive_back):
            r = 8 * line[i]
            out_ref[w, row + r : row + r + 8, :] = win_ref[w, r : r + 8, :] + v


def force_kernel(elem_ref, flux_ref, out_ref, win_ref, line_ref):
    for f in range(2):
        force_terms(elem_ref, f, 2 + f, flux_ref, line_ref, win_ref, 0)
        summed_along_x(win_ref, OWN_AT, out_ref, LANES * f)


def step_kernel(
    force_ref, near_win_ref, near_flux_ref, prev_ref, fwd_hbm, fwd_speed_hbm, adj_hbm, adj_speed_hbm, mass_hbm, after_ref,
    fwd_out_ref, fwd_speed_out_ref, adj_out_ref, adj_speed_out_ref,
    fwd_ref, fwd_speed_ref, adj_ref, adj_speed_ref, mass_ref, plane_ref, line_ref,
    flux_ref, win_ref, elem_ref, fold_ref, near_ref, sem,
):
    copies = fetch(
        sem,
        (fwd_hbm, fwd_ref),
        (fwd_speed_hbm, fwd_speed_ref),
        (adj_hbm, adj_ref),
        (adj_speed_hbm, adj_speed_ref),
        (mass_hbm, mass_ref),
    )
    lane9 = lax.broadcasted_iota(jnp.int32, (9, LANES), 1)
    place_flux(flux_ref, message_flux(prev_ref), lambda i: [(0, 8 * NEAR_AT[0][i], 8)])
    scaled(flux_ref, lane_weight([NEAR_AT[0]]))
    flux_ref[...] = flux_ref[...] + near_flux_ref[...]
    for f in range(2):
        win_ref[...] = jnp.zeros(win_ref.shape, F32)
        for row in NEAR_AT:
            for w, i, v in along_x(near_win_ref, LANES * f, row, derive):
                win_ref[w, 8 * row[i] : 8 * row[i] + 8, :] = v
        turned(near_win_ref, LANES * f, elem_ref, 0)
        turned(win_ref, 0, elem_ref, 1)
        force_terms(elem_ref, 0, 1, flux_ref, fold_ref, win_ref, 0)
        summed_along_x(win_ref, NEAR_AT, near_ref, LANES * f)
    for n in range(4):
        for h in range(2):
            source = force_ref if n < 2 else near_ref
            for t, tile in enumerate(gathered(source, 128 * (n % 2), h)):
                plane_ref[n * 144 + t * 16 + 8 * h : n * 144 + t * 16 + 8 * h + 8, :] = tile
    line_ref[...] = jnp.zeros(line_ref.shape, F32)
    for f in range(2):
        for x in range(PXU):
            r0, off = divmod(PYZ * x, LANES)
            i, m = x % 4, x // 4
            rows = [144 * f + OWN_AT[m][i] if m < 3 else 288 + 144 * f + NEAR_AT[1][i]]
            if i == 0:
                rows.append(144 * f + OWN_AT[m - 1][4] if m > 0 else 288 + 144 * f + NEAR_AT[0][4])
            flat = plane_ref[pl.ds(rows[0], 9, stride=16), :]
            if i == 0:
                flat = flat + plane_ref[pl.ds(rows[1], 9, stride=16), :]
            if off:
                flat = pltpu.roll(flat, off, 1)
                spill = jnp.where(lane9 < off, flat, 0.0)
                flat = jnp.where(lane9 < off, 0.0, flat)
            line_ref[f, r0 : r0 + 9, :] = line_ref[f, r0 : r0 + 9, :] + flat
            if off:
                line_ref[f, r0 + 1 : r0 + 10, :] = line_ref[f, r0 + 1 : r0 + 10, :] + spill

    def step(lo, hi, force):
        shape = (hi - lo) // force[0].shape[1], force[0].shape[1]
        take = lambda ref: ref[0:1, lo:hi].reshape(shape)
        scale = TIME_STEP * mass_ref[lo:hi].reshape(shape)
        speed = take(fwd_speed_ref) + scale * force[0]
        fwd_speed_out_ref[0:1, lo:hi] = speed.reshape(1, hi - lo)
        fwd_out_ref[0:1, lo:hi] = (take(fwd_ref) - TIME_STEP * speed).reshape(1, hi - lo)
        speed = take(adj_speed_ref) - scale * force[1]
        adj_speed_out_ref[0:1, lo:hi] = speed.reshape(1, hi - lo)
        adj_out_ref[0:1, lo:hi] = (take(adj_ref) + TIME_STEP * speed).reshape(1, hi - lo)

    for c in copies:
        c.wait()
    for r in range(0, 136, 8):
        step(r * LANES, (r + 8) * LANES, [line_ref[f, r : r + 8, :] for f in range(2)])
    step(NPTS - 16, NPTS, [line_ref[f, 136:137, 0:16] for f in range(2)])


def band_kernel(parity_ref, own_ref, first_ref, second_ref, band_ref, out_ref):
    flat = jnp.concatenate([own_ref[...], first_ref[...], second_ref[...]], axis=0)
    k1 = flat.astype(BF16)
    rest = flat - k1.astype(F32)
    k2 = rest.astype(BF16)
    k3 = (rest - k2.astype(F32)).astype(BF16)
    stacked = jnp.concatenate([k1, k2, k3, k1, k2, k1], axis=0)
    band = band_ref[parity_ref[0]]
    out_ref[...] = jnp.dot(band, stacked, preferred_element_type=F32)[:, :PYZ]


def on_device(
    forward_displacement,
    forward_velocity,
    adjoint_displacement,
    adjoint_velocity,
    inverse_mass,
    shear_modulus,
    connectivity,
    face_points,
    element_count,
):
    events = lax.axis_size("event")
    cuts = lax.axis_size("cuts")
    parity = (lax.axis_index("cuts") % 2).astype(jnp.int32).reshape(1)
    pairs_first = [(i, (i - 1 if i % 2 == 0 else i + 1) % cuts) for i in range(cuts)]
    pairs_second = [(i, (i + 1 if i % 2 == 0 else i - 1) % cuts) for i in range(cuts)]

    vmem = pl.BlockSpec(memory_space=pltpu.VMEM)
    smem = pl.BlockSpec(memory_space=pltpu.SMEM)
    anywhere = pl.BlockSpec(memory_space=pl.ANY)

    def held(block):
        return pltpu.with_memory_space_constraint(block, pltpu.VMEM)

    def in_hbm(block):
        return pltpu.with_memory_space_constraint(block, pltpu.HBM)

    def cost(flops):
        return pl.CostEstimate(flops=flops, bytes_accessed=1000000, transcendentals=0)

    dma = pltpu.SemaphoreType.DMA
    point_row = pltpu.VMEM((1, NPTS), F32)
    flux_block = pltpu.VMEM((200, LANES), F32)
    kern_block = pltpu.VMEM((16, 9 * LANES), F32)
    cross_block = pltpu.VMEM((24, 9 * LANES), F32)
    line_block = pltpu.VMEM((256, LANES), F32)

    def elements(n):
        return pltpu.VMEM((n, 168, LANES), F32)

    def windows(n):
        return pltpu.VMEM((2, n * LANES, LANES), F32)

    fields = (in_hbm(forward_displacement), in_hbm(adjoint_displacement))
    cross = in_hbm(jnp.asarray(cross_table()))
    right, left, own, code, parts = pl.pallas_call(
        pack_kernel,
        out_shape=[
            pltpu.VMEM((160, LANES), F32),
            pltpu.VMEM((32, LANES), F32),
            pltpu.VMEM((2 * ROWS, LANES), F32),
            pltpu.VMEM((8, 256), jnp.int32),
            pltpu.VMEM((480, 256), BF16),
        ],
        in_specs=[smem] + [anywhere] * 4,
        scratch_shapes=[
            pltpu.VMEM((8, 256), jnp.int32),
            pltpu.VMEM((125, 256), F32),
            point_row,
            point_row,
            pltpu.VMEM((160, 256), F32),
            dma((4,)),
        ],
        cost_estimate=cost(100000000),
        name="pack",
    )(element_count, in_hbm(connectivity), in_hbm(shear_modulus), *fields)
    prev = lax.ppermute(right, "cuts", [(i, (i + 1) % cuts) for i in range(cuts)])
    left, right = lax.optimization_barrier((left, right))
    after = lax.ppermute(left, "cuts", [((i + 1) % cuts, i) for i in range(cuts)])

    elem, flux, near_flux, near_win, near_kern, kern = pl.pallas_call(
        own_kernel,
        out_shape=[elements(4), flux_block, flux_block, windows(1), flux_block, kern_block],
        in_specs=[vmem] * 3 + [anywhere],
        scratch_shapes=[
            cross_block, pltpu.VMEM((2 * 9 * 24, LANES), F32), windows(4), line_block, elements(1), dma((1,))
        ],
        cost_estimate=cost(300000000),
        name="own_layers",
    )(held(own), held(code), held(parts), cross)
    near_win, kern = pl.pallas_call(
        near_kernel,
        out_shape=[windows(2), kern_block],
        in_specs=[vmem] * 6 + [anywhere],
        scratch_shapes=[
            cross_block, pltpu.VMEM((2 * 72, LANES), F32), windows(1), elements(1), flux_block, line_block, dma((1,))
        ],
        cost_estimate=cost(200000000),
        name="near_layers",
    )(held(prev), held(after), held(near_flux), held(near_win), held(near_kern), held(kern), cross)

    (force,) = pl.pallas_call(
        force_kernel,
        out_shape=[windows(2)],
        in_specs=[vmem] * 2,
        scratch_shapes=[windows(2), line_block],
        cost_estimate=cost(200000000),
        name="forces",
    )(held(elem), held(flux))

    if events == 2:
        other = lax.ppermute(kern, "event", [(0, 1), (1, 0)])
        other, force = lax.optimization_barrier((other, force))
        kern = kern + other
    elif events > 2:
        kern = lax.psum(kern, "event")
    kern_first = lax.ppermute(kern, "cuts", pairs_first)
    kern_second = lax.ppermute(kern, "cuts", pairs_second)

    points = jax.ShapeDtypeStruct((1, NPTS), F32)
    outs = pl.pallas_call(
        step_kernel,
        out_shape=[points] * 4,
        in_specs=[vmem] * 4 + [anywhere] * 5 + [vmem],
        scratch_shapes=[point_row] * 4
        + [pltpu.VMEM((NPTS,), F32), pltpu.VMEM((4 * 144, LANES), F32), pltpu.VMEM((2, ROWS, LANES), F32)]
        + [flux_block, windows(2), elements(2), line_block, windows(2), dma((5,))],
        cost_estimate=cost(200000000),
        name="step",
    )(
        held(force),
        held(near_win),
        held(near_flux),
        held(prev),
        fields[0],
        in_hbm(forward_velocity),
        fields[1],
        in_hbm(adjoint_velocity),
        in_hbm(inverse_mass),
        held(kern),
    )
    shear_kernel = pl.pallas_call(
        band_kernel,
        out_shape=jax.ShapeDtypeStruct((PXU, PYZ), F32),
        in_specs=[smem] + [vmem] * 4,
        cost_estimate=cost(20000000),
        name="band",
    )(parity, held(kern), held(kern_first), held(kern_second), held(jnp.asarray(band_table())))
    return (*outs, shear_kernel)


def solution(mesh):
    in_specs = (
        P("event", "cuts"),
        P("event", "cuts"),
        P("event", "cuts"),
        P("event", "cuts"),
        P("cuts"),
        P(None, "cuts"),
        P(None, "cuts"),
        P("cuts", None),
        P("cuts"),
    )
    out_specs = (
        P("event", "cuts"),
        P("event", "cuts"),
        P("event", "cuts"),
        P("event", "cuts"),
        P("cuts", None),
    )
    return jax.shard_map(on_device, mesh=mesh, in_specs=in_specs, out_specs=out_specs, check_vma=False)
```

```python
import numpy as np
import jax
import jax.numpy as jnp
import ml_dtypes
from jax import lax
from jax.experimental import pallas as pl
from jax.experimental.pallas import tpu as pltpu
from jax.sharding import PartitionSpec as P

NGLL = 5
EX, EY, EZ = 4, 8, 8
PXU = 16
PY = 33
PZ = 33
PYZ = 1089
NPTS = 17424
LANES = 128
ROWS = 144
TIME_STEP = 0.02
F32 = jnp.float32
BF16 = jnp.bfloat16


def gll():
    nodes = np.array([-1.0, -np.sqrt(3.0 / 7.0), 0.0, np.sqrt(3.0 / 7.0), 1.0])
    bary = np.array([1.0 / np.prod([nodes[r] - nodes[c] for c in range(5) if c != r]) for r in range(5)])
    d = np.zeros((5, 5))
    for r in range(5):
        for c in range(5):
            if c != r:
                d[r, c] = bary[c] / bary[r] / (nodes[r] - nodes[c])
        d[r, r] = -np.sum(d[r])
    return d


DERIV = gll()


def split_np(x):
    x = np.asarray(x, np.float32)
    parts = []
    for _ in range(3):
        p = x.astype(ml_dtypes.bfloat16)
        parts.append(p)
        x = x - p.astype(np.float32)
    return parts


ROW_PLANE = np.array([4 * (r % 3) + r // 3 for r in range(12)] + [12, 13, 14, 15])
OWN_AT = [[3 * i + m for i in range(5)] for m in range(3)]
NEAR_AT = [[8, 9, 10, 11, 0], [4, 5, 6, 7, 12]]


def band_table():
    offsets = np.arange(-PXU, PXU + 1)
    w = lambda d: np.exp(-d * d / (2.0 * (PXU / 4.0) ** 2))
    total = w(offsets.astype(np.float64)).sum()
    out = []
    for first in (-PXU, PXU):
        source = np.concatenate([ROW_PLANE, ROW_PLANE + first, ROW_PLANE - first])
        spread = np.arange(PXU)[:, None] - source[None, :]
        band = w(spread.astype(np.float64)) * (np.abs(spread) <= PXU) / total
        b1, b2, b3 = split_np(band)
        out.append(np.concatenate([b1, b1, b1, b2, b2, b3], axis=1))
    return np.stack(out)


def cross_table():
    off = np.arange(-4, 5)
    k = np.exp(-off * off / (2.0 * 1.5 * 1.5))
    point = np.arange(33)
    inside = ((point[None, :] + off[:, None]) >= 0) & ((point[None, :] + off[:, None]) < 33)
    taps = k[:, None] * inside
    taps = taps / taps.sum(axis=0, keepdims=True)
    out = np.zeros((24, 1152), np.float32)
    out[0:9, :PYZ] = np.tile(taps, (1, PY))
    out[9:18, :PYZ] = np.repeat(taps, PZ, axis=1)
    return out


def split3(x):
    hi = x.astype(BF16)
    rest = x - hi.astype(F32)
    mid = rest.astype(BF16)
    low = (rest - mid.astype(F32)).astype(BF16)
    return hi, mid, low


def dot_nt(a, b):
    return lax.dot_general(a, b, (((1,), (1,)), ((), ())), preferred_element_type=F32)


def fetch(sem, *pairs):
    copies = [pltpu.make_async_copy(src, dst, sem.at[n]) for n, (src, dst) in enumerate(pairs)]
    for c in copies:
        c.start()
    return copies


def add_parts(stacked):
    n = stacked.shape[0] // 3
    return stacked[0:n] + (stacked[n : 2 * n] + stacked[2 * n : 3 * n])


def pack_kernel(
    count_ref, conn_hbm, shear_hbm, fwd_hbm, adj_hbm,
    right_ref, left_ref, own_ref, code_ref, parts_ref,
    conn_ref, shear_ref, fwd_ref, adj_ref, block_ref, sem,
):
    copies = fetch(
        sem, (shear_hbm, shear_ref), (conn_hbm.at[0:8], conn_ref), (fwd_hbm, fwd_ref), (adj_hbm, adj_ref)
    )
    copies[1].wait()
    point = conn_ref[0:1, :].astype(F32)
    x = jnp.floor((point + 0.5) * (1.0 / PYZ))
    rest = point - x * PYZ
    y = jnp.floor((rest + 0.5) * (1.0 / PZ))
    z = rest - y * PZ
    code = (8.0 * z + 2.0 * x + 0.25 * y).astype(jnp.int32)
    slot = lax.broadcasted_iota(jnp.int32, (1, 256), 1)
    code = jnp.where(slot < count_ref[0], code, -1)
    code_ref[...] = jnp.broadcast_to(code, (8, 256))
    lane = lax.broadcasted_iota(jnp.int32, (LANES, 256), 0)
    pick = jnp.where(code == ((lane >> 3) & 7) * 32 + 24 + (lane & 7), 1.0, 0.0).astype(BF16)
    for f, ref in enumerate((fwd_ref, adj_ref)):
        copies[2 + f].wait()
        for r in range(0, 136, 8):
            own_ref[ROWS * f + r : ROWS * f + r + 8, :] = ref[0:1, r * LANES : (r + 8) * LANES].reshape(8, LANES)
        own_ref[ROWS * f + 136 : ROWS * f + 144, :] = jnp.zeros((8, LANES), F32)
        own_ref[ROWS * f + 136 : ROWS * f + 137, 0:16] = ref[0:1, NPTS - 16 : NPTS]
        right_ref[40 * f : 40 * f + 40, :] = own_ref[ROWS * f + 102 : ROWS * f + 142, :]
        left_ref[16 * f : 16 * f + 16, :] = own_ref[ROWS * f : ROWS * f + 16, :]
    copies[0].wait()
    block_ref[...] = jnp.zeros(block_ref.shape, F32)
    for i in range(NGLL):
        block_ref[32 * i : 32 * i + 25, :] = shear_ref[25 * i : 25 * i + 25, :]
    parts = jnp.concatenate(split3(block_ref[...]), axis=0)
    parts_ref[...] = parts
    flux = add_parts(dot_nt(parts, pick))
    low = lax.broadcasted_iota(jnp.int32, (80, LANES), 1) < 64
    right_ref[80:160, :] = jnp.where(low, flux[0:80], flux[80:160])


def gll_weight(i):
    return (0.1, 49.0 / 90.0, 32.0 / 45.0, 49.0 / 90.0, 0.1)[i]


def lane_weight(places):
    chunk = lax.broadcasted_iota(jnp.int32, (8, LANES), 1) >> 3
    weight = jnp.zeros((8, LANES), F32)
    for row in places:
        for i, place in enumerate(row):
            weight = jnp.where(chunk == place, gll_weight(i), weight)
    return weight


def scaled(ref, weight):
    for j in range(5):
        for k in range(5):
            r = (j * 5 + k) * 8
            ref[r : r + 8, :] = ref[r : r + 8, :] * (weight * (gll_weight(j) * gll_weight(k)))


def place_flux(ref, tile_of, moves, layers=range(NGLL)):
    lane = lax.broadcasted_iota(jnp.int32, (32, LANES), 1)
    for ez in range(EZ):
        total = jnp.zeros((32, LANES), F32)
        for i in layers:
            tile, start = tile_of(i, ez)
            for source, target, width in moves(i):
                shift = (target - source - start) % LANES
                moved = pltpu.roll(tile, shift, 1) if shift else tile
                total = jnp.where((lane >= target) & (lane < target + width), moved, total)
        ref[pl.ds(ez, 25, stride=8), :] = total[0:25]


def derive(e):
    d = DERIV
    s0, s1 = e[0] + e[4], e[1] + e[3]
    d0, d1 = e[0] - e[4], e[1] - e[3]
    out = [None] * 5
    for i in (0, 1):
        even = float((d[i, 0] - d[i, 4]) / 2) * d0 + float((d[i, 1] - d[i, 3]) / 2) * d1
        odd = float((d[i, 0] + d[i, 4]) / 2) * s0 + float((d[i, 1] + d[i, 3]) / 2) * s1 + float(d[i, 2]) * e[2]
        out[i] = odd + even
        out[4 - i] = even - odd
    out[2] = float(d[2, 0]) * d0 + float(d[2, 1]) * d1
    return out


def derive_back(t):
    d = DERIV
    s0, s1 = t[0] + t[4], t[1] + t[3]
    d0, d1 = t[0] - t[4], t[1] - t[3]
    out = [None] * 5
    for i in (0, 1):
        even = float((d[0, i] - d[4, i]) / 2) * d0 + float((d[1, i] - d[3, i]) / 2) * d1
        odd = float((d[0, i] + d[4, i]) / 2) * s0 + float((d[1, i] + d[3, i]) / 2) * s1 + float(d[2, i]) * t[2]
        out[i] = odd + even
        out[4 - i] = even - odd
    out[2] = float(d[0, 2]) * d0 + float(d[1, 2]) * d1
    return out


def shifted(tiles, distance, lane):
    skip, part = divmod(distance, LANES)
    if part == 0:
        moved = tiles
        pick = None
    else:
        moved = [pltpu.roll(t, LANES - part, 1) for t in tiles]
        pick = lane < LANES - part
    n = len(tiles)
    out = []
    for i in range(n):
        a = moved[(i + skip) % n]
        b = moved[(i + skip + 1) % n]
        out.append(a if pick is None else jnp.where(pick, a, b))
    return out


def plane_of(ref, start, row):
    r0, off = divmod(start, LANES)
    lane9 = lax.broadcasted_iota(jnp.int32, (9, LANES), 1)
    flat = ref[row + r0 : row + r0 + 9, :]
    if off:
        flat = jnp.where(
            lane9 < LANES - off,
            pltpu.roll(flat, LANES - off, 1),
            pltpu.roll(ref[row + r0 + 1 : row + r0 + 10, :], LANES - off, 1),
        )
    return flat


def store_plane(ref, row, flat):
    ref[pl.ds(row, 9, stride=16), :] = flat


def make_windows(plane_ref, base, pitch, win_ref, row):
    lane = lax.broadcasted_iota(jnp.int32, (8, LANES), 1)
    tiles = [plane_ref[base + t * pitch : base + t * pitch + 8, :] for t in range(9)]
    for ey in range(EY):
        near = [tiles[ey], tiles[ey + 1], tiles[min(ey + 2, 8)]]
        if ey:
            near = [pltpu.roll(t, LANES - 4 * ey, 1) for t in near]
            keep = lane < LANES - 4 * ey
            near = [jnp.where(keep, near[0], near[1]), jnp.where(keep, near[1], near[2])]
        for w in range(2):
            win_ref[w, pl.ds(row + ey, 8, stride=8), :] = near[w]


def along_x(win_ref, base, row, combine):
    for w in range(2):
        values = combine([win_ref[w, base + 8 * c : base + 8 * c + 8, :] for c in row])
        for i, v in enumerate(values):
            yield w, i, v


def turned(win_ref, base, elem_ref, column):
    elem_ref[column, 0:LANES, :] = win_ref[0, base : base + LANES, :].T
    elem_ref[column, LANES:168, :] = win_ref[1, base : base + LANES, :].T[0:40, :]


def part(ref, column, j, k):
    return ref[column, pl.ds(j * PZ + k, 8, stride=4), :]


def flux_part(ref, j, k):
    r = (j * 5 + k) * 8
    return ref[r : r + 8, :]


def folded(term, line_ref, win_ref, base):
    row = lax.broadcasted_iota(jnp.int32, (8, LANES), 0)
    line_ref[160:256, :] = jnp.zeros((96, LANES), F32)
    for j in range(5):
        for k in range(1, 4):
            line_ref[pl.ds(j * PZ + k, 8, stride=4), :] = term[j][k]
        last = term[j][4]
        line_ref[pl.ds(j * PZ, 8, stride=4), :] = term[j][0] + jnp.where(row == 0, 0.0, pltpu.roll(last, 1, 0))
        line_ref[j * PZ + 32 : j * PZ + 33, :] = last[7:8, :]
    for w in range(2):
        win_ref[w, base : base + LANES, :] = line_ref[w * LANES : (w + 1) * LANES, :].T


def force_terms(elem_ref, value, slope, flux_ref, line_ref, win_ref, row):
    term = [[None] * 5 for _ in range(5)]
    for k in range(5):
        grads = derive([part(elem_ref, value, j, k) for j in range(5)])
        for j, v in enumerate(derive_back([g * flux_part(flux_ref, j, k) for j, g in enumerate(grads)])):
            term[j][k] = v
    for j in range(5):
        grads = derive([part(elem_ref, value, j, k) for k in range(5)])
        for k, v in enumerate(derive_back([g * flux_part(flux_ref, j, k) for k, g in enumerate(grads)])):
            term[j][k] = term[j][k] + v
    folded(term, line_ref, win_ref, row)
    term = [[part(elem_ref, slope, j, k) * flux_part(flux_ref, j, k) for k in range(5)] for j in range(5)]
    folded(term, line_ref, win_ref, row + LANES)


def cross_smoothed(tiles, cross_ref):
    lane = lax.broadcasted_iota(jnp.int32, tiles[0].shape, 1)
    for base, step in ((0, 1), (9, PZ)):
        total = None
        for tap in range(9):
            moved = shifted(tiles, step * (tap - 4), lane) if tap != 4 else tiles
            terms = [v * cross_ref[base + tap : base + tap + 1, t * LANES : (t + 1) * LANES] for t, v in enumerate(moved)]
            total = terms if total is None else [a + b for a, b in zip(total, terms)]
        tiles = total
    return tiles


def own_kernel(
    own_ref, code_ref, parts_ref, cross_hbm,
    elem_ref, flux_ref, near_flux_ref, near_win_ref, near_kern_ref, kern_ref,
    cross_ref, plane_ref, win_ref, line_ref, near_elem_ref, sem,
):
    copies = fetch(sem, (cross_hbm, cross_ref))
    plane_ref[...] = jnp.zeros(plane_ref.shape, F32)
    for f in range(2):
        base = 24 * 9 * f
        for x in range(PXU):
            flat = plane_of(own_ref, PYZ * x, ROWS * f)
            rows = [OWN_AT[x // 4][x % 4]] if x < 12 else [16 + NEAR_AT[1][x - 12]]
            if x % 4 == 0:
                rows.append(OWN_AT[x // 4 - 1][4] if x else 16 + NEAR_AT[0][4])
            for r in rows:
                plane_ref[pl.ds(base + r, 9, stride=24), :] = flat
        for h in range(2):
            make_windows(plane_ref, base + 8 * h, 24, win_ref, 128 * f + 64 * h)
        make_windows(plane_ref, base + 16, 24, near_win_ref, 64 * f)
        win_ref[:, 256 + 128 * f : 384 + 128 * f, :] = jnp.zeros((2, LANES, LANES), F32)
        for row in OWN_AT:
            for w, i, v in along_x(win_ref, 128 * f, row, derive):
                r = 256 + 128 * f + 8 * row[i]
                win_ref[w, r : r + 8, :] = v
    for column in range(4):
        turned(win_ref, 128 * column, elem_ref, column)
    turned(near_win_ref, 0, near_elem_ref, 0)

    element = lax.broadcasted_iota(jnp.int32, (256, 256), 0)
    pick = jnp.where(code_ref[0:1, :] == element, 1.0, 0.0).astype(BF16)
    moved = add_parts(dot_nt(parts_ref[...], pick))

    def tile_of(i, ez):
        t = ez // 4
        return moved[32 * i : 32 * i + 32, t * LANES : (t + 1) * LANES], 32 * (ez % 4)

    place_flux(flux_ref, tile_of, lambda i: [(0, 24 * i, 24)])
    place_flux(near_flux_ref, tile_of, lambda i: [(24, 8 * NEAR_AT[1][i], 8)])
    scaled(flux_ref, lane_weight(OWN_AT))
    scaled(near_flux_ref, lane_weight(NEAR_AT))

    kern = [[None] * 5 for _ in range(5)]
    near = [[None] * 5 for _ in range(5)]
    for k in range(5):
        fwd, adj, both = [derive([part(ref, c, j, k) for j in range(5)]) for ref, c in ((elem_ref, 0), (elem_ref, 1), (near_elem_ref, 0))]
        for j in range(5):
            kern[j][k] = fwd[j] * adj[j] + part(elem_ref, 2, j, k) * part(elem_ref, 3, j, k)
            near[j][k] = both[j] * pltpu.roll(both[j], 64, 1)
    for j in range(5):
        fwd, adj, both = [derive([part(ref, c, j, k) for k in range(5)]) for ref, c in ((elem_ref, 0), (elem_ref, 1), (near_elem_ref, 0))]
        for k in range(5):
            kern[j][k] = -(kern[j][k] + fwd[k] * adj[k]) * flux_part(flux_ref, j, k)
            r = (j * 5 + k) * 8
            near_kern_ref[r : r + 8, :] = near[j][k] + both[k] * pltpu.roll(both[k], 64, 1)
    folded(kern, line_ref, win_ref, 0)
    low, high = [gathered(win_ref, 0, h) for h in range(2)]
    row = lax.broadcasted_iota(jnp.int32, (8, LANES), 0)
    tiles = []
    for t in range(9):
        first = low[t] + jnp.where((row == 1) | (row == 2), pltpu.roll(high[t], 5, 0), 0.0)
        second = jnp.where(row < 4, high[t], jnp.where(row == 4, pltpu.roll(high[t], 6, 0), 0.0))
        tiles.append(jnp.concatenate([first, second], axis=0))
    copies[0].wait()
    for t, tile in enumerate(cross_smoothed(tiles, cross_ref)):
        kern_ref[:, t * LANES : (t + 1) * LANES] = tile


def message_flux(prev_ref):
    def tile_of(i, ez):
        blocks = []
        for r in range(32 * i, 32 * i + 32, 16):
            at = 80 + r % 80
            blocks.append((prev_ref[at : at + 16, :], 64 * (r // 80)))
        (a, p), (b, q) = blocks
        if p != q:
            b = pltpu.roll(b, 64, 1)
        return jnp.concatenate([a, b], axis=0), 8 * ez + p

    return tile_of


def near_kernel(
    prev_ref, next_ref, flux_in_ref, near_in_ref, near_kern_ref, kern_in_ref, cross_hbm,
    near_win_ref, kern_ref,
    cross_ref, plane_ref, win_ref, elem_ref, flux_ref, line_ref, sem,
):
    copies = fetch(sem, (cross_hbm, cross_ref))
    plane_ref[...] = jnp.zeros(plane_ref.shape, F32)
    for f in range(2):
        for i in range(5):
            flat = plane_of(prev_ref, 12 + PYZ * i, 40 * f) if i < 4 else plane_of(next_ref, 0, 16 * f)
            plane_ref[pl.ds(72 * f + i, 9, stride=8), :] = flat
        near_win_ref[:, 128 * f : 128 * f + 64, :] = near_in_ref[:, 64 * f : 64 * f + 64, :]
        make_windows(plane_ref, 72 * f, 8, near_win_ref, 128 * f + 64)
        win_ref[:, 64 * f : 64 * f + 64, :] = jnp.zeros((2, 64, LANES), F32)
        for layer, row in enumerate(NEAR_AT):
            for w, i, v in along_x(near_win_ref, 128 * f, row, derive):
                if (layer == 0) == (i == 4):
                    r = 64 * f + 8 * row[i]
                    win_ref[w, r : r + 8, :] = v
    turned(win_ref, 0, elem_ref, 0)
    place_flux(flux_ref, message_flux(prev_ref), lambda i: [(0, 8 * NEAR_AT[0][i], 8)], (4,))
    scaled(flux_ref, lane_weight([NEAR_AT[0]]))
    kern = [[None] * 5 for _ in range(5)]
    for j in range(5):
        for k in range(5):
            slope = part(elem_ref, 0, j, k)
            total = flux_part(near_kern_ref, j, k) + slope * pltpu.roll(slope, 64, 1)
            kern[j][k] = -total * (flux_part(flux_ref, j, k) + flux_part(flux_in_ref, j, k))
    folded(kern, line_ref, win_ref, 0)
    row = lax.broadcasted_iota(jnp.int32, (8, LANES), 0)
    tiles = [jnp.where((row == 0) | (row >= 4), v, 0.0) for v in gathered(win_ref, 0, 0)]
    copies[0].wait()
    for t, tile in enumerate(cross_smoothed(tiles, cross_ref)):
        columns = slice(t * LANES, (t + 1) * LANES)
        kern_ref[0:8, columns] = kern_in_ref[0:8, columns] + jnp.where(row == 0, tile, 0.0)
        kern_ref[8:16, columns] = kern_in_ref[8:16, columns] + jnp.where(row >= 4, tile, 0.0)


def gathered(win_ref, base, h):
    lane = lax.broadcasted_iota(jnp.int32, (8, LANES), 1)
    tiles = [None] * 9
    for ey in range(EY):
        rows = pl.ds(base + h * 64 + ey, 8, stride=8)
        a, b = win_ref[0, rows, :], win_ref[1, rows, :]
        if ey:
            a, b = pltpu.roll(a, 4 * ey, 1), pltpu.roll(b, 4 * ey, 1)
            keep = lane >= 4 * ey
            a, b = jnp.where(keep, a, 0.0), jnp.where(keep, b, a)
        tiles[ey] = a if ey == 0 else tiles[ey] + a
        tiles[ey + 1] = b
    return tiles


def summed_along_x(win_ref, places, out_ref, row):
    for line in places:
        for w, i, v in along_x(win_ref, LANES, line, derive_back):
            r = 8 * line[i]
            out_ref[w, row + r : row + r + 8, :] = win_ref[w, r : r + 8, :] + v


def force_kernel(elem_ref, flux_ref, out_ref, win_ref, line_ref):
    for f in range(2):
        force_terms(elem_ref, f, 2 + f, flux_ref, line_ref, win_ref, 0)
        summed_along_x(win_ref, OWN_AT, out_ref, LANES * f)


def step_kernel(
    force_ref, near_win_ref, near_flux_ref, prev_ref, fwd_hbm, fwd_speed_hbm, adj_hbm, adj_speed_hbm, mass_hbm,
    fwd_out_ref, fwd_speed_out_ref, adj_out_ref, adj_speed_out_ref,
    fwd_ref, fwd_speed_ref, adj_ref, adj_speed_ref, mass_ref, plane_ref, line_ref,
    flux_ref, win_ref, elem_ref, fold_ref, near_ref, sem,
):
    copies = fetch(
        sem,
        (fwd_hbm, fwd_ref),
        (fwd_speed_hbm, fwd_speed_ref),
        (adj_hbm, adj_ref),
        (adj_speed_hbm, adj_speed_ref),
        (mass_hbm, mass_ref),
    )
    lane9 = lax.broadcasted_iota(jnp.int32, (9, LANES), 1)
    place_flux(flux_ref, message_flux(prev_ref), lambda i: [(0, 8 * NEAR_AT[0][i], 8)])
    scaled(flux_ref, lane_weight([NEAR_AT[0]]))
    flux_ref[...] = flux_ref[...] + near_flux_ref[...]
    for f in range(2):
        win_ref[...] = jnp.zeros(win_ref.shape, F32)
        for row in NEAR_AT:
            for w, i, v in along_x(near_win_ref, LANES * f, row, derive):
                win_ref[w, 8 * row[i] : 8 * row[i] + 8, :] = v
        turned(near_win_ref, LANES * f, elem_ref, 0)
        turned(win_ref, 0, elem_ref, 1)
        force_terms(elem_ref, 0, 1, flux_ref, fold_ref, win_ref, 0)
        summed_along_x(win_ref, NEAR_AT, near_ref, LANES * f)
    for n in range(4):
        for h in range(2):
            source = force_ref if n < 2 else near_ref
            for t, tile in enumerate(gathered(source, 128 * (n % 2), h)):
                plane_ref[n * 144 + t * 16 + 8 * h : n * 144 + t * 16 + 8 * h + 8, :] = tile
    line_ref[...] = jnp.zeros(line_ref.shape, F32)
    for f in range(2):
        for x in range(PXU):
            r0, off = divmod(PYZ * x, LANES)
            i, m = x % 4, x // 4
            rows = [144 * f + OWN_AT[m][i] if m < 3 else 288 + 144 * f + NEAR_AT[1][i]]
            if i == 0:
                rows.append(144 * f + OWN_AT[m - 1][4] if m > 0 else 288 + 144 * f + NEAR_AT[0][4])
            flat = plane_ref[pl.ds(rows[0], 9, stride=16), :]
            if i == 0:
                flat = flat + plane_ref[pl.ds(rows[1], 9, stride=16), :]
            if off:
                flat = pltpu.roll(flat, off, 1)
                spill = jnp.where(lane9 < off, flat, 0.0)
                flat = jnp.where(lane9 < off, 0.0, flat)
            line_ref[f, r0 : r0 + 9, :] = line_ref[f, r0 : r0 + 9, :] + flat
            if off:
                line_ref[f, r0 + 1 : r0 + 10, :] = line_ref[f, r0 + 1 : r0 + 10, :] + spill

    def step(lo, hi, force):
        shape = (hi - lo) // force[0].shape[1], force[0].shape[1]
        take = lambda ref: ref[0:1, lo:hi].reshape(shape)
        scale = TIME_STEP * mass_ref[lo:hi].reshape(shape)
        speed = take(fwd_speed_ref) + scale * force[0]
        fwd_speed_out_ref[0:1, lo:hi] = speed.reshape(1, hi - lo)
        fwd_out_ref[0:1, lo:hi] = (take(fwd_ref) - TIME_STEP * speed).reshape(1, hi - lo)
        speed = take(adj_speed_ref) - scale * force[1]
        adj_speed_out_ref[0:1, lo:hi] = speed.reshape(1, hi - lo)
        adj_out_ref[0:1, lo:hi] = (take(adj_ref) + TIME_STEP * speed).reshape(1, hi - lo)

    for c in copies:
        c.wait()
    for r in range(0, 136, 8):
        step(r * LANES, (r + 8) * LANES, [line_ref[f, r : r + 8, :] for f in range(2)])
    step(NPTS - 16, NPTS, [line_ref[f, 136:137, 0:16] for f in range(2)])


def band_kernel(parity_ref, own_ref, first_ref, second_ref, band_ref, out_ref):
    flat = jnp.concatenate([own_ref[...], first_ref[...], second_ref[...]], axis=0)
    k1 = flat.astype(BF16)
    rest = flat - k1.astype(F32)
    k2 = rest.astype(BF16)
    k3 = (rest - k2.astype(F32)).astype(BF16)
    stacked = jnp.concatenate([k1, k2, k3, k1, k2, k1], axis=0)
    band = band_ref[parity_ref[0]]
    out_ref[...] = jnp.dot(band, stacked, preferred_element_type=F32)[:, :PYZ]


def on_device(
    forward_displacement,
    forward_velocity,
    adjoint_displacement,
    adjoint_velocity,
    inverse_mass,
    shear_modulus,
    connectivity,
    face_points,
    element_count,
):
    events = lax.axis_size("event")
    cuts = lax.axis_size("cuts")
    parity = (lax.axis_index("cuts") % 2).astype(jnp.int32).reshape(1)
    pairs_first = [(i, (i - 1 if i % 2 == 0 else i + 1) % cuts) for i in range(cuts)]
    pairs_second = [(i, (i + 1 if i % 2 == 0 else i - 1) % cuts) for i in range(cuts)]

    vmem = pl.BlockSpec(memory_space=pltpu.VMEM)
    smem = pl.BlockSpec(memory_space=pltpu.SMEM)
    anywhere = pl.BlockSpec(memory_space=pl.ANY)

    def held(block):
        return pltpu.with_memory_space_constraint(block, pltpu.VMEM)

    def in_hbm(block):
        return pltpu.with_memory_space_constraint(block, pltpu.HBM)

    def cost(flops):
        return pl.CostEstimate(flops=flops, bytes_accessed=1000000, transcendentals=0)

    dma = pltpu.SemaphoreType.DMA
    point_row = pltpu.VMEM((1, NPTS), F32)
    flux_block = pltpu.VMEM((200, LANES), F32)
    kern_block = pltpu.VMEM((16, 9 * LANES), F32)
    cross_block = pltpu.VMEM((24, 9 * LANES), F32)
    line_block = pltpu.VMEM((256, LANES), F32)

    def elements(n):
        return pltpu.VMEM((n, 168, LANES), F32)

    def windows(n):
        return pltpu.VMEM((2, n * LANES, LANES), F32)

    fields = (in_hbm(forward_displacement), in_hbm(adjoint_displacement))
    cross = in_hbm(jnp.asarray(cross_table()))
    right, left, own, code, parts = pl.pallas_call(
        pack_kernel,
        out_shape=[
            pltpu.VMEM((160, LANES), F32),
            pltpu.VMEM((32, LANES), F32),
            pltpu.VMEM((2 * ROWS, LANES), F32),
            pltpu.VMEM((8, 256), jnp.int32),
            pltpu.VMEM((480, 256), BF16),
        ],
        in_specs=[smem] + [anywhere] * 4,
        scratch_shapes=[
            pltpu.VMEM((8, 256), jnp.int32),
            pltpu.VMEM((125, 256), F32),
            point_row,
            point_row,
            pltpu.VMEM((160, 256), F32),
            dma((4,)),
        ],
        cost_estimate=cost(100000000),
        name="pack",
    )(element_count, in_hbm(connectivity), in_hbm(shear_modulus), *fields)
    prev = lax.ppermute(right, "cuts", [(i, (i + 1) % cuts) for i in range(cuts)])
    left, right = lax.optimization_barrier((left, right))
    after = lax.ppermute(left, "cuts", [((i + 1) % cuts, i) for i in range(cuts)])

    elem, flux, near_flux, near_win, near_kern, kern = pl.pallas_call(
        own_kernel,
        out_shape=[elements(4), flux_block, flux_block, windows(1), flux_block, kern_block],
        in_specs=[vmem] * 3 + [anywhere],
        scratch_shapes=[
            cross_block, pltpu.VMEM((2 * 9 * 24, LANES), F32), windows(4), line_block, elements(1), dma((1,))
        ],
        cost_estimate=cost(300000000),
        name="own_layers",
    )(held(own), held(code), held(parts), cross)
    near_win, kern = pl.pallas_call(
        near_kernel,
        out_shape=[windows(2), kern_block],
        in_specs=[vmem] * 6 + [anywhere],
        scratch_shapes=[
            cross_block, pltpu.VMEM((2 * 72, LANES), F32), windows(1), elements(1), flux_block, line_block, dma((1,))
        ],
        cost_estimate=cost(200000000),
        name="near_layers",
    )(held(prev), held(after), held(near_flux), held(near_win), held(near_kern), held(kern), cross)

    (force,) = pl.pallas_call(
        force_kernel,
        out_shape=[windows(2)],
        in_specs=[vmem] * 2,
        scratch_shapes=[windows(2), line_block],
        cost_estimate=cost(200000000),
        name="forces",
    )(held(elem), held(flux))

    kern_first = lax.ppermute(kern, "cuts", pairs_first)
    kern_second = lax.ppermute(kern, "cuts", pairs_second)

    points = jax.ShapeDtypeStruct((1, NPTS), F32)
    outs = pl.pallas_call(
        step_kernel,
        out_shape=[points] * 4,
        in_specs=[vmem] * 4 + [anywhere] * 5,
        scratch_shapes=[point_row] * 4
        + [pltpu.VMEM((NPTS,), F32), pltpu.VMEM((4 * 144, LANES), F32), pltpu.VMEM((2, ROWS, LANES), F32)]
        + [flux_block, windows(2), elements(2), line_block, windows(2), dma((5,))],
        cost_estimate=cost(200000000),
        name="step",
    )(
        held(force),
        held(near_win),
        held(near_flux),
        held(prev),
        fields[0],
        in_hbm(forward_velocity),
        fields[1],
        in_hbm(adjoint_velocity),
        in_hbm(inverse_mass),
    )
    kern_first, kern_second, *outs = lax.optimization_barrier((kern_first, kern_second, *outs))
    share = pl.pallas_call(
        band_kernel,
        out_shape=pltpu.VMEM((PXU, PYZ), F32),
        in_specs=[smem] + [vmem] * 4,
        cost_estimate=cost(20000000),
        name="band",
    )(parity, held(kern), held(kern_first), held(kern_second), held(jnp.asarray(band_table())))
    if events == 2:
        shear_kernel = share + lax.ppermute(share, "event", [(0, 1), (1, 0)])
    else:
        shear_kernel = lax.psum(share, "event")
    return (*outs, shear_kernel)


def solution(mesh):
    in_specs = (
        P("event", "cuts"),
        P("event", "cuts"),
        P("event", "cuts"),
        P("event", "cuts"),
        P("cuts"),
        P(None, "cuts"),
        P(None, "cuts"),
        P("cuts", None),
        P("cuts"),
    )
    out_specs = (
        P("event", "cuts"),
        P("event", "cuts"),
        P("event", "cuts"),
        P("event", "cuts"),
        P("cuts", None),
    )
    return jax.shard_map(on_device, mesh=mesh, in_specs=in_specs, out_specs=out_specs, check_vma=False)
```

```python
import functools

import numpy as np
import jax
import jax.numpy as jnp
import ml_dtypes
from jax import lax
from jax.experimental import pallas as pl
from jax.experimental.pallas import tpu as pltpu
from jax.sharding import PartitionSpec as P

NGLL = 5
EX, EY, EZ = 4, 8, 8
PXU = 16
PY = 33
PZ = 33
PYZ = 1089
NPTS = 17424
LANES = 128
ROWS = 144
TIME_STEP = 0.02
OWN_OUTS, OWN_SCRATCH = 7, 5
F32 = jnp.float32
BF16 = jnp.bfloat16


def gll():
    nodes = np.array([-1.0, -np.sqrt(3.0 / 7.0), 0.0, np.sqrt(3.0 / 7.0), 1.0])
    bary = np.array([1.0 / np.prod([nodes[r] - nodes[c] for c in range(5) if c != r]) for r in range(5)])
    d = np.zeros((5, 5))
    for r in range(5):
        for c in range(5):
            if c != r:
                d[r, c] = bary[c] / bary[r] / (nodes[r] - nodes[c])
        d[r, r] = -np.sum(d[r])
    return d


DERIV = gll()


def split_np(x):
    x = np.asarray(x, np.float32)
    parts = []
    for _ in range(3):
        p = x.astype(ml_dtypes.bfloat16)
        parts.append(p)
        x = x - p.astype(np.float32)
    return parts


ROW_PLANE = np.array([4 * (r % 3) + r // 3 for r in range(12)] + [12, 13, 14, 15])
OWN_AT = [[3 * i + m for i in range(5)] for m in range(3)]
NEAR_AT = [[8, 9, 10, 11, 0], [4, 5, 6, 7, 12]]


def band_table():
    offsets = np.arange(-PXU, PXU + 1)
    w = lambda d: np.exp(-d * d / (2.0 * (PXU / 4.0) ** 2))
    total = w(offsets.astype(np.float64)).sum()
    out = []
    for first in (-PXU, PXU):
        source = np.concatenate([ROW_PLANE, ROW_PLANE + first, ROW_PLANE - first])
        spread = np.arange(PXU)[:, None] - source[None, :]
        band = w(spread.astype(np.float64)) * (np.abs(spread) <= PXU) / total
        b1, b2, b3 = split_np(band)
        out.append(np.concatenate([b1, b1, b1, b2, b2, b3], axis=1))
    return np.stack(out)


def cross_table():
    off = np.arange(-4, 5)
    k = np.exp(-off * off / (2.0 * 1.5 * 1.5))
    point = np.arange(33)
    inside = ((point[None, :] + off[:, None]) >= 0) & ((point[None, :] + off[:, None]) < 33)
    taps = k[:, None] * inside
    taps = taps / taps.sum(axis=0, keepdims=True)
    out = np.zeros((24, 1152), np.float32)
    out[0:9, :PYZ] = np.tile(taps, (1, PY))
    out[9:18, :PYZ] = np.repeat(taps, PZ, axis=1)
    return out


def split3(x):
    hi = x.astype(BF16)
    rest = x - hi.astype(F32)
    mid = rest.astype(BF16)
    low = (rest - mid.astype(F32)).astype(BF16)
    return hi, mid, low


def dot_nt(a, b):
    return lax.dot_general(a, b, (((1,), (1,)), ((), ())), preferred_element_type=F32)


def fetch(sem, *pairs):
    copies = [pltpu.make_async_copy(src, dst, sem.at[n]) for n, (src, dst) in enumerate(pairs)]
    for c in copies:
        c.start()
    return copies


def add_parts(stacked):
    n = stacked.shape[0] // 3
    return stacked[0:n] + (stacked[n : 2 * n] + stacked[2 * n : 3 * n])


def pack_kernel(
    count_hbm, conn_hbm, shear_hbm, fwd_hbm, adj_hbm,
    right_ref, left_ref, own_ref, code_ref, parts_ref,
    count_ref, conn_ref, shear_ref, fwd_ref, adj_ref, block_ref, sem,
):
    copies = fetch(
        sem,
        (shear_hbm, shear_ref),
        (conn_hbm.at[0:8], conn_ref),
        (fwd_hbm, fwd_ref),
        (adj_hbm, adj_ref),
        (count_hbm, count_ref),
    )
    copies[1].wait()
    copies[4].wait()
    point = conn_ref[0:1, :].astype(F32)
    x = jnp.floor((point + 0.5) * (1.0 / PYZ))
    rest = point - x * PYZ
    y = jnp.floor((rest + 0.5) * (1.0 / PZ))
    z = rest - y * PZ
    code = (8.0 * z + 2.0 * x + 0.25 * y).astype(jnp.int32)
    slot = lax.broadcasted_iota(jnp.int32, (1, 256), 1)
    code = jnp.where(slot < count_ref[0], code, -1)
    code_ref[...] = jnp.broadcast_to(code, (8, 256))
    lane = lax.broadcasted_iota(jnp.int32, (LANES, 256), 0)
    pick = jnp.where(code == ((lane >> 3) & 7) * 32 + 24 + (lane & 7), 1.0, 0.0).astype(BF16)
    for f, ref in enumerate((fwd_ref, adj_ref)):
        copies[2 + f].wait()
        for r in range(0, 136, 8):
            own_ref[ROWS * f + r : ROWS * f + r + 8, :] = ref[0:1, r * LANES : (r + 8) * LANES].reshape(8, LANES)
        own_ref[ROWS * f + 136 : ROWS * f + 144, :] = jnp.zeros((8, LANES), F32)
        own_ref[ROWS * f + 136 : ROWS * f + 137, 0:16] = ref[0:1, NPTS - 16 : NPTS]
        right_ref[40 * f : 40 * f + 40, :] = own_ref[ROWS * f + 102 : ROWS * f + 142, :]
        left_ref[16 * f : 16 * f + 16, :] = own_ref[ROWS * f : ROWS * f + 16, :]
    copies[0].wait()
    block_ref[0:125, :] = shear_ref[...]
    block_ref[125:128, :] = jnp.zeros((3, 256), F32)
    parts = jnp.concatenate(split3(block_ref[...]), axis=0)
    parts_ref[...] = parts
    flux = add_parts(dot_nt(parts, pick))
    low = lax.broadcasted_iota(jnp.int32, (64, LANES), 1) < 64
    right_ref[80:144, :] = jnp.where(low, flux[0:64], flux[64:128])


def gll_weight(i):
    return (0.1, 49.0 / 90.0, 32.0 / 45.0, 49.0 / 90.0, 0.1)[i]


def lane_weight(places):
    chunk = lax.broadcasted_iota(jnp.int32, (8, LANES), 1) >> 3
    weight = jnp.zeros((8, LANES), F32)
    for row in places:
        for i, place in enumerate(row):
            weight = jnp.where(chunk == place, gll_weight(i), weight)
    return weight


def scaled(ref, weight):
    for j in range(5):
        for k in range(5):
            r = (j * 5 + k) * 8
            ref[r : r + 8, :] = ref[r : r + 8, :] * (weight * (gll_weight(j) * gll_weight(k)))


def place_flux(ref, tile_of, moves, layers=range(NGLL)):
    lane = lax.broadcasted_iota(jnp.int32, (32, LANES), 1)
    for ez in range(EZ):
        total = jnp.zeros((32, LANES), F32)
        for i in layers:
            tile, start = tile_of(i, ez)
            for source, target, width in moves(i):
                shift = (target - source - start) % LANES
                moved = pltpu.roll(tile, shift, 1) if shift else tile
                total = jnp.where((lane >= target) & (lane < target + width), moved, total)
        ref[pl.ds(ez, 25, stride=8), :] = total[0:25]


def derive(e):
    d = DERIV
    s0, s1 = e[0] + e[4], e[1] + e[3]
    d0, d1 = e[0] - e[4], e[1] - e[3]
    out = [None] * 5
    for i in (0, 1):
        even = float((d[i, 0] - d[i, 4]) / 2) * d0 + float((d[i, 1] - d[i, 3]) / 2) * d1
        odd = float((d[i, 0] + d[i, 4]) / 2) * s0 + float((d[i, 1] + d[i, 3]) / 2) * s1 + float(d[i, 2]) * e[2]
        out[i] = odd + even
        out[4 - i] = even - odd
    out[2] = float(d[2, 0]) * d0 + float(d[2, 1]) * d1
    return out


def derive_back(t):
    d = DERIV
    s0, s1 = t[0] + t[4], t[1] + t[3]
    d0, d1 = t[0] - t[4], t[1] - t[3]
    out = [None] * 5
    for i in (0, 1):
        even = float((d[0, i] - d[4, i]) / 2) * d0 + float((d[1, i] - d[3, i]) / 2) * d1
        odd = float((d[0, i] + d[4, i]) / 2) * s0 + float((d[1, i] + d[3, i]) / 2) * s1 + float(d[2, i]) * t[2]
        out[i] = odd + even
        out[4 - i] = even - odd
    out[2] = float(d[0, 2]) * d0 + float(d[1, 2]) * d1
    return out


def shifted(tiles, distance, lane):
    skip, part = divmod(distance, LANES)
    if part == 0:
        moved = tiles
        pick = None
    else:
        moved = [pltpu.roll(t, LANES - part, 1) for t in tiles]
        pick = lane < LANES - part
    n = len(tiles)
    out = []
    for i in range(n):
        a = moved[(i + skip) % n]
        b = moved[(i + skip + 1) % n]
        out.append(a if pick is None else jnp.where(pick, a, b))
    return out


def plane_of(ref, start, row):
    r0, off = divmod(start, LANES)
    lane9 = lax.broadcasted_iota(jnp.int32, (9, LANES), 1)
    flat = ref[row + r0 : row + r0 + 9, :]
    if off:
        flat = jnp.where(
            lane9 < LANES - off,
            pltpu.roll(flat, LANES - off, 1),
            pltpu.roll(ref[row + r0 + 1 : row + r0 + 10, :], LANES - off, 1),
        )
    return flat


def store_plane(ref, row, flat):
    ref[pl.ds(row, 9, stride=16), :] = flat


def make_windows(plane_ref, base, pitch, win_ref, row):
    lane = lax.broadcasted_iota(jnp.int32, (8, LANES), 1)
    tiles = [plane_ref[base + t * pitch : base + t * pitch + 8, :] for t in range(9)]
    for ey in range(EY):
        near = [tiles[ey], tiles[ey + 1], tiles[min(ey + 2, 8)]]
        if ey:
            near = [pltpu.roll(t, LANES - 4 * ey, 1) for t in near]
            keep = lane < LANES - 4 * ey
            near = [jnp.where(keep, near[0], near[1]), jnp.where(keep, near[1], near[2])]
        for w in range(2):
            win_ref[w, pl.ds(row + ey, 8, stride=8), :] = near[w]


def along_x(win_ref, base, row, combine):
    for w in range(2):
        values = combine([win_ref[w, base + 8 * c : base + 8 * c + 8, :] for c in row])
        for i, v in enumerate(values):
            yield w, i, v


def turned(win_ref, base, elem_ref, column):
    elem_ref[column, 0:LANES, :] = win_ref[0, base : base + LANES, :].T
    elem_ref[column, LANES:168, :] = win_ref[1, base : base + LANES, :].T[0:40, :]


def part(ref, column, j, k):
    return ref[column, pl.ds(j * PZ + k, 8, stride=4), :]


def flux_part(ref, j, k):
    r = (j * 5 + k) * 8
    return ref[r : r + 8, :]


def folded(term, line_ref, win_ref, base):
    row = lax.broadcasted_iota(jnp.int32, (8, LANES), 0)
    line_ref[160:256, :] = jnp.zeros((96, LANES), F32)
    for j in range(5):
        for k in range(1, 4):
            line_ref[pl.ds(j * PZ + k, 8, stride=4), :] = term[j][k]
        last = term[j][4]
        line_ref[pl.ds(j * PZ, 8, stride=4), :] = term[j][0] + jnp.where(row == 0, 0.0, pltpu.roll(last, 1, 0))
        line_ref[j * PZ + 32 : j * PZ + 33, :] = last[7:8, :]
    for w in range(2):
        win_ref[w, base : base + LANES, :] = line_ref[w * LANES : (w + 1) * LANES, :].T


def force_terms(elem_ref, value, slope, flux_ref, line_ref, win_ref, row):
    term = [[None] * 5 for _ in range(5)]
    for k in range(5):
        grads = derive([part(elem_ref, value, j, k) for j in range(5)])
        for j, v in enumerate(derive_back([g * flux_part(flux_ref, j, k) for j, g in enumerate(grads)])):
            term[j][k] = v
    for j in range(5):
        grads = derive([part(elem_ref, value, j, k) for k in range(5)])
        for k, v in enumerate(derive_back([g * flux_part(flux_ref, j, k) for k, g in enumerate(grads)])):
            term[j][k] = term[j][k] + v
    folded(term, line_ref, win_ref, row)
    term = [[part(elem_ref, slope, j, k) * flux_part(flux_ref, j, k) for k in range(5)] for j in range(5)]
    folded(term, line_ref, win_ref, row + LANES)


def cross_smoothed(tiles, cross_ref):
    lane = lax.broadcasted_iota(jnp.int32, tiles[0].shape, 1)
    for base, step in ((0, 1), (9, PZ)):
        total = None
        for tap in range(9):
            moved = shifted(tiles, step * (tap - 4), lane) if tap != 4 else tiles
            terms = [v * cross_ref[base + tap : base + tap + 1, t * LANES : (t + 1) * LANES] for t, v in enumerate(moved)]
            total = terms if total is None else [a + b for a, b in zip(total, terms)]
        tiles = total
    return tiles


def own_kernel(turn, cut_ref, own_ref, code_ref, parts_ref, cross_ref, *refs):
    refs = refs[-OWN_OUTS - OWN_SCRATCH :]
    mine = (cut_ref[0] == 0) if turn == 0 else (cut_ref[0] != 0)

    @pl.when(mine)
    def _():
        own_layers(own_ref, code_ref, parts_ref, cross_ref, *refs)


def own_layers(
    own_ref, code_ref, parts_ref, cross_ref,
    elem_ref, flux_ref, near_flux_ref, near_win_ref, near_slope_ref, near_kern_ref, kern_ref,
    plane_ref, win_ref, line_ref, near_elem_ref, moved_ref,
):
    plane_ref[...] = jnp.zeros(plane_ref.shape, F32)
    for f in range(2):
        base = 24 * 9 * f
        for x in range(PXU):
            flat = plane_of(own_ref, PYZ * x, ROWS * f)
            rows = [OWN_AT[x // 4][x % 4]] if x < 12 else [16 + NEAR_AT[1][x - 12]]
            if x % 4 == 0:
                rows.append(OWN_AT[x // 4 - 1][4] if x else 16 + NEAR_AT[0][4])
            for r in rows:
                plane_ref[pl.ds(base + r, 9, stride=24), :] = flat
        for h in range(2):
            make_windows(plane_ref, base + 8 * h, 24, win_ref, 128 * f + 64 * h)
        make_windows(plane_ref, base + 16, 24, near_win_ref, 64 * f)
        win_ref[:, 256 + 128 * f : 384 + 128 * f, :] = jnp.zeros((2, LANES, LANES), F32)
        for row in OWN_AT:
            for w, i, v in along_x(win_ref, 128 * f, row, derive):
                r = 256 + 128 * f + 8 * row[i]
                win_ref[w, r : r + 8, :] = v
    for column in range(4):
        turned(win_ref, 128 * column, elem_ref, column)
    turned(near_win_ref, 0, near_elem_ref, 0)
    near_slope_ref[...] = jnp.zeros(near_slope_ref.shape, F32)
    for f in range(2):
        for w in range(2):
            value = [near_win_ref[w, 64 * f + 8 * c : 64 * f + 8 * c + 8, :] for c in (0, 4, 5, 6, 7)]
            near_slope_ref[w, 64 * f : 64 * f + 8, :] = float(DERIV[4, 4]) * value[0]
            for i, v in enumerate(derive(value[1:] + [jnp.zeros((8, LANES), F32)])[:4]):
                r = 64 * f + 8 * NEAR_AT[1][i]
                near_slope_ref[w, r : r + 8, :] = v

    element = lax.broadcasted_iota(jnp.int32, (256, 256), 0)
    pick = jnp.where(code_ref[0:1, :] == element, 1.0, 0.0).astype(BF16)
    moved_ref[0:128, :] = add_parts(dot_nt(parts_ref[...], pick))
    moved_ref[128:136, :] = jnp.zeros((8, 256), F32)

    def tile_of(i, ez):
        t = ez // 4
        return moved_ref[25 * i : 25 * i + 32, t * LANES : (t + 1) * LANES], 32 * (ez % 4)

    place_flux(flux_ref, tile_of, lambda i: [(0, 24 * i, 24)])
    place_flux(near_flux_ref, tile_of, lambda i: [(24, 8 * NEAR_AT[1][i], 8)])
    scaled(flux_ref, lane_weight(OWN_AT))
    scaled(near_flux_ref, lane_weight(NEAR_AT))

    kern = [[None] * 5 for _ in range(5)]
    near = [[None] * 5 for _ in range(5)]
    for k in range(5):
        fwd, adj, both = [derive([part(ref, c, j, k) for j in range(5)]) for ref, c in ((elem_ref, 0), (elem_ref, 1), (near_elem_ref, 0))]
        for j in range(5):
            kern[j][k] = fwd[j] * adj[j] + part(elem_ref, 2, j, k) * part(elem_ref, 3, j, k)
            near[j][k] = both[j] * pltpu.roll(both[j], 64, 1)
    for j in range(5):
        fwd, adj, both = [derive([part(ref, c, j, k) for k in range(5)]) for ref, c in ((elem_ref, 0), (elem_ref, 1), (near_elem_ref, 0))]
        for k in range(5):
            kern[j][k] = -(kern[j][k] + fwd[k] * adj[k]) * flux_part(flux_ref, j, k)
            r = (j * 5 + k) * 8
            near_kern_ref[r : r + 8, :] = near[j][k] + both[k] * pltpu.roll(both[k], 64, 1)
    folded(kern, line_ref, win_ref, 0)
    low, high = [gathered(win_ref, 0, h) for h in range(2)]
    row = lax.broadcasted_iota(jnp.int32, (8, LANES), 0)
    tiles = []
    for t in range(9):
        first = low[t] + jnp.where((row == 1) | (row == 2), pltpu.roll(high[t], 5, 0), 0.0)
        second = jnp.where(row < 4, high[t], jnp.where(row == 4, pltpu.roll(high[t], 6, 0), 0.0))
        tiles.append(jnp.concatenate([first, second], axis=0))
    for t, tile in enumerate(cross_smoothed(tiles, cross_ref)):
        kern_ref[:, t * LANES : (t + 1) * LANES] = tile


def message_flux(prev_ref, spread_ref):
    spread_ref[0:64, :] = prev_ref[80:144, :]
    spread_ref[64:128, :] = pltpu.roll(prev_ref[80:144, :], 64, 1)
    spread_ref[128:136, :] = jnp.zeros((8, LANES), F32)
    return lambda i, ez: (spread_ref[25 * i : 25 * i + 32, :], 8 * ez)


def near_kernel(
    prev_ref, next_ref, flux_in_ref, slope_ref, near_kern_ref, kern_in_ref, cross_ref,
    kern_ref,
    plane_ref, new_ref, win_ref, elem_ref, flux_ref, line_ref, spread_ref,
):
    plane_ref[...] = jnp.zeros(plane_ref.shape, F32)
    for f in range(2):
        share = None
        for l in range(4):
            term = float(DERIV[4, l]) * plane_of(prev_ref, 12 + PYZ * l, 40 * f)
            share = term if share is None else share + term
        plane_ref[pl.ds(f, 9, stride=8), :] = share
        plane_ref[pl.ds(2 + f, 9, stride=8), :] = plane_of(next_ref, 0, 16 * f)
    make_windows(plane_ref, 0, 8, new_ref, 0)
    win_ref[...] = slope_ref[...]
    for f in range(2):
        for w in range(2):
            r = 64 * f
            win_ref[w, r : r + 8, :] = win_ref[w, r : r + 8, :] + new_ref[w, 8 * f : 8 * f + 8, :]
            for i in range(4):
                r = 64 * f + 8 * NEAR_AT[1][i]
                new = float(DERIV[i, 4]) * new_ref[w, 16 + 8 * f : 24 + 8 * f, :]
                win_ref[w, r : r + 8, :] = win_ref[w, r : r + 8, :] + new
    turned(win_ref, 0, elem_ref, 0)
    place_flux(flux_ref, message_flux(prev_ref, spread_ref), lambda i: [(0, 8 * NEAR_AT[0][i], 8)], (4,))
    scaled(flux_ref, lane_weight([NEAR_AT[0]]))
    kern = [[None] * 5 for _ in range(5)]
    for j in range(5):
        for k in range(5):
            slope = part(elem_ref, 0, j, k)
            total = flux_part(near_kern_ref, j, k) + slope * pltpu.roll(slope, 64, 1)
            kern[j][k] = -total * (flux_part(flux_ref, j, k) + flux_part(flux_in_ref, j, k))
    folded(kern, line_ref, win_ref, 0)
    row = lax.broadcasted_iota(jnp.int32, (8, LANES), 0)
    tiles = [jnp.where((row == 0) | (row >= 4), v, 0.0) for v in gathered(win_ref, 0, 0)]
    for t, tile in enumerate(cross_smoothed(tiles, cross_ref)):
        columns = slice(t * LANES, (t + 1) * LANES)
        kern_ref[0:8, columns] = kern_in_ref[0:8, columns] + jnp.where(row == 0, tile, 0.0)
        kern_ref[8:16, columns] = kern_in_ref[8:16, columns] + jnp.where(row >= 4, tile, 0.0)


def gathered(win_ref, base, h):
    lane = lax.broadcasted_iota(jnp.int32, (8, LANES), 1)
    tiles = [None] * 9
    for ey in range(EY):
        rows = pl.ds(base + h * 64 + ey, 8, stride=8)
        a, b = win_ref[0, rows, :], win_ref[1, rows, :]
        if ey:
            a, b = pltpu.roll(a, 4 * ey, 1), pltpu.roll(b, 4 * ey, 1)
            keep = lane >= 4 * ey
            a, b = jnp.where(keep, a, 0.0), jnp.where(keep, b, a)
        tiles[ey] = a if ey == 0 else tiles[ey] + a
        tiles[ey + 1] = b
    return tiles


def summed_along_x(win_ref, places, out_ref, row):
    for line in places:
        for w, i, v in along_x(win_ref, LANES, line, derive_back):
            r = 8 * line[i]
            out_ref[w, row + r : row + r + 8, :] = win_ref[w, r : r + 8, :] + v


def force_kernel(elem_ref, flux_ref, out_ref, win_ref, line_ref):
    for f in range(2):
        force_terms(elem_ref, f, 2 + f, flux_ref, line_ref, win_ref, 0)
        summed_along_x(win_ref, OWN_AT, out_ref, LANES * f)


def step_kernel(
    force_ref, near_half_ref, near_flux_ref, prev_ref, next_ref, fwd_hbm, fwd_speed_hbm, adj_hbm, adj_speed_hbm, mass_hbm, after_ref,
    fwd_out_ref, fwd_speed_out_ref, adj_out_ref, adj_speed_out_ref,
    fwd_ref, fwd_speed_ref, adj_ref, adj_speed_ref, mass_ref, plane_ref, line_ref,
    flux_ref, win_ref, elem_ref, fold_ref, near_ref, near_win_ref, near_plane_ref, spread_ref, sem,
):
    copies = fetch(
        sem,
        (fwd_hbm, fwd_ref),
        (fwd_speed_hbm, fwd_speed_ref),
        (adj_hbm, adj_ref),
        (adj_speed_hbm, adj_speed_ref),
        (mass_hbm, mass_ref),
    )
    lane9 = lax.broadcasted_iota(jnp.int32, (9, LANES), 1)
    near_plane_ref[...] = jnp.zeros(near_plane_ref.shape, F32)
    for f in range(2):
        for i in range(5):
            flat = plane_of(prev_ref, 12 + PYZ * i, 40 * f) if i < 4 else plane_of(next_ref, 0, 16 * f)
            near_plane_ref[pl.ds(72 * f + i, 9, stride=8), :] = flat
        near_win_ref[:, 128 * f : 128 * f + 64, :] = near_half_ref[:, 64 * f : 64 * f + 64, :]
        make_windows(near_plane_ref, 72 * f, 8, near_win_ref, 128 * f + 64)
    place_flux(flux_ref, message_flux(prev_ref, spread_ref), lambda i: [(0, 8 * NEAR_AT[0][i], 8)])
    scaled(flux_ref, lane_weight([NEAR_AT[0]]))
    flux_ref[...] = flux_ref[...] + near_flux_ref[...]
    for f in range(2):
        win_ref[...] = jnp.zeros(win_ref.shape, F32)
        for row in NEAR_AT:
            for w, i, v in along_x(near_win_ref, LANES * f, row, derive):
                win_ref[w, 8 * row[i] : 8 * row[i] + 8, :] = v
        turned(near_win_ref, LANES * f, elem_ref, 0)
        turned(win_ref, 0, elem_ref, 1)
        force_terms(elem_ref, 0, 1, flux_ref, fold_ref, win_ref, 0)
        summed_along_x(win_ref, NEAR_AT, near_ref, LANES * f)
    for n in range(4):
        for h in range(2):
            source = force_ref if n < 2 else near_ref
            for t, tile in enumerate(gathered(source, 128 * (n % 2), h)):
                plane_ref[n * 144 + t * 16 + 8 * h : n * 144 + t * 16 + 8 * h + 8, :] = tile
    line_ref[...] = jnp.zeros(line_ref.shape, F32)
    for f in range(2):
        for x in range(PXU):
            r0, off = divmod(PYZ * x, LANES)
            i, m = x % 4, x // 4
            rows = [144 * f + OWN_AT[m][i] if m < 3 else 288 + 144 * f + NEAR_AT[1][i]]
            if i == 0:
                rows.append(144 * f + OWN_AT[m - 1][4] if m > 0 else 288 + 144 * f + NEAR_AT[0][4])
            flat = plane_ref[pl.ds(rows[0], 9, stride=16), :]
            if i == 0:
                flat = flat + plane_ref[pl.ds(rows[1], 9, stride=16), :]
            if off:
                flat = pltpu.roll(flat, off, 1)
                spill = jnp.where(lane9 < off, flat, 0.0)
                flat = jnp.where(lane9 < off, 0.0, flat)
            line_ref[f, r0 : r0 + 9, :] = line_ref[f, r0 : r0 + 9, :] + flat
            if off:
                line_ref[f, r0 + 1 : r0 + 10, :] = line_ref[f, r0 + 1 : r0 + 10, :] + spill

    def step(lo, hi, force):
        shape = (hi - lo) // force[0].shape[1], force[0].shape[1]
        take = lambda ref: ref[0:1, lo:hi].reshape(shape)
        scale = TIME_STEP * mass_ref[lo:hi].reshape(shape)
        speed = take(fwd_speed_ref) + scale * force[0]
        fwd_speed_out_ref[0:1, lo:hi] = speed.reshape(1, hi - lo)
        fwd_out_ref[0:1, lo:hi] = (take(fwd_ref) - TIME_STEP * speed).reshape(1, hi - lo)
        speed = take(adj_speed_ref) - scale * force[1]
        adj_speed_out_ref[0:1, lo:hi] = speed.reshape(1, hi - lo)
        adj_out_ref[0:1, lo:hi] = (take(adj_ref) + TIME_STEP * speed).reshape(1, hi - lo)

    for c in copies:
        c.wait()
    for r in range(0, 136, 8):
        step(r * LANES, (r + 8) * LANES, [line_ref[f, r : r + 8, :] for f in range(2)])
    step(NPTS - 16, NPTS, [line_ref[f, 136:137, 0:16] for f in range(2)])


def band_kernel(cut_ref, own_ref, first_ref, second_ref, band_ref, out_ref):
    flat = jnp.concatenate([own_ref[...], first_ref[...], second_ref[...]], axis=0)
    k1 = flat.astype(BF16)
    rest = flat - k1.astype(F32)
    k2 = rest.astype(BF16)
    k3 = (rest - k2.astype(F32)).astype(BF16)
    stacked = jnp.concatenate([k1, k2, k3, k1, k2, k1], axis=0)
    band = band_ref[cut_ref[0] & 1]
    out_ref[...] = jnp.dot(band, stacked, preferred_element_type=F32)[:, :PYZ]


def on_device(
    forward_displacement,
    forward_velocity,
    adjoint_displacement,
    adjoint_velocity,
    inverse_mass,
    shear_modulus,
    connectivity,
    face_points,
    element_count,
):
    events = lax.axis_size("event")
    cuts = lax.axis_size("cuts")
    cut = lax.axis_index("cuts").astype(jnp.int32).reshape(1)
    pairs_first = [(i, (i - 1 if i % 2 == 0 else i + 1) % cuts) for i in range(cuts)]
    pairs_second = [(i, (i + 1 if i % 2 == 0 else i - 1) % cuts) for i in range(cuts)]

    vmem = pl.BlockSpec(memory_space=pltpu.VMEM)
    smem = pl.BlockSpec(memory_space=pltpu.SMEM)
    anywhere = pl.BlockSpec(memory_space=pl.ANY)

    def held(block):
        return pltpu.with_memory_space_constraint(block, pltpu.VMEM)

    def in_hbm(block):
        return pltpu.with_memory_space_constraint(block, pltpu.HBM)

    def cost(flops):
        return pl.CostEstimate(flops=flops, bytes_accessed=1000000, transcendentals=0)

    dma = pltpu.SemaphoreType.DMA
    point_row = pltpu.VMEM((1, NPTS), F32)
    flux_block = pltpu.VMEM((200, LANES), F32)
    kern_block = pltpu.VMEM((16, 9 * LANES), F32)
    line_block = pltpu.VMEM((256, LANES), F32)

    def elements(n):
        return pltpu.VMEM((n, 168, LANES), F32)

    def windows(n):
        return pltpu.VMEM((2, n * LANES, LANES), F32)

    fields = (in_hbm(forward_displacement), in_hbm(adjoint_displacement))
    cross = held(jnp.asarray(cross_table()))
    right, left, own, code, parts = pl.pallas_call(
        pack_kernel,
        out_shape=[
            pltpu.VMEM((144, LANES), F32),
            pltpu.VMEM((32, LANES), F32),
            pltpu.VMEM((2 * ROWS, LANES), F32),
            pltpu.VMEM((8, 256), jnp.int32),
            pltpu.VMEM((384, 256), BF16),
        ],
        in_specs=[anywhere] * 5,
        scratch_shapes=[
            pltpu.SMEM((1,), jnp.int32),
            pltpu.VMEM((8, 256), jnp.int32),
            pltpu.VMEM((125, 256), F32),
            point_row,
            point_row,
            pltpu.VMEM((128, 256), F32),
            dma((5,)),
        ],
        cost_estimate=cost(100000000),
        name="pack",
    )(element_count, in_hbm(connectivity), in_hbm(shear_modulus), *fields)
    prev = lax.ppermute(right, "cuts", [(i, (i + 1) % cuts) for i in range(cuts)])

    own_blocks = [elements(4), flux_block, flux_block, windows(1), windows(1), flux_block, kern_block]

    def own_part(turn, before):
        given = (cut, held(own), held(code), held(parts), cross)
        return pl.pallas_call(
            functools.partial(own_kernel, turn),
            out_shape=own_blocks,
            in_specs=[smem] + [vmem] * (4 + len(before)),
            scratch_shapes=[
                pltpu.VMEM((2 * 9 * 24, LANES), F32),
                windows(4),
                line_block,
                elements(1),
                pltpu.VMEM((136, 256), F32),
            ],
            input_output_aliases={len(given) + n: n for n in range(len(before))},
            cost_estimate=cost(300000000),
            name="own_layers",
        )(*given, *[held(block) for block in before])

    left, *blocks = lax.optimization_barrier((left, *own_part(0, [])))
    after = lax.ppermute(left, "cuts", [((i + 1) % cuts, i) for i in range(cuts)])
    elem, flux, near_flux, near_win, near_slope, near_kern, kern = own_part(1, blocks)
    kern = pl.pallas_call(
        near_kernel,
        out_shape=kern_block,
        in_specs=[vmem] * 7,
        scratch_shapes=[
            pltpu.VMEM((72, LANES), F32),
            pltpu.VMEM((2, 64, LANES), F32),
            windows(1),
            elements(1),
            flux_block,
            line_block,
            pltpu.VMEM((136, LANES), F32),
        ],
        cost_estimate=cost(200000000),
        name="near_layers",
    )(held(prev), held(after), held(near_flux), held(near_slope), held(near_kern), held(kern), cross)

    (force,) = pl.pallas_call(
        force_kernel,
        out_shape=[windows(2)],
        in_specs=[vmem] * 2,
        scratch_shapes=[windows(2), line_block],
        cost_estimate=cost(200000000),
        name="forces",
    )(held(elem), held(flux))

    if events == 2:
        other = lax.ppermute(kern, "event", [(0, 1), (1, 0)])
        other, force = lax.optimization_barrier((other, force))
        kern = kern + other
    elif events > 2:
        kern = lax.psum(kern, "event")
    kern_first = lax.ppermute(kern, "cuts", pairs_first)
    kern_second = lax.ppermute(kern, "cuts", pairs_second)

    points = jax.ShapeDtypeStruct((1, NPTS), F32)
    outs = pl.pallas_call(
        step_kernel,
        out_shape=[points] * 4,
        in_specs=[vmem] * 5 + [anywhere] * 5 + [vmem],
        scratch_shapes=[point_row] * 4
        + [pltpu.VMEM((NPTS,), F32), pltpu.VMEM((4 * 144, LANES), F32), pltpu.VMEM((2, ROWS, LANES), F32)]
        + [flux_block, windows(2), elements(2), line_block, windows(2), windows(2)]
        + [pltpu.VMEM((2 * 72, LANES), F32), pltpu.VMEM((136, LANES), F32), dma((5,))],
        cost_estimate=cost(200000000),
        name="step",
    )(
        held(force),
        held(near_win),
        held(near_flux),
        held(prev),
        held(after),
        fields[0],
        in_hbm(forward_velocity),
        fields[1],
        in_hbm(adjoint_velocity),
        in_hbm(inverse_mass),
        held(kern),
    )
    shear_kernel = pl.pallas_call(
        band_kernel,
        out_shape=jax.ShapeDtypeStruct((PXU, PYZ), F32),
        in_specs=[smem] + [vmem] * 4,
        cost_estimate=cost(20000000),
        name="band",
    )(cut, held(kern), held(kern_first), held(kern_second), held(jnp.asarray(band_table())))
    return (*outs, shear_kernel)


def solution(mesh):
    in_specs = (
        P("event", "cuts"),
        P("event", "cuts"),
        P("event", "cuts"),
        P("event", "cuts"),
        P("cuts"),
        P(None, "cuts"),
        P(None, "cuts"),
        P("cuts", None),
        P("cuts"),
    )
    out_specs = (
        P("event", "cuts"),
        P("event", "cuts"),
        P("event", "cuts"),
        P("event", "cuts"),
        P("cuts", None),
    )
    return jax.shard_map(on_device, mesh=mesh, in_specs=in_specs, out_specs=out_specs, check_vma=False)
```

```python
import functools

import numpy as np
import jax
import jax.numpy as jnp
import ml_dtypes
from jax import lax
from jax.experimental import pallas as pl
from jax.experimental.pallas import tpu as pltpu
from jax.sharding import PartitionSpec as P

NGLL = 5
EX, EY, EZ = 4, 8, 8
PXU = 16
PY = 33
PZ = 33
PYZ = 1089
NPTS = 17424
LANES = 128
ROWS = 144
TIME_STEP = 0.02
OWN_OUTS, OWN_SCRATCH = 7, 5
F32 = jnp.float32
BF16 = jnp.bfloat16


def gll():
    nodes = np.array([-1.0, -np.sqrt(3.0 / 7.0), 0.0, np.sqrt(3.0 / 7.0), 1.0])
    bary = np.array([1.0 / np.prod([nodes[r] - nodes[c] for c in range(5) if c != r]) for r in range(5)])
    d = np.zeros((5, 5))
    for r in range(5):
        for c in range(5):
            if c != r:
                d[r, c] = bary[c] / bary[r] / (nodes[r] - nodes[c])
        d[r, r] = -np.sum(d[r])
    return d


DERIV = gll()


def split_np(x):
    x = np.asarray(x, np.float32)
    parts = []
    for _ in range(3):
        p = x.astype(ml_dtypes.bfloat16)
        parts.append(p)
        x = x - p.astype(np.float32)
    return parts


ROW_PLANE = np.array([4 * (r % 3) + r // 3 for r in range(12)] + [12, 13, 14, 15])
OWN_AT = [[3 * i + m for i in range(5)] for m in range(3)]
NEAR_AT = [[8, 9, 10, 11, 0], [4, 5, 6, 7, 12]]


def band_table():
    offsets = np.arange(-PXU, PXU + 1)
    w = lambda d: np.exp(-d * d / (2.0 * (PXU / 4.0) ** 2))
    total = w(offsets.astype(np.float64)).sum()
    out = []
    for first in (-PXU, PXU):
        source = np.concatenate([ROW_PLANE, ROW_PLANE + first, ROW_PLANE - first])
        spread = np.arange(PXU)[:, None] - source[None, :]
        band = w(spread.astype(np.float64)) * (np.abs(spread) <= PXU) / total
        b1, b2, b3 = split_np(band)
        out.append(np.concatenate([b1, b1, b1, b2, b2, b3], axis=1))
    return np.stack(out)


def cross_table():
    off = np.arange(-4, 5)
    k = np.exp(-off * off / (2.0 * 1.5 * 1.5))
    point = np.arange(33)
    inside = ((point[None, :] + off[:, None]) >= 0) & ((point[None, :] + off[:, None]) < 33)
    taps = k[:, None] * inside
    taps = taps / taps.sum(axis=0, keepdims=True)
    out = np.zeros((24, 1152), np.float32)
    out[0:9, :PYZ] = np.tile(taps, (1, PY))
    out[9:18, :PYZ] = np.repeat(taps, PZ, axis=1)
    return out


def split3(x):
    hi = x.astype(BF16)
    rest = x - hi.astype(F32)
    mid = rest.astype(BF16)
    low = (rest - mid.astype(F32)).astype(BF16)
    return hi, mid, low


def dot_nt(a, b):
    return lax.dot_general(a, b, (((1,), (1,)), ((), ())), preferred_element_type=F32)


def fetch(sem, *pairs):
    copies = [pltpu.make_async_copy(src, dst, sem.at[n]) for n, (src, dst) in enumerate(pairs)]
    for c in copies:
        c.start()
    return copies


def add_parts(stacked):
    n = stacked.shape[0] // 3
    return stacked[0:n] + (stacked[n : 2 * n] + stacked[2 * n : 3 * n])


def pack_kernel(
    conn_hbm, shear_hbm, fwd_hbm, adj_hbm,
    right_ref, left_ref, own_ref, code_ref, parts_ref,
    conn_ref, shear_ref, fwd_ref, adj_ref, block_ref, sem,
):
    copies = fetch(
        sem,
        (shear_hbm, shear_ref),
        (conn_hbm.at[0:8], conn_ref),
        (fwd_hbm, fwd_ref),
        (adj_hbm, adj_ref),
    )
    copies[1].wait()
    point = conn_ref[0:1, :].astype(F32)
    x = jnp.floor((point + 0.5) * (1.0 / PYZ))
    rest = point - x * PYZ
    y = jnp.floor((rest + 0.5) * (1.0 / PZ))
    z = rest - y * PZ
    code = (8.0 * z + 2.0 * x + 0.25 * y).astype(jnp.int32)
    slot = lax.broadcasted_iota(jnp.int32, (1, 256), 1)
    code_ref[...] = jnp.broadcast_to(code, (8, 256))
    lane = lax.broadcasted_iota(jnp.int32, (LANES, 256), 0)
    pick = jnp.where(code == ((lane >> 3) & 7) * 32 + 24 + (lane & 7), 1.0, 0.0).astype(BF16)
    for f, ref in enumerate((fwd_ref, adj_ref)):
        copies[2 + f].wait()
        for r in range(0, 136, 8):
            own_ref[ROWS * f + r : ROWS * f + r + 8, :] = ref[0:1, r * LANES : (r + 8) * LANES].reshape(8, LANES)
        own_ref[ROWS * f + 136 : ROWS * f + 144, :] = jnp.zeros((8, LANES), F32)
        own_ref[ROWS * f + 136 : ROWS * f + 137, 0:16] = ref[0:1, NPTS - 16 : NPTS]
        right_ref[40 * f : 40 * f + 40, :] = own_ref[ROWS * f + 102 : ROWS * f + 142, :]
        left_ref[16 * f : 16 * f + 16, :] = own_ref[ROWS * f : ROWS * f + 16, :]
    copies[0].wait()
    block_ref[0:125, :] = shear_ref[...]
    block_ref[125:126, :] = slot.astype(F32)
    block_ref[126:128, :] = jnp.zeros((2, 256), F32)
    parts = jnp.concatenate(split3(block_ref[...]), axis=0)
    parts_ref[...] = parts
    flux = add_parts(dot_nt(parts, pick))
    low = lax.broadcasted_iota(jnp.int32, (64, LANES), 1) < 64
    right_ref[80:144, :] = jnp.where(low, flux[0:64], flux[64:128])


def gll_weight(i):
    return (0.1, 49.0 / 90.0, 32.0 / 45.0, 49.0 / 90.0, 0.1)[i]


def lane_weight(places):
    chunk = lax.broadcasted_iota(jnp.int32, (8, LANES), 1) >> 3
    weight = jnp.zeros((8, LANES), F32)
    for row in places:
        for i, place in enumerate(row):
            weight = jnp.where(chunk == place, gll_weight(i), weight)
    return weight


def scaled(ref, weight):
    for j in range(5):
        for k in range(5):
            r = (j * 5 + k) * 8
            ref[r : r + 8, :] = ref[r : r + 8, :] * (weight * (gll_weight(j) * gll_weight(k)))


def place_flux(ref, tile_of, moves, layers=range(NGLL)):
    lane = lax.broadcasted_iota(jnp.int32, (32, LANES), 1)
    for ez in range(EZ):
        total = jnp.zeros((32, LANES), F32)
        for i in layers:
            tile, start = tile_of(i, ez)
            for source, target, width in moves(i):
                shift = (target - source - start) % LANES
                moved = pltpu.roll(tile, shift, 1) if shift else tile
                total = jnp.where((lane >= target) & (lane < target + width), moved, total)
        ref[pl.ds(ez, 25, stride=8), :] = total[0:25]


def derive(e):
    d = DERIV
    s0, s1 = e[0] + e[4], e[1] + e[3]
    d0, d1 = e[0] - e[4], e[1] - e[3]
    out = [None] * 5
    for i in (0, 1):
        even = float((d[i, 0] - d[i, 4]) / 2) * d0 + float((d[i, 1] - d[i, 3]) / 2) * d1
        odd = float((d[i, 0] + d[i, 4]) / 2) * s0 + float((d[i, 1] + d[i, 3]) / 2) * s1 + float(d[i, 2]) * e[2]
        out[i] = odd + even
        out[4 - i] = even - odd
    out[2] = float(d[2, 0]) * d0 + float(d[2, 1]) * d1
    return out


def derive_back(t):
    d = DERIV
    s0, s1 = t[0] + t[4], t[1] + t[3]
    d0, d1 = t[0] - t[4], t[1] - t[3]
    out = [None] * 5
    for i in (0, 1):
        even = float((d[0, i] - d[4, i]) / 2) * d0 + float((d[1, i] - d[3, i]) / 2) * d1
        odd = float((d[0, i] + d[4, i]) / 2) * s0 + float((d[1, i] + d[3, i]) / 2) * s1 + float(d[2, i]) * t[2]
        out[i] = odd + even
        out[4 - i] = even - odd
    out[2] = float(d[0, 2]) * d0 + float(d[1, 2]) * d1
    return out


def shifted(tiles, distance, lane):
    skip, part = divmod(distance, LANES)
    if part == 0:
        moved = tiles
        pick = None
    else:
        moved = [pltpu.roll(t, LANES - part, 1) for t in tiles]
        pick = lane < LANES - part
    n = len(tiles)
    out = []
    for i in range(n):
        a = moved[(i + skip) % n]
        b = moved[(i + skip + 1) % n]
        out.append(a if pick is None else jnp.where(pick, a, b))
    return out


def plane_of(ref, start, row):
    r0, off = divmod(start, LANES)
    lane9 = lax.broadcasted_iota(jnp.int32, (9, LANES), 1)
    flat = ref[row + r0 : row + r0 + 9, :]
    if off:
        flat = jnp.where(
            lane9 < LANES - off,
            pltpu.roll(flat, LANES - off, 1),
            pltpu.roll(ref[row + r0 + 1 : row + r0 + 10, :], LANES - off, 1),
        )
    return flat


def store_plane(ref, row, flat):
    ref[pl.ds(row, 9, stride=16), :] = flat


def make_windows(plane_ref, base, pitch, win_ref, row):
    lane = lax.broadcasted_iota(jnp.int32, (8, LANES), 1)
    tiles = [plane_ref[base + t * pitch : base + t * pitch + 8, :] for t in range(9)]
    for ey in range(EY):
        near = [tiles[ey], tiles[ey + 1], tiles[min(ey + 2, 8)]]
        if ey:
            near = [pltpu.roll(t, LANES - 4 * ey, 1) for t in near]
            keep = lane < LANES - 4 * ey
            near = [jnp.where(keep, near[0], near[1]), jnp.where(keep, near[1], near[2])]
        for w in range(2):
            win_ref[w, pl.ds(row + ey, 8, stride=8), :] = near[w]


def along_x(win_ref, base, row, combine):
    for w in range(2):
        values = combine([win_ref[w, base + 8 * c : base + 8 * c + 8, :] for c in row])
        for i, v in enumerate(values):
            yield w, i, v


def turned(win_ref, base, elem_ref, column):
    elem_ref[column, 0:LANES, :] = win_ref[0, base : base + LANES, :].T
    elem_ref[column, LANES:168, :] = win_ref[1, base : base + LANES, :].T[0:40, :]


def part(ref, column, j, k):
    return ref[column, pl.ds(j * PZ + k, 8, stride=4), :]


def flux_part(ref, j, k):
    r = (j * 5 + k) * 8
    return ref[r : r + 8, :]


def folded(term, line_ref, win_ref, base):
    row = lax.broadcasted_iota(jnp.int32, (8, LANES), 0)
    line_ref[160:256, :] = jnp.zeros((96, LANES), F32)
    for j in range(5):
        for k in range(1, 4):
            line_ref[pl.ds(j * PZ + k, 8, stride=4), :] = term[j][k]
        last = term[j][4]
        line_ref[pl.ds(j * PZ, 8, stride=4), :] = term[j][0] + jnp.where(row == 0, 0.0, pltpu.roll(last, 1, 0))
        line_ref[j * PZ + 32 : j * PZ + 33, :] = last[7:8, :]
    for w in range(2):
        win_ref[w, base : base + LANES, :] = line_ref[w * LANES : (w + 1) * LANES, :].T


def force_terms(elem_ref, value, slope, flux_ref, line_ref, win_ref, row):
    term = [[None] * 5 for _ in range(5)]
    for k in range(5):
        grads = derive([part(elem_ref, value, j, k) for j in range(5)])
        for j, v in enumerate(derive_back([g * flux_part(flux_ref, j, k) for j, g in enumerate(grads)])):
            term[j][k] = v
    for j in range(5):
        grads = derive([part(elem_ref, value, j, k) for k in range(5)])
        for k, v in enumerate(derive_back([g * flux_part(flux_ref, j, k) for k, g in enumerate(grads)])):
            term[j][k] = term[j][k] + v
    folded(term, line_ref, win_ref, row)
    term = [[part(elem_ref, slope, j, k) * flux_part(flux_ref, j, k) for k in range(5)] for j in range(5)]
    folded(term, line_ref, win_ref, row + LANES)


def cross_smoothed(tiles, cross_ref):
    lane = lax.broadcasted_iota(jnp.int32, tiles[0].shape, 1)
    for base, step in ((0, 1), (9, PZ)):
        total = None
        for tap in range(9):
            moved = shifted(tiles, step * (tap - 4), lane) if tap != 4 else tiles
            terms = [v * cross_ref[base + tap : base + tap + 1, t * LANES : (t + 1) * LANES] for t, v in enumerate(moved)]
            total = terms if total is None else [a + b for a, b in zip(total, terms)]
        tiles = total
    return tiles


def own_kernel(turn, cut_ref, count_ref, own_ref, code_ref, parts_ref, cross_ref, *refs):
    refs = refs[-OWN_OUTS - OWN_SCRATCH :]
    mine = (cut_ref[0] == 0) if turn == 0 else (cut_ref[0] != 0)

    @pl.when(mine)
    def _():
        own_layers(count_ref, own_ref, code_ref, parts_ref, cross_ref, *refs)


def own_layers(
    count_ref, own_ref, code_ref, parts_ref, cross_ref,
    elem_ref, flux_ref, near_flux_ref, near_win_ref, near_slope_ref, near_kern_ref, kern_ref,
    plane_ref, win_ref, line_ref, near_elem_ref, moved_ref,
):
    plane_ref[...] = jnp.zeros(plane_ref.shape, F32)
    for f in range(2):
        base = 24 * 9 * f
        for x in range(PXU):
            flat = plane_of(own_ref, PYZ * x, ROWS * f)
            rows = [OWN_AT[x // 4][x % 4]] if x < 12 else [16 + NEAR_AT[1][x - 12]]
            if x % 4 == 0:
                rows.append(OWN_AT[x // 4 - 1][4] if x else 16 + NEAR_AT[0][4])
            for r in rows:
                plane_ref[pl.ds(base + r, 9, stride=24), :] = flat
        for h in range(2):
            make_windows(plane_ref, base + 8 * h, 24, win_ref, 128 * f + 64 * h)
        make_windows(plane_ref, base + 16, 24, near_win_ref, 64 * f)
        win_ref[:, 256 + 128 * f : 384 + 128 * f, :] = jnp.zeros((2, LANES, LANES), F32)
        for row in OWN_AT:
            for w, i, v in along_x(win_ref, 128 * f, row, derive):
                r = 256 + 128 * f + 8 * row[i]
                win_ref[w, r : r + 8, :] = v
    for column in range(4):
        turned(win_ref, 128 * column, elem_ref, column)
    turned(near_win_ref, 0, near_elem_ref, 0)
    near_slope_ref[...] = jnp.zeros(near_slope_ref.shape, F32)
    for f in range(2):
        for w in range(2):
            value = [near_win_ref[w, 64 * f + 8 * c : 64 * f + 8 * c + 8, :] for c in (0, 4, 5, 6, 7)]
            near_slope_ref[w, 64 * f : 64 * f + 8, :] = float(DERIV[4, 4]) * value[0]
            for i, v in enumerate(derive(value[1:] + [jnp.zeros((8, LANES), F32)])[:4]):
                r = 64 * f + 8 * NEAR_AT[1][i]
                near_slope_ref[w, r : r + 8, :] = v

    element = lax.broadcasted_iota(jnp.int32, (256, 256), 0)
    slot = lax.broadcasted_iota(jnp.int32, (1, 256), 1)
    live = jnp.concatenate([count_ref[0:1, :], count_ref[0:1, :]], axis=1)
    code = jnp.where(slot < live, code_ref[0:1, :], -1)
    pick = jnp.where(code == element, 1.0, 0.0).astype(BF16)
    moved_ref[0:128, :] = add_parts(dot_nt(parts_ref[...], pick))
    moved_ref[128:136, :] = jnp.zeros((8, 256), F32)

    def tile_of(i, ez):
        t = ez // 4
        return moved_ref[25 * i : 25 * i + 32, t * LANES : (t + 1) * LANES], 32 * (ez % 4)

    place_flux(flux_ref, tile_of, lambda i: [(0, 24 * i, 24)])
    place_flux(near_flux_ref, tile_of, lambda i: [(24, 8 * NEAR_AT[1][i], 8)])
    scaled(flux_ref, lane_weight(OWN_AT))
    scaled(near_flux_ref, lane_weight(NEAR_AT))

    kern = [[None] * 5 for _ in range(5)]
    near = [[None] * 5 for _ in range(5)]
    for k in range(5):
        fwd, adj, both = [derive([part(ref, c, j, k) for j in range(5)]) for ref, c in ((elem_ref, 0), (elem_ref, 1), (near_elem_ref, 0))]
        for j in range(5):
            kern[j][k] = fwd[j] * adj[j] + part(elem_ref, 2, j, k) * part(elem_ref, 3, j, k)
            near[j][k] = both[j] * pltpu.roll(both[j], 64, 1)
    for j in range(5):
        fwd, adj, both = [derive([part(ref, c, j, k) for k in range(5)]) for ref, c in ((elem_ref, 0), (elem_ref, 1), (near_elem_ref, 0))]
        for k in range(5):
            kern[j][k] = -(kern[j][k] + fwd[k] * adj[k]) * flux_part(flux_ref, j, k)
            r = (j * 5 + k) * 8
            near_kern_ref[r : r + 8, :] = near[j][k] + both[k] * pltpu.roll(both[k], 64, 1)
    folded(kern, line_ref, win_ref, 0)
    low, high = [gathered(win_ref, 0, h) for h in range(2)]
    row = lax.broadcasted_iota(jnp.int32, (8, LANES), 0)
    tiles = []
    for t in range(9):
        first = low[t] + jnp.where((row == 1) | (row == 2), pltpu.roll(high[t], 5, 0), 0.0)
        second = jnp.where(row < 4, high[t], jnp.where(row == 4, pltpu.roll(high[t], 6, 0), 0.0))
        tiles.append(jnp.concatenate([first, second], axis=0))
    for t, tile in enumerate(cross_smoothed(tiles, cross_ref)):
        kern_ref[:, t * LANES : (t + 1) * LANES] = tile


def message_flux(prev_ref, count_ref, spread_ref):
    upper = pltpu.roll(prev_ref[80:144, :], 64, 1)
    live = upper[61:62, :] < count_ref[0:1, :].astype(F32)
    spread_ref[0:64, :] = jnp.where(live, prev_ref[80:144, :], 0.0)
    spread_ref[64:128, :] = jnp.where(live, upper, 0.0)
    spread_ref[128:136, :] = jnp.zeros((8, LANES), F32)
    return lambda i, ez: (spread_ref[25 * i : 25 * i + 32, :], 8 * ez)


def near_kernel(
    prev_ref, next_ref, count_ref, flux_in_ref, slope_ref, near_kern_ref, kern_in_ref, cross_ref,
    kern_ref,
    plane_ref, new_ref, win_ref, elem_ref, flux_ref, line_ref, spread_ref,
):
    plane_ref[...] = jnp.zeros(plane_ref.shape, F32)
    for f in range(2):
        share = None
        for l in range(4):
            term = float(DERIV[4, l]) * plane_of(prev_ref, 12 + PYZ * l, 40 * f)
            share = term if share is None else share + term
        plane_ref[pl.ds(f, 9, stride=8), :] = share
        plane_ref[pl.ds(2 + f, 9, stride=8), :] = plane_of(next_ref, 0, 16 * f)
    make_windows(plane_ref, 0, 8, new_ref, 0)
    win_ref[...] = slope_ref[...]
    for f in range(2):
        for w in range(2):
            r = 64 * f
            win_ref[w, r : r + 8, :] = win_ref[w, r : r + 8, :] + new_ref[w, 8 * f : 8 * f + 8, :]
            for i in range(4):
                r = 64 * f + 8 * NEAR_AT[1][i]
                new = float(DERIV[i, 4]) * new_ref[w, 16 + 8 * f : 24 + 8 * f, :]
                win_ref[w, r : r + 8, :] = win_ref[w, r : r + 8, :] + new
    turned(win_ref, 0, elem_ref, 0)
    place_flux(flux_ref, message_flux(prev_ref, count_ref, spread_ref), lambda i: [(0, 8 * NEAR_AT[0][i], 8)], (4,))
    scaled(flux_ref, lane_weight([NEAR_AT[0]]))
    kern = [[None] * 5 for _ in range(5)]
    for j in range(5):
        for k in range(5):
            slope = part(elem_ref, 0, j, k)
            total = flux_part(near_kern_ref, j, k) + slope * pltpu.roll(slope, 64, 1)
            kern[j][k] = -total * (flux_part(flux_ref, j, k) + flux_part(flux_in_ref, j, k))
    folded(kern, line_ref, win_ref, 0)
    row = lax.broadcasted_iota(jnp.int32, (8, LANES), 0)
    tiles = [jnp.where((row == 0) | (row >= 4), v, 0.0) for v in gathered(win_ref, 0, 0)]
    for t, tile in enumerate(cross_smoothed(tiles, cross_ref)):
        columns = slice(t * LANES, (t + 1) * LANES)
        kern_ref[0:8, columns] = kern_in_ref[0:8, columns] + jnp.where(row == 0, tile, 0.0)
        kern_ref[8:16, columns] = kern_in_ref[8:16, columns] + jnp.where(row >= 4, tile, 0.0)


def gathered(win_ref, base, h):
    lane = lax.broadcasted_iota(jnp.int32, (8, LANES), 1)
    tiles = [None] * 9
    for ey in range(EY):
        rows = pl.ds(base + h * 64 + ey, 8, stride=8)
        a, b = win_ref[0, rows, :], win_ref[1, rows, :]
        if ey:
            a, b = pltpu.roll(a, 4 * ey, 1), pltpu.roll(b, 4 * ey, 1)
            keep = lane >= 4 * ey
            a, b = jnp.where(keep, a, 0.0), jnp.where(keep, b, a)
        tiles[ey] = a if ey == 0 else tiles[ey] + a
        tiles[ey + 1] = b
    return tiles


def summed_along_x(win_ref, places, out_ref, row):
    for line in places:
        for w, i, v in along_x(win_ref, LANES, line, derive_back):
            r = 8 * line[i]
            out_ref[w, row + r : row + r + 8, :] = win_ref[w, r : r + 8, :] + v


def force_kernel(elem_ref, flux_ref, out_ref, win_ref, line_ref):
    for f in range(2):
        force_terms(elem_ref, f, 2 + f, flux_ref, line_ref, win_ref, 0)
        summed_along_x(win_ref, OWN_AT, out_ref, LANES * f)


def step_kernel(
    force_ref, near_half_ref, near_flux_ref, prev_ref, next_ref, count_ref, fwd_hbm, fwd_speed_hbm, adj_hbm, adj_speed_hbm, mass_hbm, after_ref,
    fwd_out_ref, fwd_speed_out_ref, adj_out_ref, adj_speed_out_ref,
    fwd_ref, fwd_speed_ref, adj_ref, adj_speed_ref, mass_ref, plane_ref, line_ref,
    flux_ref, win_ref, elem_ref, fold_ref, near_ref, near_win_ref, near_plane_ref, spread_ref, sem,
):
    copies = fetch(
        sem,
        (fwd_hbm, fwd_ref),
        (fwd_speed_hbm, fwd_speed_ref),
        (adj_hbm, adj_ref),
        (adj_speed_hbm, adj_speed_ref),
        (mass_hbm, mass_ref),
    )
    lane9 = lax.broadcasted_iota(jnp.int32, (9, LANES), 1)
    near_plane_ref[...] = jnp.zeros(near_plane_ref.shape, F32)
    for f in range(2):
        for i in range(5):
            flat = plane_of(prev_ref, 12 + PYZ * i, 40 * f) if i < 4 else plane_of(next_ref, 0, 16 * f)
            near_plane_ref[pl.ds(72 * f + i, 9, stride=8), :] = flat
        near_win_ref[:, 128 * f : 128 * f + 64, :] = near_half_ref[:, 64 * f : 64 * f + 64, :]
        make_windows(near_plane_ref, 72 * f, 8, near_win_ref, 128 * f + 64)
    place_flux(flux_ref, message_flux(prev_ref, count_ref, spread_ref), lambda i: [(0, 8 * NEAR_AT[0][i], 8)])
    scaled(flux_ref, lane_weight([NEAR_AT[0]]))
    flux_ref[...] = flux_ref[...] + near_flux_ref[...]
    for f in range(2):
        win_ref[...] = jnp.zeros(win_ref.shape, F32)
        for row in NEAR_AT:
            for w, i, v in along_x(near_win_ref, LANES * f, row, derive):
                win_ref[w, 8 * row[i] : 8 * row[i] + 8, :] = v
        turned(near_win_ref, LANES * f, elem_ref, 0)
        turned(win_ref, 0, elem_ref, 1)
        force_terms(elem_ref, 0, 1, flux_ref, fold_ref, win_ref, 0)
        summed_along_x(win_ref, NEAR_AT, near_ref, LANES * f)
    for n in range(4):
        for h in range(2):
            source = force_ref if n < 2 else near_ref
            for t, tile in enumerate(gathered(source, 128 * (n % 2), h)):
                plane_ref[n * 144 + t * 16 + 8 * h : n * 144 + t * 16 + 8 * h + 8, :] = tile
    line_ref[...] = jnp.zeros(line_ref.shape, F32)
    for f in range(2):
        for x in range(PXU):
            r0, off = divmod(PYZ * x, LANES)
            i, m = x % 4, x // 4
            rows = [144 * f + OWN_AT[m][i] if m < 3 else 288 + 144 * f + NEAR_AT[1][i]]
            if i == 0:
                rows.append(144 * f + OWN_AT[m - 1][4] if m > 0 else 288 + 144 * f + NEAR_AT[0][4])
            flat = plane_ref[pl.ds(rows[0], 9, stride=16), :]
            if i == 0:
                flat = flat + plane_ref[pl.ds(rows[1], 9, stride=16), :]
            if off:
                flat = pltpu.roll(flat, off, 1)
                spill = jnp.where(lane9 < off, flat, 0.0)
                flat = jnp.where(lane9 < off, 0.0, flat)
            line_ref[f, r0 : r0 + 9, :] = line_ref[f, r0 : r0 + 9, :] + flat
            if off:
                line_ref[f, r0 + 1 : r0 + 10, :] = line_ref[f, r0 + 1 : r0 + 10, :] + spill

    def step(lo, hi, force):
        shape = (hi - lo) // force[0].shape[1], force[0].shape[1]
        take = lambda ref: ref[0:1, lo:hi].reshape(shape)
        scale = TIME_STEP * mass_ref[lo:hi].reshape(shape)
        speed = take(fwd_speed_ref) + scale * force[0]
        fwd_speed_out_ref[0:1, lo:hi] = speed.reshape(1, hi - lo)
        fwd_out_ref[0:1, lo:hi] = (take(fwd_ref) - TIME_STEP * speed).reshape(1, hi - lo)
        speed = take(adj_speed_ref) - scale * force[1]
        adj_speed_out_ref[0:1, lo:hi] = speed.reshape(1, hi - lo)
        adj_out_ref[0:1, lo:hi] = (take(adj_ref) + TIME_STEP * speed).reshape(1, hi - lo)

    for c in copies:
        c.wait()
    for r in range(0, 136, 8):
        step(r * LANES, (r + 8) * LANES, [line_ref[f, r : r + 8, :] for f in range(2)])
    step(NPTS - 16, NPTS, [line_ref[f, 136:137, 0:16] for f in range(2)])


def band_kernel(cut_ref, own_ref, first_ref, second_ref, band_ref, out_ref):
    flat = jnp.concatenate([own_ref[...], first_ref[...], second_ref[...]], axis=0)
    k1 = flat.astype(BF16)
    rest = flat - k1.astype(F32)
    k2 = rest.astype(BF16)
    k3 = (rest - k2.astype(F32)).astype(BF16)
    stacked = jnp.concatenate([k1, k2, k3, k1, k2, k1], axis=0)
    band = band_ref[cut_ref[0] & 1]
    out_ref[...] = jnp.dot(band, stacked, preferred_element_type=F32)[:, :PYZ]


def on_device(
    forward_displacement,
    forward_velocity,
    adjoint_displacement,
    adjoint_velocity,
    inverse_mass,
    shear_modulus,
    connectivity,
    face_points,
    element_count,
):
    events = lax.axis_size("event")
    cuts = lax.axis_size("cuts")
    cut = lax.axis_index("cuts").astype(jnp.int32).reshape(1)
    pairs_first = [(i, (i - 1 if i % 2 == 0 else i + 1) % cuts) for i in range(cuts)]
    pairs_second = [(i, (i + 1 if i % 2 == 0 else i - 1) % cuts) for i in range(cuts)]

    vmem = pl.BlockSpec(memory_space=pltpu.VMEM)
    smem = pl.BlockSpec(memory_space=pltpu.SMEM)
    anywhere = pl.BlockSpec(memory_space=pl.ANY)

    def held(block):
        return pltpu.with_memory_space_constraint(block, pltpu.VMEM)

    def in_hbm(block):
        return pltpu.with_memory_space_constraint(block, pltpu.HBM)

    def cost(flops):
        return pl.CostEstimate(flops=flops, bytes_accessed=1000000, transcendentals=0)

    dma = pltpu.SemaphoreType.DMA
    point_row = pltpu.VMEM((1, NPTS), F32)
    flux_block = pltpu.VMEM((200, LANES), F32)
    kern_block = pltpu.VMEM((16, 9 * LANES), F32)
    line_block = pltpu.VMEM((256, LANES), F32)

    def elements(n):
        return pltpu.VMEM((n, 168, LANES), F32)

    def windows(n):
        return pltpu.VMEM((2, n * LANES, LANES), F32)

    fields = (in_hbm(forward_displacement), in_hbm(adjoint_displacement))
    cross = held(jnp.asarray(cross_table()))
    right, left, own, code, parts = pl.pallas_call(
        pack_kernel,
        out_shape=[
            pltpu.VMEM((144, LANES), F32),
            pltpu.VMEM((32, LANES), F32),
            pltpu.VMEM((2 * ROWS, LANES), F32),
            pltpu.VMEM((8, 256), jnp.int32),
            pltpu.VMEM((384, 256), BF16),
        ],
        in_specs=[anywhere] * 4,
        scratch_shapes=[
            pltpu.VMEM((8, 256), jnp.int32),
            pltpu.VMEM((125, 256), F32),
            point_row,
            point_row,
            pltpu.VMEM((128, 256), F32),
            dma((4,)),
        ],
        cost_estimate=cost(100000000),
        name="pack",
    )(in_hbm(connectivity), in_hbm(shear_modulus), *fields)
    to_next = [(i, (i + 1) % cuts) for i in range(cuts)]
    prev = lax.ppermute(right, "cuts", to_next)
    count, left = lax.optimization_barrier((element_count, left))
    count = jnp.broadcast_to(count.reshape(1, 1), (8, LANES))
    prev_count = lax.ppermute(count, "cuts", to_next)
    count, left = lax.optimization_barrier((count, left))

    own_blocks = [elements(4), flux_block, flux_block, windows(1), windows(1), flux_block, kern_block]

    def own_part(turn, before):
        given = (cut, held(count), held(own), held(code), held(parts), cross)
        return pl.pallas_call(
            functools.partial(own_kernel, turn),
            out_shape=own_blocks,
            in_specs=[smem] + [vmem] * (5 + len(before)),
            scratch_shapes=[
                pltpu.VMEM((2 * 9 * 24, LANES), F32),
                windows(4),
                line_block,
                elements(1),
                pltpu.VMEM((136, 256), F32),
            ],
            input_output_aliases={len(given) + n: n for n in range(len(before))},
            cost_estimate=cost(300000000),
            name="own_layers",
        )(*given, *[held(block) for block in before])

    left, *blocks = lax.optimization_barrier((left, *own_part(0, [])))
    after = lax.ppermute(left, "cuts", [((i + 1) % cuts, i) for i in range(cuts)])
    elem, flux, near_flux, near_win, near_slope, near_kern, kern = own_part(1, blocks)
    kern = pl.pallas_call(
        near_kernel,
        out_shape=kern_block,
        in_specs=[vmem] * 8,
        scratch_shapes=[
            pltpu.VMEM((72, LANES), F32),
            pltpu.VMEM((2, 64, LANES), F32),
            windows(1),
            elements(1),
            flux_block,
            line_block,
            pltpu.VMEM((136, LANES), F32),
        ],
        cost_estimate=cost(200000000),
        name="near_layers",
    )(held(prev), held(after), held(prev_count), held(near_flux), held(near_slope), held(near_kern), held(kern), cross)

    (force,) = pl.pallas_call(
        force_kernel,
        out_shape=[windows(2)],
        in_specs=[vmem] * 2,
        scratch_shapes=[windows(2), line_block],
        cost_estimate=cost(200000000),
        name="forces",
    )(held(elem), held(flux))

    if events == 2:
        other = lax.ppermute(kern, "event", [(0, 1), (1, 0)])
        other, force = lax.optimization_barrier((other, force))
        kern = kern + other
    elif events > 2:
        kern = lax.psum(kern, "event")
    kern_first = lax.ppermute(kern, "cuts", pairs_first)
    kern_second = lax.ppermute(kern, "cuts", pairs_second)

    points = jax.ShapeDtypeStruct((1, NPTS), F32)
    outs = pl.pallas_call(
        step_kernel,
        out_shape=[points] * 4,
        in_specs=[vmem] * 6 + [anywhere] * 5 + [vmem],
        scratch_shapes=[point_row] * 4
        + [pltpu.VMEM((NPTS,), F32), pltpu.VMEM((4 * 144, LANES), F32), pltpu.VMEM((2, ROWS, LANES), F32)]
        + [flux_block, windows(2), elements(2), line_block, windows(2), windows(2)]
        + [pltpu.VMEM((2 * 72, LANES), F32), pltpu.VMEM((136, LANES), F32), dma((5,))],
        cost_estimate=cost(200000000),
        name="step",
    )(
        held(force),
        held(near_win),
        held(near_flux),
        held(prev),
        held(after),
        held(prev_count),
        fields[0],
        in_hbm(forward_velocity),
        fields[1],
        in_hbm(adjoint_velocity),
        in_hbm(inverse_mass),
        held(kern),
    )
    shear_kernel = pl.pallas_call(
        band_kernel,
        out_shape=jax.ShapeDtypeStruct((PXU, PYZ), F32),
        in_specs=[smem] + [vmem] * 4,
        cost_estimate=cost(20000000),
        name="band",
    )(cut, held(kern), held(kern_first), held(kern_second), held(jnp.asarray(band_table())))
    return (*outs, shear_kernel)


def solution(mesh):
    in_specs = (
        P("event", "cuts"),
        P("event", "cuts"),
        P("event", "cuts"),
        P("event", "cuts"),
        P("cuts"),
        P(None, "cuts"),
        P(None, "cuts"),
        P("cuts", None),
        P("cuts"),
    )
    out_specs = (
        P("event", "cuts"),
        P("event", "cuts"),
        P("event", "cuts"),
        P("event", "cuts"),
        P("cuts", None),
    )
    return jax.shard_map(on_device, mesh=mesh, in_specs=in_specs, out_specs=out_specs, check_vma=False)
```

```python
import functools

import numpy as np
import jax
import jax.numpy as jnp
import ml_dtypes
from jax import lax
from jax.experimental import pallas as pl
from jax.experimental.pallas import tpu as pltpu
from jax.sharding import PartitionSpec as P

NGLL = 5
EX, EY, EZ = 4, 8, 8
PXU = 16
PY = 33
PZ = 33
PYZ = 1089
NPTS = 17424
LANES = 128
ROWS = 144
TIME_STEP = 0.02
OWN_OUTS, OWN_SCRATCH = 7, 5
F32 = jnp.float32
BF16 = jnp.bfloat16


def gll():
    nodes = np.array([-1.0, -np.sqrt(3.0 / 7.0), 0.0, np.sqrt(3.0 / 7.0), 1.0])
    bary = np.array([1.0 / np.prod([nodes[r] - nodes[c] for c in range(5) if c != r]) for r in range(5)])
    d = np.zeros((5, 5))
    for r in range(5):
        for c in range(5):
            if c != r:
                d[r, c] = bary[c] / bary[r] / (nodes[r] - nodes[c])
        d[r, r] = -np.sum(d[r])
    return d


DERIV = gll()


def split_np(x):
    x = np.asarray(x, np.float32)
    parts = []
    for _ in range(3):
        p = x.astype(ml_dtypes.bfloat16)
        parts.append(p)
        x = x - p.astype(np.float32)
    return parts


ROW_PLANE = np.array([4 * (r % 3) + r // 3 for r in range(12)] + [12, 13, 14, 15])
OWN_AT = [[3 * i + m for i in range(5)] for m in range(3)]
NEAR_AT = [[8, 9, 10, 11, 0], [4, 5, 6, 7, 12]]


def band_table():
    offsets = np.arange(-PXU, PXU + 1)
    w = lambda d: np.exp(-d * d / (2.0 * (PXU / 4.0) ** 2))
    total = w(offsets.astype(np.float64)).sum()
    out = []
    for first in (-PXU, PXU):
        source = np.concatenate([ROW_PLANE, ROW_PLANE + first, ROW_PLANE - first])
        spread = np.arange(PXU)[:, None] - source[None, :]
        band = w(spread.astype(np.float64)) * (np.abs(spread) <= PXU) / total
        b1, b2, b3 = split_np(band)
        out.append(np.concatenate([b1, b1, b1, b2, b2, b3], axis=1))
    return np.stack(out)


def cross_table():
    off = np.arange(-4, 5)
    k = np.exp(-off * off / (2.0 * 1.5 * 1.5))
    point = np.arange(33)
    inside = ((point[None, :] + off[:, None]) >= 0) & ((point[None, :] + off[:, None]) < 33)
    taps = k[:, None] * inside
    taps = taps / taps.sum(axis=0, keepdims=True)
    out = np.zeros((24, 1152), np.float32)
    out[0:9, :PYZ] = np.tile(taps, (1, PY))
    out[9:18, :PYZ] = np.repeat(taps, PZ, axis=1)
    return out


def split3(x):
    hi = x.astype(BF16)
    rest = x - hi.astype(F32)
    mid = rest.astype(BF16)
    low = (rest - mid.astype(F32)).astype(BF16)
    return hi, mid, low


def dot_nt(a, b):
    return lax.dot_general(a, b, (((1,), (1,)), ((), ())), preferred_element_type=F32)


def fetch(sem, *pairs):
    copies = [pltpu.make_async_copy(src, dst, sem.at[n]) for n, (src, dst) in enumerate(pairs)]
    for c in copies:
        c.start()
    return copies


def add_parts(stacked):
    n = stacked.shape[0] // 3
    return stacked[0:n] + (stacked[n : 2 * n] + stacked[2 * n : 3 * n])


def pack_kernel(
    conn_hbm, shear_hbm, fwd_hbm, adj_hbm,
    right_ref, left_ref, own_ref, code_ref, parts_ref,
    conn_ref, shear_ref, fwd_ref, adj_ref, block_ref, sem,
):
    copies = fetch(
        sem,
        (shear_hbm, shear_ref),
        (conn_hbm.at[0:8], conn_ref),
        (fwd_hbm, fwd_ref),
        (adj_hbm, adj_ref),
    )
    copies[1].wait()
    point = conn_ref[0:1, :].astype(F32)
    x = jnp.floor((point + 0.5) * (1.0 / PYZ))
    rest = point - x * PYZ
    y = jnp.floor((rest + 0.5) * (1.0 / PZ))
    z = rest - y * PZ
    code = (8.0 * z + 2.0 * x + 0.25 * y).astype(jnp.int32)
    slot = lax.broadcasted_iota(jnp.int32, (1, 256), 1)
    code_ref[...] = jnp.broadcast_to(code, (8, 256))
    lane = lax.broadcasted_iota(jnp.int32, (LANES, 256), 0)
    pick = jnp.where(code == ((lane >> 3) & 7) * 32 + 24 + (lane & 7), 1.0, 0.0).astype(BF16)
    for f, ref in enumerate((fwd_ref, adj_ref)):
        copies[2 + f].wait()
        for r in range(0, 136, 8):
            own_ref[ROWS * f + r : ROWS * f + r + 8, :] = ref[0:1, r * LANES : (r + 8) * LANES].reshape(8, LANES)
        own_ref[ROWS * f + 136 : ROWS * f + 144, :] = jnp.zeros((8, LANES), F32)
        own_ref[ROWS * f + 136 : ROWS * f + 137, 0:16] = ref[0:1, NPTS - 16 : NPTS]
        right_ref[40 * f : 40 * f + 40, :] = own_ref[ROWS * f + 102 : ROWS * f + 142, :]
        left_ref[16 * f : 16 * f + 16, :] = own_ref[ROWS * f : ROWS * f + 16, :]
    copies[0].wait()
    block_ref[0:125, :] = shear_ref[...]
    block_ref[125:126, :] = slot.astype(F32)
    block_ref[126:128, :] = jnp.zeros((2, 256), F32)
    parts = jnp.concatenate(split3(block_ref[...]), axis=0)
    parts_ref[...] = parts
    flux = add_parts(dot_nt(parts, pick))
    low = lax.broadcasted_iota(jnp.int32, (64, LANES), 1) < 64
    right_ref[80:144, :] = jnp.where(low, flux[0:64], flux[64:128])


def gll_weight(i):
    return (0.1, 49.0 / 90.0, 32.0 / 45.0, 49.0 / 90.0, 0.1)[i]


def lane_weight(places):
    chunk = lax.broadcasted_iota(jnp.int32, (8, LANES), 1) >> 3
    weight = jnp.zeros((8, LANES), F32)
    for row in places:
        for i, place in enumerate(row):
            weight = jnp.where(chunk == place, gll_weight(i), weight)
    return weight


def scaled(ref, weight):
    for j in range(5):
        for k in range(5):
            r = (j * 5 + k) * 8
            ref[r : r + 8, :] = ref[r : r + 8, :] * (weight * (gll_weight(j) * gll_weight(k)))


def place_flux(ref, tile_of, moves, layers=range(NGLL)):
    lane = lax.broadcasted_iota(jnp.int32, (32, LANES), 1)
    for ez in range(EZ):
        total = jnp.zeros((32, LANES), F32)
        for i in layers:
            tile, start = tile_of(i, ez)
            for source, target, width in moves(i):
                shift = (target - source - start) % LANES
                moved = pltpu.roll(tile, shift, 1) if shift else tile
                total = jnp.where((lane >= target) & (lane < target + width), moved, total)
        ref[pl.ds(ez, 25, stride=8), :] = total[0:25]


def derive(e):
    d = DERIV
    s0, s1 = e[0] + e[4], e[1] + e[3]
    d0, d1 = e[0] - e[4], e[1] - e[3]
    out = [None] * 5
    for i in (0, 1):
        even = float((d[i, 0] - d[i, 4]) / 2) * d0 + float((d[i, 1] - d[i, 3]) / 2) * d1
        odd = float((d[i, 0] + d[i, 4]) / 2) * s0 + float((d[i, 1] + d[i, 3]) / 2) * s1 + float(d[i, 2]) * e[2]
        out[i] = odd + even
        out[4 - i] = even - odd
    out[2] = float(d[2, 0]) * d0 + float(d[2, 1]) * d1
    return out


def derive_back(t):
    d = DERIV
    s0, s1 = t[0] + t[4], t[1] + t[3]
    d0, d1 = t[0] - t[4], t[1] - t[3]
    out = [None] * 5
    for i in (0, 1):
        even = float((d[0, i] - d[4, i]) / 2) * d0 + float((d[1, i] - d[3, i]) / 2) * d1
        odd = float((d[0, i] + d[4, i]) / 2) * s0 + float((d[1, i] + d[3, i]) / 2) * s1 + float(d[2, i]) * t[2]
        out[i] = odd + even
        out[4 - i] = even - odd
    out[2] = float(d[0, 2]) * d0 + float(d[1, 2]) * d1
    return out


def shifted(tiles, distance, lane):
    skip, part = divmod(distance, LANES)
    if part == 0:
        moved = tiles
        pick = None
    else:
        moved = [pltpu.roll(t, LANES - part, 1) for t in tiles]
        pick = lane < LANES - part
    n = len(tiles)
    out = []
    for i in range(n):
        a = moved[(i + skip) % n]
        b = moved[(i + skip + 1) % n]
        out.append(a if pick is None else jnp.where(pick, a, b))
    return out


def plane_of(ref, start, row):
    r0, off = divmod(start, LANES)
    lane9 = lax.broadcasted_iota(jnp.int32, (9, LANES), 1)
    flat = ref[row + r0 : row + r0 + 9, :]
    if off:
        flat = jnp.where(
            lane9 < LANES - off,
            pltpu.roll(flat, LANES - off, 1),
            pltpu.roll(ref[row + r0 + 1 : row + r0 + 10, :], LANES - off, 1),
        )
    return flat


def store_plane(ref, row, flat):
    ref[pl.ds(row, 9, stride=16), :] = flat


def make_windows(plane_ref, base, pitch, win_ref, row):
    lane = lax.broadcasted_iota(jnp.int32, (8, LANES), 1)
    tiles = [plane_ref[base + t * pitch : base + t * pitch + 8, :] for t in range(9)]
    for ey in range(EY):
        near = [tiles[ey], tiles[ey + 1], tiles[min(ey + 2, 8)]]
        if ey:
            near = [pltpu.roll(t, LANES - 4 * ey, 1) for t in near]
            keep = lane < LANES - 4 * ey
            near = [jnp.where(keep, near[0], near[1]), jnp.where(keep, near[1], near[2])]
        for w in range(2):
            win_ref[w, pl.ds(row + ey, 8, stride=8), :] = near[w]


def along_x(win_ref, base, row, combine):
    for w in range(2):
        values = combine([win_ref[w, base + 8 * c : base + 8 * c + 8, :] for c in row])
        for i, v in enumerate(values):
            yield w, i, v


def turned(win_ref, base, elem_ref, column):
    elem_ref[column, 0:LANES, :] = win_ref[0, base : base + LANES, :].T
    elem_ref[column, LANES:168, :] = win_ref[1, base : base + LANES, :].T[0:40, :]


def part(ref, column, j, k):
    return ref[column, pl.ds(j * PZ + k, 8, stride=4), :]


def flux_part(ref, j, k):
    r = (j * 5 + k) * 8
    return ref[r : r + 8, :]


def folded(term, line_ref, win_ref, base):
    row = lax.broadcasted_iota(jnp.int32, (8, LANES), 0)
    line_ref[160:256, :] = jnp.zeros((96, LANES), F32)
    for j in range(5):
        for k in range(1, 4):
            line_ref[pl.ds(j * PZ + k, 8, stride=4), :] = term[j][k]
        last = term[j][4]
        line_ref[pl.ds(j * PZ, 8, stride=4), :] = term[j][0] + jnp.where(row == 0, 0.0, pltpu.roll(last, 1, 0))
        line_ref[j * PZ + 32 : j * PZ + 33, :] = last[7:8, :]
    for w in range(2):
        win_ref[w, base : base + LANES, :] = line_ref[w * LANES : (w + 1) * LANES, :].T


def force_terms(elem_ref, value, slope, flux_ref, line_ref, win_ref, row):
    term = [[None] * 5 for _ in range(5)]
    for k in range(5):
        grads = derive([part(elem_ref, value, j, k) for j in range(5)])
        for j, v in enumerate(derive_back([g * flux_part(flux_ref, j, k) for j, g in enumerate(grads)])):
            term[j][k] = v
    for j in range(5):
        grads = derive([part(elem_ref, value, j, k) for k in range(5)])
        for k, v in enumerate(derive_back([g * flux_part(flux_ref, j, k) for k, g in enumerate(grads)])):
            term[j][k] = term[j][k] + v
    folded(term, line_ref, win_ref, row)
    term = [[part(elem_ref, slope, j, k) * flux_part(flux_ref, j, k) for k in range(5)] for j in range(5)]
    folded(term, line_ref, win_ref, row + LANES)


def cross_smoothed(tiles, cross_ref):
    lane = lax.broadcasted_iota(jnp.int32, tiles[0].shape, 1)
    for base, step in ((0, 1), (9, PZ)):
        total = None
        for tap in range(9):
            moved = shifted(tiles, step * (tap - 4), lane) if tap != 4 else tiles
            terms = [v * cross_ref[base + tap : base + tap + 1, t * LANES : (t + 1) * LANES] for t, v in enumerate(moved)]
            total = terms if total is None else [a + b for a, b in zip(total, terms)]
        tiles = total
    return tiles


def own_kernel(turn, cut_ref, count_ref, own_ref, code_ref, parts_ref, cross_ref, *refs):
    refs = refs[-OWN_OUTS - OWN_SCRATCH :]
    mine = (cut_ref[0] == 0) if turn == 0 else (cut_ref[0] != 0)

    @pl.when(mine)
    def _():
        own_layers(count_ref, own_ref, code_ref, parts_ref, cross_ref, *refs)


def own_layers(
    count_ref, own_ref, code_ref, parts_ref, cross_ref,
    elem_ref, flux_ref, near_flux_ref, near_win_ref, near_slope_ref, near_kern_ref, kern_ref,
    plane_ref, win_ref, line_ref, near_elem_ref, moved_ref,
):
    plane_ref[...] = jnp.zeros(plane_ref.shape, F32)
    for f in range(2):
        base = 24 * 9 * f
        for x in range(PXU):
            flat = plane_of(own_ref, PYZ * x, ROWS * f)
            rows = [OWN_AT[x // 4][x % 4]] if x < 12 else [16 + NEAR_AT[1][x - 12]]
            if x % 4 == 0:
                rows.append(OWN_AT[x // 4 - 1][4] if x else 16 + NEAR_AT[0][4])
            for r in rows:
                plane_ref[pl.ds(base + r, 9, stride=24), :] = flat
        for h in range(2):
            make_windows(plane_ref, base + 8 * h, 24, win_ref, 128 * f + 64 * h)
        make_windows(plane_ref, base + 16, 24, near_win_ref, 64 * f)
        win_ref[:, 256 + 128 * f : 384 + 128 * f, :] = jnp.zeros((2, LANES, LANES), F32)
        for row in OWN_AT:
            for w, i, v in along_x(win_ref, 128 * f, row, derive):
                r = 256 + 128 * f + 8 * row[i]
                win_ref[w, r : r + 8, :] = v
    for column in range(4):
        turned(win_ref, 128 * column, elem_ref, column)
    turned(near_win_ref, 0, near_elem_ref, 0)
    near_slope_ref[...] = jnp.zeros(near_slope_ref.shape, F32)
    for f in range(2):
        for w in range(2):
            value = [near_win_ref[w, 64 * f + 8 * c : 64 * f + 8 * c + 8, :] for c in (0, 4, 5, 6, 7)]
            near_slope_ref[w, 64 * f : 64 * f + 8, :] = float(DERIV[4, 4]) * value[0]
            for i, v in enumerate(derive(value[1:] + [jnp.zeros((8, LANES), F32)])[:4]):
                r = 64 * f + 8 * NEAR_AT[1][i]
                near_slope_ref[w, r : r + 8, :] = v

    element = lax.broadcasted_iota(jnp.int32, (256, 256), 0)
    slot = lax.broadcasted_iota(jnp.int32, (1, 256), 1)
    code = jnp.where(slot < count_ref[0:1, 0:1], code_ref[0:1, :], -1)
    pick = jnp.where(code == element, 1.0, 0.0).astype(BF16)
    moved_ref[0:128, :] = add_parts(dot_nt(parts_ref[...], pick))
    moved_ref[128:136, :] = jnp.zeros((8, 256), F32)

    def tile_of(i, ez):
        t = ez // 4
        return moved_ref[25 * i : 25 * i + 32, t * LANES : (t + 1) * LANES], 32 * (ez % 4)

    place_flux(flux_ref, tile_of, lambda i: [(0, 24 * i, 24)])
    place_flux(near_flux_ref, tile_of, lambda i: [(24, 8 * NEAR_AT[1][i], 8)])
    scaled(flux_ref, lane_weight(OWN_AT))
    scaled(near_flux_ref, lane_weight(NEAR_AT))

    kern = [[None] * 5 for _ in range(5)]
    near = [[None] * 5 for _ in range(5)]
    for k in range(5):
        fwd, adj, both = [derive([part(ref, c, j, k) for j in range(5)]) for ref, c in ((elem_ref, 0), (elem_ref, 1), (near_elem_ref, 0))]
        for j in range(5):
            kern[j][k] = fwd[j] * adj[j] + part(elem_ref, 2, j, k) * part(elem_ref, 3, j, k)
            near[j][k] = both[j] * pltpu.roll(both[j], 64, 1)
    for j in range(5):
        fwd, adj, both = [derive([part(ref, c, j, k) for k in range(5)]) for ref, c in ((elem_ref, 0), (elem_ref, 1), (near_elem_ref, 0))]
        for k in range(5):
            kern[j][k] = -(kern[j][k] + fwd[k] * adj[k]) * flux_part(flux_ref, j, k)
            r = (j * 5 + k) * 8
            near_kern_ref[r : r + 8, :] = near[j][k] + both[k] * pltpu.roll(both[k], 64, 1)
    folded(kern, line_ref, win_ref, 0)
    low, high = [gathered(win_ref, 0, h) for h in range(2)]
    row = lax.broadcasted_iota(jnp.int32, (8, LANES), 0)
    tiles = []
    for t in range(9):
        first = low[t] + jnp.where((row == 1) | (row == 2), pltpu.roll(high[t], 5, 0), 0.0)
        second = jnp.where(row < 4, high[t], jnp.where(row == 4, pltpu.roll(high[t], 6, 0), 0.0))
        tiles.append(jnp.concatenate([first, second], axis=0))
    for t, tile in enumerate(cross_smoothed(tiles, cross_ref)):
        kern_ref[:, t * LANES : (t + 1) * LANES] = tile


def message_flux(prev_ref, count_ref, spread_ref):
    upper = pltpu.roll(prev_ref[80:144, :], 64, 1)
    live = upper[61:62, :] < count_ref[0:1, 0:1].astype(F32)
    spread_ref[0:64, :] = jnp.where(live, prev_ref[80:144, :], 0.0)
    spread_ref[64:128, :] = jnp.where(live, upper, 0.0)
    spread_ref[128:136, :] = jnp.zeros((8, LANES), F32)
    return lambda i, ez: (spread_ref[25 * i : 25 * i + 32, :], 8 * ez)


def near_kernel(
    prev_ref, next_ref, count_ref, flux_in_ref, slope_ref, near_kern_ref, cross_ref,
    kern_ref,
    plane_ref, new_ref, win_ref, elem_ref, flux_ref, line_ref, spread_ref,
):
    plane_ref[...] = jnp.zeros(plane_ref.shape, F32)
    for f in range(2):
        share = None
        for l in range(4):
            term = float(DERIV[4, l]) * plane_of(prev_ref, 12 + PYZ * l, 40 * f)
            share = term if share is None else share + term
        plane_ref[pl.ds(f, 9, stride=8), :] = share
        plane_ref[pl.ds(2 + f, 9, stride=8), :] = plane_of(next_ref, 0, 16 * f)
    make_windows(plane_ref, 0, 8, new_ref, 0)
    win_ref[...] = slope_ref[...]
    for f in range(2):
        for w in range(2):
            r = 64 * f
            win_ref[w, r : r + 8, :] = win_ref[w, r : r + 8, :] + new_ref[w, 8 * f : 8 * f + 8, :]
            for i in range(4):
                r = 64 * f + 8 * NEAR_AT[1][i]
                new = float(DERIV[i, 4]) * new_ref[w, 16 + 8 * f : 24 + 8 * f, :]
                win_ref[w, r : r + 8, :] = win_ref[w, r : r + 8, :] + new
    turned(win_ref, 0, elem_ref, 0)
    place_flux(flux_ref, message_flux(prev_ref, count_ref, spread_ref), lambda i: [(0, 8 * NEAR_AT[0][i], 8)], (4,))
    scaled(flux_ref, lane_weight([NEAR_AT[0]]))
    kern = [[None] * 5 for _ in range(5)]
    for j in range(5):
        for k in range(5):
            slope = part(elem_ref, 0, j, k)
            total = flux_part(near_kern_ref, j, k) + slope * pltpu.roll(slope, 64, 1)
            kern[j][k] = -total * (flux_part(flux_ref, j, k) + flux_part(flux_in_ref, j, k))
    folded(kern, line_ref, win_ref, 0)
    row = lax.broadcasted_iota(jnp.int32, (8, LANES), 0)
    tiles = [jnp.where((row == 0) | (row >= 4), v, 0.0) for v in gathered(win_ref, 0, 0)]
    for t, tile in enumerate(cross_smoothed(tiles, cross_ref)):
        kern_ref[:, t * LANES : (t + 1) * LANES] = tile


def gathered(win_ref, base, h):
    lane = lax.broadcasted_iota(jnp.int32, (8, LANES), 1)
    tiles = [None] * 9
    for ey in range(EY):
        rows = pl.ds(base + h * 64 + ey, 8, stride=8)
        a, b = win_ref[0, rows, :], win_ref[1, rows, :]
        if ey:
            a, b = pltpu.roll(a, 4 * ey, 1), pltpu.roll(b, 4 * ey, 1)
            keep = lane >= 4 * ey
            a, b = jnp.where(keep, a, 0.0), jnp.where(keep, b, a)
        tiles[ey] = a if ey == 0 else tiles[ey] + a
        tiles[ey + 1] = b
    return tiles


def summed_along_x(win_ref, places, out_ref, row):
    for line in places:
        for w, i, v in along_x(win_ref, LANES, line, derive_back):
            r = 8 * line[i]
            out_ref[w, row + r : row + r + 8, :] = win_ref[w, r : r + 8, :] + v


def to_planes(win_ref, base, plane_ref):
    for h in range(2):
        for t, tile in enumerate(gathered(win_ref, base, h)):
            plane_ref[t * 16 + 8 * h : t * 16 + 8 * h + 8, :] = tile


def add_plane(line_ref, f, x, flat):
    lane9 = lax.broadcasted_iota(jnp.int32, (9, LANES), 1)
    r0, off = divmod(PYZ * x, LANES)
    if off:
        flat = pltpu.roll(flat, off, 1)
        spill = jnp.where(lane9 < off, flat, 0.0)
        flat = jnp.where(lane9 < off, 0.0, flat)
    line_ref[f, r0 : r0 + 9, :] = line_ref[f, r0 : r0 + 9, :] + flat
    if off:
        line_ref[f, r0 + 1 : r0 + 10, :] = line_ref[f, r0 + 1 : r0 + 10, :] + spill


def force_kernel(elem_ref, flux_ref, out_ref, win_ref, line_ref, force_ref, plane_ref):
    out_ref[...] = jnp.zeros(out_ref.shape, F32)
    for f in range(2):
        force_terms(elem_ref, f, 2 + f, flux_ref, line_ref, win_ref, 0)
        summed_along_x(win_ref, OWN_AT, force_ref, 0)
        to_planes(force_ref, 0, plane_ref)
        for x in range(13):
            i, m = x % 4, x // 4
            rows = [OWN_AT[m][i]] if m < 3 else []
            if i == 0 and m > 0:
                rows.append(OWN_AT[m - 1][4])
            flat = [plane_ref[pl.ds(r, 9, stride=16), :] for r in rows]
            add_plane(out_ref, f, x, sum(flat[1:], flat[0]))


def step_kernel(
    force_ref, near_half_ref, near_flux_ref, prev_ref, next_ref, count_ref, fwd_hbm, fwd_speed_hbm, adj_hbm, adj_speed_hbm, mass_hbm, after_ref,
    fwd_out_ref, fwd_speed_out_ref, adj_out_ref, adj_speed_out_ref,
    fwd_ref, fwd_speed_ref, adj_ref, adj_speed_ref, mass_ref, plane_ref, line_ref,
    flux_ref, win_ref, elem_ref, fold_ref, near_ref, near_win_ref, near_plane_ref, spread_ref, sem,
):
    copies = fetch(
        sem,
        (fwd_hbm, fwd_ref),
        (fwd_speed_hbm, fwd_speed_ref),
        (adj_hbm, adj_ref),
        (adj_speed_hbm, adj_speed_ref),
        (mass_hbm, mass_ref),
    )
    line_ref[...] = force_ref[...]
    near_plane_ref[...] = jnp.zeros(near_plane_ref.shape, F32)
    for f in range(2):
        for i in range(5):
            flat = plane_of(prev_ref, 12 + PYZ * i, 40 * f) if i < 4 else plane_of(next_ref, 0, 16 * f)
            near_plane_ref[pl.ds(72 * f + i, 9, stride=8), :] = flat
        near_win_ref[:, 128 * f : 128 * f + 64, :] = near_half_ref[:, 64 * f : 64 * f + 64, :]
        make_windows(near_plane_ref, 72 * f, 8, near_win_ref, 128 * f + 64)
    place_flux(flux_ref, message_flux(prev_ref, count_ref, spread_ref), lambda i: [(0, 8 * NEAR_AT[0][i], 8)])
    scaled(flux_ref, lane_weight([NEAR_AT[0]]))
    flux_ref[...] = flux_ref[...] + near_flux_ref[...]
    for f in range(2):
        win_ref[...] = jnp.zeros(win_ref.shape, F32)
        for row in NEAR_AT:
            for w, i, v in along_x(near_win_ref, LANES * f, row, derive):
                win_ref[w, 8 * row[i] : 8 * row[i] + 8, :] = v
        turned(near_win_ref, LANES * f, elem_ref, 0)
        turned(win_ref, 0, elem_ref, 1)
        force_terms(elem_ref, 0, 1, flux_ref, fold_ref, win_ref, 0)
        summed_along_x(win_ref, NEAR_AT, near_ref, 0)
        to_planes(near_ref, 0, plane_ref)
        for x, r in [(0, NEAR_AT[0][4])] + [(12 + i, NEAR_AT[1][i]) for i in range(4)]:
            add_plane(line_ref, f, x, plane_ref[pl.ds(r, 9, stride=16), :])

    def step(lo, hi, force):
        shape = (hi - lo) // force[0].shape[1], force[0].shape[1]
        take = lambda ref: ref[0:1, lo:hi].reshape(shape)
        scale = TIME_STEP * mass_ref[lo:hi].reshape(shape)
        speed = take(fwd_speed_ref) + scale * force[0]
        fwd_speed_out_ref[0:1, lo:hi] = speed.reshape(1, hi - lo)
        fwd_out_ref[0:1, lo:hi] = (take(fwd_ref) - TIME_STEP * speed).reshape(1, hi - lo)
        speed = take(adj_speed_ref) - scale * force[1]
        adj_speed_out_ref[0:1, lo:hi] = speed.reshape(1, hi - lo)
        adj_out_ref[0:1, lo:hi] = (take(adj_ref) + TIME_STEP * speed).reshape(1, hi - lo)

    for c in copies:
        c.wait()
    for r in range(0, 136, 8):
        step(r * LANES, (r + 8) * LANES, [line_ref[f, r : r + 8, :] for f in range(2)])
    step(NPTS - 16, NPTS, [line_ref[f, 136:137, 0:16] for f in range(2)])


def band_kernel(cut_ref, own_ref, first_ref, second_ref, band_ref, out_ref):
    flat = jnp.concatenate([own_ref[...], first_ref[...], second_ref[...]], axis=0)
    k1 = flat.astype(BF16)
    rest = flat - k1.astype(F32)
    k2 = rest.astype(BF16)
    k3 = (rest - k2.astype(F32)).astype(BF16)
    stacked = jnp.concatenate([k1, k2, k3, k1, k2, k1], axis=0)
    band = band_ref[cut_ref[0] & 1]
    out_ref[...] = jnp.dot(band, stacked, preferred_element_type=F32)[:, :PYZ]


def on_device(
    forward_displacement,
    forward_velocity,
    adjoint_displacement,
    adjoint_velocity,
    inverse_mass,
    shear_modulus,
    connectivity,
    face_points,
    element_count,
):
    events = lax.axis_size("event")
    cuts = lax.axis_size("cuts")
    cut = lax.axis_index("cuts").astype(jnp.int32).reshape(1)
    pairs_first = [(i, (i - 1 if i % 2 == 0 else i + 1) % cuts) for i in range(cuts)]
    pairs_second = [(i, (i + 1 if i % 2 == 0 else i - 1) % cuts) for i in range(cuts)]

    vmem = pl.BlockSpec(memory_space=pltpu.VMEM)
    smem = pl.BlockSpec(memory_space=pltpu.SMEM)
    anywhere = pl.BlockSpec(memory_space=pl.ANY)

    def held(block):
        return pltpu.with_memory_space_constraint(block, pltpu.VMEM)

    def in_hbm(block):
        return pltpu.with_memory_space_constraint(block, pltpu.HBM)

    def cost(flops, moved=1000000):
        return pl.CostEstimate(flops=flops, bytes_accessed=moved, transcendentals=0)

    dma = pltpu.SemaphoreType.DMA
    point_row = pltpu.VMEM((1, NPTS), F32)
    flux_block = pltpu.VMEM((200, LANES), F32)
    kern_block = pltpu.VMEM((16, 9 * LANES), F32)
    line_block = pltpu.VMEM((256, LANES), F32)

    def elements(n):
        return pltpu.VMEM((n, 168, LANES), F32)

    def windows(n):
        return pltpu.VMEM((2, n * LANES, LANES), F32)

    fields = (in_hbm(forward_displacement), in_hbm(adjoint_displacement))
    cross = held(jnp.asarray(cross_table()))
    right, left, own, code, parts = pl.pallas_call(
        pack_kernel,
        out_shape=[
            pltpu.VMEM((144, LANES), F32),
            pltpu.VMEM((32, LANES), F32),
            pltpu.VMEM((2 * ROWS, LANES), F32),
            pltpu.VMEM((8, 256), jnp.int32),
            pltpu.VMEM((384, 256), BF16),
        ],
        in_specs=[anywhere] * 4,
        scratch_shapes=[
            pltpu.VMEM((8, 256), jnp.int32),
            pltpu.VMEM((125, 256), F32),
            point_row,
            point_row,
            pltpu.VMEM((128, 256), F32),
            dma((4,)),
        ],
        cost_estimate=cost(100000000),
        name="pack",
    )(in_hbm(connectivity), in_hbm(shear_modulus), *fields)
    to_next = [(i, (i + 1) % cuts) for i in range(cuts)]
    prev = lax.ppermute(right, "cuts", to_next)
    count, left = lax.optimization_barrier((element_count, left))
    count = jnp.broadcast_to(count.reshape(1, 1), (8, LANES))
    prev_count = lax.ppermute(count, "cuts", to_next)
    count, left = lax.optimization_barrier((count, left))

    own_blocks = [elements(4), flux_block, flux_block, windows(1), windows(1), flux_block, kern_block]

    def own_part(turn, before, waits=()):
        given = (cut, held(count), held(own), held(code), held(parts), cross)
        return pl.pallas_call(
            functools.partial(own_kernel, turn),
            out_shape=own_blocks,
            in_specs=[smem] + [vmem] * (5 + len(before)) + [anywhere] * len(waits),
            scratch_shapes=[
                pltpu.VMEM((2 * 9 * 24, LANES), F32),
                windows(4),
                line_block,
                elements(1),
                pltpu.VMEM((136, 256), F32),
            ],
            input_output_aliases={len(given) + n: n for n in range(len(before))},
            cost_estimate=cost(300000000),
            name="own_layers",
        )(*given, *[held(block) for block in before], *[held(block) for block in waits])

    left, *blocks = lax.optimization_barrier((left, *own_part(0, [])))
    after = lax.ppermute(left, "cuts", [((i + 1) % cuts, i) for i in range(cuts)])
    elem, flux, near_flux, near_win, near_slope, near_kern, kern = own_part(1, blocks, [prev])
    near = pl.pallas_call(
        near_kernel,
        out_shape=pltpu.VMEM((8, 9 * LANES), F32),
        in_specs=[vmem] * 7,
        scratch_shapes=[
            pltpu.VMEM((72, LANES), F32),
            pltpu.VMEM((2, 64, LANES), F32),
            windows(1),
            elements(1),
            flux_block,
            line_block,
            pltpu.VMEM((136, LANES), F32),
        ],
        cost_estimate=cost(200000000, 40000000),
        name="near_layers",
    )(held(prev), held(after), held(prev_count), held(near_flux), held(near_slope), held(near_kern), cross)

    force = pl.pallas_call(
        force_kernel,
        out_shape=pltpu.VMEM((2, ROWS, LANES), F32),
        in_specs=[vmem] * 2,
        scratch_shapes=[windows(2), line_block, windows(1), pltpu.VMEM((144, LANES), F32)],
        cost_estimate=cost(200000000, 40000000),
        name="forces",
    )(held(elem), held(flux))

    def joined(rows, near):
        low = (lax.broadcasted_iota(jnp.int32, (8, 1), 0) < 4).astype(F32)
        return rows + jnp.concatenate([near * low, near * (1.0 - low)], axis=0)

    if events == 2:
        swap = [(0, 1), (1, 0)]
        both = kern + lax.ppermute(kern, "event", swap)
        other = lax.ppermute(near, "event", swap)
        other, both, force = lax.optimization_barrier((other, both, force))
        kern = joined(both, near + other)
    else:
        kern = lax.psum(joined(kern, near), "event")
    kern_first = lax.ppermute(kern, "cuts", pairs_first)
    kern_second = lax.ppermute(kern, "cuts", pairs_second)

    points = jax.ShapeDtypeStruct((1, NPTS), F32)
    outs = pl.pallas_call(
        step_kernel,
        out_shape=[points] * 4,
        in_specs=[vmem] * 6 + [anywhere] * 5 + [vmem],
        scratch_shapes=[point_row] * 4
        + [pltpu.VMEM((NPTS,), F32), pltpu.VMEM((144, LANES), F32), pltpu.VMEM((2, ROWS, LANES), F32)]
        + [flux_block, windows(2), elements(2), line_block, windows(1), windows(2)]
        + [pltpu.VMEM((2 * 72, LANES), F32), pltpu.VMEM((136, LANES), F32), dma((5,))],
        cost_estimate=cost(200000000),
        name="step",
    )(
        held(force),
        held(near_win),
        held(near_flux),
        held(prev),
        held(after),
        held(prev_count),
        fields[0],
        in_hbm(forward_velocity),
        fields[1],
        in_hbm(adjoint_velocity),
        in_hbm(inverse_mass),
        held(kern),
    )
    shear_kernel = pl.pallas_call(
        band_kernel,
        out_shape=jax.ShapeDtypeStruct((PXU, PYZ), F32),
        in_specs=[smem] + [vmem] * 4,
        cost_estimate=cost(20000000),
        name="band",
    )(cut, held(kern), held(kern_first), held(kern_second), held(jnp.asarray(band_table())))
    return (*outs, shear_kernel)


def solution(mesh):
    in_specs = (
        P("event", "cuts"),
        P("event", "cuts"),
        P("event", "cuts"),
        P("event", "cuts"),
        P("cuts"),
        P(None, "cuts"),
        P(None, "cuts"),
        P("cuts", None),
        P("cuts"),
    )
    out_specs = (
        P("event", "cuts"),
        P("event", "cuts"),
        P("event", "cuts"),
        P("event", "cuts"),
        P("cuts", None),
    )
    return jax.shard_map(on_device, mesh=mesh, in_specs=in_specs, out_specs=out_specs, check_vma=False)
```

```python
import functools

import numpy as np
import jax
import jax.numpy as jnp
import ml_dtypes
from jax import lax
from jax.experimental import pallas as pl
from jax.experimental.pallas import tpu as pltpu
from jax.sharding import PartitionSpec as P

NGLL = 5
EX, EY, EZ = 4, 8, 8
PXU = 16
PY = 33
PZ = 33
PYZ = 1089
NPTS = 17424
LANES = 128
ROWS = 144
TIME_STEP = 0.02
OWN_OUTS, OWN_SCRATCH = 7, 5
F32 = jnp.float32
BF16 = jnp.bfloat16


def gll():
    nodes = np.array([-1.0, -np.sqrt(3.0 / 7.0), 0.0, np.sqrt(3.0 / 7.0), 1.0])
    bary = np.array([1.0 / np.prod([nodes[r] - nodes[c] for c in range(5) if c != r]) for r in range(5)])
    d = np.zeros((5, 5))
    for r in range(5):
        for c in range(5):
            if c != r:
                d[r, c] = bary[c] / bary[r] / (nodes[r] - nodes[c])
        d[r, r] = -np.sum(d[r])
    return d


DERIV = gll()


def split_np(x):
    x = np.asarray(x, np.float32)
    parts = []
    for _ in range(3):
        p = x.astype(ml_dtypes.bfloat16)
        parts.append(p)
        x = x - p.astype(np.float32)
    return parts


ROW_PLANE = np.array([4 * (r % 3) + r // 3 for r in range(12)] + [12, 13, 14, 15])
OWN_AT = [[3 * i + m for i in range(5)] for m in range(3)]
NEAR_AT = [[8, 9, 10, 11, 0], [4, 5, 6, 7, 12]]


def band_table():
    offsets = np.arange(-PXU, PXU + 1)
    w = lambda d: np.exp(-d * d / (2.0 * (PXU / 4.0) ** 2))
    total = w(offsets.astype(np.float64)).sum()
    out = []
    for first in (-PXU, PXU):
        source = np.concatenate([ROW_PLANE, ROW_PLANE + first, ROW_PLANE - first])
        spread = np.arange(PXU)[:, None] - source[None, :]
        band = w(spread.astype(np.float64)) * (np.abs(spread) <= PXU) / total
        b1, b2, b3 = split_np(band)
        out.append(np.concatenate([b1, b1, b1, b2, b2, b3], axis=1))
    return np.stack(out)


def cross_table():
    off = np.arange(-4, 5)
    k = np.exp(-off * off / (2.0 * 1.5 * 1.5))
    point = np.arange(33)
    inside = ((point[None, :] + off[:, None]) >= 0) & ((point[None, :] + off[:, None]) < 33)
    taps = k[:, None] * inside
    taps = taps / taps.sum(axis=0, keepdims=True)
    out = np.zeros((24, 1152), np.float32)
    out[0:9, :PYZ] = np.tile(taps, (1, PY))
    out[9:18, :PYZ] = np.repeat(taps, PZ, axis=1)
    return out


def split3(x):
    hi = x.astype(BF16)
    rest = x - hi.astype(F32)
    mid = rest.astype(BF16)
    low = (rest - mid.astype(F32)).astype(BF16)
    return hi, mid, low


def dot_nt(a, b):
    return lax.dot_general(a, b, (((1,), (1,)), ((), ())), preferred_element_type=F32)


def fetch(sem, *pairs):
    copies = [pltpu.make_async_copy(src, dst, sem.at[n]) for n, (src, dst) in enumerate(pairs)]
    for c in copies:
        c.start()
    return copies


def add_parts(stacked):
    n = stacked.shape[0] // 3
    return stacked[0:n] + (stacked[n : 2 * n] + stacked[2 * n : 3 * n])


def pack_kernel(
    conn_hbm, shear_hbm, fwd_hbm, adj_hbm,
    small_ref, right_ref, left_ref, own_ref, code_ref, parts_ref,
    conn_ref, shear_ref, fwd_ref, adj_ref, block_ref, sem,
):
    copies = fetch(
        sem,
        (shear_hbm, shear_ref),
        (conn_hbm.at[0:8], conn_ref),
        (fwd_hbm, fwd_ref),
        (adj_hbm, adj_ref),
    )
    copies[1].wait()
    point = conn_ref[0:1, :].astype(F32)
    x = jnp.floor((point + 0.5) * (1.0 / PYZ))
    rest = point - x * PYZ
    y = jnp.floor((rest + 0.5) * (1.0 / PZ))
    z = rest - y * PZ
    code = (8.0 * z + 2.0 * x + 0.25 * y).astype(jnp.int32)
    slot = lax.broadcasted_iota(jnp.int32, (1, 256), 1)
    code_ref[...] = jnp.broadcast_to(code, (8, 256))
    lane = lax.broadcasted_iota(jnp.int32, (LANES, 256), 0)
    pick = jnp.where(code == ((lane >> 3) & 7) * 32 + 24 + (lane & 7), 1.0, 0.0).astype(BF16)
    for f, ref in enumerate((fwd_ref, adj_ref)):
        copies[2 + f].wait()
        for r in range(0, 136, 8):
            own_ref[ROWS * f + r : ROWS * f + r + 8, :] = ref[0:1, r * LANES : (r + 8) * LANES].reshape(8, LANES)
        own_ref[ROWS * f + 136 : ROWS * f + 144, :] = jnp.zeros((8, LANES), F32)
        own_ref[ROWS * f + 136 : ROWS * f + 137, 0:16] = ref[0:1, NPTS - 16 : NPTS]
        right_ref[40 * f : 40 * f + 40, :] = own_ref[ROWS * f + 102 : ROWS * f + 142, :]
        left_ref[16 * f : 16 * f + 16, :] = own_ref[ROWS * f : ROWS * f + 16, :]
        share = [float(DERIV[4, l]) * plane_of(own_ref, PYZ * (12 + l), ROWS * f) for l in range(4)]
        small_ref[16 * f : 16 * f + 9, :] = (share[0] + share[1]) + (share[2] + share[3])
        small_ref[16 * f + 9 : 16 * f + 16, :] = jnp.zeros((7, LANES), F32)
    copies[0].wait()
    block_ref[0:125, :] = shear_ref[...]
    block_ref[125:126, :] = slot.astype(F32)
    block_ref[126:128, :] = jnp.zeros((2, 256), F32)
    parts = jnp.concatenate(split3(block_ref[...]), axis=0)
    parts_ref[...] = parts
    flux = add_parts(dot_nt(parts, pick))
    low = lax.broadcasted_iota(jnp.int32, (64, LANES), 1) < 64
    right_ref[80:144, :] = jnp.where(low, flux[0:64], flux[64:128])
    small_ref[32:48, :] = jnp.where(low[0:16], flux[96:112], flux[112:128])


def gll_weight(i):
    return (0.1, 49.0 / 90.0, 32.0 / 45.0, 49.0 / 90.0, 0.1)[i]


def lane_weight(places):
    chunk = lax.broadcasted_iota(jnp.int32, (8, LANES), 1) >> 3
    weight = jnp.zeros((8, LANES), F32)
    for row in places:
        for i, place in enumerate(row):
            weight = jnp.where(chunk == place, gll_weight(i), weight)
    return weight


def scaled(ref, weight):
    for j in range(5):
        for k in range(5):
            r = (j * 5 + k) * 8
            ref[r : r + 8, :] = ref[r : r + 8, :] * (weight * (gll_weight(j) * gll_weight(k)))


def place_flux(ref, tile_of, moves, layers=range(NGLL)):
    lane = lax.broadcasted_iota(jnp.int32, (32, LANES), 1)
    for ez in range(EZ):
        total = jnp.zeros((32, LANES), F32)
        for i in layers:
            tile, start = tile_of(i, ez)
            for source, target, width in moves(i):
                shift = (target - source - start) % LANES
                moved = pltpu.roll(tile, shift, 1) if shift else tile
                total = jnp.where((lane >= target) & (lane < target + width), moved, total)
        ref[pl.ds(ez, 25, stride=8), :] = total[0:25]


def derive(e):
    d = DERIV
    s0, s1 = e[0] + e[4], e[1] + e[3]
    d0, d1 = e[0] - e[4], e[1] - e[3]
    out = [None] * 5
    for i in (0, 1):
        even = float((d[i, 0] - d[i, 4]) / 2) * d0 + float((d[i, 1] - d[i, 3]) / 2) * d1
        odd = float((d[i, 0] + d[i, 4]) / 2) * s0 + float((d[i, 1] + d[i, 3]) / 2) * s1 + float(d[i, 2]) * e[2]
        out[i] = odd + even
        out[4 - i] = even - odd
    out[2] = float(d[2, 0]) * d0 + float(d[2, 1]) * d1
    return out


def derive_back(t):
    d = DERIV
    s0, s1 = t[0] + t[4], t[1] + t[3]
    d0, d1 = t[0] - t[4], t[1] - t[3]
    out = [None] * 5
    for i in (0, 1):
        even = float((d[0, i] - d[4, i]) / 2) * d0 + float((d[1, i] - d[3, i]) / 2) * d1
        odd = float((d[0, i] + d[4, i]) / 2) * s0 + float((d[1, i] + d[3, i]) / 2) * s1 + float(d[2, i]) * t[2]
        out[i] = odd + even
        out[4 - i] = even - odd
    out[2] = float(d[0, 2]) * d0 + float(d[1, 2]) * d1
    return out


def shifted(tiles, distance, lane):
    skip, part = divmod(distance, LANES)
    if part == 0:
        moved = tiles
        pick = None
    else:
        moved = [pltpu.roll(t, LANES - part, 1) for t in tiles]
        pick = lane < LANES - part
    n = len(tiles)
    out = []
    for i in range(n):
        a = moved[(i + skip) % n]
        b = moved[(i + skip + 1) % n]
        out.append(a if pick is None else jnp.where(pick, a, b))
    return out


def plane_of(ref, start, row):
    r0, off = divmod(start, LANES)
    lane9 = lax.broadcasted_iota(jnp.int32, (9, LANES), 1)
    flat = ref[row + r0 : row + r0 + 9, :]
    if off:
        flat = jnp.where(
            lane9 < LANES - off,
            pltpu.roll(flat, LANES - off, 1),
            pltpu.roll(ref[row + r0 + 1 : row + r0 + 10, :], LANES - off, 1),
        )
    return flat


def store_plane(ref, row, flat):
    ref[pl.ds(row, 9, stride=16), :] = flat


def make_windows(plane_ref, base, pitch, win_ref, row):
    lane = lax.broadcasted_iota(jnp.int32, (8, LANES), 1)
    tiles = [plane_ref[base + t * pitch : base + t * pitch + 8, :] for t in range(9)]
    for ey in range(EY):
        near = [tiles[ey], tiles[ey + 1], tiles[min(ey + 2, 8)]]
        if ey:
            near = [pltpu.roll(t, LANES - 4 * ey, 1) for t in near]
            keep = lane < LANES - 4 * ey
            near = [jnp.where(keep, near[0], near[1]), jnp.where(keep, near[1], near[2])]
        for w in range(2):
            win_ref[w, pl.ds(row + ey, 8, stride=8), :] = near[w]


def along_x(win_ref, base, row, combine):
    for w in range(2):
        values = combine([win_ref[w, base + 8 * c : base + 8 * c + 8, :] for c in row])
        for i, v in enumerate(values):
            yield w, i, v


def turned(win_ref, base, elem_ref, column):
    elem_ref[column, 0:LANES, :] = win_ref[0, base : base + LANES, :].T
    elem_ref[column, LANES:168, :] = win_ref[1, base : base + LANES, :].T[0:40, :]


def part(ref, column, j, k):
    return ref[column, pl.ds(j * PZ + k, 8, stride=4), :]


def flux_part(ref, j, k):
    r = (j * 5 + k) * 8
    return ref[r : r + 8, :]


def folded(term, line_ref, win_ref, base):
    row = lax.broadcasted_iota(jnp.int32, (8, LANES), 0)
    line_ref[160:256, :] = jnp.zeros((96, LANES), F32)
    for j in range(5):
        for k in range(1, 4):
            line_ref[pl.ds(j * PZ + k, 8, stride=4), :] = term[j][k]
        last = term[j][4]
        line_ref[pl.ds(j * PZ, 8, stride=4), :] = term[j][0] + jnp.where(row == 0, 0.0, pltpu.roll(last, 1, 0))
        line_ref[j * PZ + 32 : j * PZ + 33, :] = last[7:8, :]
    for w in range(2):
        win_ref[w, base : base + LANES, :] = line_ref[w * LANES : (w + 1) * LANES, :].T


def force_terms(elem_ref, value, slope, flux_ref, line_ref, win_ref, row):
    term = [[None] * 5 for _ in range(5)]
    for k in range(5):
        grads = derive([part(elem_ref, value, j, k) for j in range(5)])
        for j, v in enumerate(derive_back([g * flux_part(flux_ref, j, k) for j, g in enumerate(grads)])):
            term[j][k] = v
    for j in range(5):
        grads = derive([part(elem_ref, value, j, k) for k in range(5)])
        for k, v in enumerate(derive_back([g * flux_part(flux_ref, j, k) for k, g in enumerate(grads)])):
            term[j][k] = term[j][k] + v
    folded(term, line_ref, win_ref, row)
    term = [[part(elem_ref, slope, j, k) * flux_part(flux_ref, j, k) for k in range(5)] for j in range(5)]
    folded(term, line_ref, win_ref, row + LANES)


def cross_smoothed(tiles, cross_ref):
    lane = lax.broadcasted_iota(jnp.int32, tiles[0].shape, 1)
    for base, step in ((0, 1), (9, PZ)):
        total = None
        for tap in range(9):
            moved = shifted(tiles, step * (tap - 4), lane) if tap != 4 else tiles
            terms = [v * cross_ref[base + tap : base + tap + 1, t * LANES : (t + 1) * LANES] for t, v in enumerate(moved)]
            total = terms if total is None else [a + b for a, b in zip(total, terms)]
        tiles = total
    return tiles


def own_kernel(turn, cut_ref, count_ref, own_ref, code_ref, parts_ref, cross_ref, *refs):
    outs = refs[len(refs) - OWN_SCRATCH - OWN_OUTS - turn : len(refs) - OWN_SCRATCH - turn]
    refs = outs + refs[len(refs) - OWN_SCRATCH :]
    mine = (cut_ref[0] == 0) if turn == 0 else (cut_ref[0] != 0)

    @pl.when(mine)
    def _():
        own_layers(count_ref, own_ref, code_ref, parts_ref, cross_ref, *refs)


def own_layers(
    count_ref, own_ref, code_ref, parts_ref, cross_ref,
    elem_ref, flux_ref, near_flux_ref, near_win_ref, near_slope_ref, near_kern_ref, kern_ref,
    plane_ref, win_ref, line_ref, near_elem_ref, moved_ref,
):
    plane_ref[...] = jnp.zeros(plane_ref.shape, F32)
    for f in range(2):
        base = 24 * 9 * f
        for x in range(PXU):
            flat = plane_of(own_ref, PYZ * x, ROWS * f)
            rows = [OWN_AT[x // 4][x % 4]] if x < 12 else [16 + NEAR_AT[1][x - 12]]
            if x % 4 == 0:
                rows.append(OWN_AT[x // 4 - 1][4] if x else 16 + NEAR_AT[0][4])
            for r in rows:
                plane_ref[pl.ds(base + r, 9, stride=24), :] = flat
        for h in range(2):
            make_windows(plane_ref, base + 8 * h, 24, win_ref, 128 * f + 64 * h)
        make_windows(plane_ref, base + 16, 24, near_win_ref, 64 * f)
        win_ref[:, 256 + 128 * f : 384 + 128 * f, :] = jnp.zeros((2, LANES, LANES), F32)
        for row in OWN_AT:
            for w, i, v in along_x(win_ref, 128 * f, row, derive):
                r = 256 + 128 * f + 8 * row[i]
                win_ref[w, r : r + 8, :] = v
    for column in range(4):
        turned(win_ref, 128 * column, elem_ref, column)
    turned(near_win_ref, 0, near_elem_ref, 0)
    near_slope_ref[...] = jnp.zeros(near_slope_ref.shape, F32)
    for f in range(2):
        for w in range(2):
            value = [near_win_ref[w, 64 * f + 8 * c : 64 * f + 8 * c + 8, :] for c in (0, 4, 5, 6, 7)]
            near_slope_ref[w, 64 * f : 64 * f + 8, :] = float(DERIV[4, 4]) * value[0]
            for i, v in enumerate(derive(value[1:] + [jnp.zeros((8, LANES), F32)])[:4]):
                r = 64 * f + 8 * NEAR_AT[1][i]
                near_slope_ref[w, r : r + 8, :] = v

    element = lax.broadcasted_iota(jnp.int32, (256, 256), 0)
    slot = lax.broadcasted_iota(jnp.int32, (1, 256), 1)
    live = jnp.concatenate([count_ref[0:1, :], count_ref[0:1, :]], axis=1)
    code = jnp.where(slot < live, code_ref[0:1, :], -1)
    pick = jnp.where(code == element, 1.0, 0.0).astype(BF16)
    moved_ref[0:128, :] = add_parts(dot_nt(parts_ref[...], pick))
    moved_ref[128:136, :] = jnp.zeros((8, 256), F32)

    def tile_of(i, ez):
        t = ez // 4
        return moved_ref[25 * i : 25 * i + 32, t * LANES : (t + 1) * LANES], 32 * (ez % 4)

    place_flux(flux_ref, tile_of, lambda i: [(0, 24 * i, 24)])
    place_flux(near_flux_ref, tile_of, lambda i: [(24, 8 * NEAR_AT[1][i], 8)])
    scaled(flux_ref, lane_weight(OWN_AT))
    scaled(near_flux_ref, lane_weight(NEAR_AT))

    kern = [[None] * 5 for _ in range(5)]
    near = [[None] * 5 for _ in range(5)]
    for k in range(5):
        fwd, adj, both = [derive([part(ref, c, j, k) for j in range(5)]) for ref, c in ((elem_ref, 0), (elem_ref, 1), (near_elem_ref, 0))]
        for j in range(5):
            kern[j][k] = fwd[j] * adj[j] + part(elem_ref, 2, j, k) * part(elem_ref, 3, j, k)
            near[j][k] = both[j] * pltpu.roll(both[j], 64, 1)
    for j in range(5):
        fwd, adj, both = [derive([part(ref, c, j, k) for k in range(5)]) for ref, c in ((elem_ref, 0), (elem_ref, 1), (near_elem_ref, 0))]
        for k in range(5):
            kern[j][k] = -(kern[j][k] + fwd[k] * adj[k]) * flux_part(flux_ref, j, k)
            r = (j * 5 + k) * 8
            near_kern_ref[r : r + 8, :] = near[j][k] + both[k] * pltpu.roll(both[k], 64, 1)
    folded(kern, line_ref, win_ref, 0)
    low, high = [gathered(win_ref, 0, h) for h in range(2)]
    row = lax.broadcasted_iota(jnp.int32, (8, LANES), 0)
    tiles = []
    for t in range(9):
        first = low[t] + jnp.where((row == 1) | (row == 2), pltpu.roll(high[t], 5, 0), 0.0)
        second = jnp.where(row < 4, high[t], jnp.where(row == 4, pltpu.roll(high[t], 6, 0), 0.0))
        tiles.append(jnp.concatenate([first, second], axis=0))
    for t, tile in enumerate(cross_smoothed(tiles, cross_ref)):
        kern_ref[:, t * LANES : (t + 1) * LANES] = tile


def message_flux(prev_ref, count_ref, spread_ref):
    upper = pltpu.roll(prev_ref[80:144, :], 64, 1)
    live = upper[61:62, :] < count_ref[0:1, :].astype(F32)
    spread_ref[0:64, :] = jnp.where(live, prev_ref[80:144, :], 0.0)
    spread_ref[64:128, :] = jnp.where(live, upper, 0.0)
    spread_ref[128:136, :] = jnp.zeros((8, LANES), F32)
    return lambda i, ez: (spread_ref[25 * i : 25 * i + 32, :], 8 * ez)


def near_kernel(
    small_ref, next_ref, count_ref, flux_in_ref, slope_ref, near_kern_ref, kern_in_ref, cross_ref,
    kern_ref,
    plane_ref, new_ref, win_ref, elem_ref, flux_ref, line_ref, spread_ref,
):
    plane_ref[...] = jnp.zeros(plane_ref.shape, F32)
    for f in range(2):
        share = small_ref[16 * f : 16 * f + 9, :]
        plane_ref[pl.ds(f, 9, stride=8), :] = share
        plane_ref[pl.ds(2 + f, 9, stride=8), :] = plane_of(next_ref, 0, 16 * f)
    make_windows(plane_ref, 0, 8, new_ref, 0)
    win_ref[...] = slope_ref[...]
    for f in range(2):
        for w in range(2):
            r = 64 * f
            win_ref[w, r : r + 8, :] = win_ref[w, r : r + 8, :] + new_ref[w, 8 * f : 8 * f + 8, :]
            for i in range(4):
                r = 64 * f + 8 * NEAR_AT[1][i]
                new = float(DERIV[i, 4]) * new_ref[w, 16 + 8 * f : 24 + 8 * f, :]
                win_ref[w, r : r + 8, :] = win_ref[w, r : r + 8, :] + new
    turned(win_ref, 0, elem_ref, 0)
    lower, upper = small_ref[32:48, :], pltpu.roll(small_ref[32:48, :], 64, 1)
    live = upper[13:14, :] < count_ref[0:1, 0:1].astype(F32)
    spread_ref[0:16, :] = jnp.where(live, lower, 0.0)
    spread_ref[16:32, :] = jnp.where(live, upper, 0.0)
    spread_ref[32:40, :] = jnp.zeros((8, LANES), F32)
    place_flux(flux_ref, lambda i, ez: (spread_ref[4:36, :], 8 * ez), lambda i: [(0, 8 * NEAR_AT[0][i], 8)], (4,))
    scaled(flux_ref, lane_weight([NEAR_AT[0]]))
    kern = [[None] * 5 for _ in range(5)]
    for j in range(5):
        for k in range(5):
            slope = part(elem_ref, 0, j, k)
            total = flux_part(near_kern_ref, j, k) + slope * pltpu.roll(slope, 64, 1)
            kern[j][k] = -total * (flux_part(flux_ref, j, k) + flux_part(flux_in_ref, j, k))
    folded(kern, line_ref, win_ref, 0)
    row = lax.broadcasted_iota(jnp.int32, (8, LANES), 0)
    tiles = [jnp.where((row == 0) | (row >= 4), v, 0.0) for v in gathered(win_ref, 0, 0)]
    for t, tile in enumerate(cross_smoothed(tiles, cross_ref)):
        columns = slice(t * LANES, (t + 1) * LANES)
        kern_ref[0:8, columns] = kern_in_ref[0:8, columns] + jnp.where(row == 0, tile, 0.0)
        kern_ref[8:16, columns] = kern_in_ref[8:16, columns] + jnp.where(row >= 4, tile, 0.0)


def gathered(win_ref, base, h):
    lane = lax.broadcasted_iota(jnp.int32, (8, LANES), 1)
    tiles = [None] * 9
    for ey in range(EY):
        rows = pl.ds(base + h * 64 + ey, 8, stride=8)
        a, b = win_ref[0, rows, :], win_ref[1, rows, :]
        if ey:
            a, b = pltpu.roll(a, 4 * ey, 1), pltpu.roll(b, 4 * ey, 1)
            keep = lane >= 4 * ey
            a, b = jnp.where(keep, a, 0.0), jnp.where(keep, b, a)
        tiles[ey] = a if ey == 0 else tiles[ey] + a
        tiles[ey + 1] = b
    return tiles


def summed_along_x(win_ref, places, out_ref, row):
    for line in places:
        for w, i, v in along_x(win_ref, LANES, line, derive_back):
            r = 8 * line[i]
            out_ref[w, row + r : row + r + 8, :] = win_ref[w, r : r + 8, :] + v


def to_planes(win_ref, base, plane_ref):
    for h in range(2):
        for t, tile in enumerate(gathered(win_ref, base, h)):
            plane_ref[t * 16 + 8 * h : t * 16 + 8 * h + 8, :] = tile


def add_plane(line_ref, f, x, flat):
    lane9 = lax.broadcasted_iota(jnp.int32, (9, LANES), 1)
    r0, off = divmod(PYZ * x, LANES)
    if off:
        flat = pltpu.roll(flat, off, 1)
        spill = jnp.where(lane9 < off, flat, 0.0)
        flat = jnp.where(lane9 < off, 0.0, flat)
    line_ref[f, r0 : r0 + 9, :] = line_ref[f, r0 : r0 + 9, :] + flat
    if off:
        line_ref[f, r0 + 1 : r0 + 10, :] = line_ref[f, r0 + 1 : r0 + 10, :] + spill


def force_kernel(elem_ref, flux_ref, out_ref, win_ref, fold_ref, force_ref, plane_ref):
    out_ref[...] = jnp.zeros(out_ref.shape, F32)
    for f in range(2):
        force_terms(elem_ref, f, 2 + f, flux_ref, fold_ref, win_ref, 0)
        summed_along_x(win_ref, OWN_AT, force_ref, 0)
        to_planes(force_ref, 0, plane_ref)
        for x in range(13):
            i, m = x % 4, x // 4
            rows = [OWN_AT[m][i]] if m < 3 else []
            if i == 0 and m > 0:
                rows.append(OWN_AT[m - 1][4])
            flat = [plane_ref[pl.ds(r, 9, stride=16), :] for r in rows]
            add_plane(out_ref, f, x, sum(flat[1:], flat[0]))


def near_force_kernel(
    force_ref, near_half_ref, near_flux_ref, prev_ref, next_ref, count_ref, after_ref,
    out_ref,
    win_ref, fold_ref, near_force_ref, plane_ref, flux_ref, elem_ref, near_win_ref, near_plane_ref, spread_ref,
):
    out_ref[...] = force_ref[...]
    near_plane_ref[...] = jnp.zeros(near_plane_ref.shape, F32)
    for f in range(2):
        for i in range(5):
            flat = plane_of(prev_ref, 12 + PYZ * i, 40 * f) if i < 4 else plane_of(next_ref, 0, 16 * f)
            near_plane_ref[pl.ds(72 * f + i, 9, stride=8), :] = flat
        near_win_ref[:, 128 * f : 128 * f + 64, :] = near_half_ref[:, 64 * f : 64 * f + 64, :]
        make_windows(near_plane_ref, 72 * f, 8, near_win_ref, 128 * f + 64)
    place_flux(flux_ref, message_flux(prev_ref, count_ref, spread_ref), lambda i: [(0, 8 * NEAR_AT[0][i], 8)])
    scaled(flux_ref, lane_weight([NEAR_AT[0]]))
    flux_ref[...] = flux_ref[...] + near_flux_ref[...]
    for f in range(2):
        win_ref[...] = jnp.zeros(win_ref.shape, F32)
        for row in NEAR_AT:
            for w, i, v in along_x(near_win_ref, LANES * f, row, derive):
                win_ref[w, 8 * row[i] : 8 * row[i] + 8, :] = v
        turned(near_win_ref, LANES * f, elem_ref, 0)
        turned(win_ref, 0, elem_ref, 1)
        force_terms(elem_ref, 0, 1, flux_ref, fold_ref, win_ref, 0)
        summed_along_x(win_ref, NEAR_AT, near_force_ref, 0)
        to_planes(near_force_ref, 0, plane_ref)
        for x, r in [(0, NEAR_AT[0][4])] + [(12 + i, NEAR_AT[1][i]) for i in range(4)]:
            add_plane(out_ref, f, x, plane_ref[pl.ds(r, 9, stride=16), :])


def step_kernel(
    line_ref, fwd_ref, fwd_speed_ref, adj_ref, adj_speed_ref, mass_ref,
    fwd_out_ref, fwd_speed_out_ref, adj_out_ref, adj_speed_out_ref,
):
    def step(lo, hi, force):
        shape = (hi - lo) // force[0].shape[1], force[0].shape[1]
        take = lambda ref: ref[0:1, lo:hi].reshape(shape)
        scale = TIME_STEP * mass_ref[lo:hi].reshape(shape)
        speed = take(fwd_speed_ref) + scale * force[0]
        fwd_speed_out_ref[0:1, lo:hi] = speed.reshape(1, hi - lo)
        fwd_out_ref[0:1, lo:hi] = (take(fwd_ref) - TIME_STEP * speed).reshape(1, hi - lo)
        speed = take(adj_speed_ref) - scale * force[1]
        adj_speed_out_ref[0:1, lo:hi] = speed.reshape(1, hi - lo)
        adj_out_ref[0:1, lo:hi] = (take(adj_ref) + TIME_STEP * speed).reshape(1, hi - lo)

    for r in range(0, 136, 8):
        step(r * LANES, (r + 8) * LANES, [line_ref[f, r : r + 8, :] for f in range(2)])
    step(NPTS - 16, NPTS, [line_ref[f, 136:137, 0:16] for f in range(2)])


def band_kernel(cut_ref, own_ref, first_ref, second_ref, band_ref, out_ref):
    flat = jnp.concatenate([own_ref[...], first_ref[...], second_ref[...]], axis=0)
    k1 = flat.astype(BF16)
    rest = flat - k1.astype(F32)
    k2 = rest.astype(BF16)
    k3 = (rest - k2.astype(F32)).astype(BF16)
    stacked = jnp.concatenate([k1, k2, k3, k1, k2, k1], axis=0)
    band = band_ref[cut_ref[0] & 1]
    out_ref[...] = jnp.dot(band, stacked, preferred_element_type=F32)[:, :PYZ]


def on_device(
    forward_displacement,
    forward_velocity,
    adjoint_displacement,
    adjoint_velocity,
    inverse_mass,
    shear_modulus,
    connectivity,
    face_points,
    element_count,
):
    events = lax.axis_size("event")
    cuts = lax.axis_size("cuts")
    cut = lax.axis_index("cuts").astype(jnp.int32).reshape(1)
    pairs_first = [(i, (i - 1 if i % 2 == 0 else i + 1) % cuts) for i in range(cuts)]
    pairs_second = [(i, (i + 1 if i % 2 == 0 else i - 1) % cuts) for i in range(cuts)]

    vmem = pl.BlockSpec(memory_space=pltpu.VMEM)
    smem = pl.BlockSpec(memory_space=pltpu.SMEM)
    anywhere = pl.BlockSpec(memory_space=pl.ANY)

    def held(block):
        return pltpu.with_memory_space_constraint(block, pltpu.VMEM)

    def in_hbm(block):
        return pltpu.with_memory_space_constraint(block, pltpu.HBM)

    def cost(flops):
        return pl.CostEstimate(flops=flops, bytes_accessed=1000000, transcendentals=0)

    dma = pltpu.SemaphoreType.DMA
    point_row = pltpu.VMEM((1, NPTS), F32)
    flux_block = pltpu.VMEM((200, LANES), F32)
    kern_block = pltpu.VMEM((16, 9 * LANES), F32)
    line_block = pltpu.VMEM((256, LANES), F32)

    def elements(n):
        return pltpu.VMEM((n, 168, LANES), F32)

    def windows(n):
        return pltpu.VMEM((2, n * LANES, LANES), F32)

    fields = (in_hbm(forward_displacement), in_hbm(adjoint_displacement))
    cross = held(jnp.asarray(cross_table()))
    small, right, left, own, code, parts = pl.pallas_call(
        pack_kernel,
        out_shape=[
            pltpu.VMEM((48, LANES), F32),
            pltpu.VMEM((144, LANES), F32),
            pltpu.VMEM((32, LANES), F32),
            pltpu.VMEM((2 * ROWS, LANES), F32),
            pltpu.VMEM((8, 256), jnp.int32),
            pltpu.VMEM((384, 256), BF16),
        ],
        in_specs=[anywhere] * 4,
        scratch_shapes=[
            pltpu.VMEM((8, 256), jnp.int32),
            pltpu.VMEM((125, 256), F32),
            point_row,
            point_row,
            pltpu.VMEM((128, 256), F32),
            dma((4,)),
        ],
        cost_estimate=cost(100000000),
        name="pack",
    )(in_hbm(connectivity), in_hbm(shear_modulus), *fields)
    to_next = [(i, (i + 1) % cuts) for i in range(cuts)]
    small = lax.ppermute(small, "cuts", to_next)
    count, left = lax.optimization_barrier((element_count, left))
    count = jnp.broadcast_to(count.reshape(1, 1), (8, LANES))
    prev_count = lax.ppermute(count, "cuts", to_next)
    count, left = lax.optimization_barrier((count, left))

    own_blocks = [elements(4), flux_block, flux_block, windows(1), windows(1), flux_block, kern_block]

    def own_part(turn, before, waits=()):
        given = (cut, held(count), held(own), held(code), held(parts), cross)
        return pl.pallas_call(
            functools.partial(own_kernel, turn),
            out_shape=own_blocks + [pltpu.VMEM((144, LANES), F32)] * turn,
            in_specs=[smem] + [vmem] * (5 + len(before)) + [anywhere] * len(waits),
            scratch_shapes=[
                pltpu.VMEM((2 * 9 * 24, LANES), F32),
                windows(4),
                line_block,
                elements(1),
                pltpu.VMEM((136, 256), F32),
            ],
            input_output_aliases={len(given) + n: n for n in range(len(before))},
            cost_estimate=cost(300000000),
            name="own_layers",
        )(*given, *[held(block) for block in before], *[held(block) for block in waits])

    left, *blocks = lax.optimization_barrier((left, *own_part(0, [])))
    after = lax.ppermute(left, "cuts", [((i + 1) % cuts, i) for i in range(cuts)])
    elem, flux, near_flux, near_win, near_slope, near_kern, kern, right = own_part(1, blocks + [right], [small])
    prev = lax.ppermute(right, "cuts", to_next)
    kern = pl.pallas_call(
        near_kernel,
        out_shape=kern_block,
        in_specs=[vmem] * 8,
        scratch_shapes=[
            pltpu.VMEM((72, LANES), F32),
            pltpu.VMEM((2, 64, LANES), F32),
            windows(1),
            elements(1),
            flux_block,
            line_block,
            pltpu.VMEM((136, LANES), F32),
        ],
        cost_estimate=cost(200000000),
        name="near_layers",
    )(held(small), held(after), held(prev_count), held(near_flux), held(near_slope), held(near_kern), held(kern), cross)

    force = pl.pallas_call(
        force_kernel,
        out_shape=pltpu.VMEM((2, ROWS, LANES), F32),
        in_specs=[vmem] * 2,
        scratch_shapes=[windows(2), line_block, windows(1), pltpu.VMEM((144, LANES), F32)],
        cost_estimate=cost(200000000),
        name="forces",
    )(held(elem), held(flux))

    if events == 2:
        other = lax.ppermute(kern, "event", [(0, 1), (1, 0)])
        other, force = lax.optimization_barrier((other, force))
        kern = kern + other
    elif events > 2:
        kern = lax.psum(kern, "event")
    kern_first = lax.ppermute(kern, "cuts", pairs_first)
    kern_second = lax.ppermute(kern, "cuts", pairs_second)

    force = pl.pallas_call(
        near_force_kernel,
        out_shape=pltpu.VMEM((2, ROWS, LANES), F32),
        in_specs=[vmem] * 7,
        scratch_shapes=[
            windows(2),
            line_block,
            windows(1),
            pltpu.VMEM((144, LANES), F32),
            flux_block,
            elements(2),
            windows(2),
            pltpu.VMEM((2 * 72, LANES), F32),
            pltpu.VMEM((136, LANES), F32),
        ],
        cost_estimate=cost(200000000),
        name="near_forces",
    )(held(force), held(near_win), held(near_flux), held(prev), held(after), held(prev_count), held(kern))
    points = jax.ShapeDtypeStruct((1, NPTS), F32)
    outs = pl.pallas_call(
        step_kernel,
        out_shape=[points] * 4,
        in_specs=[vmem] * 6,
        cost_estimate=cost(200000000),
        name="step",
    )(
        held(force),
        held(forward_displacement),
        held(forward_velocity),
        held(adjoint_displacement),
        held(adjoint_velocity),
        held(inverse_mass),
    )
    shear_kernel = pl.pallas_call(
        band_kernel,
        out_shape=jax.ShapeDtypeStruct((PXU, PYZ), F32),
        in_specs=[smem] + [vmem] * 4,
        cost_estimate=cost(20000000),
        name="band",
    )(cut, held(kern), held(kern_first), held(kern_second), held(jnp.asarray(band_table())))
    return (*outs, shear_kernel)


def solution(mesh):
    in_specs = (
        P("event", "cuts"),
        P("event", "cuts"),
        P("event", "cuts"),
        P("event", "cuts"),
        P("cuts"),
        P(None, "cuts"),
        P(None, "cuts"),
        P("cuts", None),
        P("cuts"),
    )
    out_specs = (
        P("event", "cuts"),
        P("event", "cuts"),
        P("event", "cuts"),
        P("event", "cuts"),
        P("cuts", None),
    )
    return jax.shard_map(on_device, mesh=mesh, in_specs=in_specs, out_specs=out_specs, check_vma=False)
```

```python
import functools

import numpy as np
import jax
import jax.numpy as jnp
import ml_dtypes
from jax import lax
from jax.experimental import pallas as pl
from jax.experimental.pallas import tpu as pltpu
from jax.sharding import PartitionSpec as P

NGLL = 5
EX, EY, EZ = 4, 8, 8
PXU = 16
PY = 33
PZ = 33
PYZ = 1089
NPTS = 17424
LANES = 128
ROWS = 144
TIME_STEP = 0.02
OWN_OUTS, OWN_SCRATCH = 8, 12
F32 = jnp.float32
BF16 = jnp.bfloat16


def gll():
    nodes = np.array([-1.0, -np.sqrt(3.0 / 7.0), 0.0, np.sqrt(3.0 / 7.0), 1.0])
    bary = np.array([1.0 / np.prod([nodes[r] - nodes[c] for c in range(5) if c != r]) for r in range(5)])
    d = np.zeros((5, 5))
    for r in range(5):
        for c in range(5):
            if c != r:
                d[r, c] = bary[c] / bary[r] / (nodes[r] - nodes[c])
        d[r, r] = -np.sum(d[r])
    return d


DERIV = gll()


def split_np(x):
    x = np.asarray(x, np.float32)
    parts = []
    for _ in range(3):
        p = x.astype(ml_dtypes.bfloat16)
        parts.append(p)
        x = x - p.astype(np.float32)
    return parts


ROW_PLANE = np.array([4 * (r % 3) + r // 3 for r in range(12)] + [12, 13, 14, 15])
OWN_AT = [[3 * i + m for i in range(5)] for m in range(3)]
NEAR_AT = [[8, 9, 10, 11, 0], [4, 5, 6, 7, 12]]


def band_table():
    offsets = np.arange(-PXU, PXU + 1)
    w = lambda d: np.exp(-d * d / (2.0 * (PXU / 4.0) ** 2))
    total = w(offsets.astype(np.float64)).sum()
    out = []
    for first in (-PXU, PXU):
        source = np.concatenate([ROW_PLANE, ROW_PLANE + first, ROW_PLANE - first])
        spread = np.arange(PXU)[:, None] - source[None, :]
        band = w(spread.astype(np.float64)) * (np.abs(spread) <= PXU) / total
        b1, b2, b3 = split_np(band)
        out.append(np.concatenate([b1, b1, b1, b2, b2, b3], axis=1))
    return np.stack(out)


def cross_table():
    off = np.arange(-4, 5)
    k = np.exp(-off * off / (2.0 * 1.5 * 1.5))
    point = np.arange(33)
    inside = ((point[None, :] + off[:, None]) >= 0) & ((point[None, :] + off[:, None]) < 33)
    taps = k[:, None] * inside
    taps = taps / taps.sum(axis=0, keepdims=True)
    out = np.zeros((24, 1152), np.float32)
    out[0:9, :PYZ] = np.tile(taps, (1, PY))
    out[9:18, :PYZ] = np.repeat(taps, PZ, axis=1)
    return out


def split3(x):
    hi = x.astype(BF16)
    rest = x - hi.astype(F32)
    mid = rest.astype(BF16)
    low = (rest - mid.astype(F32)).astype(BF16)
    return hi, mid, low


def dot_nt(a, b):
    return lax.dot_general(a, b, (((1,), (1,)), ((), ())), preferred_element_type=F32)


def fetch(sem, *pairs):
    copies = [pltpu.make_async_copy(src, dst, sem.at[n]) for n, (src, dst) in enumerate(pairs)]
    for c in copies:
        c.start()
    return copies


def add_parts(stacked):
    n = stacked.shape[0] // 3
    return stacked[0:n] + (stacked[n : 2 * n] + stacked[2 * n : 3 * n])


def slot_elements(conn_ref):
    point = conn_ref[0:1, :].astype(F32)
    x = jnp.floor((point + 0.5) * (1.0 / PYZ))
    rest = point - x * PYZ
    y = jnp.floor((rest + 0.5) * (1.0 / PZ))
    z = rest - y * PZ
    return (8.0 * z + 2.0 * x + 0.25 * y).astype(jnp.int32)


def last_layer(code):
    lane = lax.broadcasted_iota(jnp.int32, (LANES, 256), 0)
    return jnp.where(code == ((lane >> 3) & 7) * 32 + 24 + (lane & 7), 1.0, 0.0).astype(BF16)


def halves(flux):
    n = flux.shape[0] // 2
    low = lax.broadcasted_iota(jnp.int32, (n, LANES), 1) < 64
    return jnp.where(low, flux[0:n], flux[n : 2 * n])


def lay_rows(ref, target, first, last):
    for r in range(first, last, 8):
        full = min(r + 8, last, NPTS // LANES)
        if full > r:
            target[r - first : full - first, :] = ref[0:1, r * LANES : full * LANES].reshape(full - r, LANES)
        if full < min(r + 8, last):
            target[full - first : min(r + 8, last) - first, :] = jnp.zeros((min(r + 8, last) - full, LANES), F32)
            target[full - first : full - first + 1, 0 : NPTS % LANES] = ref[0:1, full * LANES : NPTS]


def pack_kernel(
    conn_hbm, shear_hbm, fwd_hbm, adj_hbm,
    small_ref, left_ref,
    conn_ref, shear_ref, fwd_ref, adj_ref, block_ref, line_ref, sem,
):
    copies = fetch(
        sem,
        (shear_hbm, shear_ref),
        (conn_hbm.at[0:8], conn_ref),
        (fwd_hbm, fwd_ref),
        (adj_hbm, adj_ref),
    )
    copies[1].wait()
    pick = last_layer(slot_elements(conn_ref))
    copies[0].wait()
    block_ref[0:29, :] = shear_ref[96:125, :]
    block_ref[29:30, :] = lax.broadcasted_iota(jnp.int32, (1, 256), 1).astype(F32)
    block_ref[30:32, :] = jnp.zeros((2, 256), F32)
    flux = add_parts(dot_nt(jnp.concatenate(split3(block_ref[...]), axis=0), pick))
    small_ref[32:48, :] = halves(flux)
    for f, ref in enumerate((fwd_ref, adj_ref)):
        copies[2 + f].wait()
        lay_rows(ref, left_ref.at[16 * f : 16 * f + 16], 0, 16)
        lay_rows(ref, line_ref, 102, 142)
        share = [float(DERIV[4, l]) * plane_of(line_ref, 12 + PYZ * l, 0) for l in range(4)]
        small_ref[16 * f : 16 * f + 9, :] = (share[0] + share[1]) + (share[2] + share[3])
        small_ref[16 * f + 9 : 16 * f + 16, :] = jnp.zeros((7, LANES), F32)


def gll_weight(i):
    return (0.1, 49.0 / 90.0, 32.0 / 45.0, 49.0 / 90.0, 0.1)[i]


def lane_weight(places):
    chunk = lax.broadcasted_iota(jnp.int32, (8, LANES), 1) >> 3
    weight = jnp.zeros((8, LANES), F32)
    for row in places:
        for i, place in enumerate(row):
            weight = jnp.where(chunk == place, gll_weight(i), weight)
    return weight


def scaled(ref, weight):
    for j in range(5):
        for k in range(5):
            r = (j * 5 + k) * 8
            ref[r : r + 8, :] = ref[r : r + 8, :] * (weight * (gll_weight(j) * gll_weight(k)))


def place_flux(ref, tile_of, moves, layers=range(NGLL)):
    lane = lax.broadcasted_iota(jnp.int32, (32, LANES), 1)
    for ez in range(EZ):
        total = jnp.zeros((32, LANES), F32)
        for i in layers:
            tile, start = tile_of(i, ez)
            for source, target, width in moves(i):
                shift = (target - source - start) % LANES
                moved = pltpu.roll(tile, shift, 1) if shift else tile
                total = jnp.where((lane >= target) & (lane < target + width), moved, total)
        ref[pl.ds(ez, 25, stride=8), :] = total[0:25]


def derive(e):
    d = DERIV
    s0, s1 = e[0] + e[4], e[1] + e[3]
    d0, d1 = e[0] - e[4], e[1] - e[3]
    out = [None] * 5
    for i in (0, 1):
        even = float((d[i, 0] - d[i, 4]) / 2) * d0 + float((d[i, 1] - d[i, 3]) / 2) * d1
        odd = float((d[i, 0] + d[i, 4]) / 2) * s0 + float((d[i, 1] + d[i, 3]) / 2) * s1 + float(d[i, 2]) * e[2]
        out[i] = odd + even
        out[4 - i] = even - odd
    out[2] = float(d[2, 0]) * d0 + float(d[2, 1]) * d1
    return out


def derive_back(t):
    d = DERIV
    s0, s1 = t[0] + t[4], t[1] + t[3]
    d0, d1 = t[0] - t[4], t[1] - t[3]
    out = [None] * 5
    for i in (0, 1):
        even = float((d[0, i] - d[4, i]) / 2) * d0 + float((d[1, i] - d[3, i]) / 2) * d1
        odd = float((d[0, i] + d[4, i]) / 2) * s0 + float((d[1, i] + d[3, i]) / 2) * s1 + float(d[2, i]) * t[2]
        out[i] = odd + even
        out[4 - i] = even - odd
    out[2] = float(d[0, 2]) * d0 + float(d[1, 2]) * d1
    return out


def shifted(tiles, distance, lane):
    skip, part = divmod(distance, LANES)
    if part == 0:
        moved = tiles
        pick = None
    else:
        moved = [pltpu.roll(t, LANES - part, 1) for t in tiles]
        pick = lane < LANES - part
    n = len(tiles)
    out = []
    for i in range(n):
        a = moved[(i + skip) % n]
        b = moved[(i + skip + 1) % n]
        out.append(a if pick is None else jnp.where(pick, a, b))
    return out


def plane_of(ref, start, row):
    r0, off = divmod(start, LANES)
    lane9 = lax.broadcasted_iota(jnp.int32, (9, LANES), 1)
    flat = ref[row + r0 : row + r0 + 9, :]
    if off:
        flat = jnp.where(
            lane9 < LANES - off,
            pltpu.roll(flat, LANES - off, 1),
            pltpu.roll(ref[row + r0 + 1 : row + r0 + 10, :], LANES - off, 1),
        )
    return flat


def store_plane(ref, row, flat):
    ref[pl.ds(row, 9, stride=16), :] = flat


def make_windows(plane_ref, base, pitch, win_ref, row):
    lane = lax.broadcasted_iota(jnp.int32, (8, LANES), 1)
    tiles = [plane_ref[base + t * pitch : base + t * pitch + 8, :] for t in range(9)]
    for ey in range(EY):
        near = [tiles[ey], tiles[ey + 1], tiles[min(ey + 2, 8)]]
        if ey:
            near = [pltpu.roll(t, LANES - 4 * ey, 1) for t in near]
            keep = lane < LANES - 4 * ey
            near = [jnp.where(keep, near[0], near[1]), jnp.where(keep, near[1], near[2])]
        for w in range(2):
            win_ref[w, pl.ds(row + ey, 8, stride=8), :] = near[w]


def along_x(win_ref, base, row, combine):
    for w in range(2):
        values = combine([win_ref[w, base + 8 * c : base + 8 * c + 8, :] for c in row])
        for i, v in enumerate(values):
            yield w, i, v


def turned(win_ref, base, elem_ref, column):
    elem_ref[column, 0:LANES, :] = win_ref[0, base : base + LANES, :].T
    elem_ref[column, LANES:168, :] = win_ref[1, base : base + LANES, :].T[0:40, :]


def part(ref, column, j, k):
    return ref[column, pl.ds(j * PZ + k, 8, stride=4), :]


def flux_part(ref, j, k):
    r = (j * 5 + k) * 8
    return ref[r : r + 8, :]


def folded(term, line_ref, win_ref, base):
    row = lax.broadcasted_iota(jnp.int32, (8, LANES), 0)
    line_ref[160:256, :] = jnp.zeros((96, LANES), F32)
    for j in range(5):
        for k in range(1, 4):
            line_ref[pl.ds(j * PZ + k, 8, stride=4), :] = term[j][k]
        last = term[j][4]
        line_ref[pl.ds(j * PZ, 8, stride=4), :] = term[j][0] + jnp.where(row == 0, 0.0, pltpu.roll(last, 1, 0))
        line_ref[j * PZ + 32 : j * PZ + 33, :] = last[7:8, :]
    for w in range(2):
        win_ref[w, base : base + LANES, :] = line_ref[w * LANES : (w + 1) * LANES, :].T


def force_terms(elem_ref, value, slope, flux_ref, line_ref, win_ref, row):
    term = [[None] * 5 for _ in range(5)]
    for k in range(5):
        grads = derive([part(elem_ref, value, j, k) for j in range(5)])
        for j, v in enumerate(derive_back([g * flux_part(flux_ref, j, k) for j, g in enumerate(grads)])):
            term[j][k] = v
    for j in range(5):
        grads = derive([part(elem_ref, value, j, k) for k in range(5)])
        for k, v in enumerate(derive_back([g * flux_part(flux_ref, j, k) for k, g in enumerate(grads)])):
            term[j][k] = term[j][k] + v
    folded(term, line_ref, win_ref, row)
    term = [[part(elem_ref, slope, j, k) * flux_part(flux_ref, j, k) for k in range(5)] for j in range(5)]
    folded(term, line_ref, win_ref, row + LANES)


def cross_smoothed(tiles, cross_ref):
    lane = lax.broadcasted_iota(jnp.int32, tiles[0].shape, 1)
    for base, step in ((0, 1), (9, PZ)):
        total = None
        for tap in range(9):
            moved = shifted(tiles, step * (tap - 4), lane) if tap != 4 else tiles
            terms = [v * cross_ref[base + tap : base + tap + 1, t * LANES : (t + 1) * LANES] for t, v in enumerate(moved)]
            total = terms if total is None else [a + b for a, b in zip(total, terms)]
        tiles = total
    return tiles


def own_kernel(turn, cut_ref, count_ref, conn_hbm, shear_hbm, fwd_hbm, adj_hbm, cross_ref, *refs):
    refs = refs[len(refs) - OWN_OUTS - OWN_SCRATCH :]
    mine = (cut_ref[0] == 0) if turn == 0 else (cut_ref[0] != 0)

    @pl.when(mine)
    def _():
        own_layers(count_ref, conn_hbm, shear_hbm, fwd_hbm, adj_hbm, cross_ref, *refs)


def own_layers(
    count_ref, conn_hbm, shear_hbm, fwd_hbm, adj_hbm, cross_ref,
    elem_ref, flux_ref, near_flux_ref, near_win_ref, near_slope_ref, near_kern_ref, kern_ref, right_ref,
    plane_ref, win_ref, line_ref, near_elem_ref, moved_ref,
    conn_ref, shear_ref, fwd_ref, adj_ref, block_ref, own_ref, sem,
):
    copies = fetch(
        sem,
        (fwd_hbm, fwd_ref),
        (adj_hbm, adj_ref),
        (conn_hbm.at[0:8], conn_ref),
        (shear_hbm, shear_ref),
    )
    for f, ref in enumerate((fwd_ref, adj_ref)):
        copies[f].wait()
        lay_rows(ref, own_ref.at[ROWS * f : ROWS * f + ROWS], 0, ROWS)
        right_ref[40 * f : 40 * f + 40, :] = own_ref[ROWS * f + 102 : ROWS * f + 142, :]
    plane_ref[...] = jnp.zeros(plane_ref.shape, F32)
    for f in range(2):
        base = 24 * 9 * f
        for x in range(PXU):
            flat = plane_of(own_ref, PYZ * x, ROWS * f)
            rows = [OWN_AT[x // 4][x % 4]] if x < 12 else [16 + NEAR_AT[1][x - 12]]
            if x % 4 == 0:
                rows.append(OWN_AT[x // 4 - 1][4] if x else 16 + NEAR_AT[0][4])
            for r in rows:
                plane_ref[pl.ds(base + r, 9, stride=24), :] = flat
        for h in range(2):
            make_windows(plane_ref, base + 8 * h, 24, win_ref, 128 * f + 64 * h)
        make_windows(plane_ref, base + 16, 24, near_win_ref, 64 * f)
        win_ref[:, 256 + 128 * f : 384 + 128 * f, :] = jnp.zeros((2, LANES, LANES), F32)
        for row in OWN_AT:
            for w, i, v in along_x(win_ref, 128 * f, row, derive):
                r = 256 + 128 * f + 8 * row[i]
                win_ref[w, r : r + 8, :] = v
    for column in range(4):
        turned(win_ref, 128 * column, elem_ref, column)
    turned(near_win_ref, 0, near_elem_ref, 0)
    near_slope_ref[...] = jnp.zeros(near_slope_ref.shape, F32)
    for f in range(2):
        for w in range(2):
            value = [near_win_ref[w, 64 * f + 8 * c : 64 * f + 8 * c + 8, :] for c in (0, 4, 5, 6, 7)]
            near_slope_ref[w, 64 * f : 64 * f + 8, :] = float(DERIV[4, 4]) * value[0]
            for i, v in enumerate(derive(value[1:] + [jnp.zeros((8, LANES), F32)])[:4]):
                r = 64 * f + 8 * NEAR_AT[1][i]
                near_slope_ref[w, r : r + 8, :] = v

    copies[2].wait()
    copies[3].wait()
    slot = lax.broadcasted_iota(jnp.int32, (1, 256), 1)
    code = jnp.where(slot < count_ref[0:1, 0:1], slot_elements(conn_ref), -1)
    element = lax.broadcasted_iota(jnp.int32, (256, 256), 0)
    pick = jnp.concatenate([jnp.where(code == element, 1.0, 0.0).astype(BF16), last_layer(code)], axis=0)
    block_ref[0:125, :] = shear_ref[...]
    block_ref[125:128, :] = jnp.zeros((3, 256), F32)
    moved = add_parts(dot_nt(jnp.concatenate(split3(block_ref[...]), axis=0), pick))
    right_ref[80:144, :] = halves(moved[:, 256:])
    moved_ref[0:128, :] = moved[:, 0:256]
    moved_ref[128:136, :] = jnp.zeros((8, 256), F32)

    def tile_of(i, ez):
        t = ez // 4
        return moved_ref[25 * i : 25 * i + 32, t * LANES : (t + 1) * LANES], 32 * (ez % 4)

    place_flux(flux_ref, tile_of, lambda i: [(0, 24 * i, 24)])
    place_flux(near_flux_ref, tile_of, lambda i: [(24, 8 * NEAR_AT[1][i], 8)])
    scaled(flux_ref, lane_weight(OWN_AT))
    scaled(near_flux_ref, lane_weight(NEAR_AT))

    kern = [[None] * 5 for _ in range(5)]
    near = [[None] * 5 for _ in range(5)]
    for k in range(5):
        fwd, adj, both = [derive([part(ref, c, j, k) for j in range(5)]) for ref, c in ((elem_ref, 0), (elem_ref, 1), (near_elem_ref, 0))]
        for j in range(5):
            kern[j][k] = fwd[j] * adj[j] + part(elem_ref, 2, j, k) * part(elem_ref, 3, j, k)
            near[j][k] = both[j] * pltpu.roll(both[j], 64, 1)
    for j in range(5):
        fwd, adj, both = [derive([part(ref, c, j, k) for k in range(5)]) for ref, c in ((elem_ref, 0), (elem_ref, 1), (near_elem_ref, 0))]
        for k in range(5):
            kern[j][k] = -(kern[j][k] + fwd[k] * adj[k]) * flux_part(flux_ref, j, k)
            r = (j * 5 + k) * 8
            near_kern_ref[r : r + 8, :] = near[j][k] + both[k] * pltpu.roll(both[k], 64, 1)
    folded(kern, line_ref, win_ref, 0)
    low, high = [gathered(win_ref, 0, h) for h in range(2)]
    row = lax.broadcasted_iota(jnp.int32, (8, LANES), 0)
    tiles = []
    for t in range(9):
        first = low[t] + jnp.where((row == 1) | (row == 2), pltpu.roll(high[t], 5, 0), 0.0)
        second = jnp.where(row < 4, high[t], jnp.where(row == 4, pltpu.roll(high[t], 6, 0), 0.0))
        tiles.append(jnp.concatenate([first, second], axis=0))
    for t, tile in enumerate(cross_smoothed(tiles, cross_ref)):
        kern_ref[:, t * LANES : (t + 1) * LANES] = tile


def message_flux(prev_ref, spread_ref):
    spread_ref[0:64, :] = prev_ref[80:144, :]
    spread_ref[64:128, :] = pltpu.roll(prev_ref[80:144, :], 64, 1)
    spread_ref[128:136, :] = jnp.zeros((8, LANES), F32)
    return lambda i, ez: (spread_ref[25 * i : 25 * i + 32, :], 8 * ez)


def near_kernel(
    small_ref, next_ref, count_ref, flux_in_ref, slope_ref, near_kern_ref, kern_in_ref, cross_ref,
    kern_ref,
    plane_ref, new_ref, win_ref, elem_ref, flux_ref, line_ref, spread_ref,
):
    plane_ref[...] = jnp.zeros(plane_ref.shape, F32)
    for f in range(2):
        share = small_ref[16 * f : 16 * f + 9, :]
        plane_ref[pl.ds(f, 9, stride=8), :] = share
        plane_ref[pl.ds(2 + f, 9, stride=8), :] = plane_of(next_ref, 0, 16 * f)
    make_windows(plane_ref, 0, 8, new_ref, 0)
    win_ref[...] = slope_ref[...]
    for f in range(2):
        for w in range(2):
            r = 64 * f
            win_ref[w, r : r + 8, :] = win_ref[w, r : r + 8, :] + new_ref[w, 8 * f : 8 * f + 8, :]
            for i in range(4):
                r = 64 * f + 8 * NEAR_AT[1][i]
                new = float(DERIV[i, 4]) * new_ref[w, 16 + 8 * f : 24 + 8 * f, :]
                win_ref[w, r : r + 8, :] = win_ref[w, r : r + 8, :] + new
    turned(win_ref, 0, elem_ref, 0)
    lower, upper = small_ref[32:48, :], pltpu.roll(small_ref[32:48, :], 64, 1)
    live = upper[13:14, :] < count_ref[0:1, 0:1].astype(F32)
    spread_ref[0:16, :] = jnp.where(live, lower, 0.0)
    spread_ref[16:32, :] = jnp.where(live, upper, 0.0)
    spread_ref[32:40, :] = jnp.zeros((8, LANES), F32)
    place_flux(flux_ref, lambda i, ez: (spread_ref[4:36, :], 8 * ez), lambda i: [(0, 8 * NEAR_AT[0][i], 8)], (4,))
    scaled(flux_ref, lane_weight([NEAR_AT[0]]))
    kern = [[None] * 5 for _ in range(5)]
    for j in range(5):
        for k in range(5):
            slope = part(elem_ref, 0, j, k)
            total = flux_part(near_kern_ref, j, k) + slope * pltpu.roll(slope, 64, 1)
            kern[j][k] = -total * (flux_part(flux_ref, j, k) + flux_part(flux_in_ref, j, k))
    folded(kern, line_ref, win_ref, 0)
    row = lax.broadcasted_iota(jnp.int32, (8, LANES), 0)
    tiles = [jnp.where((row == 0) | (row >= 4), v, 0.0) for v in gathered(win_ref, 0, 0)]
    for t, tile in enumerate(cross_smoothed(tiles, cross_ref)):
        columns = slice(t * LANES, (t + 1) * LANES)
        kern_ref[0:8, columns] = kern_in_ref[0:8, columns] + jnp.where(row == 0, tile, 0.0)
        kern_ref[8:16, columns] = kern_in_ref[8:16, columns] + jnp.where(row >= 4, tile, 0.0)


def gathered(win_ref, base, h):
    lane = lax.broadcasted_iota(jnp.int32, (8, LANES), 1)
    tiles = [None] * 9
    for ey in range(EY):
        rows = pl.ds(base + h * 64 + ey, 8, stride=8)
        a, b = win_ref[0, rows, :], win_ref[1, rows, :]
        if ey:
            a, b = pltpu.roll(a, 4 * ey, 1), pltpu.roll(b, 4 * ey, 1)
            keep = lane >= 4 * ey
            a, b = jnp.where(keep, a, 0.0), jnp.where(keep, b, a)
        tiles[ey] = a if ey == 0 else tiles[ey] + a
        tiles[ey + 1] = b
    return tiles


def summed_along_x(win_ref, places, out_ref, row):
    for line in places:
        for w, i, v in along_x(win_ref, LANES, line, derive_back):
            r = 8 * line[i]
            out_ref[w, row + r : row + r + 8, :] = win_ref[w, r : r + 8, :] + v


def to_planes(win_ref, base, plane_ref):
    for h in range(2):
        for t, tile in enumerate(gathered(win_ref, base, h)):
            plane_ref[t * 16 + 8 * h : t * 16 + 8 * h + 8, :] = tile


def add_plane(line_ref, f, x, flat):
    lane9 = lax.broadcasted_iota(jnp.int32, (9, LANES), 1)
    r0, off = divmod(PYZ * x, LANES)
    if off:
        flat = pltpu.roll(flat, off, 1)
        spill = jnp.where(lane9 < off, flat, 0.0)
        flat = jnp.where(lane9 < off, 0.0, flat)
    line_ref[f, r0 : r0 + 9, :] = line_ref[f, r0 : r0 + 9, :] + flat
    if off:
        line_ref[f, r0 + 1 : r0 + 10, :] = line_ref[f, r0 + 1 : r0 + 10, :] + spill


def force_kernel(elem_ref, flux_ref, out_ref, win_ref, fold_ref, force_ref, plane_ref):
    out_ref[...] = jnp.zeros(out_ref.shape, F32)
    for f in range(2):
        force_terms(elem_ref, f, 2 + f, flux_ref, fold_ref, win_ref, 0)
        summed_along_x(win_ref, OWN_AT, force_ref, 0)
        to_planes(force_ref, 0, plane_ref)
        for x in range(13):
            i, m = x % 4, x // 4
            rows = [OWN_AT[m][i]] if m < 3 else []
            if i == 0 and m > 0:
                rows.append(OWN_AT[m - 1][4])
            flat = [plane_ref[pl.ds(r, 9, stride=16), :] for r in rows]
            add_plane(out_ref, f, x, sum(flat[1:], flat[0]))


def near_force_kernel(
    force_ref, near_half_ref, near_flux_ref, prev_ref, next_ref, after_ref,
    out_ref,
    win_ref, fold_ref, near_force_ref, plane_ref, flux_ref, elem_ref, near_win_ref, near_plane_ref, spread_ref,
):
    out_ref[...] = force_ref[...]
    near_plane_ref[...] = jnp.zeros(near_plane_ref.shape, F32)
    for f in range(2):
        for i in range(5):
            flat = plane_of(prev_ref, 12 + PYZ * i, 40 * f) if i < 4 else plane_of(next_ref, 0, 16 * f)
            near_plane_ref[pl.ds(72 * f + i, 9, stride=8), :] = flat
        near_win_ref[:, 128 * f : 128 * f + 64, :] = near_half_ref[:, 64 * f : 64 * f + 64, :]
        make_windows(near_plane_ref, 72 * f, 8, near_win_ref, 128 * f + 64)
    place_flux(flux_ref, message_flux(prev_ref, spread_ref), lambda i: [(0, 8 * NEAR_AT[0][i], 8)])
    scaled(flux_ref, lane_weight([NEAR_AT[0]]))
    flux_ref[...] = flux_ref[...] + near_flux_ref[...]
    for f in range(2):
        win_ref[...] = jnp.zeros(win_ref.shape, F32)
        for row in NEAR_AT:
            for w, i, v in along_x(near_win_ref, LANES * f, row, derive):
                win_ref[w, 8 * row[i] : 8 * row[i] + 8, :] = v
        turned(near_win_ref, LANES * f, elem_ref, 0)
        turned(win_ref, 0, elem_ref, 1)
        force_terms(elem_ref, 0, 1, flux_ref, fold_ref, win_ref, 0)
        summed_along_x(win_ref, NEAR_AT, near_force_ref, 0)
        to_planes(near_force_ref, 0, plane_ref)
        for x, r in [(0, NEAR_AT[0][4])] + [(12 + i, NEAR_AT[1][i]) for i in range(4)]:
            add_plane(out_ref, f, x, plane_ref[pl.ds(r, 9, stride=16), :])


def step_kernel(
    line_ref, fwd_ref, fwd_speed_ref, adj_ref, adj_speed_ref, mass_ref,
    fwd_out_ref, fwd_speed_out_ref, adj_out_ref, adj_speed_out_ref,
):
    def step(lo, hi, force):
        shape = (hi - lo) // force[0].shape[1], force[0].shape[1]
        take = lambda ref: ref[0:1, lo:hi].reshape(shape)
        scale = TIME_STEP * mass_ref[lo:hi].reshape(shape)
        speed = take(fwd_speed_ref) + scale * force[0]
        fwd_speed_out_ref[0:1, lo:hi] = speed.reshape(1, hi - lo)
        fwd_out_ref[0:1, lo:hi] = (take(fwd_ref) - TIME_STEP * speed).reshape(1, hi - lo)
        speed = take(adj_speed_ref) - scale * force[1]
        adj_speed_out_ref[0:1, lo:hi] = speed.reshape(1, hi - lo)
        adj_out_ref[0:1, lo:hi] = (take(adj_ref) + TIME_STEP * speed).reshape(1, hi - lo)

    for r in range(0, 136, 8):
        step(r * LANES, (r + 8) * LANES, [line_ref[f, r : r + 8, :] for f in range(2)])
    step(NPTS - 16, NPTS, [line_ref[f, 136:137, 0:16] for f in range(2)])


def band_kernel(cut_ref, own_ref, first_ref, second_ref, band_ref, out_ref):
    flat = jnp.concatenate([own_ref[...], first_ref[...], second_ref[...]], axis=0)
    k1 = flat.astype(BF16)
    rest = flat - k1.astype(F32)
    k2 = rest.astype(BF16)
    k3 = (rest - k2.astype(F32)).astype(BF16)
    stacked = jnp.concatenate([k1, k2, k3, k1, k2, k1], axis=0)
    band = band_ref[cut_ref[0] & 1]
    out_ref[...] = jnp.dot(band, stacked, preferred_element_type=F32)[:, :PYZ]


def on_device(
    forward_displacement,
    forward_velocity,
    adjoint_displacement,
    adjoint_velocity,
    inverse_mass,
    shear_modulus,
    connectivity,
    face_points,
    element_count,
):
    events = lax.axis_size("event")
    cuts = lax.axis_size("cuts")
    cut = lax.axis_index("cuts").astype(jnp.int32).reshape(1)
    pairs_first = [(i, (i - 1 if i % 2 == 0 else i + 1) % cuts) for i in range(cuts)]
    pairs_second = [(i, (i + 1 if i % 2 == 0 else i - 1) % cuts) for i in range(cuts)]

    vmem = pl.BlockSpec(memory_space=pltpu.VMEM)
    smem = pl.BlockSpec(memory_space=pltpu.SMEM)
    anywhere = pl.BlockSpec(memory_space=pl.ANY)

    def held(block):
        return pltpu.with_memory_space_constraint(block, pltpu.VMEM)

    def in_hbm(block):
        return pltpu.with_memory_space_constraint(block, pltpu.HBM)

    def cost(flops):
        return pl.CostEstimate(flops=flops, bytes_accessed=1000000, transcendentals=0)

    dma = pltpu.SemaphoreType.DMA
    point_row = pltpu.VMEM((1, NPTS), F32)
    flux_block = pltpu.VMEM((200, LANES), F32)
    kern_block = pltpu.VMEM((16, 9 * LANES), F32)
    line_block = pltpu.VMEM((256, LANES), F32)

    def elements(n):
        return pltpu.VMEM((n, 168, LANES), F32)

    def windows(n):
        return pltpu.VMEM((2, n * LANES, LANES), F32)

    fields = (in_hbm(forward_displacement), in_hbm(adjoint_displacement))
    cross = held(jnp.asarray(cross_table()))
    conn, shear = in_hbm(connectivity), in_hbm(shear_modulus)
    inputs = [pltpu.VMEM((8, 256), jnp.int32), pltpu.VMEM((125, 256), F32), point_row, point_row]
    small, left = pl.pallas_call(
        pack_kernel,
        out_shape=[pltpu.VMEM((48, LANES), F32), pltpu.VMEM((32, LANES), F32)],
        in_specs=[anywhere] * 4,
        scratch_shapes=inputs + [pltpu.VMEM((32, 256), F32), pltpu.VMEM((40, LANES), F32), dma((4,))],
        cost_estimate=cost(100000000),
        name="pack",
    )(conn, shear, *fields)
    to_next = [(i, (i + 1) % cuts) for i in range(cuts)]
    small = lax.ppermute(small, "cuts", to_next)
    count, left = lax.optimization_barrier((element_count, left))
    count = jnp.broadcast_to(count.reshape(1, 1), (8, LANES))
    prev_count = lax.ppermute(count, "cuts", to_next)
    count, left = lax.optimization_barrier((count, left))

    message = pltpu.VMEM((144, LANES), F32)
    own_blocks = [elements(4), flux_block, flux_block, windows(1), windows(1), flux_block, kern_block, message]

    def own_part(turn, before, waits=()):
        given = (cut, held(count), conn, shear, *fields, cross)
        return pl.pallas_call(
            functools.partial(own_kernel, turn),
            out_shape=own_blocks,
            in_specs=[smem, vmem] + [anywhere] * 4 + [vmem] * (1 + len(before)) + [anywhere] * len(waits),
            scratch_shapes=[
                pltpu.VMEM((2 * 9 * 24, LANES), F32),
                windows(4),
                line_block,
                elements(1),
                pltpu.VMEM((136, 256), F32),
                *inputs,
                pltpu.VMEM((128, 256), F32),
                pltpu.VMEM((2 * ROWS, LANES), F32),
                dma((4,)),
            ],
            input_output_aliases={len(given) + n: n for n in range(len(before))},
            cost_estimate=cost(300000000),
            name="own_layers",
        )(*given, *[held(block) for block in before], *[held(block) for block in waits])

    left, *blocks = lax.optimization_barrier((left, *own_part(0, [])))
    after = lax.ppermute(left, "cuts", [((i + 1) % cuts, i) for i in range(cuts)])
    elem, flux, near_flux, near_win, near_slope, near_kern, kern, right = own_part(1, blocks, [small])
    prev = lax.ppermute(right, "cuts", to_next)
    kern = pl.pallas_call(
        near_kernel,
        out_shape=kern_block,
        in_specs=[vmem] * 8,
        scratch_shapes=[
            pltpu.VMEM((72, LANES), F32),
            pltpu.VMEM((2, 64, LANES), F32),
            windows(1),
            elements(1),
            flux_block,
            line_block,
            pltpu.VMEM((136, LANES), F32),
        ],
        cost_estimate=cost(200000000),
        name="near_layers",
    )(held(small), held(after), held(prev_count), held(near_flux), held(near_slope), held(near_kern), held(kern), cross)

    force = pl.pallas_call(
        force_kernel,
        out_shape=pltpu.VMEM((2, ROWS, LANES), F32),
        in_specs=[vmem] * 2,
        scratch_shapes=[windows(2), line_block, windows(1), pltpu.VMEM((144, LANES), F32)],
        cost_estimate=cost(200000000),
        name="forces",
    )(held(elem), held(flux))

    if events == 2:
        other = lax.ppermute(kern, "event", [(0, 1), (1, 0)])
        other, force = lax.optimization_barrier((other, force))
        kern = kern + other
    elif events > 2:
        kern = lax.psum(kern, "event")
    kern_first = lax.ppermute(kern, "cuts", pairs_first)
    kern_second = lax.ppermute(kern, "cuts", pairs_second)

    force = pl.pallas_call(
        near_force_kernel,
        out_shape=pltpu.VMEM((2, ROWS, LANES), F32),
        in_specs=[vmem] * 6,
        scratch_shapes=[
            windows(2),
            line_block,
            windows(1),
            pltpu.VMEM((144, LANES), F32),
            flux_block,
            elements(2),
            windows(2),
            pltpu.VMEM((2 * 72, LANES), F32),
            pltpu.VMEM((136, LANES), F32),
        ],
        cost_estimate=cost(200000000),
        name="near_forces",
    )(held(force), held(near_win), held(near_flux), held(prev), held(after), held(kern))
    points = jax.ShapeDtypeStruct((1, NPTS), F32)
    outs = pl.pallas_call(
        step_kernel,
        out_shape=[points] * 4,
        in_specs=[vmem] * 6,
        cost_estimate=cost(200000000),
        name="step",
    )(
        held(force),
        held(forward_displacement),
        held(forward_velocity),
        held(adjoint_displacement),
        held(adjoint_velocity),
        held(inverse_mass),
    )
    shear_kernel = pl.pallas_call(
        band_kernel,
        out_shape=jax.ShapeDtypeStruct((PXU, PYZ), F32),
        in_specs=[smem] + [vmem] * 4,
        cost_estimate=cost(20000000),
        name="band",
    )(cut, held(kern), held(kern_first), held(kern_second), held(jnp.asarray(band_table())))
    return (*outs, shear_kernel)


def solution(mesh):
    in_specs = (
        P("event", "cuts"),
        P("event", "cuts"),
        P("event", "cuts"),
        P("event", "cuts"),
        P("cuts"),
        P(None, "cuts"),
        P(None, "cuts"),
        P("cuts", None),
        P("cuts"),
    )
    out_specs = (
        P("event", "cuts"),
        P("event", "cuts"),
        P("event", "cuts"),
        P("event", "cuts"),
        P("cuts", None),
    )
    return jax.shard_map(on_device, mesh=mesh, in_specs=in_specs, out_specs=out_specs, check_vma=False)
```

```python
import functools

import numpy as np
import jax
import jax.numpy as jnp
import ml_dtypes
from jax import lax
from jax.experimental import pallas as pl
from jax.experimental.pallas import tpu as pltpu
from jax.sharding import PartitionSpec as P

NGLL = 5
EX, EY, EZ = 4, 8, 8
PXU = 16
PY = 33
PZ = 33
PYZ = 1089
NPTS = 17424
LANES = 128
ROWS = 144
TIME_STEP = 0.02
OWN_OUTS, OWN_SCRATCH = 7, 5
F32 = jnp.float32
BF16 = jnp.bfloat16


def gll():
    nodes = np.array([-1.0, -np.sqrt(3.0 / 7.0), 0.0, np.sqrt(3.0 / 7.0), 1.0])
    bary = np.array([1.0 / np.prod([nodes[r] - nodes[c] for c in range(5) if c != r]) for r in range(5)])
    d = np.zeros((5, 5))
    for r in range(5):
        for c in range(5):
            if c != r:
                d[r, c] = bary[c] / bary[r] / (nodes[r] - nodes[c])
        d[r, r] = -np.sum(d[r])
    return d


DERIV = gll()


def split_np(x):
    x = np.asarray(x, np.float32)
    parts = []
    for _ in range(3):
        p = x.astype(ml_dtypes.bfloat16)
        parts.append(p)
        x = x - p.astype(np.float32)
    return parts


ROW_PLANE = np.array([4 * (r % 3) + r // 3 for r in range(12)] + [12, 13, 14, 15])
OWN_AT = [[3 * i + m for i in range(5)] for m in range(3)]
NEAR_AT = [[8, 9, 10, 11, 0], [4, 5, 6, 7, 12]]


def band_table():
    offsets = np.arange(-PXU, PXU + 1)
    w = lambda d: np.exp(-d * d / (2.0 * (PXU / 4.0) ** 2))
    total = w(offsets.astype(np.float64)).sum()
    out = []
    for first in (-PXU, PXU):
        source = np.concatenate([ROW_PLANE, ROW_PLANE + first, ROW_PLANE - first])
        spread = np.arange(PXU)[:, None] - source[None, :]
        band = w(spread.astype(np.float64)) * (np.abs(spread) <= PXU) / total
        b1, b2, b3 = split_np(band)
        out.append(np.concatenate([b1, b1, b1, b2, b2, b3], axis=1))
    return np.stack(out)


def cross_table():
    off = np.arange(-4, 5)
    k = np.exp(-off * off / (2.0 * 1.5 * 1.5))
    point = np.arange(33)
    inside = ((point[None, :] + off[:, None]) >= 0) & ((point[None, :] + off[:, None]) < 33)
    taps = k[:, None] * inside
    taps = taps / taps.sum(axis=0, keepdims=True)
    out = np.zeros((24, 1152), np.float32)
    out[0:9, :PYZ] = np.tile(taps, (1, PY))
    out[9:18, :PYZ] = np.repeat(taps, PZ, axis=1)
    return out


def split3(x):
    hi = x.astype(BF16)
    rest = x - hi.astype(F32)
    mid = rest.astype(BF16)
    low = (rest - mid.astype(F32)).astype(BF16)
    return hi, mid, low


def dot_nt(a, b):
    return lax.dot_general(a, b, (((1,), (1,)), ((), ())), preferred_element_type=F32)


def fetch(sem, *pairs):
    copies = [pltpu.make_async_copy(src, dst, sem.at[n]) for n, (src, dst) in enumerate(pairs)]
    for c in copies:
        c.start()
    return copies


def add_parts(stacked):
    n = stacked.shape[0] // 3
    return stacked[0:n] + (stacked[n : 2 * n] + stacked[2 * n : 3 * n])


def pack_kernel(
    conn_hbm, shear_hbm, fwd_hbm, adj_hbm,
    right_ref, left_ref, own_ref, code_ref, parts_ref,
    conn_ref, shear_ref, fwd_ref, adj_ref, block_ref, sem,
):
    copies = fetch(
        sem,
        (shear_hbm, shear_ref),
        (conn_hbm.at[0:8], conn_ref),
        (fwd_hbm, fwd_ref),
        (adj_hbm, adj_ref),
    )
    copies[1].wait()
    point = conn_ref[0:1, :].astype(F32)
    x = jnp.floor((point + 0.5) * (1.0 / PYZ))
    rest = point - x * PYZ
    y = jnp.floor((rest + 0.5) * (1.0 / PZ))
    z = rest - y * PZ
    code = (8.0 * z + 2.0 * x + 0.25 * y).astype(jnp.int32)
    slot = lax.broadcasted_iota(jnp.int32, (1, 256), 1)
    code_ref[...] = jnp.broadcast_to(code, (8, 256))
    lane = lax.broadcasted_iota(jnp.int32, (LANES, 256), 0)
    pick = jnp.where(code == ((lane >> 3) & 7) * 32 + 24 + (lane & 7), 1.0, 0.0).astype(BF16)
    for f, ref in enumerate((fwd_ref, adj_ref)):
        copies[2 + f].wait()
        for r in range(0, 136, 8):
            own_ref[ROWS * f + r : ROWS * f + r + 8, :] = ref[0:1, r * LANES : (r + 8) * LANES].reshape(8, LANES)
        own_ref[ROWS * f + 136 : ROWS * f + 144, :] = jnp.zeros((8, LANES), F32)
        own_ref[ROWS * f + 136 : ROWS * f + 137, 0:16] = ref[0:1, NPTS - 16 : NPTS]
        right_ref[40 * f : 40 * f + 40, :] = own_ref[ROWS * f + 102 : ROWS * f + 142, :]
        left_ref[16 * f : 16 * f + 16, :] = own_ref[ROWS * f : ROWS * f + 16, :]
    copies[0].wait()
    block_ref[0:125, :] = shear_ref[...]
    block_ref[125:126, :] = slot.astype(F32)
    block_ref[126:128, :] = jnp.zeros((2, 256), F32)
    parts = jnp.concatenate(split3(block_ref[...]), axis=0)
    parts_ref[...] = parts
    flux = add_parts(dot_nt(parts, pick))
    low = lax.broadcasted_iota(jnp.int32, (64, LANES), 1) < 64
    right_ref[80:144, :] = jnp.where(low, flux[0:64], flux[64:128])


def gll_weight(i):
    return (0.1, 49.0 / 90.0, 32.0 / 45.0, 49.0 / 90.0, 0.1)[i]


def lane_weight(places):
    chunk = lax.broadcasted_iota(jnp.int32, (8, LANES), 1) >> 3
    weight = jnp.zeros((8, LANES), F32)
    for row in places:
        for i, place in enumerate(row):
            weight = jnp.where(chunk == place, gll_weight(i), weight)
    return weight


def scaled(ref, weight):
    for j in range(5):
        for k in range(5):
            r = (j * 5 + k) * 8
            ref[r : r + 8, :] = ref[r : r + 8, :] * (weight * (gll_weight(j) * gll_weight(k)))


def place_flux(ref, tile_of, moves, layers=range(NGLL)):
    lane = lax.broadcasted_iota(jnp.int32, (32, LANES), 1)
    for ez in range(EZ):
        total = jnp.zeros((32, LANES), F32)
        for i in layers:
            tile, start = tile_of(i, ez)
            for source, target, width in moves(i):
                shift = (target - source - start) % LANES
                moved = pltpu.roll(tile, shift, 1) if shift else tile
                total = jnp.where((lane >= target) & (lane < target + width), moved, total)
        ref[pl.ds(ez, 25, stride=8), :] = total[0:25]


def derive(e):
    d = DERIV
    s0, s1 = e[0] + e[4], e[1] + e[3]
    d0, d1 = e[0] - e[4], e[1] - e[3]
    out = [None] * 5
    for i in (0, 1):
        even = float((d[i, 0] - d[i, 4]) / 2) * d0 + float((d[i, 1] - d[i, 3]) / 2) * d1
        odd = float((d[i, 0] + d[i, 4]) / 2) * s0 + float((d[i, 1] + d[i, 3]) / 2) * s1 + float(d[i, 2]) * e[2]
        out[i] = odd + even
        out[4 - i] = even - odd
    out[2] = float(d[2, 0]) * d0 + float(d[2, 1]) * d1
    return out


def derive_back(t):
    d = DERIV
    s0, s1 = t[0] + t[4], t[1] + t[3]
    d0, d1 = t[0] - t[4], t[1] - t[3]
    out = [None] * 5
    for i in (0, 1):
        even = float((d[0, i] - d[4, i]) / 2) * d0 + float((d[1, i] - d[3, i]) / 2) * d1
        odd = float((d[0, i] + d[4, i]) / 2) * s0 + float((d[1, i] + d[3, i]) / 2) * s1 + float(d[2, i]) * t[2]
        out[i] = odd + even
        out[4 - i] = even - odd
    out[2] = float(d[0, 2]) * d0 + float(d[1, 2]) * d1
    return out


def shifted(tiles, distance, lane):
    skip, part = divmod(distance, LANES)
    if part == 0:
        moved = tiles
        pick = None
    else:
        moved = [pltpu.roll(t, LANES - part, 1) for t in tiles]
        pick = lane < LANES - part
    n = len(tiles)
    out = []
    for i in range(n):
        a = moved[(i + skip) % n]
        b = moved[(i + skip + 1) % n]
        out.append(a if pick is None else jnp.where(pick, a, b))
    return out


def plane_of(ref, start, row):
    r0, off = divmod(start, LANES)
    lane9 = lax.broadcasted_iota(jnp.int32, (9, LANES), 1)
    flat = ref[row + r0 : row + r0 + 9, :]
    if off:
        flat = jnp.where(
            lane9 < LANES - off,
            pltpu.roll(flat, LANES - off, 1),
            pltpu.roll(ref[row + r0 + 1 : row + r0 + 10, :], LANES - off, 1),
        )
    return flat


def store_plane(ref, row, flat):
    ref[pl.ds(row, 9, stride=16), :] = flat


def make_windows(plane_ref, base, pitch, win_ref, row):
    lane = lax.broadcasted_iota(jnp.int32, (8, LANES), 1)
    tiles = [plane_ref[base + t * pitch : base + t * pitch + 8, :] for t in range(9)]
    for ey in range(EY):
        near = [tiles[ey], tiles[ey + 1], tiles[min(ey + 2, 8)]]
        if ey:
            near = [pltpu.roll(t, LANES - 4 * ey, 1) for t in near]
            keep = lane < LANES - 4 * ey
            near = [jnp.where(keep, near[0], near[1]), jnp.where(keep, near[1], near[2])]
        for w in range(2):
            win_ref[w, pl.ds(row + ey, 8, stride=8), :] = near[w]


def along_x(win_ref, base, row, combine):
    for w in range(2):
        values = combine([win_ref[w, base + 8 * c : base + 8 * c + 8, :] for c in row])
        for i, v in enumerate(values):
            yield w, i, v


def turned(win_ref, base, elem_ref, column):
    elem_ref[column, 0:LANES, :] = win_ref[0, base : base + LANES, :].T
    elem_ref[column, LANES:168, :] = win_ref[1, base : base + LANES, :].T[0:40, :]


def part(ref, column, j, k):
    return ref[column, pl.ds(j * PZ + k, 8, stride=4), :]


def flux_part(ref, j, k):
    r = (j * 5 + k) * 8
    return ref[r : r + 8, :]


def folded(term, line_ref, win_ref, base):
    row = lax.broadcasted_iota(jnp.int32, (8, LANES), 0)
    line_ref[160:256, :] = jnp.zeros((96, LANES), F32)
    for j in range(5):
        for k in range(1, 4):
            line_ref[pl.ds(j * PZ + k, 8, stride=4), :] = term[j][k]
        last = term[j][4]
        line_ref[pl.ds(j * PZ, 8, stride=4), :] = term[j][0] + jnp.where(row == 0, 0.0, pltpu.roll(last, 1, 0))
        line_ref[j * PZ + 32 : j * PZ + 33, :] = last[7:8, :]
    for w in range(2):
        win_ref[w, base : base + LANES, :] = line_ref[w * LANES : (w + 1) * LANES, :].T


def force_terms(elem_ref, value, slope, flux_ref, line_ref, win_ref, row):
    term = [[None] * 5 for _ in range(5)]
    for k in range(5):
        grads = derive([part(elem_ref, value, j, k) for j in range(5)])
        for j, v in enumerate(derive_back([g * flux_part(flux_ref, j, k) for j, g in enumerate(grads)])):
            term[j][k] = v
    for j in range(5):
        grads = derive([part(elem_ref, value, j, k) for k in range(5)])
        for k, v in enumerate(derive_back([g * flux_part(flux_ref, j, k) for k, g in enumerate(grads)])):
            term[j][k] = term[j][k] + v
    folded(term, line_ref, win_ref, row)
    term = [[part(elem_ref, slope, j, k) * flux_part(flux_ref, j, k) for k in range(5)] for j in range(5)]
    folded(term, line_ref, win_ref, row + LANES)


def cross_smoothed(tiles, cross_ref):
    lane = lax.broadcasted_iota(jnp.int32, tiles[0].shape, 1)
    for base, step in ((0, 1), (9, PZ)):
        total = None
        for tap in range(9):
            moved = shifted(tiles, step * (tap - 4), lane) if tap != 4 else tiles
            terms = [v * cross_ref[base + tap : base + tap + 1, t * LANES : (t + 1) * LANES] for t, v in enumerate(moved)]
            total = terms if total is None else [a + b for a, b in zip(total, terms)]
        tiles = total
    return tiles


def own_kernel(turn, cut_ref, count_ref, own_ref, code_ref, parts_ref, cross_ref, *refs):
    refs = refs[-OWN_OUTS - OWN_SCRATCH :]
    mine = (cut_ref[0] == 0) if turn == 0 else (cut_ref[0] != 0)

    @pl.when(mine)
    def _():
        own_layers(count_ref, own_ref, code_ref, parts_ref, cross_ref, *refs)


def own_layers(
    count_ref, own_ref, code_ref, parts_ref, cross_ref,
    elem_ref, flux_ref, near_flux_ref, near_win_ref, near_slope_ref, near_kern_ref, kern_ref,
    plane_ref, win_ref, line_ref, near_elem_ref, moved_ref,
):
    plane_ref[...] = jnp.zeros(plane_ref.shape, F32)
    for f in range(2):
        base = 24 * 9 * f
        for x in range(PXU):
            flat = plane_of(own_ref, PYZ * x, ROWS * f)
            rows = [OWN_AT[x // 4][x % 4]] if x < 12 else [16 + NEAR_AT[1][x - 12]]
            if x % 4 == 0:
                rows.append(OWN_AT[x // 4 - 1][4] if x else 16 + NEAR_AT[0][4])
            for r in rows:
                plane_ref[pl.ds(base + r, 9, stride=24), :] = flat
        for h in range(2):
            make_windows(plane_ref, base + 8 * h, 24, win_ref, 128 * f + 64 * h)
        make_windows(plane_ref, base + 16, 24, near_win_ref, 64 * f)
        win_ref[:, 256 + 128 * f : 384 + 128 * f, :] = jnp.zeros((2, LANES, LANES), F32)
        for row in OWN_AT:
            for w, i, v in along_x(win_ref, 128 * f, row, derive):
                r = 256 + 128 * f + 8 * row[i]
                win_ref[w, r : r + 8, :] = v
    for column in range(4):
        turned(win_ref, 128 * column, elem_ref, column)
    turned(near_win_ref, 0, near_elem_ref, 0)
    near_slope_ref[...] = jnp.zeros(near_slope_ref.shape, F32)
    for f in range(2):
        for w in range(2):
            value = [near_win_ref[w, 64 * f + 8 * c : 64 * f + 8 * c + 8, :] for c in (0, 4, 5, 6, 7)]
            near_slope_ref[w, 64 * f : 64 * f + 8, :] = float(DERIV[4, 4]) * value[0]
            for i, v in enumerate(derive(value[1:] + [jnp.zeros((8, LANES), F32)])[:4]):
                r = 64 * f + 8 * NEAR_AT[1][i]
                near_slope_ref[w, r : r + 8, :] = v

    element = lax.broadcasted_iota(jnp.int32, (256, 256), 0)
    slot = lax.broadcasted_iota(jnp.int32, (1, 256), 1)
    live = jnp.concatenate([count_ref[0:1, :], count_ref[0:1, :]], axis=1)
    code = jnp.where(slot < live, code_ref[0:1, :], -1)
    pick = jnp.where(code == element, 1.0, 0.0).astype(BF16)
    moved_ref[0:128, :] = add_parts(dot_nt(parts_ref[...], pick))
    moved_ref[128:136, :] = jnp.zeros((8, 256), F32)

    def tile_of(i, ez):
        t = ez // 4
        return moved_ref[25 * i : 25 * i + 32, t * LANES : (t + 1) * LANES], 32 * (ez % 4)

    place_flux(flux_ref, tile_of, lambda i: [(0, 24 * i, 24)])
    place_flux(near_flux_ref, tile_of, lambda i: [(24, 8 * NEAR_AT[1][i], 8)])
    scaled(flux_ref, lane_weight(OWN_AT))
    scaled(near_flux_ref, lane_weight(NEAR_AT))

    kern = [[None] * 5 for _ in range(5)]
    near = [[None] * 5 for _ in range(5)]
    for k in range(5):
        fwd, adj, both = [derive([part(ref, c, j, k) for j in range(5)]) for ref, c in ((elem_ref, 0), (elem_ref, 1), (near_elem_ref, 0))]
        for j in range(5):
            kern[j][k] = fwd[j] * adj[j] + part(elem_ref, 2, j, k) * part(elem_ref, 3, j, k)
            near[j][k] = both[j] * pltpu.roll(both[j], 64, 1)
    for j in range(5):
        fwd, adj, both = [derive([part(ref, c, j, k) for k in range(5)]) for ref, c in ((elem_ref, 0), (elem_ref, 1), (near_elem_ref, 0))]
        for k in range(5):
            kern[j][k] = -(kern[j][k] + fwd[k] * adj[k]) * flux_part(flux_ref, j, k)
            r = (j * 5 + k) * 8
            near_kern_ref[r : r + 8, :] = near[j][k] + both[k] * pltpu.roll(both[k], 64, 1)
    folded(kern, line_ref, win_ref, 0)
    low, high = [gathered(win_ref, 0, h) for h in range(2)]
    row = lax.broadcasted_iota(jnp.int32, (8, LANES), 0)
    tiles = []
    for t in range(9):
        first = low[t] + jnp.where((row == 1) | (row == 2), pltpu.roll(high[t], 5, 0), 0.0)
        second = jnp.where(row < 4, high[t], jnp.where(row == 4, pltpu.roll(high[t], 6, 0), 0.0))
        tiles.append(jnp.concatenate([first, second], axis=0))
    for t, tile in enumerate(cross_smoothed(tiles, cross_ref)):
        kern_ref[:, t * LANES : (t + 1) * LANES] = tile


def message_flux(prev_ref, count_ref, spread_ref):
    upper = pltpu.roll(prev_ref[80:144, :], 64, 1)
    live = upper[61:62, :] < count_ref[0:1, :].astype(F32)
    spread_ref[0:64, :] = jnp.where(live, prev_ref[80:144, :], 0.0)
    spread_ref[64:128, :] = jnp.where(live, upper, 0.0)
    spread_ref[128:136, :] = jnp.zeros((8, LANES), F32)
    return lambda i, ez: (spread_ref[25 * i : 25 * i + 32, :], 8 * ez)


def near_kernel(
    prev_ref, next_ref, count_ref, flux_in_ref, slope_ref, near_kern_ref, kern_in_ref, cross_ref,
    kern_ref,
    plane_ref, new_ref, win_ref, elem_ref, flux_ref, line_ref, spread_ref,
):
    plane_ref[...] = jnp.zeros(plane_ref.shape, F32)
    for f in range(2):
        share = None
        for l in range(4):
            term = float(DERIV[4, l]) * plane_of(prev_ref, 12 + PYZ * l, 40 * f)
            share = term if share is None else share + term
        plane_ref[pl.ds(f, 9, stride=8), :] = share
        plane_ref[pl.ds(2 + f, 9, stride=8), :] = plane_of(next_ref, 0, 16 * f)
    make_windows(plane_ref, 0, 8, new_ref, 0)
    win_ref[...] = slope_ref[...]
    for f in range(2):
        for w in range(2):
            r = 64 * f
            win_ref[w, r : r + 8, :] = win_ref[w, r : r + 8, :] + new_ref[w, 8 * f : 8 * f + 8, :]
            for i in range(4):
                r = 64 * f + 8 * NEAR_AT[1][i]
                new = float(DERIV[i, 4]) * new_ref[w, 16 + 8 * f : 24 + 8 * f, :]
                win_ref[w, r : r + 8, :] = win_ref[w, r : r + 8, :] + new
    turned(win_ref, 0, elem_ref, 0)
    place_flux(flux_ref, message_flux(prev_ref, count_ref, spread_ref), lambda i: [(0, 8 * NEAR_AT[0][i], 8)], (4,))
    scaled(flux_ref, lane_weight([NEAR_AT[0]]))
    kern = [[None] * 5 for _ in range(5)]
    for j in range(5):
        for k in range(5):
            slope = part(elem_ref, 0, j, k)
            total = flux_part(near_kern_ref, j, k) + slope * pltpu.roll(slope, 64, 1)
            kern[j][k] = -total * (flux_part(flux_ref, j, k) + flux_part(flux_in_ref, j, k))
    folded(kern, line_ref, win_ref, 0)
    row = lax.broadcasted_iota(jnp.int32, (8, LANES), 0)
    tiles = [jnp.where((row == 0) | (row >= 4), v, 0.0) for v in gathered(win_ref, 0, 0)]
    for t, tile in enumerate(cross_smoothed(tiles, cross_ref)):
        columns = slice(t * LANES, (t + 1) * LANES)
        kern_ref[0:8, columns] = kern_in_ref[0:8, columns] + jnp.where(row == 0, tile, 0.0)
        kern_ref[8:16, columns] = kern_in_ref[8:16, columns] + jnp.where(row >= 4, tile, 0.0)


def gathered(win_ref, base, h):
    lane = lax.broadcasted_iota(jnp.int32, (8, LANES), 1)
    tiles = [None] * 9
    for ey in range(EY):
        rows = pl.ds(base + h * 64 + ey, 8, stride=8)
        a, b = win_ref[0, rows, :], win_ref[1, rows, :]
        if ey:
            a, b = pltpu.roll(a, 4 * ey, 1), pltpu.roll(b, 4 * ey, 1)
            keep = lane >= 4 * ey
            a, b = jnp.where(keep, a, 0.0), jnp.where(keep, b, a)
        tiles[ey] = a if ey == 0 else tiles[ey] + a
        tiles[ey + 1] = b
    return tiles


def summed_along_x(win_ref, places, out_ref, row):
    for line in places:
        for w, i, v in along_x(win_ref, LANES, line, derive_back):
            r = 8 * line[i]
            out_ref[w, row + r : row + r + 8, :] = win_ref[w, r : r + 8, :] + v


def to_planes(win_ref, base, plane_ref):
    for h in range(2):
        for t, tile in enumerate(gathered(win_ref, base, h)):
            plane_ref[t * 16 + 8 * h : t * 16 + 8 * h + 8, :] = tile


def add_plane(line_ref, f, x, flat):
    lane9 = lax.broadcasted_iota(jnp.int32, (9, LANES), 1)
    r0, off = divmod(PYZ * x, LANES)
    if off:
        flat = pltpu.roll(flat, off, 1)
        spill = jnp.where(lane9 < off, flat, 0.0)
        flat = jnp.where(lane9 < off, 0.0, flat)
    line_ref[f, r0 : r0 + 9, :] = line_ref[f, r0 : r0 + 9, :] + flat
    if off:
        line_ref[f, r0 + 1 : r0 + 10, :] = line_ref[f, r0 + 1 : r0 + 10, :] + spill


def force_kernel(elem_ref, flux_ref, out_ref, win_ref, fold_ref, force_ref, plane_ref):
    out_ref[...] = jnp.zeros(out_ref.shape, F32)
    for f in range(2):
        force_terms(elem_ref, f, 2 + f, flux_ref, fold_ref, win_ref, 0)
        summed_along_x(win_ref, OWN_AT, force_ref, 0)
        to_planes(force_ref, 0, plane_ref)
        for x in range(13):
            i, m = x % 4, x // 4
            rows = [OWN_AT[m][i]] if m < 3 else []
            if i == 0 and m > 0:
                rows.append(OWN_AT[m - 1][4])
            flat = [plane_ref[pl.ds(r, 9, stride=16), :] for r in rows]
            add_plane(out_ref, f, x, sum(flat[1:], flat[0]))


def near_force_kernel(
    force_ref, near_half_ref, near_flux_ref, prev_ref, next_ref, count_ref, after_ref,
    out_ref,
    win_ref, fold_ref, near_force_ref, plane_ref, flux_ref, elem_ref, near_win_ref, near_plane_ref, spread_ref,
):
    out_ref[...] = force_ref[...]
    near_plane_ref[...] = jnp.zeros(near_plane_ref.shape, F32)
    for f in range(2):
        for i in range(5):
            flat = plane_of(prev_ref, 12 + PYZ * i, 40 * f) if i < 4 else plane_of(next_ref, 0, 16 * f)
            near_plane_ref[pl.ds(72 * f + i, 9, stride=8), :] = flat
        near_win_ref[:, 128 * f : 128 * f + 64, :] = near_half_ref[:, 64 * f : 64 * f + 64, :]
        make_windows(near_plane_ref, 72 * f, 8, near_win_ref, 128 * f + 64)
    place_flux(flux_ref, message_flux(prev_ref, count_ref, spread_ref), lambda i: [(0, 8 * NEAR_AT[0][i], 8)])
    scaled(flux_ref, lane_weight([NEAR_AT[0]]))
    flux_ref[...] = flux_ref[...] + near_flux_ref[...]
    for f in range(2):
        win_ref[...] = jnp.zeros(win_ref.shape, F32)
        for row in NEAR_AT:
            for w, i, v in along_x(near_win_ref, LANES * f, row, derive):
                win_ref[w, 8 * row[i] : 8 * row[i] + 8, :] = v
        turned(near_win_ref, LANES * f, elem_ref, 0)
        turned(win_ref, 0, elem_ref, 1)
        force_terms(elem_ref, 0, 1, flux_ref, fold_ref, win_ref, 0)
        summed_along_x(win_ref, NEAR_AT, near_force_ref, 0)
        to_planes(near_force_ref, 0, plane_ref)
        for x, r in [(0, NEAR_AT[0][4])] + [(12 + i, NEAR_AT[1][i]) for i in range(4)]:
            add_plane(out_ref, f, x, plane_ref[pl.ds(r, 9, stride=16), :])


def step_kernel(
    line_ref, fwd_ref, fwd_speed_ref, adj_ref, adj_speed_ref, mass_ref, after_ref,
    fwd_out_ref, fwd_speed_out_ref, adj_out_ref, adj_speed_out_ref,
):
    def step(lo, hi, force):
        shape = (hi - lo) // force[0].shape[1], force[0].shape[1]
        take = lambda ref: ref[0:1, lo:hi].reshape(shape)
        scale = TIME_STEP * mass_ref[lo:hi].reshape(shape)
        speed = take(fwd_speed_ref) + scale * force[0]
        fwd_speed_out_ref[0:1, lo:hi] = speed.reshape(1, hi - lo)
        fwd_out_ref[0:1, lo:hi] = (take(fwd_ref) - TIME_STEP * speed).reshape(1, hi - lo)
        speed = take(adj_speed_ref) - scale * force[1]
        adj_speed_out_ref[0:1, lo:hi] = speed.reshape(1, hi - lo)
        adj_out_ref[0:1, lo:hi] = (take(adj_ref) + TIME_STEP * speed).reshape(1, hi - lo)

    for r in range(0, 136, 8):
        step(r * LANES, (r + 8) * LANES, [line_ref[f, r : r + 8, :] for f in range(2)])
    step(NPTS - 16, NPTS, [line_ref[f, 136:137, 0:16] for f in range(2)])


def band_kernel(cut_ref, own_ref, first_ref, second_ref, band_ref, before_ref, out_ref):
    flat = jnp.concatenate([own_ref[...], first_ref[...], second_ref[...]], axis=0)
    k1 = flat.astype(BF16)
    rest = flat - k1.astype(F32)
    k2 = rest.astype(BF16)
    k3 = (rest - k2.astype(F32)).astype(BF16)
    stacked = jnp.concatenate([k1, k2, k3, k1, k2, k1], axis=0)
    band = band_ref[cut_ref[0] & 1]
    out_ref[...] = jnp.dot(band, stacked, preferred_element_type=F32)[:, :PYZ]


def on_device(
    forward_displacement,
    forward_velocity,
    adjoint_displacement,
    adjoint_velocity,
    inverse_mass,
    shear_modulus,
    connectivity,
    face_points,
    element_count,
):
    events = lax.axis_size("event")
    cuts = lax.axis_size("cuts")
    cut = lax.axis_index("cuts").astype(jnp.int32).reshape(1)
    pairs_first = [(i, (i - 1 if i % 2 == 0 else i + 1) % cuts) for i in range(cuts)]
    pairs_second = [(i, (i + 1 if i % 2 == 0 else i - 1) % cuts) for i in range(cuts)]

    vmem = pl.BlockSpec(memory_space=pltpu.VMEM)
    smem = pl.BlockSpec(memory_space=pltpu.SMEM)
    anywhere = pl.BlockSpec(memory_space=pl.ANY)

    def held(block):
        return pltpu.with_memory_space_constraint(block, pltpu.VMEM)

    def in_hbm(block):
        return pltpu.with_memory_space_constraint(block, pltpu.HBM)

    def cost(flops):
        return pl.CostEstimate(flops=flops, bytes_accessed=1000000, transcendentals=0)

    dma = pltpu.SemaphoreType.DMA
    point_row = pltpu.VMEM((1, NPTS), F32)
    flux_block = pltpu.VMEM((200, LANES), F32)
    kern_block = pltpu.VMEM((16, 9 * LANES), F32)
    line_block = pltpu.VMEM((256, LANES), F32)

    def elements(n):
        return pltpu.VMEM((n, 168, LANES), F32)

    def windows(n):
        return pltpu.VMEM((2, n * LANES, LANES), F32)

    fields = (in_hbm(forward_displacement), in_hbm(adjoint_displacement))
    cross = held(jnp.asarray(cross_table()))
    right, left, own, code, parts = pl.pallas_call(
        pack_kernel,
        out_shape=[
            pltpu.VMEM((144, LANES), F32),
            pltpu.VMEM((32, LANES), F32),
            pltpu.VMEM((2 * ROWS, LANES), F32),
            pltpu.VMEM((8, 256), jnp.int32),
            pltpu.VMEM((384, 256), BF16),
        ],
        in_specs=[anywhere] * 4,
        scratch_shapes=[
            pltpu.VMEM((8, 256), jnp.int32),
            pltpu.VMEM((125, 256), F32),
            point_row,
            point_row,
            pltpu.VMEM((128, 256), F32),
            dma((4,)),
        ],
        cost_estimate=cost(100000000),
        name="pack",
    )(in_hbm(connectivity), in_hbm(shear_modulus), *fields)
    to_next = [(i, (i + 1) % cuts) for i in range(cuts)]
    prev = lax.ppermute(right, "cuts", to_next)
    count, left = lax.optimization_barrier((element_count, left))
    count = jnp.broadcast_to(count.reshape(1, 1), (8, LANES))
    prev_count = lax.ppermute(count, "cuts", to_next)
    count, left = lax.optimization_barrier((count, left))

    own_blocks = [elements(4), flux_block, flux_block, windows(1), windows(1), flux_block, kern_block]

    def own_part(turn, before):
        given = (cut, held(count), held(own), held(code), held(parts), cross)
        return pl.pallas_call(
            functools.partial(own_kernel, turn),
            out_shape=own_blocks,
            in_specs=[smem] + [vmem] * (5 + len(before)),
            scratch_shapes=[
                pltpu.VMEM((2 * 9 * 24, LANES), F32),
                windows(4),
                line_block,
                elements(1),
                pltpu.VMEM((136, 256), F32),
            ],
            input_output_aliases={len(given) + n: n for n in range(len(before))},
            cost_estimate=cost(300000000),
            name="own_layers",
        )(*given, *[held(block) for block in before])

    left, *blocks = lax.optimization_barrier((left, *own_part(0, [])))
    after = lax.ppermute(left, "cuts", [((i + 1) % cuts, i) for i in range(cuts)])
    elem, flux, near_flux, near_win, near_slope, near_kern, kern = own_part(1, blocks)
    kern = pl.pallas_call(
        near_kernel,
        out_shape=kern_block,
        in_specs=[vmem] * 8,
        scratch_shapes=[
            pltpu.VMEM((72, LANES), F32),
            pltpu.VMEM((2, 64, LANES), F32),
            windows(1),
            elements(1),
            flux_block,
            line_block,
            pltpu.VMEM((136, LANES), F32),
        ],
        cost_estimate=cost(200000000),
        name="near_layers",
    )(held(prev), held(after), held(prev_count), held(near_flux), held(near_slope), held(near_kern), held(kern), cross)

    force = pl.pallas_call(
        force_kernel,
        out_shape=pltpu.VMEM((2, ROWS, LANES), F32),
        in_specs=[vmem] * 2,
        scratch_shapes=[windows(2), line_block, windows(1), pltpu.VMEM((144, LANES), F32)],
        cost_estimate=cost(200000000),
        name="forces",
    )(held(elem), held(flux))

    kern_first = lax.ppermute(kern, "cuts", pairs_first)
    kern_second = lax.ppermute(kern, "cuts", pairs_second)

    force = pl.pallas_call(
        near_force_kernel,
        out_shape=pltpu.VMEM((2, ROWS, LANES), F32),
        in_specs=[vmem] * 7,
        scratch_shapes=[
            windows(2),
            line_block,
            windows(1),
            pltpu.VMEM((144, LANES), F32),
            flux_block,
            elements(2),
            windows(2),
            pltpu.VMEM((2 * 72, LANES), F32),
            pltpu.VMEM((136, LANES), F32),
        ],
        cost_estimate=cost(200000000),
        name="near_forces",
    )(held(force), held(near_win), held(near_flux), held(prev), held(after), held(prev_count), held(kern))
    share = pl.pallas_call(
        band_kernel,
        out_shape=pltpu.VMEM((PXU, PYZ), F32),
        in_specs=[smem] + [vmem] * 5,
        cost_estimate=cost(20000000),
        name="band",
    )(cut, held(kern), held(kern_first), held(kern_second), held(jnp.asarray(band_table())), held(force))
    if events == 2:
        shear_kernel = share + lax.ppermute(share, "event", [(0, 1), (1, 0)])
    else:
        shear_kernel = lax.psum(share, "event")
    points = jax.ShapeDtypeStruct((1, NPTS), F32)
    outs = pl.pallas_call(
        step_kernel,
        out_shape=[points] * 4,
        in_specs=[vmem] * 7,
        cost_estimate=cost(200000000),
        name="step",
    )(
        held(force),
        held(forward_displacement),
        held(forward_velocity),
        held(adjoint_displacement),
        held(adjoint_velocity),
        held(inverse_mass),
        held(share),
    )
    return (*outs, shear_kernel)


def solution(mesh):
    in_specs = (
        P("event", "cuts"),
        P("event", "cuts"),
        P("event", "cuts"),
        P("event", "cuts"),
        P("cuts"),
        P(None, "cuts"),
        P(None, "cuts"),
        P("cuts", None),
        P("cuts"),
    )
    out_specs = (
        P("event", "cuts"),
        P("event", "cuts"),
        P("event", "cuts"),
        P("event", "cuts"),
        P("cuts", None),
    )
    return jax.shard_map(on_device, mesh=mesh, in_specs=in_specs, out_specs=out_specs, check_vma=False)
```

```python
import functools

import numpy as np
import jax
import jax.numpy as jnp
import ml_dtypes
from jax import lax
from jax.experimental import pallas as pl
from jax.experimental.pallas import tpu as pltpu
from jax.sharding import PartitionSpec as P

NGLL = 5
EX, EY, EZ = 4, 8, 8
PXU = 16
PY = 33
PZ = 33
PYZ = 1089
NPTS = 17424
LANES = 128
ROWS = 144
TIME_STEP = 0.02
OWN_OUTS, OWN_SCRATCH = 7, 5
F32 = jnp.float32
BF16 = jnp.bfloat16


def gll():
    nodes = np.array([-1.0, -np.sqrt(3.0 / 7.0), 0.0, np.sqrt(3.0 / 7.0), 1.0])
    bary = np.array([1.0 / np.prod([nodes[r] - nodes[c] for c in range(5) if c != r]) for r in range(5)])
    d = np.zeros((5, 5))
    for r in range(5):
        for c in range(5):
            if c != r:
                d[r, c] = bary[c] / bary[r] / (nodes[r] - nodes[c])
        d[r, r] = -np.sum(d[r])
    return d


DERIV = gll()


def split_np(x):
    x = np.asarray(x, np.float32)
    parts = []
    for _ in range(3):
        p = x.astype(ml_dtypes.bfloat16)
        parts.append(p)
        x = x - p.astype(np.float32)
    return parts


ROW_PLANE = np.array([4 * (r % 3) + r // 3 for r in range(12)] + [12, 13, 14, 15])
OWN_AT = [[3 * i + m for i in range(5)] for m in range(3)]
NEAR_AT = [[8, 9, 10, 11, 0], [4, 5, 6, 7, 12]]


def band_table():
    offsets = np.arange(-PXU, PXU + 1)
    w = lambda d: np.exp(-d * d / (2.0 * (PXU / 4.0) ** 2))
    total = w(offsets.astype(np.float64)).sum()
    out = []
    for first in (-PXU, PXU):
        source = np.concatenate([ROW_PLANE, ROW_PLANE + first, ROW_PLANE - first])
        spread = np.arange(PXU)[:, None] - source[None, :]
        band = w(spread.astype(np.float64)) * (np.abs(spread) <= PXU) / total
        b1, b2, b3 = split_np(band)
        out.append(np.concatenate([b1, b1, b1, b2, b2, b3], axis=1))
    return np.stack(out)


def cross_table():
    off = np.arange(-4, 5)
    k = np.exp(-off * off / (2.0 * 1.5 * 1.5))
    point = np.arange(33)
    inside = ((point[None, :] + off[:, None]) >= 0) & ((point[None, :] + off[:, None]) < 33)
    taps = k[:, None] * inside
    taps = taps / taps.sum(axis=0, keepdims=True)
    out = np.zeros((24, 1152), np.float32)
    out[0:9, :PYZ] = np.tile(taps, (1, PY))
    out[9:18, :PYZ] = np.repeat(taps, PZ, axis=1)
    return out


def split3(x):
    hi = x.astype(BF16)
    rest = x - hi.astype(F32)
    mid = rest.astype(BF16)
    low = (rest - mid.astype(F32)).astype(BF16)
    return hi, mid, low


def dot_nt(a, b):
    return lax.dot_general(a, b, (((1,), (1,)), ((), ())), preferred_element_type=F32)


def fetch(sem, *pairs):
    copies = [pltpu.make_async_copy(src, dst, sem.at[n]) for n, (src, dst) in enumerate(pairs)]
    for c in copies:
        c.start()
    return copies


def add_parts(stacked):
    n = stacked.shape[0] // 3
    return stacked[0:n] + (stacked[n : 2 * n] + stacked[2 * n : 3 * n])


def pack_kernel(
    conn_hbm, shear_hbm, fwd_hbm, adj_hbm,
    right_ref, left_ref, own_ref, code_ref, parts_ref,
    conn_ref, shear_ref, fwd_ref, adj_ref, block_ref, sem,
):
    copies = fetch(
        sem,
        (shear_hbm, shear_ref),
        (conn_hbm.at[0:8], conn_ref),
        (fwd_hbm, fwd_ref),
        (adj_hbm, adj_ref),
    )
    copies[1].wait()
    point = conn_ref[0:1, :].astype(F32)
    x = jnp.floor((point + 0.5) * (1.0 / PYZ))
    rest = point - x * PYZ
    y = jnp.floor((rest + 0.5) * (1.0 / PZ))
    z = rest - y * PZ
    code = (8.0 * z + 2.0 * x + 0.25 * y).astype(jnp.int32)
    slot = lax.broadcasted_iota(jnp.int32, (1, 256), 1)
    code_ref[...] = jnp.broadcast_to(code, (8, 256))
    lane = lax.broadcasted_iota(jnp.int32, (LANES, 256), 0)
    pick = jnp.where(code == ((lane >> 3) & 7) * 32 + 24 + (lane & 7), 1.0, 0.0).astype(BF16)
    for f, ref in enumerate((fwd_ref, adj_ref)):
        copies[2 + f].wait()
        for r in range(0, 136, 8):
            own_ref[ROWS * f + r : ROWS * f + r + 8, :] = ref[0:1, r * LANES : (r + 8) * LANES].reshape(8, LANES)
        own_ref[ROWS * f + 136 : ROWS * f + 144, :] = jnp.zeros((8, LANES), F32)
        own_ref[ROWS * f + 136 : ROWS * f + 137, 0:16] = ref[0:1, NPTS - 16 : NPTS]
        right_ref[40 * f : 40 * f + 40, :] = own_ref[ROWS * f + 102 : ROWS * f + 142, :]
        left_ref[16 * f : 16 * f + 16, :] = own_ref[ROWS * f : ROWS * f + 16, :]
    copies[0].wait()
    block_ref[0:125, :] = shear_ref[...]
    block_ref[125:126, :] = slot.astype(F32)
    block_ref[126:128, :] = jnp.zeros((2, 256), F32)
    parts = jnp.concatenate(split3(block_ref[...]), axis=0)
    parts_ref[...] = parts
    flux = add_parts(dot_nt(parts, pick))
    low = lax.broadcasted_iota(jnp.int32, (64, LANES), 1) < 64
    right_ref[80:144, :] = jnp.where(low, flux[0:64], flux[64:128])


def gll_weight(i):
    return (0.1, 49.0 / 90.0, 32.0 / 45.0, 49.0 / 90.0, 0.1)[i]


def lane_weight(places):
    chunk = lax.broadcasted_iota(jnp.int32, (8, LANES), 1) >> 3
    weight = jnp.zeros((8, LANES), F32)
    for row in places:
        for i, place in enumerate(row):
            weight = jnp.where(chunk == place, gll_weight(i), weight)
    return weight


def scaled(ref, weight):
    for j in range(5):
        for k in range(5):
            r = (j * 5 + k) * 8
            ref[r : r + 8, :] = ref[r : r + 8, :] * (weight * (gll_weight(j) * gll_weight(k)))


def place_flux(ref, tile_of, moves, layers=range(NGLL)):
    lane = lax.broadcasted_iota(jnp.int32, (32, LANES), 1)
    for ez in range(EZ):
        total = jnp.zeros((32, LANES), F32)
        for i in layers:
            tile, start = tile_of(i, ez)
            for source, target, width in moves(i):
                shift = (target - source - start) % LANES
                moved = pltpu.roll(tile, shift, 1) if shift else tile
                total = jnp.where((lane >= target) & (lane < target + width), moved, total)
        ref[pl.ds(ez, 25, stride=8), :] = total[0:25]


def derive(e):
    d = DERIV
    s0, s1 = e[0] + e[4], e[1] + e[3]
    d0, d1 = e[0] - e[4], e[1] - e[3]
    out = [None] * 5
    for i in (0, 1):
        even = float((d[i, 0] - d[i, 4]) / 2) * d0 + float((d[i, 1] - d[i, 3]) / 2) * d1
        odd = float((d[i, 0] + d[i, 4]) / 2) * s0 + float((d[i, 1] + d[i, 3]) / 2) * s1 + float(d[i, 2]) * e[2]
        out[i] = odd + even
        out[4 - i] = even - odd
    out[2] = float(d[2, 0]) * d0 + float(d[2, 1]) * d1
    return out


def derive_back(t):
    d = DERIV
    s0, s1 = t[0] + t[4], t[1] + t[3]
    d0, d1 = t[0] - t[4], t[1] - t[3]
    out = [None] * 5
    for i in (0, 1):
        even = float((d[0, i] - d[4, i]) / 2) * d0 + float((d[1, i] - d[3, i]) / 2) * d1
        odd = float((d[0, i] + d[4, i]) / 2) * s0 + float((d[1, i] + d[3, i]) / 2) * s1 + float(d[2, i]) * t[2]
        out[i] = odd + even
        out[4 - i] = even - odd
    out[2] = float(d[0, 2]) * d0 + float(d[1, 2]) * d1
    return out


def shifted(tiles, distance, lane):
    skip, part = divmod(distance, LANES)
    if part == 0:
        moved = tiles
        pick = None
    else:
        moved = [pltpu.roll(t, LANES - part, 1) for t in tiles]
        pick = lane < LANES - part
    n = len(tiles)
    out = []
    for i in range(n):
        a = moved[(i + skip) % n]
        b = moved[(i + skip + 1) % n]
        out.append(a if pick is None else jnp.where(pick, a, b))
    return out


def plane_of(ref, start, row):
    r0, off = divmod(start, LANES)
    lane9 = lax.broadcasted_iota(jnp.int32, (9, LANES), 1)
    flat = ref[row + r0 : row + r0 + 9, :]
    if off:
        flat = jnp.where(
            lane9 < LANES - off,
            pltpu.roll(flat, LANES - off, 1),
            pltpu.roll(ref[row + r0 + 1 : row + r0 + 10, :], LANES - off, 1),
        )
    return flat


def store_plane(ref, row, flat):
    ref[pl.ds(row, 9, stride=16), :] = flat


def make_windows(plane_ref, base, pitch, win_ref, row):
    lane = lax.broadcasted_iota(jnp.int32, (8, LANES), 1)
    tiles = [plane_ref[base + t * pitch : base + t * pitch + 8, :] for t in range(9)]
    for ey in range(EY):
        near = [tiles[ey], tiles[ey + 1], tiles[min(ey + 2, 8)]]
        if ey:
            near = [pltpu.roll(t, LANES - 4 * ey, 1) for t in near]
            keep = lane < LANES - 4 * ey
            near = [jnp.where(keep, near[0], near[1]), jnp.where(keep, near[1], near[2])]
        for w in range(2):
            win_ref[w, pl.ds(row + ey, 8, stride=8), :] = near[w]


def along_x(win_ref, base, row, combine):
    for w in range(2):
        values = combine([win_ref[w, base + 8 * c : base + 8 * c + 8, :] for c in row])
        for i, v in enumerate(values):
            yield w, i, v


def turned(win_ref, base, elem_ref, column):
    elem_ref[column, 0:LANES, :] = win_ref[0, base : base + LANES, :].T
    elem_ref[column, LANES:168, :] = win_ref[1, base : base + LANES, :].T[0:40, :]


def part(ref, column, j, k):
    return ref[column, pl.ds(j * PZ + k, 8, stride=4), :]


def flux_part(ref, j, k):
    r = (j * 5 + k) * 8
    return ref[r : r + 8, :]


def folded(term, line_ref, win_ref, base):
    row = lax.broadcasted_iota(jnp.int32, (8, LANES), 0)
    line_ref[160:256, :] = jnp.zeros((96, LANES), F32)
    for j in range(5):
        for k in range(1, 4):
            line_ref[pl.ds(j * PZ + k, 8, stride=4), :] = term[j][k]
        last = term[j][4]
        line_ref[pl.ds(j * PZ, 8, stride=4), :] = term[j][0] + jnp.where(row == 0, 0.0, pltpu.roll(last, 1, 0))
        line_ref[j * PZ + 32 : j * PZ + 33, :] = last[7:8, :]
    for w in range(2):
        win_ref[w, base : base + LANES, :] = line_ref[w * LANES : (w + 1) * LANES, :].T


def force_terms(elem_ref, value, slope, flux_ref, line_ref, win_ref, row):
    term = [[None] * 5 for _ in range(5)]
    for k in range(5):
        grads = derive([part(elem_ref, value, j, k) for j in range(5)])
        for j, v in enumerate(derive_back([g * flux_part(flux_ref, j, k) for j, g in enumerate(grads)])):
            term[j][k] = v
    for j in range(5):
        grads = derive([part(elem_ref, value, j, k) for k in range(5)])
        for k, v in enumerate(derive_back([g * flux_part(flux_ref, j, k) for k, g in enumerate(grads)])):
            term[j][k] = term[j][k] + v
    folded(term, line_ref, win_ref, row)
    term = [[part(elem_ref, slope, j, k) * flux_part(flux_ref, j, k) for k in range(5)] for j in range(5)]
    folded(term, line_ref, win_ref, row + LANES)


def cross_smoothed(tiles, cross_ref):
    lane = lax.broadcasted_iota(jnp.int32, tiles[0].shape, 1)
    for base, step in ((0, 1), (9, PZ)):
        total = None
        for tap in range(9):
            moved = shifted(tiles, step * (tap - 4), lane) if tap != 4 else tiles
            terms = [v * cross_ref[base + tap : base + tap + 1, t * LANES : (t + 1) * LANES] for t, v in enumerate(moved)]
            total = terms if total is None else [a + b for a, b in zip(total, terms)]
        tiles = total
    return tiles


def own_kernel(turn, cut_ref, count_ref, own_ref, code_ref, parts_ref, cross_ref, *refs):
    refs = refs[-OWN_OUTS - OWN_SCRATCH :]
    mine = (cut_ref[0] == 0) if turn == 0 else (cut_ref[0] != 0)

    @pl.when(mine)
    def _():
        own_layers(count_ref, own_ref, code_ref, parts_ref, cross_ref, *refs)


def own_layers(
    count_ref, own_ref, code_ref, parts_ref, cross_ref,
    elem_ref, flux_ref, near_flux_ref, near_win_ref, near_slope_ref, near_kern_ref, kern_ref,
    plane_ref, win_ref, line_ref, near_elem_ref, moved_ref,
):
    plane_ref[...] = jnp.zeros(plane_ref.shape, F32)
    for f in range(2):
        base = 24 * 9 * f
        for x in range(PXU):
            flat = plane_of(own_ref, PYZ * x, ROWS * f)
            rows = [OWN_AT[x // 4][x % 4]] if x < 12 else [16 + NEAR_AT[1][x - 12]]
            if x % 4 == 0:
                rows.append(OWN_AT[x // 4 - 1][4] if x else 16 + NEAR_AT[0][4])
            for r in rows:
                plane_ref[pl.ds(base + r, 9, stride=24), :] = flat
        for h in range(2):
            make_windows(plane_ref, base + 8 * h, 24, win_ref, 128 * f + 64 * h)
        make_windows(plane_ref, base + 16, 24, near_win_ref, 64 * f)
        win_ref[:, 256 + 128 * f : 384 + 128 * f, :] = jnp.zeros((2, LANES, LANES), F32)
        for row in OWN_AT:
            for w, i, v in along_x(win_ref, 128 * f, row, derive):
                r = 256 + 128 * f + 8 * row[i]
                win_ref[w, r : r + 8, :] = v
    for column in range(4):
        turned(win_ref, 128 * column, elem_ref, column)
    turned(near_win_ref, 0, near_elem_ref, 0)
    near_slope_ref[...] = jnp.zeros(near_slope_ref.shape, F32)
    for f in range(2):
        for w in range(2):
            value = [near_win_ref[w, 64 * f + 8 * c : 64 * f + 8 * c + 8, :] for c in (0, 4, 5, 6, 7)]
            near_slope_ref[w, 64 * f : 64 * f + 8, :] = float(DERIV[4, 4]) * value[0]
            for i, v in enumerate(derive(value[1:] + [jnp.zeros((8, LANES), F32)])[:4]):
                r = 64 * f + 8 * NEAR_AT[1][i]
                near_slope_ref[w, r : r + 8, :] = v

    element = lax.broadcasted_iota(jnp.int32, (256, 256), 0)
    slot = lax.broadcasted_iota(jnp.int32, (1, 256), 1)
    live = jnp.concatenate([count_ref[0:1, :], count_ref[0:1, :]], axis=1)
    code = jnp.where(slot < live, code_ref[0:1, :], -1)
    pick = jnp.where(code == element, 1.0, 0.0).astype(BF16)
    moved_ref[0:128, :] = add_parts(dot_nt(parts_ref[...], pick))
    moved_ref[128:136, :] = jnp.zeros((8, 256), F32)

    def tile_of(i, ez):
        t = ez // 4
        return moved_ref[25 * i : 25 * i + 32, t * LANES : (t + 1) * LANES], 32 * (ez % 4)

    place_flux(flux_ref, tile_of, lambda i: [(0, 24 * i, 24)])
    place_flux(near_flux_ref, tile_of, lambda i: [(24, 8 * NEAR_AT[1][i], 8)])
    scaled(flux_ref, lane_weight(OWN_AT))
    scaled(near_flux_ref, lane_weight(NEAR_AT))

    kern = [[None] * 5 for _ in range(5)]
    near = [[None] * 5 for _ in range(5)]
    for k in range(5):
        fwd, adj, both = [derive([part(ref, c, j, k) for j in range(5)]) for ref, c in ((elem_ref, 0), (elem_ref, 1), (near_elem_ref, 0))]
        for j in range(5):
            kern[j][k] = fwd[j] * adj[j] + part(elem_ref, 2, j, k) * part(elem_ref, 3, j, k)
            near[j][k] = both[j] * pltpu.roll(both[j], 64, 1)
    for j in range(5):
        fwd, adj, both = [derive([part(ref, c, j, k) for k in range(5)]) for ref, c in ((elem_ref, 0), (elem_ref, 1), (near_elem_ref, 0))]
        for k in range(5):
            kern[j][k] = -(kern[j][k] + fwd[k] * adj[k]) * flux_part(flux_ref, j, k)
            r = (j * 5 + k) * 8
            near_kern_ref[r : r + 8, :] = near[j][k] + both[k] * pltpu.roll(both[k], 64, 1)
    folded(kern, line_ref, win_ref, 0)
    low, high = [gathered(win_ref, 0, h) for h in range(2)]
    row = lax.broadcasted_iota(jnp.int32, (8, LANES), 0)
    tiles = []
    for t in range(9):
        first = low[t] + jnp.where((row == 1) | (row == 2), pltpu.roll(high[t], 5, 0), 0.0)
        second = jnp.where(row < 4, high[t], jnp.where(row == 4, pltpu.roll(high[t], 6, 0), 0.0))
        tiles.append(jnp.concatenate([first, second], axis=0))
    for t, tile in enumerate(cross_smoothed(tiles, cross_ref)):
        kern_ref[:, t * LANES : (t + 1) * LANES] = tile


def message_flux(prev_ref, count_ref, spread_ref):
    upper = pltpu.roll(prev_ref[80:144, :], 64, 1)
    live = upper[61:62, :] < count_ref[0:1, :].astype(F32)
    spread_ref[0:64, :] = jnp.where(live, prev_ref[80:144, :], 0.0)
    spread_ref[64:128, :] = jnp.where(live, upper, 0.0)
    spread_ref[128:136, :] = jnp.zeros((8, LANES), F32)
    return lambda i, ez: (spread_ref[25 * i : 25 * i + 32, :], 8 * ez)


def near_kernel(
    prev_ref, next_ref, count_ref, flux_in_ref, slope_ref, near_kern_ref, kern_in_ref, cross_ref,
    kern_ref,
    plane_ref, new_ref, win_ref, elem_ref, flux_ref, line_ref, spread_ref,
):
    plane_ref[...] = jnp.zeros(plane_ref.shape, F32)
    for f in range(2):
        share = None
        for l in range(4):
            term = float(DERIV[4, l]) * plane_of(prev_ref, 12 + PYZ * l, 40 * f)
            share = term if share is None else share + term
        plane_ref[pl.ds(f, 9, stride=8), :] = share
        plane_ref[pl.ds(2 + f, 9, stride=8), :] = plane_of(next_ref, 0, 16 * f)
    make_windows(plane_ref, 0, 8, new_ref, 0)
    win_ref[...] = slope_ref[...]
    for f in range(2):
        for w in range(2):
            r = 64 * f
            win_ref[w, r : r + 8, :] = win_ref[w, r : r + 8, :] + new_ref[w, 8 * f : 8 * f + 8, :]
            for i in range(4):
                r = 64 * f + 8 * NEAR_AT[1][i]
                new = float(DERIV[i, 4]) * new_ref[w, 16 + 8 * f : 24 + 8 * f, :]
                win_ref[w, r : r + 8, :] = win_ref[w, r : r + 8, :] + new
    turned(win_ref, 0, elem_ref, 0)
    place_flux(flux_ref, message_flux(prev_ref, count_ref, spread_ref), lambda i: [(0, 8 * NEAR_AT[0][i], 8)], (4,))
    scaled(flux_ref, lane_weight([NEAR_AT[0]]))
    kern = [[None] * 5 for _ in range(5)]
    for j in range(5):
        for k in range(5):
            slope = part(elem_ref, 0, j, k)
            total = flux_part(near_kern_ref, j, k) + slope * pltpu.roll(slope, 64, 1)
            kern[j][k] = -total * (flux_part(flux_ref, j, k) + flux_part(flux_in_ref, j, k))
    folded(kern, line_ref, win_ref, 0)
    row = lax.broadcasted_iota(jnp.int32, (8, LANES), 0)
    tiles = [jnp.where((row == 0) | (row >= 4), v, 0.0) for v in gathered(win_ref, 0, 0)]
    for t, tile in enumerate(cross_smoothed(tiles, cross_ref)):
        columns = slice(t * LANES, (t + 1) * LANES)
        kern_ref[0:8, columns] = kern_in_ref[0:8, columns] + jnp.where(row == 0, tile, 0.0)
        kern_ref[8:16, columns] = kern_in_ref[8:16, columns] + jnp.where(row >= 4, tile, 0.0)


def gathered(win_ref, base, h):
    lane = lax.broadcasted_iota(jnp.int32, (8, LANES), 1)
    tiles = [None] * 9
    for ey in range(EY):
        rows = pl.ds(base + h * 64 + ey, 8, stride=8)
        a, b = win_ref[0, rows, :], win_ref[1, rows, :]
        if ey:
            a, b = pltpu.roll(a, 4 * ey, 1), pltpu.roll(b, 4 * ey, 1)
            keep = lane >= 4 * ey
            a, b = jnp.where(keep, a, 0.0), jnp.where(keep, b, a)
        tiles[ey] = a if ey == 0 else tiles[ey] + a
        tiles[ey + 1] = b
    return tiles


def summed_along_x(win_ref, places, out_ref, row):
    for line in places:
        for w, i, v in along_x(win_ref, LANES, line, derive_back):
            r = 8 * line[i]
            out_ref[w, row + r : row + r + 8, :] = win_ref[w, r : r + 8, :] + v


def to_planes(win_ref, base, plane_ref):
    for h in range(2):
        for t, tile in enumerate(gathered(win_ref, base, h)):
            plane_ref[t * 16 + 8 * h : t * 16 + 8 * h + 8, :] = tile


def add_plane(line_ref, f, x, flat):
    lane9 = lax.broadcasted_iota(jnp.int32, (9, LANES), 1)
    r0, off = divmod(PYZ * x, LANES)
    if off:
        flat = pltpu.roll(flat, off, 1)
        spill = jnp.where(lane9 < off, flat, 0.0)
        flat = jnp.where(lane9 < off, 0.0, flat)
    line_ref[f, r0 : r0 + 9, :] = line_ref[f, r0 : r0 + 9, :] + flat
    if off:
        line_ref[f, r0 + 1 : r0 + 10, :] = line_ref[f, r0 + 1 : r0 + 10, :] + spill


def force_kernel(elem_ref, flux_ref, out_ref, win_ref, fold_ref, force_ref, plane_ref):
    out_ref[...] = jnp.zeros(out_ref.shape, F32)
    for f in range(2):
        force_terms(elem_ref, f, 2 + f, flux_ref, fold_ref, win_ref, 0)
        summed_along_x(win_ref, OWN_AT, force_ref, 0)
        to_planes(force_ref, 0, plane_ref)
        for x in range(13):
            i, m = x % 4, x // 4
            rows = [OWN_AT[m][i]] if m < 3 else []
            if i == 0 and m > 0:
                rows.append(OWN_AT[m - 1][4])
            flat = [plane_ref[pl.ds(r, 9, stride=16), :] for r in rows]
            add_plane(out_ref, f, x, sum(flat[1:], flat[0]))


def near_force_kernel(
    force_ref, near_half_ref, near_flux_ref, prev_ref, next_ref, count_ref, after_ref,
    out_ref,
    win_ref, fold_ref, near_force_ref, plane_ref, flux_ref, elem_ref, near_win_ref, near_plane_ref, spread_ref,
):
    out_ref[...] = force_ref[...]
    near_plane_ref[...] = jnp.zeros(near_plane_ref.shape, F32)
    for f in range(2):
        for i in range(5):
            flat = plane_of(prev_ref, 12 + PYZ * i, 40 * f) if i < 4 else plane_of(next_ref, 0, 16 * f)
            near_plane_ref[pl.ds(72 * f + i, 9, stride=8), :] = flat
        near_win_ref[:, 128 * f : 128 * f + 64, :] = near_half_ref[:, 64 * f : 64 * f + 64, :]
        make_windows(near_plane_ref, 72 * f, 8, near_win_ref, 128 * f + 64)
    place_flux(flux_ref, message_flux(prev_ref, count_ref, spread_ref), lambda i: [(0, 8 * NEAR_AT[0][i], 8)])
    scaled(flux_ref, lane_weight([NEAR_AT[0]]))
    flux_ref[...] = flux_ref[...] + near_flux_ref[...]
    for f in range(2):
        win_ref[...] = jnp.zeros(win_ref.shape, F32)
        for row in NEAR_AT:
            for w, i, v in along_x(near_win_ref, LANES * f, row, derive):
                win_ref[w, 8 * row[i] : 8 * row[i] + 8, :] = v
        turned(near_win_ref, LANES * f, elem_ref, 0)
        turned(win_ref, 0, elem_ref, 1)
        force_terms(elem_ref, 0, 1, flux_ref, fold_ref, win_ref, 0)
        summed_along_x(win_ref, NEAR_AT, near_force_ref, 0)
        to_planes(near_force_ref, 0, plane_ref)
        for x, r in [(0, NEAR_AT[0][4])] + [(12 + i, NEAR_AT[1][i]) for i in range(4)]:
            add_plane(out_ref, f, x, plane_ref[pl.ds(r, 9, stride=16), :])


def step_kernel(
    line_ref, fwd_ref, fwd_speed_ref, adj_ref, adj_speed_ref, mass_ref,
    fwd_out_ref, fwd_speed_out_ref, adj_out_ref, adj_speed_out_ref,
):
    def step(lo, hi, force):
        shape = (hi - lo) // force[0].shape[1], force[0].shape[1]
        take = lambda ref: ref[0:1, lo:hi].reshape(shape)
        scale = TIME_STEP * mass_ref[lo:hi].reshape(shape)
        speed = take(fwd_speed_ref) + scale * force[0]
        fwd_speed_out_ref[0:1, lo:hi] = speed.reshape(1, hi - lo)
        fwd_out_ref[0:1, lo:hi] = (take(fwd_ref) - TIME_STEP * speed).reshape(1, hi - lo)
        speed = take(adj_speed_ref) - scale * force[1]
        adj_speed_out_ref[0:1, lo:hi] = speed.reshape(1, hi - lo)
        adj_out_ref[0:1, lo:hi] = (take(adj_ref) + TIME_STEP * speed).reshape(1, hi - lo)

    for r in range(0, 136, 8):
        step(r * LANES, (r + 8) * LANES, [line_ref[f, r : r + 8, :] for f in range(2)])
    step(NPTS - 16, NPTS, [line_ref[f, 136:137, 0:16] for f in range(2)])


def band_kernel(cut_ref, own_ref, first_ref, second_ref, band_ref, out_ref):
    flat = jnp.concatenate([own_ref[...], first_ref[...], second_ref[...]], axis=0)
    k1 = flat.astype(BF16)
    rest = flat - k1.astype(F32)
    k2 = rest.astype(BF16)
    k3 = (rest - k2.astype(F32)).astype(BF16)
    stacked = jnp.concatenate([k1, k2, k3, k1, k2, k1], axis=0)
    band = band_ref[cut_ref[0] & 1]
    out_ref[...] = jnp.dot(band, stacked, preferred_element_type=F32)[:, :PYZ]


def on_device(
    forward_displacement,
    forward_velocity,
    adjoint_displacement,
    adjoint_velocity,
    inverse_mass,
    shear_modulus,
    connectivity,
    face_points,
    element_count,
):
    events = lax.axis_size("event")
    cuts = lax.axis_size("cuts")
    cut = lax.axis_index("cuts").astype(jnp.int32).reshape(1)
    pairs_first = [(i, (i - 1 if i % 2 == 0 else i + 1) % cuts) for i in range(cuts)]
    pairs_second = [(i, (i + 1 if i % 2 == 0 else i - 1) % cuts) for i in range(cuts)]

    vmem = pl.BlockSpec(memory_space=pltpu.VMEM)
    smem = pl.BlockSpec(memory_space=pltpu.SMEM)
    anywhere = pl.BlockSpec(memory_space=pl.ANY)

    def held(block):
        return pltpu.with_memory_space_constraint(block, pltpu.VMEM)

    def in_hbm(block):
        return pltpu.with_memory_space_constraint(block, pltpu.HBM)

    def cost(flops):
        return pl.CostEstimate(flops=flops, bytes_accessed=1000000, transcendentals=0)

    dma = pltpu.SemaphoreType.DMA
    point_row = pltpu.VMEM((1, NPTS), F32)
    flux_block = pltpu.VMEM((200, LANES), F32)
    kern_block = pltpu.VMEM((16, 9 * LANES), F32)
    line_block = pltpu.VMEM((256, LANES), F32)

    def elements(n):
        return pltpu.VMEM((n, 168, LANES), F32)

    def windows(n):
        return pltpu.VMEM((2, n * LANES, LANES), F32)

    fields = (in_hbm(forward_displacement), in_hbm(adjoint_displacement))
    cross = held(jnp.asarray(cross_table()))
    right, left, own, code, parts = pl.pallas_call(
        pack_kernel,
        out_shape=[
            pltpu.VMEM((144, LANES), F32),
            pltpu.VMEM((32, LANES), F32),
            pltpu.VMEM((2 * ROWS, LANES), F32),
            pltpu.VMEM((8, 256), jnp.int32),
            pltpu.VMEM((384, 256), BF16),
        ],
        in_specs=[anywhere] * 4,
        scratch_shapes=[
            pltpu.VMEM((8, 256), jnp.int32),
            pltpu.VMEM((125, 256), F32),
            point_row,
            point_row,
            pltpu.VMEM((128, 256), F32),
            dma((4,)),
        ],
        cost_estimate=cost(100000000),
        name="pack",
    )(in_hbm(connectivity), in_hbm(shear_modulus), *fields)
    to_next = [(i, (i + 1) % cuts) for i in range(cuts)]
    prev = lax.ppermute(right, "cuts", to_next)
    count, left = lax.optimization_barrier((element_count, left))
    count = jnp.broadcast_to(count.reshape(1, 1), (8, LANES))
    prev_count = lax.ppermute(count, "cuts", to_next)
    count, left = lax.optimization_barrier((count, left))

    own_blocks = [elements(4), flux_block, flux_block, windows(1), windows(1), flux_block, kern_block]

    def own_part(turn, before):
        given = (cut, held(count), held(own), held(code), held(parts), cross)
        return pl.pallas_call(
            functools.partial(own_kernel, turn),
            out_shape=own_blocks,
            in_specs=[smem] + [vmem] * (5 + len(before)),
            scratch_shapes=[
                pltpu.VMEM((2 * 9 * 24, LANES), F32),
                windows(4),
                line_block,
                elements(1),
                pltpu.VMEM((136, 256), F32),
            ],
            input_output_aliases={len(given) + n: n for n in range(len(before))},
            cost_estimate=cost(300000000),
            name="own_layers",
        )(*given, *[held(block) for block in before])

    left, *blocks = lax.optimization_barrier((left, *own_part(0, [])))
    after = lax.ppermute(left, "cuts", [((i + 1) % cuts, i) for i in range(cuts)])
    elem, flux, near_flux, near_win, near_slope, near_kern, kern = own_part(1, blocks)
    kern = pl.pallas_call(
        near_kernel,
        out_shape=kern_block,
        in_specs=[vmem] * 8,
        scratch_shapes=[
            pltpu.VMEM((72, LANES), F32),
            pltpu.VMEM((2, 64, LANES), F32),
            windows(1),
            elements(1),
            flux_block,
            line_block,
            pltpu.VMEM((136, LANES), F32),
        ],
        cost_estimate=cost(200000000),
        name="near_layers",
    )(held(prev), held(after), held(prev_count), held(near_flux), held(near_slope), held(near_kern), held(kern), cross)

    force = pl.pallas_call(
        force_kernel,
        out_shape=pltpu.VMEM((2, ROWS, LANES), F32),
        in_specs=[vmem] * 2,
        scratch_shapes=[windows(2), line_block, windows(1), pltpu.VMEM((144, LANES), F32)],
        cost_estimate=cost(200000000),
        name="forces",
    )(held(elem), held(flux))

    if events == 2:
        other = lax.ppermute(kern, "event", [(0, 1), (1, 0)])
        other, force = lax.optimization_barrier((other, force))
        kern = kern + other
    elif events > 2:
        kern = lax.psum(kern, "event")
    kern_first = lax.ppermute(kern, "cuts", pairs_first)
    kern_second = lax.ppermute(kern, "cuts", pairs_second)

    force = pl.pallas_call(
        near_force_kernel,
        out_shape=pltpu.VMEM((2, ROWS, LANES), F32),
        in_specs=[vmem] * 7,
        scratch_shapes=[
            windows(2),
            line_block,
            windows(1),
            pltpu.VMEM((144, LANES), F32),
            flux_block,
            elements(2),
            windows(2),
            pltpu.VMEM((2 * 72, LANES), F32),
            pltpu.VMEM((136, LANES), F32),
        ],
        cost_estimate=cost(200000000),
        name="near_forces",
    )(held(force), held(near_win), held(near_flux), held(prev), held(after), held(prev_count), held(kern))
    points = jax.ShapeDtypeStruct((1, NPTS), F32)
    outs = pl.pallas_call(
        step_kernel,
        out_shape=[points] * 4,
        in_specs=[vmem] * 6,
        cost_estimate=cost(200000000),
        name="step",
    )(
        held(force),
        held(forward_displacement),
        held(forward_velocity),
        held(adjoint_displacement),
        held(adjoint_velocity),
        held(inverse_mass),
    )
    shear_kernel = pl.pallas_call(
        band_kernel,
        out_shape=jax.ShapeDtypeStruct((PXU, PYZ), F32),
        in_specs=[smem] + [vmem] * 4,
        cost_estimate=cost(20000000),
        name="band",
    )(cut, held(kern), held(kern_first), held(kern_second), held(jnp.asarray(band_table())))
    return (*outs, shear_kernel)


def solution(mesh):
    in_specs = (
        P("event", "cuts"),
        P("event", "cuts"),
        P("event", "cuts"),
        P("event", "cuts"),
        P("cuts"),
        P(None, "cuts"),
        P(None, "cuts"),
        P("cuts", None),
        P("cuts"),
    )
    out_specs = (
        P("event", "cuts"),
        P("event", "cuts"),
        P("event", "cuts"),
        P("event", "cuts"),
        P("cuts", None),
    )
    return jax.shard_map(on_device, mesh=mesh, in_specs=in_specs, out_specs=out_specs, check_vma=False)
```

```python
import functools

import numpy as np
import jax
import jax.numpy as jnp
import ml_dtypes
from jax import lax
from jax.experimental import pallas as pl
from jax.experimental.pallas import tpu as pltpu
from jax.sharding import PartitionSpec as P

NGLL = 5
EX, EY, EZ = 4, 8, 8
PXU = 16
PY = 33
PZ = 33
PYZ = 1089
NPTS = 17424
LANES = 128
ROWS = 144
TIME_STEP = 0.02
OWN_OUTS, OWN_SCRATCH = 7, 5
F32 = jnp.float32
BF16 = jnp.bfloat16


def gll():
    nodes = np.array([-1.0, -np.sqrt(3.0 / 7.0), 0.0, np.sqrt(3.0 / 7.0), 1.0])
    bary = np.array([1.0 / np.prod([nodes[r] - nodes[c] for c in range(5) if c != r]) for r in range(5)])
    d = np.zeros((5, 5))
    for r in range(5):
        for c in range(5):
            if c != r:
                d[r, c] = bary[c] / bary[r] / (nodes[r] - nodes[c])
        d[r, r] = -np.sum(d[r])
    return d


DERIV = gll()


def split_np(x):
    x = np.asarray(x, np.float32)
    parts = []
    for _ in range(3):
        p = x.astype(ml_dtypes.bfloat16)
        parts.append(p)
        x = x - p.astype(np.float32)
    return parts


ROW_PLANE = np.array([4 * (r % 3) + r // 3 for r in range(12)] + [12, 13, 14, 15])
OWN_AT = [[3 * i + m for i in range(5)] for m in range(3)]
NEAR_AT = [[8, 9, 10, 11, 0], [4, 5, 6, 7, 12]]


def band_table():
    offsets = np.arange(-PXU, PXU + 1)
    w = lambda d: np.exp(-d * d / (2.0 * (PXU / 4.0) ** 2))
    total = w(offsets.astype(np.float64)).sum()
    out = []
    for first in (-PXU, PXU):
        source = np.concatenate([ROW_PLANE, ROW_PLANE + first, ROW_PLANE - first])
        spread = np.arange(PXU)[:, None] - source[None, :]
        band = w(spread.astype(np.float64)) * (np.abs(spread) <= PXU) / total
        b1, b2, b3 = split_np(band)
        out.append(np.concatenate([b1, b1, b1, b2, b2, b3], axis=1))
    return np.stack(out)


def cross_table():
    off = np.arange(-4, 5)
    k = np.exp(-off * off / (2.0 * 1.5 * 1.5))
    point = np.arange(33)
    inside = ((point[None, :] + off[:, None]) >= 0) & ((point[None, :] + off[:, None]) < 33)
    taps = k[:, None] * inside
    taps = taps / taps.sum(axis=0, keepdims=True)
    out = np.zeros((24, 1152), np.float32)
    out[0:9, :PYZ] = np.tile(taps, (1, PY))
    out[9:18, :PYZ] = np.repeat(taps, PZ, axis=1)
    return out


def split3(x):
    hi = x.astype(BF16)
    rest = x - hi.astype(F32)
    mid = rest.astype(BF16)
    low = (rest - mid.astype(F32)).astype(BF16)
    return hi, mid, low


def dot_nt(a, b):
    return lax.dot_general(a, b, (((1,), (1,)), ((), ())), preferred_element_type=F32)


def fetch(sem, *pairs):
    copies = [pltpu.make_async_copy(src, dst, sem.at[n]) for n, (src, dst) in enumerate(pairs)]
    for c in copies:
        c.start()
    return copies


def add_parts(stacked):
    n = stacked.shape[0] // 3
    return stacked[0:n] + (stacked[n : 2 * n] + stacked[2 * n : 3 * n])


def pack_kernel(
    conn_hbm, shear_hbm, fwd_hbm, adj_hbm,
    right_ref, left_ref, own_ref, code_ref, parts_ref,
    conn_ref, shear_ref, fwd_ref, adj_ref, block_ref, sem,
):
    copies = fetch(
        sem,
        (shear_hbm, shear_ref),
        (conn_hbm.at[0:8], conn_ref),
        (fwd_hbm, fwd_ref),
        (adj_hbm, adj_ref),
    )
    copies[1].wait()
    point = conn_ref[0:1, :].astype(F32)
    x = jnp.floor((point + 0.5) * (1.0 / PYZ))
    rest = point - x * PYZ
    y = jnp.floor((rest + 0.5) * (1.0 / PZ))
    z = rest - y * PZ
    code = (8.0 * z + 2.0 * x + 0.25 * y).astype(jnp.int32)
    slot = lax.broadcasted_iota(jnp.int32, (1, 256), 1)
    code_ref[...] = jnp.broadcast_to(code, (8, 256))
    lane = lax.broadcasted_iota(jnp.int32, (LANES, 256), 0)
    pick = jnp.where(code == ((lane >> 3) & 7) * 32 + 24 + (lane & 7), 1.0, 0.0).astype(BF16)
    for f, ref in enumerate((fwd_ref, adj_ref)):
        copies[2 + f].wait()
        for r in range(0, 136, 8):
            own_ref[ROWS * f + r : ROWS * f + r + 8, :] = ref[0:1, r * LANES : (r + 8) * LANES].reshape(8, LANES)
        own_ref[ROWS * f + 136 : ROWS * f + 144, :] = jnp.zeros((8, LANES), F32)
        own_ref[ROWS * f + 136 : ROWS * f + 137, 0:16] = ref[0:1, NPTS - 16 : NPTS]
        right_ref[40 * f : 40 * f + 40, :] = own_ref[ROWS * f + 102 : ROWS * f + 142, :]
        left_ref[16 * f : 16 * f + 16, :] = own_ref[ROWS * f : ROWS * f + 16, :]
    copies[0].wait()
    block_ref[0:125, :] = shear_ref[...]
    block_ref[125:126, :] = slot.astype(F32)
    block_ref[126:128, :] = jnp.zeros((2, 256), F32)
    parts = jnp.concatenate(split3(block_ref[...]), axis=0)
    parts_ref[...] = parts
    flux = add_parts(dot_nt(parts, pick))
    low = lax.broadcasted_iota(jnp.int32, (64, LANES), 1) < 64
    right_ref[80:144, :] = jnp.where(low, flux[0:64], flux[64:128])


def gll_weight(i):
    return (0.1, 49.0 / 90.0, 32.0 / 45.0, 49.0 / 90.0, 0.1)[i]


def lane_weight(places):
    chunk = lax.broadcasted_iota(jnp.int32, (8, LANES), 1) >> 3
    weight = jnp.zeros((8, LANES), F32)
    for row in places:
        for i, place in enumerate(row):
            weight = jnp.where(chunk == place, gll_weight(i), weight)
    return weight


def scaled(ref, weight):
    for j in range(5):
        for k in range(5):
            r = (j * 5 + k) * 8
            ref[r : r + 8, :] = ref[r : r + 8, :] * (weight * (gll_weight(j) * gll_weight(k)))


def place_flux(ref, tile_of, moves, layers=range(NGLL)):
    lane = lax.broadcasted_iota(jnp.int32, (32, LANES), 1)
    for ez in range(EZ):
        total = jnp.zeros((32, LANES), F32)
        for i in layers:
            tile, start = tile_of(i, ez)
            for source, target, width in moves(i):
                shift = (target - source - start) % LANES
                moved = pltpu.roll(tile, shift, 1) if shift else tile
                total = jnp.where((lane >= target) & (lane < target + width), moved, total)
        ref[pl.ds(ez, 25, stride=8), :] = total[0:25]


def derive(e):
    d = DERIV
    s0, s1 = e[0] + e[4], e[1] + e[3]
    d0, d1 = e[0] - e[4], e[1] - e[3]
    out = [None] * 5
    for i in (0, 1):
        even = float((d[i, 0] - d[i, 4]) / 2) * d0 + float((d[i, 1] - d[i, 3]) / 2) * d1
        odd = float((d[i, 0] + d[i, 4]) / 2) * s0 + float((d[i, 1] + d[i, 3]) / 2) * s1 + float(d[i, 2]) * e[2]
        out[i] = odd + even
        out[4 - i] = even - odd
    out[2] = float(d[2, 0]) * d0 + float(d[2, 1]) * d1
    return out


def derive_back(t):
    d = DERIV
    s0, s1 = t[0] + t[4], t[1] + t[3]
    d0, d1 = t[0] - t[4], t[1] - t[3]
    out = [None] * 5
    for i in (0, 1):
        even = float((d[0, i] - d[4, i]) / 2) * d0 + float((d[1, i] - d[3, i]) / 2) * d1
        odd = float((d[0, i] + d[4, i]) / 2) * s0 + float((d[1, i] + d[3, i]) / 2) * s1 + float(d[2, i]) * t[2]
        out[i] = odd + even
        out[4 - i] = even - odd
    out[2] = float(d[0, 2]) * d0 + float(d[1, 2]) * d1
    return out


def shifted(tiles, distance, lane):
    skip, part = divmod(distance, LANES)
    if part == 0:
        moved = tiles
        pick = None
    else:
        moved = [pltpu.roll(t, LANES - part, 1) for t in tiles]
        pick = lane < LANES - part
    n = len(tiles)
    out = []
    for i in range(n):
        a = moved[(i + skip) % n]
        b = moved[(i + skip + 1) % n]
        out.append(a if pick is None else jnp.where(pick, a, b))
    return out


def plane_of(ref, start, row):
    r0, off = divmod(start, LANES)
    lane9 = lax.broadcasted_iota(jnp.int32, (9, LANES), 1)
    flat = ref[row + r0 : row + r0 + 9, :]
    if off:
        flat = jnp.where(
            lane9 < LANES - off,
            pltpu.roll(flat, LANES - off, 1),
            pltpu.roll(ref[row + r0 + 1 : row + r0 + 10, :], LANES - off, 1),
        )
    return flat


def store_plane(ref, row, flat):
    ref[pl.ds(row, 9, stride=16), :] = flat


def make_windows(plane_ref, base, pitch, win_ref, row):
    lane = lax.broadcasted_iota(jnp.int32, (8, LANES), 1)
    tiles = [plane_ref[base + t * pitch : base + t * pitch + 8, :] for t in range(9)]
    for ey in range(EY):
        near = [tiles[ey], tiles[ey + 1], tiles[min(ey + 2, 8)]]
        if ey:
            near = [pltpu.roll(t, LANES - 4 * ey, 1) for t in near]
            keep = lane < LANES - 4 * ey
            near = [jnp.where(keep, near[0], near[1]), jnp.where(keep, near[1], near[2])]
        for w in range(2):
            win_ref[w, pl.ds(row + ey, 8, stride=8), :] = near[w]


def along_x(win_ref, base, row, combine):
    for w in range(2):
        values = combine([win_ref[w, base + 8 * c : base + 8 * c + 8, :] for c in row])
        for i, v in enumerate(values):
            yield w, i, v


def turned(win_ref, base, elem_ref, column):
    elem_ref[column, 0:LANES, :] = win_ref[0, base : base + LANES, :].T
    elem_ref[column, LANES:168, :] = win_ref[1, base : base + LANES, :].T[0:40, :]


def part(ref, column, j, k):
    return ref[column, pl.ds(j * PZ + k, 8, stride=4), :]


def flux_part(ref, j, k):
    r = (j * 5 + k) * 8
    return ref[r : r + 8, :]


def folded(term, line_ref, win_ref, base):
    row = lax.broadcasted_iota(jnp.int32, (8, LANES), 0)
    line_ref[160:256, :] = jnp.zeros((96, LANES), F32)
    for j in range(5):
        for k in range(1, 4):
            line_ref[pl.ds(j * PZ + k, 8, stride=4), :] = term[j][k]
        last = term[j][4]
        line_ref[pl.ds(j * PZ, 8, stride=4), :] = term[j][0] + jnp.where(row == 0, 0.0, pltpu.roll(last, 1, 0))
        line_ref[j * PZ + 32 : j * PZ + 33, :] = last[7:8, :]
    for w in range(2):
        win_ref[w, base : base + LANES, :] = line_ref[w * LANES : (w + 1) * LANES, :].T


def force_terms(elem_ref, value, slope, flux_ref, line_ref, win_ref, row):
    term = [[None] * 5 for _ in range(5)]
    for k in range(5):
        grads = derive([part(elem_ref, value, j, k) for j in range(5)])
        for j, v in enumerate(derive_back([g * flux_part(flux_ref, j, k) for j, g in enumerate(grads)])):
            term[j][k] = v
    for j in range(5):
        grads = derive([part(elem_ref, value, j, k) for k in range(5)])
        for k, v in enumerate(derive_back([g * flux_part(flux_ref, j, k) for k, g in enumerate(grads)])):
            term[j][k] = term[j][k] + v
    folded(term, line_ref, win_ref, row)
    term = [[part(elem_ref, slope, j, k) * flux_part(flux_ref, j, k) for k in range(5)] for j in range(5)]
    folded(term, line_ref, win_ref, row + LANES)


def cross_smoothed(tiles, cross_ref):
    lane = lax.broadcasted_iota(jnp.int32, tiles[0].shape, 1)
    for base, step in ((0, 1), (9, PZ)):
        total = None
        for tap in range(9):
            moved = shifted(tiles, step * (tap - 4), lane) if tap != 4 else tiles
            terms = [v * cross_ref[base + tap : base + tap + 1, t * LANES : (t + 1) * LANES] for t, v in enumerate(moved)]
            total = terms if total is None else [a + b for a, b in zip(total, terms)]
        tiles = total
    return tiles


def own_kernel(turn, cut_ref, count_ref, own_ref, code_ref, parts_ref, cross_ref, *refs):
    refs = refs[-OWN_OUTS - OWN_SCRATCH :]
    mine = (cut_ref[0] == 0) if turn == 0 else (cut_ref[0] != 0)

    @pl.when(mine)
    def _():
        own_layers(count_ref, own_ref, code_ref, parts_ref, cross_ref, *refs)


def own_layers(
    count_ref, own_ref, code_ref, parts_ref, cross_ref,
    elem_ref, flux_ref, near_flux_ref, near_win_ref, near_slope_ref, near_kern_ref, kern_ref,
    plane_ref, win_ref, line_ref, near_elem_ref, moved_ref,
):
    plane_ref[...] = jnp.zeros(plane_ref.shape, F32)
    for f in range(2):
        base = 24 * 9 * f
        for x in range(PXU):
            flat = plane_of(own_ref, PYZ * x, ROWS * f)
            rows = [OWN_AT[x // 4][x % 4]] if x < 12 else [16 + NEAR_AT[1][x - 12]]
            if x % 4 == 0:
                rows.append(OWN_AT[x // 4 - 1][4] if x else 16 + NEAR_AT[0][4])
            for r in rows:
                plane_ref[pl.ds(base + r, 9, stride=24), :] = flat
        for h in range(2):
            make_windows(plane_ref, base + 8 * h, 24, win_ref, 128 * f + 64 * h)
        make_windows(plane_ref, base + 16, 24, near_win_ref, 64 * f)
        win_ref[:, 256 + 128 * f : 384 + 128 * f, :] = jnp.zeros((2, LANES, LANES), F32)
        for row in OWN_AT:
            for w, i, v in along_x(win_ref, 128 * f, row, derive):
                r = 256 + 128 * f + 8 * row[i]
                win_ref[w, r : r + 8, :] = v
    for column in range(4):
        turned(win_ref, 128 * column, elem_ref, column)
    turned(near_win_ref, 0, near_elem_ref, 0)
    near_slope_ref[...] = jnp.zeros(near_slope_ref.shape, F32)
    for f in range(2):
        for w in range(2):
            value = [near_win_ref[w, 64 * f + 8 * c : 64 * f + 8 * c + 8, :] for c in (0, 4, 5, 6, 7)]
            near_slope_ref[w, 64 * f : 64 * f + 8, :] = float(DERIV[4, 4]) * value[0]
            for i, v in enumerate(derive(value[1:] + [jnp.zeros((8, LANES), F32)])[:4]):
                r = 64 * f + 8 * NEAR_AT[1][i]
                near_slope_ref[w, r : r + 8, :] = v

    element = lax.broadcasted_iota(jnp.int32, (256, 256), 0)
    slot = lax.broadcasted_iota(jnp.int32, (1, 256), 1)
    live = jnp.concatenate([count_ref[0:1, :], count_ref[0:1, :]], axis=1)
    code = jnp.where(slot < live, code_ref[0:1, :], -1)
    pick = jnp.where(code == element, 1.0, 0.0).astype(BF16)
    moved_ref[0:128, :] = add_parts(dot_nt(parts_ref[...], pick))
    moved_ref[128:136, :] = jnp.zeros((8, 256), F32)

    def tile_of(i, ez):
        t = ez // 4
        return moved_ref[25 * i : 25 * i + 32, t * LANES : (t + 1) * LANES], 32 * (ez % 4)

    place_flux(flux_ref, tile_of, lambda i: [(0, 24 * i, 24)])
    place_flux(near_flux_ref, tile_of, lambda i: [(24, 8 * NEAR_AT[1][i], 8)])
    scaled(flux_ref, lane_weight(OWN_AT))
    scaled(near_flux_ref, lane_weight(NEAR_AT))

    kern = [[None] * 5 for _ in range(5)]
    near = [[None] * 5 for _ in range(5)]
    for k in range(5):
        fwd, adj, both = [derive([part(ref, c, j, k) for j in range(5)]) for ref, c in ((elem_ref, 0), (elem_ref, 1), (near_elem_ref, 0))]
        for j in range(5):
            kern[j][k] = fwd[j] * adj[j] + part(elem_ref, 2, j, k) * part(elem_ref, 3, j, k)
            near[j][k] = both[j] * pltpu.roll(both[j], 64, 1)
    for j in range(5):
        fwd, adj, both = [derive([part(ref, c, j, k) for k in range(5)]) for ref, c in ((elem_ref, 0), (elem_ref, 1), (near_elem_ref, 0))]
        for k in range(5):
            kern[j][k] = -(kern[j][k] + fwd[k] * adj[k]) * flux_part(flux_ref, j, k)
            r = (j * 5 + k) * 8
            near_kern_ref[r : r + 8, :] = near[j][k] + both[k] * pltpu.roll(both[k], 64, 1)
    folded(kern, line_ref, win_ref, 0)
    low, high = [gathered(win_ref, 0, h) for h in range(2)]
    row = lax.broadcasted_iota(jnp.int32, (8, LANES), 0)
    tiles = []
    for t in range(9):
        first = low[t] + jnp.where((row == 1) | (row == 2), pltpu.roll(high[t], 5, 0), 0.0)
        second = jnp.where(row < 4, high[t], jnp.where(row == 4, pltpu.roll(high[t], 6, 0), 0.0))
        tiles.append(jnp.concatenate([first, second], axis=0))
    for t, tile in enumerate(cross_smoothed(tiles, cross_ref)):
        kern_ref[:, t * LANES : (t + 1) * LANES] = tile


def message_flux(prev_ref, count_ref, spread_ref):
    upper = pltpu.roll(prev_ref[80:144, :], 64, 1)
    live = upper[61:62, :] < count_ref[0:1, :].astype(F32)
    spread_ref[0:64, :] = jnp.where(live, prev_ref[80:144, :], 0.0)
    spread_ref[64:128, :] = jnp.where(live, upper, 0.0)
    spread_ref[128:136, :] = jnp.zeros((8, LANES), F32)
    return lambda i, ez: (spread_ref[25 * i : 25 * i + 32, :], 8 * ez)


def near_kernel(
    prev_ref, next_ref, count_ref, flux_in_ref, slope_ref, near_kern_ref, kern_in_ref, cross_ref,
    kern_ref,
    plane_ref, new_ref, win_ref, elem_ref, flux_ref, line_ref, spread_ref,
):
    plane_ref[...] = jnp.zeros(plane_ref.shape, F32)
    for f in range(2):
        share = None
        for l in range(4):
            term = float(DERIV[4, l]) * plane_of(prev_ref, 12 + PYZ * l, 40 * f)
            share = term if share is None else share + term
        plane_ref[pl.ds(f, 9, stride=8), :] = share
        plane_ref[pl.ds(2 + f, 9, stride=8), :] = plane_of(next_ref, 0, 16 * f)
    make_windows(plane_ref, 0, 8, new_ref, 0)
    win_ref[...] = slope_ref[...]
    for f in range(2):
        for w in range(2):
            r = 64 * f
            win_ref[w, r : r + 8, :] = win_ref[w, r : r + 8, :] + new_ref[w, 8 * f : 8 * f + 8, :]
            for i in range(4):
                r = 64 * f + 8 * NEAR_AT[1][i]
                new = float(DERIV[i, 4]) * new_ref[w, 16 + 8 * f : 24 + 8 * f, :]
                win_ref[w, r : r + 8, :] = win_ref[w, r : r + 8, :] + new
    turned(win_ref, 0, elem_ref, 0)
    place_flux(flux_ref, message_flux(prev_ref, count_ref, spread_ref), lambda i: [(0, 8 * NEAR_AT[0][i], 8)], (4,))
    scaled(flux_ref, lane_weight([NEAR_AT[0]]))
    kern = [[None] * 5 for _ in range(5)]
    for j in range(5):
        for k in range(5):
            slope = part(elem_ref, 0, j, k)
            total = flux_part(near_kern_ref, j, k) + slope * pltpu.roll(slope, 64, 1)
            kern[j][k] = -total * (flux_part(flux_ref, j, k) + flux_part(flux_in_ref, j, k))
    folded(kern, line_ref, win_ref, 0)
    row = lax.broadcasted_iota(jnp.int32, (8, LANES), 0)
    tiles = [jnp.where((row == 0) | (row >= 4), v, 0.0) for v in gathered(win_ref, 0, 0)]
    for t, tile in enumerate(cross_smoothed(tiles, cross_ref)):
        columns = slice(t * LANES, (t + 1) * LANES)
        kern_ref[0:8, columns] = kern_in_ref[0:8, columns] + jnp.where(row == 0, tile, 0.0)
        kern_ref[8:16, columns] = kern_in_ref[8:16, columns] + jnp.where(row >= 4, tile, 0.0)


def gathered(win_ref, base, h):
    lane = lax.broadcasted_iota(jnp.int32, (8, LANES), 1)
    tiles = [None] * 9
    for ey in range(EY):
        rows = pl.ds(base + h * 64 + ey, 8, stride=8)
        a, b = win_ref[0, rows, :], win_ref[1, rows, :]
        if ey:
            a, b = pltpu.roll(a, 4 * ey, 1), pltpu.roll(b, 4 * ey, 1)
            keep = lane >= 4 * ey
            a, b = jnp.where(keep, a, 0.0), jnp.where(keep, b, a)
        tiles[ey] = a if ey == 0 else tiles[ey] + a
        tiles[ey + 1] = b
    return tiles


def summed_along_x(win_ref, places, out_ref, row):
    for line in places:
        for w, i, v in along_x(win_ref, LANES, line, derive_back):
            r = 8 * line[i]
            out_ref[w, row + r : row + r + 8, :] = win_ref[w, r : r + 8, :] + v


def to_planes(win_ref, base, plane_ref):
    for h in range(2):
        for t, tile in enumerate(gathered(win_ref, base, h)):
            plane_ref[t * 16 + 8 * h : t * 16 + 8 * h + 8, :] = tile


def add_plane(line_ref, f, x, flat):
    lane9 = lax.broadcasted_iota(jnp.int32, (9, LANES), 1)
    r0, off = divmod(PYZ * x, LANES)
    if off:
        flat = pltpu.roll(flat, off, 1)
        spill = jnp.where(lane9 < off, flat, 0.0)
        flat = jnp.where(lane9 < off, 0.0, flat)
    line_ref[f, r0 : r0 + 9, :] = line_ref[f, r0 : r0 + 9, :] + flat
    if off:
        line_ref[f, r0 + 1 : r0 + 10, :] = line_ref[f, r0 + 1 : r0 + 10, :] + spill


def force_kernel(turn, cut_ref, elem_ref, flux_ref, before_ref, *refs):
    mine = (cut_ref[0] == 1) if turn == 0 else (cut_ref[0] != 1)

    @pl.when(mine)
    def _():
        own_forces(elem_ref, flux_ref, refs[0], *refs[len(refs) - 4 :])


def own_forces(elem_ref, flux_ref, out_ref, win_ref, fold_ref, force_ref, plane_ref):
    out_ref[...] = jnp.zeros(out_ref.shape, F32)
    for f in range(2):
        force_terms(elem_ref, f, 2 + f, flux_ref, fold_ref, win_ref, 0)
        summed_along_x(win_ref, OWN_AT, force_ref, 0)
        to_planes(force_ref, 0, plane_ref)
        for x in range(13):
            i, m = x % 4, x // 4
            rows = [OWN_AT[m][i]] if m < 3 else []
            if i == 0 and m > 0:
                rows.append(OWN_AT[m - 1][4])
            flat = [plane_ref[pl.ds(r, 9, stride=16), :] for r in rows]
            add_plane(out_ref, f, x, sum(flat[1:], flat[0]))


def near_force_kernel(
    force_ref, near_half_ref, near_flux_ref, prev_ref, next_ref, count_ref, after_ref,
    out_ref,
    win_ref, fold_ref, near_force_ref, plane_ref, flux_ref, elem_ref, near_win_ref, near_plane_ref, spread_ref,
):
    out_ref[...] = force_ref[...]
    near_plane_ref[...] = jnp.zeros(near_plane_ref.shape, F32)
    for f in range(2):
        for i in range(5):
            flat = plane_of(prev_ref, 12 + PYZ * i, 40 * f) if i < 4 else plane_of(next_ref, 0, 16 * f)
            near_plane_ref[pl.ds(72 * f + i, 9, stride=8), :] = flat
        near_win_ref[:, 128 * f : 128 * f + 64, :] = near_half_ref[:, 64 * f : 64 * f + 64, :]
        make_windows(near_plane_ref, 72 * f, 8, near_win_ref, 128 * f + 64)
    place_flux(flux_ref, message_flux(prev_ref, count_ref, spread_ref), lambda i: [(0, 8 * NEAR_AT[0][i], 8)])
    scaled(flux_ref, lane_weight([NEAR_AT[0]]))
    flux_ref[...] = flux_ref[...] + near_flux_ref[...]
    for f in range(2):
        win_ref[...] = jnp.zeros(win_ref.shape, F32)
        for row in NEAR_AT:
            for w, i, v in along_x(near_win_ref, LANES * f, row, derive):
                win_ref[w, 8 * row[i] : 8 * row[i] + 8, :] = v
        turned(near_win_ref, LANES * f, elem_ref, 0)
        turned(win_ref, 0, elem_ref, 1)
        force_terms(elem_ref, 0, 1, flux_ref, fold_ref, win_ref, 0)
        summed_along_x(win_ref, NEAR_AT, near_force_ref, 0)
        to_planes(near_force_ref, 0, plane_ref)
        for x, r in [(0, NEAR_AT[0][4])] + [(12 + i, NEAR_AT[1][i]) for i in range(4)]:
            add_plane(out_ref, f, x, plane_ref[pl.ds(r, 9, stride=16), :])


def step_kernel(
    line_ref, fwd_ref, fwd_speed_ref, adj_ref, adj_speed_ref, mass_ref,
    fwd_out_ref, fwd_speed_out_ref, adj_out_ref, adj_speed_out_ref,
):
    def step(lo, hi, force):
        shape = (hi - lo) // force[0].shape[1], force[0].shape[1]
        take = lambda ref: ref[0:1, lo:hi].reshape(shape)
        scale = TIME_STEP * mass_ref[lo:hi].reshape(shape)
        speed = take(fwd_speed_ref) + scale * force[0]
        fwd_speed_out_ref[0:1, lo:hi] = speed.reshape(1, hi - lo)
        fwd_out_ref[0:1, lo:hi] = (take(fwd_ref) - TIME_STEP * speed).reshape(1, hi - lo)
        speed = take(adj_speed_ref) - scale * force[1]
        adj_speed_out_ref[0:1, lo:hi] = speed.reshape(1, hi - lo)
        adj_out_ref[0:1, lo:hi] = (take(adj_ref) + TIME_STEP * speed).reshape(1, hi - lo)

    for r in range(0, 136, 8):
        step(r * LANES, (r + 8) * LANES, [line_ref[f, r : r + 8, :] for f in range(2)])
    step(NPTS - 16, NPTS, [line_ref[f, 136:137, 0:16] for f in range(2)])


def band_kernel(cut_ref, own_ref, first_ref, second_ref, band_ref, out_ref):
    flat = jnp.concatenate([own_ref[...], first_ref[...], second_ref[...]], axis=0)
    k1 = flat.astype(BF16)
    rest = flat - k1.astype(F32)
    k2 = rest.astype(BF16)
    k3 = (rest - k2.astype(F32)).astype(BF16)
    stacked = jnp.concatenate([k1, k2, k3, k1, k2, k1], axis=0)
    band = band_ref[cut_ref[0] & 1]
    out_ref[...] = jnp.dot(band, stacked, preferred_element_type=F32)[:, :PYZ]


def on_device(
    forward_displacement,
    forward_velocity,
    adjoint_displacement,
    adjoint_velocity,
    inverse_mass,
    shear_modulus,
    connectivity,
    face_points,
    element_count,
):
    events = lax.axis_size("event")
    cuts = lax.axis_size("cuts")
    cut = lax.axis_index("cuts").astype(jnp.int32).reshape(1)
    pairs_first = [(i, (i - 1 if i % 2 == 0 else i + 1) % cuts) for i in range(cuts)]
    pairs_second = [(i, (i + 1 if i % 2 == 0 else i - 1) % cuts) for i in range(cuts)]

    vmem = pl.BlockSpec(memory_space=pltpu.VMEM)
    smem = pl.BlockSpec(memory_space=pltpu.SMEM)
    anywhere = pl.BlockSpec(memory_space=pl.ANY)

    def held(block):
        return pltpu.with_memory_space_constraint(block, pltpu.VMEM)

    def in_hbm(block):
        return pltpu.with_memory_space_constraint(block, pltpu.HBM)

    def cost(flops):
        return pl.CostEstimate(flops=flops, bytes_accessed=1000000, transcendentals=0)

    dma = pltpu.SemaphoreType.DMA
    point_row = pltpu.VMEM((1, NPTS), F32)
    flux_block = pltpu.VMEM((200, LANES), F32)
    kern_block = pltpu.VMEM((16, 9 * LANES), F32)
    line_block = pltpu.VMEM((256, LANES), F32)

    def elements(n):
        return pltpu.VMEM((n, 168, LANES), F32)

    def windows(n):
        return pltpu.VMEM((2, n * LANES, LANES), F32)

    fields = (in_hbm(forward_displacement), in_hbm(adjoint_displacement))
    cross = held(jnp.asarray(cross_table()))
    right, left, own, code, parts = pl.pallas_call(
        pack_kernel,
        out_shape=[
            pltpu.VMEM((144, LANES), F32),
            pltpu.VMEM((32, LANES), F32),
            pltpu.VMEM((2 * ROWS, LANES), F32),
            pltpu.VMEM((8, 256), jnp.int32),
            pltpu.VMEM((384, 256), BF16),
        ],
        in_specs=[anywhere] * 4,
        scratch_shapes=[
            pltpu.VMEM((8, 256), jnp.int32),
            pltpu.VMEM((125, 256), F32),
            point_row,
            point_row,
            pltpu.VMEM((128, 256), F32),
            dma((4,)),
        ],
        cost_estimate=cost(100000000),
        name="pack",
    )(in_hbm(connectivity), in_hbm(shear_modulus), *fields)
    to_next = [(i, (i + 1) % cuts) for i in range(cuts)]
    prev = lax.ppermute(right, "cuts", to_next)
    count, left = lax.optimization_barrier((element_count, left))
    count = jnp.broadcast_to(count.reshape(1, 1), (8, LANES))
    prev_count = lax.ppermute(count, "cuts", to_next)
    count, left = lax.optimization_barrier((count, left))

    own_blocks = [elements(4), flux_block, flux_block, windows(1), windows(1), flux_block, kern_block]

    def own_part(turn, before):
        given = (cut, held(count), held(own), held(code), held(parts), cross)
        return pl.pallas_call(
            functools.partial(own_kernel, turn),
            out_shape=own_blocks,
            in_specs=[smem] + [vmem] * (5 + len(before)),
            scratch_shapes=[
                pltpu.VMEM((2 * 9 * 24, LANES), F32),
                windows(4),
                line_block,
                elements(1),
                pltpu.VMEM((136, 256), F32),
            ],
            input_output_aliases={len(given) + n: n for n in range(len(before))},
            cost_estimate=cost(300000000),
            name="own_layers",
        )(*given, *[held(block) for block in before])

    left, *blocks = lax.optimization_barrier((left, *own_part(0, [])))
    after = lax.ppermute(left, "cuts", [((i + 1) % cuts, i) for i in range(cuts)])
    elem, flux, near_flux, near_win, near_slope, near_kern, kern = own_part(1, blocks)
    kern = pl.pallas_call(
        near_kernel,
        out_shape=kern_block,
        in_specs=[vmem] * 8,
        scratch_shapes=[
            pltpu.VMEM((72, LANES), F32),
            pltpu.VMEM((2, 64, LANES), F32),
            windows(1),
            elements(1),
            flux_block,
            line_block,
            pltpu.VMEM((136, LANES), F32),
        ],
        cost_estimate=cost(200000000),
        name="near_layers",
    )(held(prev), held(after), held(prev_count), held(near_flux), held(near_slope), held(near_kern), held(kern), cross)

    point_block = pltpu.VMEM((2, ROWS, LANES), F32)

    def force_part(turn, before, outs, aliases):
        return pl.pallas_call(
            functools.partial(force_kernel, turn),
            out_shape=outs,
            in_specs=[smem] + [vmem] * 3,
            scratch_shapes=[windows(2), line_block, windows(1), pltpu.VMEM((144, LANES), F32)],
            input_output_aliases=aliases,
            cost_estimate=cost(200000000),
            name="forces",
        )(cut, held(elem), held(flux), held(before))

    force, kern = force_part(0, kern, [point_block, kern_block], {3: 1})
    (force,) = force_part(1, force, [point_block], {3: 0})

    if events == 2:
        other = lax.ppermute(kern, "event", [(0, 1), (1, 0)])
        other, force = lax.optimization_barrier((other, force))
        kern = kern + other
    elif events > 2:
        kern = lax.psum(kern, "event")
    kern_first = lax.ppermute(kern, "cuts", pairs_first)
    kern_second = lax.ppermute(kern, "cuts", pairs_second)

    force = pl.pallas_call(
        near_force_kernel,
        out_shape=pltpu.VMEM((2, ROWS, LANES), F32),
        in_specs=[vmem] * 7,
        scratch_shapes=[
            windows(2),
            line_block,
            windows(1),
            pltpu.VMEM((144, LANES), F32),
            flux_block,
            elements(2),
            windows(2),
            pltpu.VMEM((2 * 72, LANES), F32),
            pltpu.VMEM((136, LANES), F32),
        ],
        cost_estimate=cost(200000000),
        name="near_forces",
    )(held(force), held(near_win), held(near_flux), held(prev), held(after), held(prev_count), held(kern))
    points = jax.ShapeDtypeStruct((1, NPTS), F32)
    outs = pl.pallas_call(
        step_kernel,
        out_shape=[points] * 4,
        in_specs=[vmem] * 6,
        cost_estimate=cost(200000000),
        name="step",
    )(
        held(force),
        held(forward_displacement),
        held(forward_velocity),
        held(adjoint_displacement),
        held(adjoint_velocity),
        held(inverse_mass),
    )
    shear_kernel = pl.pallas_call(
        band_kernel,
        out_shape=jax.ShapeDtypeStruct((PXU, PYZ), F32),
        in_specs=[smem] + [vmem] * 4,
        cost_estimate=cost(20000000),
        name="band",
    )(cut, held(kern), held(kern_first), held(kern_second), held(jnp.asarray(band_table())))
    return (*outs, shear_kernel)


def solution(mesh):
    in_specs = (
        P("event", "cuts"),
        P("event", "cuts"),
        P("event", "cuts"),
        P("event", "cuts"),
        P("cuts"),
        P(None, "cuts"),
        P(None, "cuts"),
        P("cuts", None),
        P("cuts"),
    )
    out_specs = (
        P("event", "cuts"),
        P("event", "cuts"),
        P("event", "cuts"),
        P("event", "cuts"),
        P("cuts", None),
    )
    return jax.shard_map(on_device, mesh=mesh, in_specs=in_specs, out_specs=out_specs, check_vma=False)
```

```python
import functools

import numpy as np
import jax
import jax.numpy as jnp
import ml_dtypes
from jax import lax
from jax.experimental import pallas as pl
from jax.experimental.pallas import tpu as pltpu
from jax.sharding import PartitionSpec as P

NGLL = 5
EX, EY, EZ = 4, 8, 8
PXU = 16
PY = 33
PZ = 33
PYZ = 1089
NPTS = 17424
LANES = 128
ROWS = 144
TIME_STEP = 0.02
OWN_OUTS, OWN_SCRATCH = 7, 5
F32 = jnp.float32
BF16 = jnp.bfloat16


def gll():
    nodes = np.array([-1.0, -np.sqrt(3.0 / 7.0), 0.0, np.sqrt(3.0 / 7.0), 1.0])
    bary = np.array([1.0 / np.prod([nodes[r] - nodes[c] for c in range(5) if c != r]) for r in range(5)])
    d = np.zeros((5, 5))
    for r in range(5):
        for c in range(5):
            if c != r:
                d[r, c] = bary[c] / bary[r] / (nodes[r] - nodes[c])
        d[r, r] = -np.sum(d[r])
    return d


DERIV = gll()


def split_np(x):
    x = np.asarray(x, np.float32)
    parts = []
    for _ in range(3):
        p = x.astype(ml_dtypes.bfloat16)
        parts.append(p)
        x = x - p.astype(np.float32)
    return parts


ROW_PLANE = np.array([4 * (r % 3) + r // 3 for r in range(12)] + [12, 13, 14, 15])
OWN_AT = [[3 * i + m for i in range(5)] for m in range(3)]
NEAR_AT = [[8, 9, 10, 11, 0], [4, 5, 6, 7, 12]]


def band_table():
    offsets = np.arange(-PXU, PXU + 1)
    w = lambda d: np.exp(-d * d / (2.0 * (PXU / 4.0) ** 2))
    total = w(offsets.astype(np.float64)).sum()
    out = []
    for first in (-PXU, PXU):
        source = np.concatenate([ROW_PLANE, ROW_PLANE + first, ROW_PLANE - first])
        spread = np.arange(PXU)[:, None] - source[None, :]
        band = w(spread.astype(np.float64)) * (np.abs(spread) <= PXU) / total
        b1, b2, b3 = split_np(band)
        out.append(np.concatenate([b1, b1, b1, b2, b2, b3], axis=1))
    return np.stack(out)


def cross_table():
    off = np.arange(-4, 5)
    k = np.exp(-off * off / (2.0 * 1.5 * 1.5))
    point = np.arange(33)
    inside = ((point[None, :] + off[:, None]) >= 0) & ((point[None, :] + off[:, None]) < 33)
    taps = k[:, None] * inside
    taps = taps / taps.sum(axis=0, keepdims=True)
    out = np.zeros((24, 1152), np.float32)
    out[0:9, :PYZ] = np.tile(taps, (1, PY))
    out[9:18, :PYZ] = np.repeat(taps, PZ, axis=1)
    return out


def split3(x):
    hi = x.astype(BF16)
    rest = x - hi.astype(F32)
    mid = rest.astype(BF16)
    low = (rest - mid.astype(F32)).astype(BF16)
    return hi, mid, low


def dot_nt(a, b):
    return lax.dot_general(a, b, (((1,), (1,)), ((), ())), preferred_element_type=F32)


def fetch(sem, *pairs):
    copies = [pltpu.make_async_copy(src, dst, sem.at[n]) for n, (src, dst) in enumerate(pairs)]
    for c in copies:
        c.start()
    return copies


def add_parts(stacked):
    n = stacked.shape[0] // 3
    return stacked[0:n] + (stacked[n : 2 * n] + stacked[2 * n : 3 * n])


def pack_kernel(
    conn_hbm, shear_hbm, fwd_hbm, adj_hbm,
    right_ref, left_ref, own_ref, code_ref, parts_ref,
    conn_ref, shear_ref, fwd_ref, adj_ref, block_ref, sem,
):
    copies = fetch(
        sem,
        (shear_hbm, shear_ref),
        (conn_hbm.at[0:8], conn_ref),
        (fwd_hbm, fwd_ref),
        (adj_hbm, adj_ref),
    )
    copies[1].wait()
    point = conn_ref[0:1, :].astype(F32)
    x = jnp.floor((point + 0.5) * (1.0 / PYZ))
    rest = point - x * PYZ
    y = jnp.floor((rest + 0.5) * (1.0 / PZ))
    z = rest - y * PZ
    code = (8.0 * z + 2.0 * x + 0.25 * y).astype(jnp.int32)
    slot = lax.broadcasted_iota(jnp.int32, (1, 256), 1)
    code_ref[...] = jnp.broadcast_to(code, (8, 256))
    lane = lax.broadcasted_iota(jnp.int32, (LANES, 256), 0)
    pick = jnp.where(code == ((lane >> 3) & 7) * 32 + 24 + (lane & 7), 1.0, 0.0).astype(BF16)
    for f, ref in enumerate((fwd_ref, adj_ref)):
        copies[2 + f].wait()
        for r in range(0, 136, 8):
            own_ref[ROWS * f + r : ROWS * f + r + 8, :] = ref[0:1, r * LANES : (r + 8) * LANES].reshape(8, LANES)
        own_ref[ROWS * f + 136 : ROWS * f + 144, :] = jnp.zeros((8, LANES), F32)
        own_ref[ROWS * f + 136 : ROWS * f + 137, 0:16] = ref[0:1, NPTS - 16 : NPTS]
        right_ref[40 * f : 40 * f + 40, :] = own_ref[ROWS * f + 102 : ROWS * f + 142, :]
        left_ref[16 * f : 16 * f + 16, :] = own_ref[ROWS * f : ROWS * f + 16, :]
    copies[0].wait()
    block_ref[0:125, :] = shear_ref[...]
    block_ref[125:126, :] = slot.astype(F32)
    block_ref[126:128, :] = jnp.zeros((2, 256), F32)
    parts = jnp.concatenate(split3(block_ref[...]), axis=0)
    parts_ref[...] = parts
    flux = add_parts(dot_nt(parts, pick))
    low = lax.broadcasted_iota(jnp.int32, (64, LANES), 1) < 64
    right_ref[80:144, :] = jnp.where(low, flux[0:64], flux[64:128])


def gll_weight(i):
    return (0.1, 49.0 / 90.0, 32.0 / 45.0, 49.0 / 90.0, 0.1)[i]


def lane_weight(places):
    chunk = lax.broadcasted_iota(jnp.int32, (8, LANES), 1) >> 3
    weight = jnp.zeros((8, LANES), F32)
    for row in places:
        for i, place in enumerate(row):
            weight = jnp.where(chunk == place, gll_weight(i), weight)
    return weight


def scaled(ref, weight):
    for j in range(5):
        for k in range(5):
            r = (j * 5 + k) * 8
            ref[r : r + 8, :] = ref[r : r + 8, :] * (weight * (gll_weight(j) * gll_weight(k)))


def place_flux(ref, tile_of, moves, layers=range(NGLL)):
    lane = lax.broadcasted_iota(jnp.int32, (32, LANES), 1)
    for ez in range(EZ):
        total = jnp.zeros((32, LANES), F32)
        for i in layers:
            tile, start = tile_of(i, ez)
            for source, target, width in moves(i):
                shift = (target - source - start) % LANES
                moved = pltpu.roll(tile, shift, 1) if shift else tile
                total = jnp.where((lane >= target) & (lane < target + width), moved, total)
        ref[pl.ds(ez, 25, stride=8), :] = total[0:25]


def derive(e):
    d = DERIV
    s0, s1 = e[0] + e[4], e[1] + e[3]
    d0, d1 = e[0] - e[4], e[1] - e[3]
    out = [None] * 5
    for i in (0, 1):
        even = float((d[i, 0] - d[i, 4]) / 2) * d0 + float((d[i, 1] - d[i, 3]) / 2) * d1
        odd = float((d[i, 0] + d[i, 4]) / 2) * s0 + float((d[i, 1] + d[i, 3]) / 2) * s1 + float(d[i, 2]) * e[2]
        out[i] = odd + even
        out[4 - i] = even - odd
    out[2] = float(d[2, 0]) * d0 + float(d[2, 1]) * d1
    return out


def derive_back(t):
    d = DERIV
    s0, s1 = t[0] + t[4], t[1] + t[3]
    d0, d1 = t[0] - t[4], t[1] - t[3]
    out = [None] * 5
    for i in (0, 1):
        even = float((d[0, i] - d[4, i]) / 2) * d0 + float((d[1, i] - d[3, i]) / 2) * d1
        odd = float((d[0, i] + d[4, i]) / 2) * s0 + float((d[1, i] + d[3, i]) / 2) * s1 + float(d[2, i]) * t[2]
        out[i] = odd + even
        out[4 - i] = even - odd
    out[2] = float(d[0, 2]) * d0 + float(d[1, 2]) * d1
    return out


def shifted(tiles, distance, lane):
    skip, part = divmod(distance, LANES)
    if part == 0:
        moved = tiles
        pick = None
    else:
        moved = [pltpu.roll(t, LANES - part, 1) for t in tiles]
        pick = lane < LANES - part
    n = len(tiles)
    out = []
    for i in range(n):
        a = moved[(i + skip) % n]
        b = moved[(i + skip + 1) % n]
        out.append(a if pick is None else jnp.where(pick, a, b))
    return out


def plane_of(ref, start, row):
    r0, off = divmod(start, LANES)
    lane9 = lax.broadcasted_iota(jnp.int32, (9, LANES), 1)
    flat = ref[row + r0 : row + r0 + 9, :]
    if off:
        flat = jnp.where(
            lane9 < LANES - off,
            pltpu.roll(flat, LANES - off, 1),
            pltpu.roll(ref[row + r0 + 1 : row + r0 + 10, :], LANES - off, 1),
        )
    return flat


def store_plane(ref, row, flat):
    ref[pl.ds(row, 9, stride=16), :] = flat


def make_windows(plane_ref, base, pitch, win_ref, row):
    lane = lax.broadcasted_iota(jnp.int32, (8, LANES), 1)
    tiles = [plane_ref[base + t * pitch : base + t * pitch + 8, :] for t in range(9)]
    for ey in range(EY):
        near = [tiles[ey], tiles[ey + 1], tiles[min(ey + 2, 8)]]
        if ey:
            near = [pltpu.roll(t, LANES - 4 * ey, 1) for t in near]
            keep = lane < LANES - 4 * ey
            near = [jnp.where(keep, near[0], near[1]), jnp.where(keep, near[1], near[2])]
        for w in range(2):
            win_ref[w, pl.ds(row + ey, 8, stride=8), :] = near[w]


def along_x(win_ref, base, row, combine):
    for w in range(2):
        values = combine([win_ref[w, base + 8 * c : base + 8 * c + 8, :] for c in row])
        for i, v in enumerate(values):
            yield w, i, v


def turned(win_ref, base, elem_ref, column):
    elem_ref[column, 0:LANES, :] = win_ref[0, base : base + LANES, :].T
    elem_ref[column, LANES:168, :] = win_ref[1, base : base + LANES, :].T[0:40, :]


def part(ref, column, j, k):
    return ref[column, pl.ds(j * PZ + k, 8, stride=4), :]


def flux_part(ref, j, k):
    r = (j * 5 + k) * 8
    return ref[r : r + 8, :]


def folded(term, line_ref, win_ref, base):
    row = lax.broadcasted_iota(jnp.int32, (8, LANES), 0)
    line_ref[160:256, :] = jnp.zeros((96, LANES), F32)
    for j in range(5):
        for k in range(1, 4):
            line_ref[pl.ds(j * PZ + k, 8, stride=4), :] = term[j][k]
        last = term[j][4]
        line_ref[pl.ds(j * PZ, 8, stride=4), :] = term[j][0] + jnp.where(row == 0, 0.0, pltpu.roll(last, 1, 0))
        line_ref[j * PZ + 32 : j * PZ + 33, :] = last[7:8, :]
    for w in range(2):
        win_ref[w, base : base + LANES, :] = line_ref[w * LANES : (w + 1) * LANES, :].T


def force_terms(elem_ref, value, slope, flux_ref, line_ref, win_ref, row):
    term = [[None] * 5 for _ in range(5)]
    for k in range(5):
        grads = derive([part(elem_ref, value, j, k) for j in range(5)])
        for j, v in enumerate(derive_back([g * flux_part(flux_ref, j, k) for j, g in enumerate(grads)])):
            term[j][k] = v
    for j in range(5):
        grads = derive([part(elem_ref, value, j, k) for k in range(5)])
        for k, v in enumerate(derive_back([g * flux_part(flux_ref, j, k) for k, g in enumerate(grads)])):
            term[j][k] = term[j][k] + v
    folded(term, line_ref, win_ref, row)
    term = [[part(elem_ref, slope, j, k) * flux_part(flux_ref, j, k) for k in range(5)] for j in range(5)]
    folded(term, line_ref, win_ref, row + LANES)


def cross_smoothed(tiles, cross_ref):
    lane = lax.broadcasted_iota(jnp.int32, tiles[0].shape, 1)
    for base, step in ((0, 1), (9, PZ)):
        total = None
        for tap in range(9):
            moved = shifted(tiles, step * (tap - 4), lane) if tap != 4 else tiles
            terms = [v * cross_ref[base + tap : base + tap + 1, t * LANES : (t + 1) * LANES] for t, v in enumerate(moved)]
            total = terms if total is None else [a + b for a, b in zip(total, terms)]
        tiles = total
    return tiles


def own_kernel(turn, cut_ref, count_ref, own_ref, code_ref, parts_ref, cross_ref, *refs):
    refs = refs[-OWN_OUTS - OWN_SCRATCH :]
    mine = (cut_ref[0] < 2) if turn == 0 else (cut_ref[0] >= 2)

    @pl.when(mine)
    def _():
        own_layers(count_ref, own_ref, code_ref, parts_ref, cross_ref, *refs)


def own_layers(
    count_ref, own_ref, code_ref, parts_ref, cross_ref,
    elem_ref, flux_ref, near_flux_ref, near_win_ref, near_slope_ref, near_kern_ref, kern_ref,
    plane_ref, win_ref, line_ref, near_elem_ref, moved_ref,
):
    plane_ref[...] = jnp.zeros(plane_ref.shape, F32)
    for f in range(2):
        base = 24 * 9 * f
        for x in range(PXU):
            flat = plane_of(own_ref, PYZ * x, ROWS * f)
            rows = [OWN_AT[x // 4][x % 4]] if x < 12 else [16 + NEAR_AT[1][x - 12]]
            if x % 4 == 0:
                rows.append(OWN_AT[x // 4 - 1][4] if x else 16 + NEAR_AT[0][4])
            for r in rows:
                plane_ref[pl.ds(base + r, 9, stride=24), :] = flat
        for h in range(2):
            make_windows(plane_ref, base + 8 * h, 24, win_ref, 128 * f + 64 * h)
        make_windows(plane_ref, base + 16, 24, near_win_ref, 64 * f)
        win_ref[:, 256 + 128 * f : 384 + 128 * f, :] = jnp.zeros((2, LANES, LANES), F32)
        for row in OWN_AT:
            for w, i, v in along_x(win_ref, 128 * f, row, derive):
                r = 256 + 128 * f + 8 * row[i]
                win_ref[w, r : r + 8, :] = v
    for column in range(4):
        turned(win_ref, 128 * column, elem_ref, column)
    turned(near_win_ref, 0, near_elem_ref, 0)
    near_slope_ref[...] = jnp.zeros(near_slope_ref.shape, F32)
    for f in range(2):
        for w in range(2):
            value = [near_win_ref[w, 64 * f + 8 * c : 64 * f + 8 * c + 8, :] for c in (0, 4, 5, 6, 7)]
            near_slope_ref[w, 64 * f : 64 * f + 8, :] = float(DERIV[4, 4]) * value[0]
            for i, v in enumerate(derive(value[1:] + [jnp.zeros((8, LANES), F32)])[:4]):
                r = 64 * f + 8 * NEAR_AT[1][i]
                near_slope_ref[w, r : r + 8, :] = v

    element = lax.broadcasted_iota(jnp.int32, (256, 256), 0)
    slot = lax.broadcasted_iota(jnp.int32, (1, 256), 1)
    live = jnp.concatenate([count_ref[0:1, :], count_ref[0:1, :]], axis=1)
    code = jnp.where(slot < live, code_ref[0:1, :], -1)
    pick = jnp.where(code == element, 1.0, 0.0).astype(BF16)
    moved_ref[0:128, :] = add_parts(dot_nt(parts_ref[...], pick))
    moved_ref[128:136, :] = jnp.zeros((8, 256), F32)

    def tile_of(i, ez):
        t = ez // 4
        return moved_ref[25 * i : 25 * i + 32, t * LANES : (t + 1) * LANES], 32 * (ez % 4)

    place_flux(flux_ref, tile_of, lambda i: [(0, 24 * i, 24)])
    place_flux(near_flux_ref, tile_of, lambda i: [(24, 8 * NEAR_AT[1][i], 8)])
    scaled(flux_ref, lane_weight(OWN_AT))
    scaled(near_flux_ref, lane_weight(NEAR_AT))

    kern = [[None] * 5 for _ in range(5)]
    near = [[None] * 5 for _ in range(5)]
    for k in range(5):
        fwd, adj, both = [derive([part(ref, c, j, k) for j in range(5)]) for ref, c in ((elem_ref, 0), (elem_ref, 1), (near_elem_ref, 0))]
        for j in range(5):
            kern[j][k] = fwd[j] * adj[j] + part(elem_ref, 2, j, k) * part(elem_ref, 3, j, k)
            near[j][k] = both[j] * pltpu.roll(both[j], 64, 1)
    for j in range(5):
        fwd, adj, both = [derive([part(ref, c, j, k) for k in range(5)]) for ref, c in ((elem_ref, 0), (elem_ref, 1), (near_elem_ref, 0))]
        for k in range(5):
            kern[j][k] = -(kern[j][k] + fwd[k] * adj[k]) * flux_part(flux_ref, j, k)
            r = (j * 5 + k) * 8
            near_kern_ref[r : r + 8, :] = near[j][k] + both[k] * pltpu.roll(both[k], 64, 1)
    folded(kern, line_ref, win_ref, 0)
    low, high = [gathered(win_ref, 0, h) for h in range(2)]
    row = lax.broadcasted_iota(jnp.int32, (8, LANES), 0)
    tiles = []
    for t in range(9):
        first = low[t] + jnp.where((row == 1) | (row == 2), pltpu.roll(high[t], 5, 0), 0.0)
        second = jnp.where(row < 4, high[t], jnp.where(row == 4, pltpu.roll(high[t], 6, 0), 0.0))
        tiles.append(jnp.concatenate([first, second], axis=0))
    for t, tile in enumerate(cross_smoothed(tiles, cross_ref)):
        kern_ref[:, t * LANES : (t + 1) * LANES] = tile


def message_flux(prev_ref, count_ref, spread_ref):
    upper = pltpu.roll(prev_ref[80:144, :], 64, 1)
    live = upper[61:62, :] < count_ref[0:1, :].astype(F32)
    spread_ref[0:64, :] = jnp.where(live, prev_ref[80:144, :], 0.0)
    spread_ref[64:128, :] = jnp.where(live, upper, 0.0)
    spread_ref[128:136, :] = jnp.zeros((8, LANES), F32)
    return lambda i, ez: (spread_ref[25 * i : 25 * i + 32, :], 8 * ez)


def near_kernel(
    prev_ref, next_ref, count_ref, flux_in_ref, slope_ref, near_kern_ref, kern_in_ref, cross_ref,
    kern_ref,
    plane_ref, new_ref, win_ref, elem_ref, flux_ref, line_ref, spread_ref,
):
    plane_ref[...] = jnp.zeros(plane_ref.shape, F32)
    for f in range(2):
        share = None
        for l in range(4):
            term = float(DERIV[4, l]) * plane_of(prev_ref, 12 + PYZ * l, 40 * f)
            share = term if share is None else share + term
        plane_ref[pl.ds(f, 9, stride=8), :] = share
        plane_ref[pl.ds(2 + f, 9, stride=8), :] = plane_of(next_ref, 0, 16 * f)
    make_windows(plane_ref, 0, 8, new_ref, 0)
    win_ref[...] = slope_ref[...]
    for f in range(2):
        for w in range(2):
            r = 64 * f
            win_ref[w, r : r + 8, :] = win_ref[w, r : r + 8, :] + new_ref[w, 8 * f : 8 * f + 8, :]
            for i in range(4):
                r = 64 * f + 8 * NEAR_AT[1][i]
                new = float(DERIV[i, 4]) * new_ref[w, 16 + 8 * f : 24 + 8 * f, :]
                win_ref[w, r : r + 8, :] = win_ref[w, r : r + 8, :] + new
    turned(win_ref, 0, elem_ref, 0)
    place_flux(flux_ref, message_flux(prev_ref, count_ref, spread_ref), lambda i: [(0, 8 * NEAR_AT[0][i], 8)], (4,))
    scaled(flux_ref, lane_weight([NEAR_AT[0]]))
    kern = [[None] * 5 for _ in range(5)]
    for j in range(5):
        for k in range(5):
            slope = part(elem_ref, 0, j, k)
            total = flux_part(near_kern_ref, j, k) + slope * pltpu.roll(slope, 64, 1)
            kern[j][k] = -total * (flux_part(flux_ref, j, k) + flux_part(flux_in_ref, j, k))
    folded(kern, line_ref, win_ref, 0)
    row = lax.broadcasted_iota(jnp.int32, (8, LANES), 0)
    tiles = [jnp.where((row == 0) | (row >= 4), v, 0.0) for v in gathered(win_ref, 0, 0)]
    for t, tile in enumerate(cross_smoothed(tiles, cross_ref)):
        columns = slice(t * LANES, (t + 1) * LANES)
        kern_ref[0:8, columns] = kern_in_ref[0:8, columns] + jnp.where(row == 0, tile, 0.0)
        kern_ref[8:16, columns] = kern_in_ref[8:16, columns] + jnp.where(row >= 4, tile, 0.0)


def gathered(win_ref, base, h):
    lane = lax.broadcasted_iota(jnp.int32, (8, LANES), 1)
    tiles = [None] * 9
    for ey in range(EY):
        rows = pl.ds(base + h * 64 + ey, 8, stride=8)
        a, b = win_ref[0, rows, :], win_ref[1, rows, :]
        if ey:
            a, b = pltpu.roll(a, 4 * ey, 1), pltpu.roll(b, 4 * ey, 1)
            keep = lane >= 4 * ey
            a, b = jnp.where(keep, a, 0.0), jnp.where(keep, b, a)
        tiles[ey] = a if ey == 0 else tiles[ey] + a
        tiles[ey + 1] = b
    return tiles


def summed_along_x(win_ref, places, out_ref, row):
    for line in places:
        for w, i, v in along_x(win_ref, LANES, line, derive_back):
            r = 8 * line[i]
            out_ref[w, row + r : row + r + 8, :] = win_ref[w, r : r + 8, :] + v


def to_planes(win_ref, base, plane_ref):
    for h in range(2):
        for t, tile in enumerate(gathered(win_ref, base, h)):
            plane_ref[t * 16 + 8 * h : t * 16 + 8 * h + 8, :] = tile


def add_plane(line_ref, f, x, flat):
    lane9 = lax.broadcasted_iota(jnp.int32, (9, LANES), 1)
    r0, off = divmod(PYZ * x, LANES)
    if off:
        flat = pltpu.roll(flat, off, 1)
        spill = jnp.where(lane9 < off, flat, 0.0)
        flat = jnp.where(lane9 < off, 0.0, flat)
    line_ref[f, r0 : r0 + 9, :] = line_ref[f, r0 : r0 + 9, :] + flat
    if off:
        line_ref[f, r0 + 1 : r0 + 10, :] = line_ref[f, r0 + 1 : r0 + 10, :] + spill


def force_kernel(elem_ref, flux_ref, out_ref, win_ref, fold_ref, force_ref, plane_ref):
    out_ref[...] = jnp.zeros(out_ref.shape, F32)
    for f in range(2):
        force_terms(elem_ref, f, 2 + f, flux_ref, fold_ref, win_ref, 0)
        summed_along_x(win_ref, OWN_AT, force_ref, 0)
        to_planes(force_ref, 0, plane_ref)
        for x in range(13):
            i, m = x % 4, x // 4
            rows = [OWN_AT[m][i]] if m < 3 else []
            if i == 0 and m > 0:
                rows.append(OWN_AT[m - 1][4])
            flat = [plane_ref[pl.ds(r, 9, stride=16), :] for r in rows]
            add_plane(out_ref, f, x, sum(flat[1:], flat[0]))


def near_force_kernel(
    force_ref, near_half_ref, near_flux_ref, prev_ref, next_ref, count_ref, after_ref,
    out_ref,
    win_ref, fold_ref, near_force_ref, plane_ref, flux_ref, elem_ref, near_win_ref, near_plane_ref, spread_ref,
):
    out_ref[...] = force_ref[...]
    near_plane_ref[...] = jnp.zeros(near_plane_ref.shape, F32)
    for f in range(2):
        for i in range(5):
            flat = plane_of(prev_ref, 12 + PYZ * i, 40 * f) if i < 4 else plane_of(next_ref, 0, 16 * f)
            near_plane_ref[pl.ds(72 * f + i, 9, stride=8), :] = flat
        near_win_ref[:, 128 * f : 128 * f + 64, :] = near_half_ref[:, 64 * f : 64 * f + 64, :]
        make_windows(near_plane_ref, 72 * f, 8, near_win_ref, 128 * f + 64)
    place_flux(flux_ref, message_flux(prev_ref, count_ref, spread_ref), lambda i: [(0, 8 * NEAR_AT[0][i], 8)])
    scaled(flux_ref, lane_weight([NEAR_AT[0]]))
    flux_ref[...] = flux_ref[...] + near_flux_ref[...]
    for f in range(2):
        win_ref[...] = jnp.zeros(win_ref.shape, F32)
        for row in NEAR_AT:
            for w, i, v in along_x(near_win_ref, LANES * f, row, derive):
                win_ref[w, 8 * row[i] : 8 * row[i] + 8, :] = v
        turned(near_win_ref, LANES * f, elem_ref, 0)
        turned(win_ref, 0, elem_ref, 1)
        force_terms(elem_ref, 0, 1, flux_ref, fold_ref, win_ref, 0)
        summed_along_x(win_ref, NEAR_AT, near_force_ref, 0)
        to_planes(near_force_ref, 0, plane_ref)
        for x, r in [(0, NEAR_AT[0][4])] + [(12 + i, NEAR_AT[1][i]) for i in range(4)]:
            add_plane(out_ref, f, x, plane_ref[pl.ds(r, 9, stride=16), :])


def step_kernel(
    line_ref, fwd_ref, fwd_speed_ref, adj_ref, adj_speed_ref, mass_ref,
    fwd_out_ref, fwd_speed_out_ref, adj_out_ref, adj_speed_out_ref,
):
    def step(lo, hi, force):
        shape = (hi - lo) // force[0].shape[1], force[0].shape[1]
        take = lambda ref: ref[0:1, lo:hi].reshape(shape)
        scale = TIME_STEP * mass_ref[lo:hi].reshape(shape)
        speed = take(fwd_speed_ref) + scale * force[0]
        fwd_speed_out_ref[0:1, lo:hi] = speed.reshape(1, hi - lo)
        fwd_out_ref[0:1, lo:hi] = (take(fwd_ref) - TIME_STEP * speed).reshape(1, hi - lo)
        speed = take(adj_speed_ref) - scale * force[1]
        adj_speed_out_ref[0:1, lo:hi] = speed.reshape(1, hi - lo)
        adj_out_ref[0:1, lo:hi] = (take(adj_ref) + TIME_STEP * speed).reshape(1, hi - lo)

    for r in range(0, 136, 8):
        step(r * LANES, (r + 8) * LANES, [line_ref[f, r : r + 8, :] for f in range(2)])
    step(NPTS - 16, NPTS, [line_ref[f, 136:137, 0:16] for f in range(2)])


def band_kernel(cut_ref, own_ref, first_ref, second_ref, band_ref, out_ref):
    flat = jnp.concatenate([own_ref[...], first_ref[...], second_ref[...]], axis=0)
    k1 = flat.astype(BF16)
    rest = flat - k1.astype(F32)
    k2 = rest.astype(BF16)
    k3 = (rest - k2.astype(F32)).astype(BF16)
    stacked = jnp.concatenate([k1, k2, k3, k1, k2, k1], axis=0)
    band = band_ref[cut_ref[0] & 1]
    out_ref[...] = jnp.dot(band, stacked, preferred_element_type=F32)[:, :PYZ]


def on_device(
    forward_displacement,
    forward_velocity,
    adjoint_displacement,
    adjoint_velocity,
    inverse_mass,
    shear_modulus,
    connectivity,
    face_points,
    element_count,
):
    events = lax.axis_size("event")
    cuts = lax.axis_size("cuts")
    cut = lax.axis_index("cuts").astype(jnp.int32).reshape(1)
    pairs_first = [(i, (i - 1 if i % 2 == 0 else i + 1) % cuts) for i in range(cuts)]
    pairs_second = [(i, (i + 1 if i % 2 == 0 else i - 1) % cuts) for i in range(cuts)]

    vmem = pl.BlockSpec(memory_space=pltpu.VMEM)
    smem = pl.BlockSpec(memory_space=pltpu.SMEM)
    anywhere = pl.BlockSpec(memory_space=pl.ANY)

    def held(block):
        return pltpu.with_memory_space_constraint(block, pltpu.VMEM)

    def in_hbm(block):
        return pltpu.with_memory_space_constraint(block, pltpu.HBM)

    def cost(flops):
        return pl.CostEstimate(flops=flops, bytes_accessed=1000000, transcendentals=0)

    dma = pltpu.SemaphoreType.DMA
    point_row = pltpu.VMEM((1, NPTS), F32)
    flux_block = pltpu.VMEM((200, LANES), F32)
    kern_block = pltpu.VMEM((16, 9 * LANES), F32)
    line_block = pltpu.VMEM((256, LANES), F32)

    def elements(n):
        return pltpu.VMEM((n, 168, LANES), F32)

    def windows(n):
        return pltpu.VMEM((2, n * LANES, LANES), F32)

    fields = (in_hbm(forward_displacement), in_hbm(adjoint_displacement))
    cross = held(jnp.asarray(cross_table()))
    right, left, own, code, parts = pl.pallas_call(
        pack_kernel,
        out_shape=[
            pltpu.VMEM((144, LANES), F32),
            pltpu.VMEM((32, LANES), F32),
            pltpu.VMEM((2 * ROWS, LANES), F32),
            pltpu.VMEM((8, 256), jnp.int32),
            pltpu.VMEM((384, 256), BF16),
        ],
        in_specs=[anywhere] * 4,
        scratch_shapes=[
            pltpu.VMEM((8, 256), jnp.int32),
            pltpu.VMEM((125, 256), F32),
            point_row,
            point_row,
            pltpu.VMEM((128, 256), F32),
            dma((4,)),
        ],
        cost_estimate=cost(100000000),
        name="pack",
    )(in_hbm(connectivity), in_hbm(shear_modulus), *fields)
    to_next = [(i, (i + 1) % cuts) for i in range(cuts)]
    prev = lax.ppermute(right, "cuts", to_next)
    count, left = lax.optimization_barrier((element_count, left))
    count = jnp.broadcast_to(count.reshape(1, 1), (8, LANES))
    prev_count = lax.ppermute(count, "cuts", to_next)
    count, left = lax.optimization_barrier((count, left))

    own_blocks = [elements(4), flux_block, flux_block, windows(1), windows(1), flux_block, kern_block]

    def own_part(turn, before):
        given = (cut, held(count), held(own), held(code), held(parts), cross)
        return pl.pallas_call(
            functools.partial(own_kernel, turn),
            out_shape=own_blocks,
            in_specs=[smem] + [vmem] * (5 + len(before)),
            scratch_shapes=[
                pltpu.VMEM((2 * 9 * 24, LANES), F32),
                windows(4),
                line_block,
                elements(1),
                pltpu.VMEM((136, 256), F32),
            ],
            input_output_aliases={len(given) + n: n for n in range(len(before))},
            cost_estimate=cost(300000000),
            name="own_layers",
        )(*given, *[held(block) for block in before])

    left, *blocks = lax.optimization_barrier((left, *own_part(0, [])))
    after = lax.ppermute(left, "cuts", [((i + 1) % cuts, i) for i in range(cuts)])
    elem, flux, near_flux, near_win, near_slope, near_kern, kern = own_part(1, blocks)
    kern = pl.pallas_call(
        near_kernel,
        out_shape=kern_block,
        in_specs=[vmem] * 8,
        scratch_shapes=[
            pltpu.VMEM((72, LANES), F32),
            pltpu.VMEM((2, 64, LANES), F32),
            windows(1),
            elements(1),
            flux_block,
            line_block,
            pltpu.VMEM((136, LANES), F32),
        ],
        cost_estimate=cost(200000000),
        name="near_layers",
    )(held(prev), held(after), held(prev_count), held(near_flux), held(near_slope), held(near_kern), held(kern), cross)

    force = pl.pallas_call(
        force_kernel,
        out_shape=pltpu.VMEM((2, ROWS, LANES), F32),
        in_specs=[vmem] * 2,
        scratch_shapes=[windows(2), line_block, windows(1), pltpu.VMEM((144, LANES), F32)],
        cost_estimate=cost(200000000),
        name="forces",
    )(held(elem), held(flux))

    if events == 2:
        other = lax.ppermute(kern, "event", [(0, 1), (1, 0)])
        other, force = lax.optimization_barrier((other, force))
        kern = kern + other
    elif events > 2:
        kern = lax.psum(kern, "event")
    kern_first = lax.ppermute(kern, "cuts", pairs_first)
    kern_second = lax.ppermute(kern, "cuts", pairs_second)

    force = pl.pallas_call(
        near_force_kernel,
        out_shape=pltpu.VMEM((2, ROWS, LANES), F32),
        in_specs=[vmem] * 7,
        scratch_shapes=[
            windows(2),
            line_block,
            windows(1),
            pltpu.VMEM((144, LANES), F32),
            flux_block,
            elements(2),
            windows(2),
            pltpu.VMEM((2 * 72, LANES), F32),
            pltpu.VMEM((136, LANES), F32),
        ],
        cost_estimate=cost(200000000),
        name="near_forces",
    )(held(force), held(near_win), held(near_flux), held(prev), held(after), held(prev_count), held(kern))
    points = jax.ShapeDtypeStruct((1, NPTS), F32)
    outs = pl.pallas_call(
        step_kernel,
        out_shape=[points] * 4,
        in_specs=[vmem] * 6,
        cost_estimate=cost(200000000),
        name="step",
    )(
        held(force),
        held(forward_displacement),
        held(forward_velocity),
        held(adjoint_displacement),
        held(adjoint_velocity),
        held(inverse_mass),
    )
    shear_kernel = pl.pallas_call(
        band_kernel,
        out_shape=jax.ShapeDtypeStruct((PXU, PYZ), F32),
        in_specs=[smem] + [vmem] * 4,
        cost_estimate=cost(20000000),
        name="band",
    )(cut, held(kern), held(kern_first), held(kern_second), held(jnp.asarray(band_table())))
    return (*outs, shear_kernel)


def solution(mesh):
    in_specs = (
        P("event", "cuts"),
        P("event", "cuts"),
        P("event", "cuts"),
        P("event", "cuts"),
        P("cuts"),
        P(None, "cuts"),
        P(None, "cuts"),
        P("cuts", None),
        P("cuts"),
    )
    out_specs = (
        P("event", "cuts"),
        P("event", "cuts"),
        P("event", "cuts"),
        P("event", "cuts"),
        P("cuts", None),
    )
    return jax.shard_map(on_device, mesh=mesh, in_specs=in_specs, out_specs=out_specs, check_vma=False)
```

```python
import functools

import numpy as np
import jax
import jax.numpy as jnp
import ml_dtypes
from jax import lax
from jax.experimental import pallas as pl
from jax.experimental.pallas import tpu as pltpu
from jax.sharding import PartitionSpec as P

NGLL = 5
EX, EY, EZ = 4, 8, 8
PXU = 16
PY = 33
PZ = 33
PYZ = 1089
NPTS = 17424
LANES = 128
ROWS = 144
TIME_STEP = 0.02
OWN_OUTS, OWN_SCRATCH = 7, 5
F32 = jnp.float32
BF16 = jnp.bfloat16


def gll():
    nodes = np.array([-1.0, -np.sqrt(3.0 / 7.0), 0.0, np.sqrt(3.0 / 7.0), 1.0])
    bary = np.array([1.0 / np.prod([nodes[r] - nodes[c] for c in range(5) if c != r]) for r in range(5)])
    d = np.zeros((5, 5))
    for r in range(5):
        for c in range(5):
            if c != r:
                d[r, c] = bary[c] / bary[r] / (nodes[r] - nodes[c])
        d[r, r] = -np.sum(d[r])
    return d


DERIV = gll()


def split_np(x):
    x = np.asarray(x, np.float32)
    parts = []
    for _ in range(3):
        p = x.astype(ml_dtypes.bfloat16)
        parts.append(p)
        x = x - p.astype(np.float32)
    return parts


ROW_PLANE = np.array([4 * (r % 3) + r // 3 for r in range(12)] + [12, 13, 14, 15])
OWN_AT = [[3 * i + m for i in range(5)] for m in range(3)]
NEAR_AT = [[8, 9, 10, 11, 0], [4, 5, 6, 7, 12]]


def band_table():
    offsets = np.arange(-PXU, PXU + 1)
    w = lambda d: np.exp(-d * d / (2.0 * (PXU / 4.0) ** 2))
    total = w(offsets.astype(np.float64)).sum()
    out = []
    for first in (-PXU, PXU):
        source = np.concatenate([ROW_PLANE, ROW_PLANE + first, ROW_PLANE - first])
        spread = np.arange(PXU)[:, None] - source[None, :]
        band = w(spread.astype(np.float64)) * (np.abs(spread) <= PXU) / total
        b1, b2, b3 = split_np(band)
        out.append(np.concatenate([b1, b1, b1, b2, b2, b3], axis=1))
    return np.stack(out)


def cross_table():
    off = np.arange(-4, 5)
    k = np.exp(-off * off / (2.0 * 1.5 * 1.5))
    point = np.arange(33)
    inside = ((point[None, :] + off[:, None]) >= 0) & ((point[None, :] + off[:, None]) < 33)
    taps = k[:, None] * inside
    taps = taps / taps.sum(axis=0, keepdims=True)
    out = np.zeros((24, 1152), np.float32)
    out[0:9, :PYZ] = np.tile(taps, (1, PY))
    out[9:18, :PYZ] = np.repeat(taps, PZ, axis=1)
    return out


def split3(x):
    hi = x.astype(BF16)
    rest = x - hi.astype(F32)
    mid = rest.astype(BF16)
    low = (rest - mid.astype(F32)).astype(BF16)
    return hi, mid, low


def dot_nt(a, b):
    return lax.dot_general(a, b, (((1,), (1,)), ((), ())), preferred_element_type=F32)


def fetch(sem, *pairs):
    copies = [pltpu.make_async_copy(src, dst, sem.at[n]) for n, (src, dst) in enumerate(pairs)]
    for c in copies:
        c.start()
    return copies


def add_parts(stacked):
    n = stacked.shape[0] // 3
    return stacked[0:n] + (stacked[n : 2 * n] + stacked[2 * n : 3 * n])


def pack_kernel(
    conn_hbm, shear_hbm, fwd_hbm, adj_hbm,
    right_ref, left_ref, own_ref, code_ref, parts_ref,
    conn_ref, shear_ref, fwd_ref, adj_ref, block_ref, sem,
):
    copies = fetch(
        sem,
        (shear_hbm, shear_ref),
        (conn_hbm.at[0:8], conn_ref),
        (fwd_hbm, fwd_ref),
        (adj_hbm, adj_ref),
    )
    copies[1].wait()
    point = conn_ref[0:1, :].astype(F32)
    x = jnp.floor((point + 0.5) * (1.0 / PYZ))
    rest = point - x * PYZ
    y = jnp.floor((rest + 0.5) * (1.0 / PZ))
    z = rest - y * PZ
    code = (8.0 * z + 2.0 * x + 0.25 * y).astype(jnp.int32)
    slot = lax.broadcasted_iota(jnp.int32, (1, 256), 1)
    code_ref[...] = jnp.broadcast_to(code, (8, 256))
    lane = lax.broadcasted_iota(jnp.int32, (LANES, 256), 0)
    pick = jnp.where(code == ((lane >> 3) & 7) * 32 + 24 + (lane & 7), 1.0, 0.0).astype(BF16)
    for f, ref in enumerate((fwd_ref, adj_ref)):
        copies[2 + f].wait()
        for r in range(0, 136, 8):
            own_ref[ROWS * f + r : ROWS * f + r + 8, :] = ref[0:1, r * LANES : (r + 8) * LANES].reshape(8, LANES)
        own_ref[ROWS * f + 136 : ROWS * f + 144, :] = jnp.zeros((8, LANES), F32)
        own_ref[ROWS * f + 136 : ROWS * f + 137, 0:16] = ref[0:1, NPTS - 16 : NPTS]
        right_ref[40 * f : 40 * f + 40, :] = own_ref[ROWS * f + 102 : ROWS * f + 142, :]
        left_ref[16 * f : 16 * f + 16, :] = own_ref[ROWS * f : ROWS * f + 16, :]
    copies[0].wait()
    block_ref[0:125, :] = shear_ref[...]
    block_ref[125:126, :] = slot.astype(F32)
    block_ref[126:128, :] = jnp.zeros((2, 256), F32)
    parts = jnp.concatenate(split3(block_ref[...]), axis=0)
    parts_ref[...] = parts
    flux = add_parts(dot_nt(parts, pick))
    low = lax.broadcasted_iota(jnp.int32, (64, LANES), 1) < 64
    right_ref[80:144, :] = jnp.where(low, flux[0:64], flux[64:128])


def gll_weight(i):
    return (0.1, 49.0 / 90.0, 32.0 / 45.0, 49.0 / 90.0, 0.1)[i]


def lane_weight(places):
    chunk = lax.broadcasted_iota(jnp.int32, (8, LANES), 1) >> 3
    weight = jnp.zeros((8, LANES), F32)
    for row in places:
        for i, place in enumerate(row):
            weight = jnp.where(chunk == place, gll_weight(i), weight)
    return weight


def scaled(ref, weight):
    for j in range(5):
        for k in range(5):
            r = (j * 5 + k) * 8
            ref[r : r + 8, :] = ref[r : r + 8, :] * (weight * (gll_weight(j) * gll_weight(k)))


def place_flux(ref, tile_of, moves, layers=range(NGLL)):
    lane = lax.broadcasted_iota(jnp.int32, (32, LANES), 1)
    for ez in range(EZ):
        total = jnp.zeros((32, LANES), F32)
        for i in layers:
            tile, start = tile_of(i, ez)
            for source, target, width in moves(i):
                shift = (target - source - start) % LANES
                moved = pltpu.roll(tile, shift, 1) if shift else tile
                total = jnp.where((lane >= target) & (lane < target + width), moved, total)
        ref[pl.ds(ez, 25, stride=8), :] = total[0:25]


def derive(e):
    d = DERIV
    s0, s1 = e[0] + e[4], e[1] + e[3]
    d0, d1 = e[0] - e[4], e[1] - e[3]
    out = [None] * 5
    for i in (0, 1):
        even = float((d[i, 0] - d[i, 4]) / 2) * d0 + float((d[i, 1] - d[i, 3]) / 2) * d1
        odd = float((d[i, 0] + d[i, 4]) / 2) * s0 + float((d[i, 1] + d[i, 3]) / 2) * s1 + float(d[i, 2]) * e[2]
        out[i] = odd + even
        out[4 - i] = even - odd
    out[2] = float(d[2, 0]) * d0 + float(d[2, 1]) * d1
    return out


def derive_back(t):
    d = DERIV
    s0, s1 = t[0] + t[4], t[1] + t[3]
    d0, d1 = t[0] - t[4], t[1] - t[3]
    out = [None] * 5
    for i in (0, 1):
        even = float((d[0, i] - d[4, i]) / 2) * d0 + float((d[1, i] - d[3, i]) / 2) * d1
        odd = float((d[0, i] + d[4, i]) / 2) * s0 + float((d[1, i] + d[3, i]) / 2) * s1 + float(d[2, i]) * t[2]
        out[i] = odd + even
        out[4 - i] = even - odd
    out[2] = float(d[0, 2]) * d0 + float(d[1, 2]) * d1
    return out


def shifted(tiles, distance, lane):
    skip, part = divmod(distance, LANES)
    if part == 0:
        moved = tiles
        pick = None
    else:
        moved = [pltpu.roll(t, LANES - part, 1) for t in tiles]
        pick = lane < LANES - part
    n = len(tiles)
    out = []
    for i in range(n):
        a = moved[(i + skip) % n]
        b = moved[(i + skip + 1) % n]
        out.append(a if pick is None else jnp.where(pick, a, b))
    return out


def plane_of(ref, start, row):
    r0, off = divmod(start, LANES)
    lane9 = lax.broadcasted_iota(jnp.int32, (9, LANES), 1)
    flat = ref[row + r0 : row + r0 + 9, :]
    if off:
        flat = jnp.where(
            lane9 < LANES - off,
            pltpu.roll(flat, LANES - off, 1),
            pltpu.roll(ref[row + r0 + 1 : row + r0 + 10, :], LANES - off, 1),
        )
    return flat


def store_plane(ref, row, flat):
    ref[pl.ds(row, 9, stride=16), :] = flat


def make_windows(plane_ref, base, pitch, win_ref, row):
    lane = lax.broadcasted_iota(jnp.int32, (8, LANES), 1)
    tiles = [plane_ref[base + t * pitch : base + t * pitch + 8, :] for t in range(9)]
    for ey in range(EY):
        near = [tiles[ey], tiles[ey + 1], tiles[min(ey + 2, 8)]]
        if ey:
            near = [pltpu.roll(t, LANES - 4 * ey, 1) for t in near]
            keep = lane < LANES - 4 * ey
            near = [jnp.where(keep, near[0], near[1]), jnp.where(keep, near[1], near[2])]
        for w in range(2):
            win_ref[w, pl.ds(row + ey, 8, stride=8), :] = near[w]


def along_x(win_ref, base, row, combine):
    for w in range(2):
        values = combine([win_ref[w, base + 8 * c : base + 8 * c + 8, :] for c in row])
        for i, v in enumerate(values):
            yield w, i, v


def turned(win_ref, base, elem_ref, column):
    elem_ref[column, 0:LANES, :] = win_ref[0, base : base + LANES, :].T
    elem_ref[column, LANES:168, :] = win_ref[1, base : base + LANES, :].T[0:40, :]


def part(ref, column, j, k):
    return ref[column, pl.ds(j * PZ + k, 8, stride=4), :]


def flux_part(ref, j, k):
    r = (j * 5 + k) * 8
    return ref[r : r + 8, :]


def folded(term, line_ref, win_ref, base):
    row = lax.broadcasted_iota(jnp.int32, (8, LANES), 0)
    line_ref[160:256, :] = jnp.zeros((96, LANES), F32)
    for j in range(5):
        for k in range(1, 4):
            line_ref[pl.ds(j * PZ + k, 8, stride=4), :] = term[j][k]
        last = term[j][4]
        line_ref[pl.ds(j * PZ, 8, stride=4), :] = term[j][0] + jnp.where(row == 0, 0.0, pltpu.roll(last, 1, 0))
        line_ref[j * PZ + 32 : j * PZ + 33, :] = last[7:8, :]
    for w in range(2):
        win_ref[w, base : base + LANES, :] = line_ref[w * LANES : (w + 1) * LANES, :].T


def force_terms(elem_ref, value, slope, flux_ref, line_ref, win_ref, row):
    term = [[None] * 5 for _ in range(5)]
    for k in range(5):
        grads = derive([part(elem_ref, value, j, k) for j in range(5)])
        for j, v in enumerate(derive_back([g * flux_part(flux_ref, j, k) for j, g in enumerate(grads)])):
            term[j][k] = v
    for j in range(5):
        grads = derive([part(elem_ref, value, j, k) for k in range(5)])
        for k, v in enumerate(derive_back([g * flux_part(flux_ref, j, k) for k, g in enumerate(grads)])):
            term[j][k] = term[j][k] + v
    folded(term, line_ref, win_ref, row)
    term = [[part(elem_ref, slope, j, k) * flux_part(flux_ref, j, k) for k in range(5)] for j in range(5)]
    folded(term, line_ref, win_ref, row + LANES)


def cross_smoothed(tiles, cross_ref):
    lane = lax.broadcasted_iota(jnp.int32, tiles[0].shape, 1)
    for base, step in ((0, 1), (9, PZ)):
        total = None
        for tap in range(9):
            moved = shifted(tiles, step * (tap - 4), lane) if tap != 4 else tiles
            terms = [v * cross_ref[base + tap : base + tap + 1, t * LANES : (t + 1) * LANES] for t, v in enumerate(moved)]
            total = terms if total is None else [a + b for a, b in zip(total, terms)]
        tiles = total
    return tiles


def own_kernel(turn, cut_ref, count_ref, own_ref, code_ref, parts_ref, cross_ref, *refs):
    refs = refs[-OWN_OUTS - OWN_SCRATCH :]
    mine = (cut_ref[0] == 0) if turn == 0 else (cut_ref[0] != 0)

    @pl.when(mine)
    def _():
        own_layers(count_ref, own_ref, code_ref, parts_ref, cross_ref, *refs)


def own_layers(
    count_ref, own_ref, code_ref, parts_ref, cross_ref,
    elem_ref, flux_ref, near_flux_ref, near_win_ref, near_slope_ref, near_kern_ref, kern_ref,
    plane_ref, win_ref, line_ref, near_elem_ref, moved_ref,
):
    plane_ref[...] = jnp.zeros(plane_ref.shape, F32)
    for f in range(2):
        base = 24 * 9 * f
        for x in range(PXU):
            flat = plane_of(own_ref, PYZ * x, ROWS * f)
            rows = [OWN_AT[x // 4][x % 4]] if x < 12 else [16 + NEAR_AT[1][x - 12]]
            if x % 4 == 0:
                rows.append(OWN_AT[x // 4 - 1][4] if x else 16 + NEAR_AT[0][4])
            for r in rows:
                plane_ref[pl.ds(base + r, 9, stride=24), :] = flat
        for h in range(2):
            make_windows(plane_ref, base + 8 * h, 24, win_ref, 128 * f + 64 * h)
        make_windows(plane_ref, base + 16, 24, near_win_ref, 64 * f)
        win_ref[:, 256 + 128 * f : 384 + 128 * f, :] = jnp.zeros((2, LANES, LANES), F32)
        for row in OWN_AT:
            for w, i, v in along_x(win_ref, 128 * f, row, derive):
                r = 256 + 128 * f + 8 * row[i]
                win_ref[w, r : r + 8, :] = v
    for column in range(4):
        turned(win_ref, 128 * column, elem_ref, column)
    turned(near_win_ref, 0, near_elem_ref, 0)
    near_slope_ref[...] = jnp.zeros(near_slope_ref.shape, F32)
    for f in range(2):
        for w in range(2):
            value = [near_win_ref[w, 64 * f + 8 * c : 64 * f + 8 * c + 8, :] for c in (0, 4, 5, 6, 7)]
            near_slope_ref[w, 64 * f : 64 * f + 8, :] = float(DERIV[4, 4]) * value[0]
            for i, v in enumerate(derive(value[1:] + [jnp.zeros((8, LANES), F32)])[:4]):
                r = 64 * f + 8 * NEAR_AT[1][i]
                near_slope_ref[w, r : r + 8, :] = v

    element = lax.broadcasted_iota(jnp.int32, (256, 256), 0)
    slot = lax.broadcasted_iota(jnp.int32, (1, 256), 1)
    live = jnp.concatenate([count_ref[0:1, :], count_ref[0:1, :]], axis=1)
    code = jnp.where(slot < live, code_ref[0:1, :], -1)
    pick = jnp.where(code == element, 1.0, 0.0).astype(BF16)
    moved_ref[0:128, :] = add_parts(dot_nt(parts_ref[...], pick))
    moved_ref[128:136, :] = jnp.zeros((8, 256), F32)

    def tile_of(i, ez):
        t = ez // 4
        return moved_ref[25 * i : 25 * i + 32, t * LANES : (t + 1) * LANES], 32 * (ez % 4)

    place_flux(flux_ref, tile_of, lambda i: [(0, 24 * i, 24)])
    place_flux(near_flux_ref, tile_of, lambda i: [(24, 8 * NEAR_AT[1][i], 8)])
    scaled(flux_ref, lane_weight(OWN_AT))
    scaled(near_flux_ref, lane_weight(NEAR_AT))

    kern = [[None] * 5 for _ in range(5)]
    near = [[None] * 5 for _ in range(5)]
    for k in range(5):
        fwd, adj, both = [derive([part(ref, c, j, k) for j in range(5)]) for ref, c in ((elem_ref, 0), (elem_ref, 1), (near_elem_ref, 0))]
        for j in range(5):
            kern[j][k] = fwd[j] * adj[j] + part(elem_ref, 2, j, k) * part(elem_ref, 3, j, k)
            near[j][k] = both[j] * pltpu.roll(both[j], 64, 1)
    for j in range(5):
        fwd, adj, both = [derive([part(ref, c, j, k) for k in range(5)]) for ref, c in ((elem_ref, 0), (elem_ref, 1), (near_elem_ref, 0))]
        for k in range(5):
            kern[j][k] = -(kern[j][k] + fwd[k] * adj[k]) * flux_part(flux_ref, j, k)
            r = (j * 5 + k) * 8
            near_kern_ref[r : r + 8, :] = near[j][k] + both[k] * pltpu.roll(both[k], 64, 1)
    folded(kern, line_ref, win_ref, 0)
    low, high = [gathered(win_ref, 0, h) for h in range(2)]
    row = lax.broadcasted_iota(jnp.int32, (8, LANES), 0)
    tiles = []
    for t in range(9):
        first = low[t] + jnp.where((row == 1) | (row == 2), pltpu.roll(high[t], 5, 0), 0.0)
        second = jnp.where(row < 4, high[t], jnp.where(row == 4, pltpu.roll(high[t], 6, 0), 0.0))
        tiles.append(jnp.concatenate([first, second], axis=0))
    for t, tile in enumerate(cross_smoothed(tiles, cross_ref)):
        kern_ref[:, t * LANES : (t + 1) * LANES] = tile


def message_flux(prev_ref, count_ref, spread_ref):
    upper = pltpu.roll(prev_ref[80:144, :], 64, 1)
    live = upper[61:62, :] < count_ref[0:1, :].astype(F32)
    spread_ref[0:64, :] = jnp.where(live, prev_ref[80:144, :], 0.0)
    spread_ref[64:128, :] = jnp.where(live, upper, 0.0)
    spread_ref[128:136, :] = jnp.zeros((8, LANES), F32)
    return lambda i, ez: (spread_ref[25 * i : 25 * i + 32, :], 8 * ez)


def near_kernel(
    prev_ref, next_ref, count_ref, flux_in_ref, slope_ref, near_kern_ref, kern_in_ref, cross_ref,
    kern_ref,
    plane_ref, new_ref, win_ref, elem_ref, flux_ref, line_ref, spread_ref,
):
    plane_ref[...] = jnp.zeros(plane_ref.shape, F32)
    for f in range(2):
        share = None
        for l in range(4):
            term = float(DERIV[4, l]) * plane_of(prev_ref, 12 + PYZ * l, 40 * f)
            share = term if share is None else share + term
        plane_ref[pl.ds(f, 9, stride=8), :] = share
        plane_ref[pl.ds(2 + f, 9, stride=8), :] = plane_of(next_ref, 0, 16 * f)
    make_windows(plane_ref, 0, 8, new_ref, 0)
    win_ref[...] = slope_ref[...]
    for f in range(2):
        for w in range(2):
            r = 64 * f
            win_ref[w, r : r + 8, :] = win_ref[w, r : r + 8, :] + new_ref[w, 8 * f : 8 * f + 8, :]
            for i in range(4):
                r = 64 * f + 8 * NEAR_AT[1][i]
                new = float(DERIV[i, 4]) * new_ref[w, 16 + 8 * f : 24 + 8 * f, :]
                win_ref[w, r : r + 8, :] = win_ref[w, r : r + 8, :] + new
    turned(win_ref, 0, elem_ref, 0)
    place_flux(flux_ref, message_flux(prev_ref, count_ref, spread_ref), lambda i: [(0, 8 * NEAR_AT[0][i], 8)], (4,))
    scaled(flux_ref, lane_weight([NEAR_AT[0]]))
    kern = [[None] * 5 for _ in range(5)]
    for j in range(5):
        for k in range(5):
            slope = part(elem_ref, 0, j, k)
            total = flux_part(near_kern_ref, j, k) + slope * pltpu.roll(slope, 64, 1)
            kern[j][k] = -total * (flux_part(flux_ref, j, k) + flux_part(flux_in_ref, j, k))
    folded(kern, line_ref, win_ref, 0)
    row = lax.broadcasted_iota(jnp.int32, (8, LANES), 0)
    tiles = [jnp.where((row == 0) | (row >= 4), v, 0.0) for v in gathered(win_ref, 0, 0)]
    for t, tile in enumerate(cross_smoothed(tiles, cross_ref)):
        columns = slice(t * LANES, (t + 1) * LANES)
        kern_ref[0:8, columns] = kern_in_ref[0:8, columns] + jnp.where(row == 0, tile, 0.0)
        kern_ref[8:16, columns] = kern_in_ref[8:16, columns] + jnp.where(row >= 4, tile, 0.0)


def gathered(win_ref, base, h):
    lane = lax.broadcasted_iota(jnp.int32, (8, LANES), 1)
    tiles = [None] * 9
    for ey in range(EY):
        rows = pl.ds(base + h * 64 + ey, 8, stride=8)
        a, b = win_ref[0, rows, :], win_ref[1, rows, :]
        if ey:
            a, b = pltpu.roll(a, 4 * ey, 1), pltpu.roll(b, 4 * ey, 1)
            keep = lane >= 4 * ey
            a, b = jnp.where(keep, a, 0.0), jnp.where(keep, b, a)
        tiles[ey] = a if ey == 0 else tiles[ey] + a
        tiles[ey + 1] = b
    return tiles


def summed_along_x(win_ref, places, out_ref, row):
    for line in places:
        for w, i, v in along_x(win_ref, LANES, line, derive_back):
            r = 8 * line[i]
            out_ref[w, row + r : row + r + 8, :] = win_ref[w, r : r + 8, :] + v


def to_planes(win_ref, base, plane_ref):
    for h in range(2):
        for t, tile in enumerate(gathered(win_ref, base, h)):
            plane_ref[t * 16 + 8 * h : t * 16 + 8 * h + 8, :] = tile


def add_plane(line_ref, f, x, flat):
    lane9 = lax.broadcasted_iota(jnp.int32, (9, LANES), 1)
    r0, off = divmod(PYZ * x, LANES)
    if off:
        flat = pltpu.roll(flat, off, 1)
        spill = jnp.where(lane9 < off, flat, 0.0)
        flat = jnp.where(lane9 < off, 0.0, flat)
    line_ref[f, r0 : r0 + 9, :] = line_ref[f, r0 : r0 + 9, :] + flat
    if off:
        line_ref[f, r0 + 1 : r0 + 10, :] = line_ref[f, r0 + 1 : r0 + 10, :] + spill


def force_kernel(turn, cut_ref, elem_ref, flux_ref, before_ref, *refs):
    mine = (cut_ref[0] == 1) if turn == 0 else (cut_ref[0] != 1)

    @pl.when(mine)
    def _():
        own_forces(elem_ref, flux_ref, refs[0], *refs[len(refs) - 4 :])


def own_forces(elem_ref, flux_ref, out_ref, win_ref, fold_ref, force_ref, plane_ref):
    out_ref[...] = jnp.zeros(out_ref.shape, F32)
    for f in range(2):
        force_terms(elem_ref, f, 2 + f, flux_ref, fold_ref, win_ref, 0)
        summed_along_x(win_ref, OWN_AT, force_ref, 0)
        to_planes(force_ref, 0, plane_ref)
        for x in range(13):
            i, m = x % 4, x // 4
            rows = [OWN_AT[m][i]] if m < 3 else []
            if i == 0 and m > 0:
                rows.append(OWN_AT[m - 1][4])
            flat = [plane_ref[pl.ds(r, 9, stride=16), :] for r in rows]
            add_plane(out_ref, f, x, sum(flat[1:], flat[0]))


def near_force_kernel(turn, cut_ref, *refs):
    mine = (cut_ref[0] == 1) if turn == 0 else (cut_ref[0] != 1)

    @pl.when(mine)
    def _():
        near_forces(*refs[:6], refs[len(refs) - 11 + turn], *refs[len(refs) - 9 :])


def near_forces(
    force_ref, near_half_ref, near_flux_ref, prev_ref, next_ref, count_ref,
    out_ref,
    win_ref, fold_ref, near_force_ref, plane_ref, flux_ref, elem_ref, near_win_ref, near_plane_ref, spread_ref,
):
    out_ref[...] = force_ref[...]
    near_plane_ref[...] = jnp.zeros(near_plane_ref.shape, F32)
    for f in range(2):
        for i in range(5):
            flat = plane_of(prev_ref, 12 + PYZ * i, 40 * f) if i < 4 else plane_of(next_ref, 0, 16 * f)
            near_plane_ref[pl.ds(72 * f + i, 9, stride=8), :] = flat
        near_win_ref[:, 128 * f : 128 * f + 64, :] = near_half_ref[:, 64 * f : 64 * f + 64, :]
        make_windows(near_plane_ref, 72 * f, 8, near_win_ref, 128 * f + 64)
    place_flux(flux_ref, message_flux(prev_ref, count_ref, spread_ref), lambda i: [(0, 8 * NEAR_AT[0][i], 8)])
    scaled(flux_ref, lane_weight([NEAR_AT[0]]))
    flux_ref[...] = flux_ref[...] + near_flux_ref[...]
    for f in range(2):
        win_ref[...] = jnp.zeros(win_ref.shape, F32)
        for row in NEAR_AT:
            for w, i, v in along_x(near_win_ref, LANES * f, row, derive):
                win_ref[w, 8 * row[i] : 8 * row[i] + 8, :] = v
        turned(near_win_ref, LANES * f, elem_ref, 0)
        turned(win_ref, 0, elem_ref, 1)
        force_terms(elem_ref, 0, 1, flux_ref, fold_ref, win_ref, 0)
        summed_along_x(win_ref, NEAR_AT, near_force_ref, 0)
        to_planes(near_force_ref, 0, plane_ref)
        for x, r in [(0, NEAR_AT[0][4])] + [(12 + i, NEAR_AT[1][i]) for i in range(4)]:
            add_plane(out_ref, f, x, plane_ref[pl.ds(r, 9, stride=16), :])


def step_kernel(
    line_ref, fwd_ref, fwd_speed_ref, adj_ref, adj_speed_ref, mass_ref,
    fwd_out_ref, fwd_speed_out_ref, adj_out_ref, adj_speed_out_ref,
):
    def step(lo, hi, force):
        shape = (hi - lo) // force[0].shape[1], force[0].shape[1]
        take = lambda ref: ref[0:1, lo:hi].reshape(shape)
        scale = TIME_STEP * mass_ref[lo:hi].reshape(shape)
        speed = take(fwd_speed_ref) + scale * force[0]
        fwd_speed_out_ref[0:1, lo:hi] = speed.reshape(1, hi - lo)
        fwd_out_ref[0:1, lo:hi] = (take(fwd_ref) - TIME_STEP * speed).reshape(1, hi - lo)
        speed = take(adj_speed_ref) - scale * force[1]
        adj_speed_out_ref[0:1, lo:hi] = speed.reshape(1, hi - lo)
        adj_out_ref[0:1, lo:hi] = (take(adj_ref) + TIME_STEP * speed).reshape(1, hi - lo)

    for r in range(0, 136, 8):
        step(r * LANES, (r + 8) * LANES, [line_ref[f, r : r + 8, :] for f in range(2)])
    step(NPTS - 16, NPTS, [line_ref[f, 136:137, 0:16] for f in range(2)])


def band_kernel(cut_ref, own_ref, first_ref, second_ref, band_ref, out_ref):
    flat = jnp.concatenate([own_ref[...], first_ref[...], second_ref[...]], axis=0)
    k1 = flat.astype(BF16)
    rest = flat - k1.astype(F32)
    k2 = rest.astype(BF16)
    k3 = (rest - k2.astype(F32)).astype(BF16)
    stacked = jnp.concatenate([k1, k2, k3, k1, k2, k1], axis=0)
    band = band_ref[cut_ref[0] & 1]
    out_ref[...] = jnp.dot(band, stacked, preferred_element_type=F32)[:, :PYZ]


def on_device(
    forward_displacement,
    forward_velocity,
    adjoint_displacement,
    adjoint_velocity,
    inverse_mass,
    shear_modulus,
    connectivity,
    face_points,
    element_count,
):
    events = lax.axis_size("event")
    cuts = lax.axis_size("cuts")
    cut = lax.axis_index("cuts").astype(jnp.int32).reshape(1)
    pairs_first = [(i, (i - 1 if i % 2 == 0 else i + 1) % cuts) for i in range(cuts)]
    pairs_second = [(i, (i + 1 if i % 2 == 0 else i - 1) % cuts) for i in range(cuts)]

    vmem = pl.BlockSpec(memory_space=pltpu.VMEM)
    smem = pl.BlockSpec(memory_space=pltpu.SMEM)
    anywhere = pl.BlockSpec(memory_space=pl.ANY)

    def held(block):
        return pltpu.with_memory_space_constraint(block, pltpu.VMEM)

    def in_hbm(block):
        return pltpu.with_memory_space_constraint(block, pltpu.HBM)

    def cost(flops):
        return pl.CostEstimate(flops=flops, bytes_accessed=1000000, transcendentals=0)

    dma = pltpu.SemaphoreType.DMA
    point_row = pltpu.VMEM((1, NPTS), F32)
    flux_block = pltpu.VMEM((200, LANES), F32)
    kern_block = pltpu.VMEM((16, 9 * LANES), F32)
    line_block = pltpu.VMEM((256, LANES), F32)

    def elements(n):
        return pltpu.VMEM((n, 168, LANES), F32)

    def windows(n):
        return pltpu.VMEM((2, n * LANES, LANES), F32)

    fields = (in_hbm(forward_displacement), in_hbm(adjoint_displacement))
    cross = held(jnp.asarray(cross_table()))
    right, left, own, code, parts = pl.pallas_call(
        pack_kernel,
        out_shape=[
            pltpu.VMEM((144, LANES), F32),
            pltpu.VMEM((32, LANES), F32),
            pltpu.VMEM((2 * ROWS, LANES), F32),
            pltpu.VMEM((8, 256), jnp.int32),
            pltpu.VMEM((384, 256), BF16),
        ],
        in_specs=[anywhere] * 4,
        scratch_shapes=[
            pltpu.VMEM((8, 256), jnp.int32),
            pltpu.VMEM((125, 256), F32),
            point_row,
            point_row,
            pltpu.VMEM((128, 256), F32),
            dma((4,)),
        ],
        cost_estimate=cost(100000000),
        name="pack",
    )(in_hbm(connectivity), in_hbm(shear_modulus), *fields)
    to_next = [(i, (i + 1) % cuts) for i in range(cuts)]
    prev = lax.ppermute(right, "cuts", to_next)
    count, left = lax.optimization_barrier((element_count, left))
    count = jnp.broadcast_to(count.reshape(1, 1), (8, LANES))
    prev_count = lax.ppermute(count, "cuts", to_next)
    count, left = lax.optimization_barrier((count, left))

    own_blocks = [elements(4), flux_block, flux_block, windows(1), windows(1), flux_block, kern_block]

    def own_part(turn, before):
        given = (cut, held(count), held(own), held(code), held(parts), cross)
        return pl.pallas_call(
            functools.partial(own_kernel, turn),
            out_shape=own_blocks,
            in_specs=[smem] + [vmem] * (5 + len(before)),
            scratch_shapes=[
                pltpu.VMEM((2 * 9 * 24, LANES), F32),
                windows(4),
                line_block,
                elements(1),
                pltpu.VMEM((136, 256), F32),
            ],
            input_output_aliases={len(given) + n: n for n in range(len(before))},
            cost_estimate=cost(300000000),
            name="own_layers",
        )(*given, *[held(block) for block in before])

    left, *blocks = lax.optimization_barrier((left, *own_part(0, [])))
    after = lax.ppermute(left, "cuts", [((i + 1) % cuts, i) for i in range(cuts)])
    elem, flux, near_flux, near_win, near_slope, near_kern, kern = own_part(1, blocks)
    kern = pl.pallas_call(
        near_kernel,
        out_shape=kern_block,
        in_specs=[vmem] * 8,
        scratch_shapes=[
            pltpu.VMEM((72, LANES), F32),
            pltpu.VMEM((2, 64, LANES), F32),
            windows(1),
            elements(1),
            flux_block,
            line_block,
            pltpu.VMEM((136, LANES), F32),
        ],
        cost_estimate=cost(200000000),
        name="near_layers",
    )(held(prev), held(after), held(prev_count), held(near_flux), held(near_slope), held(near_kern), held(kern), cross)

    point_block = pltpu.VMEM((2, ROWS, LANES), F32)

    def force_part(turn, before, outs, aliases):
        return pl.pallas_call(
            functools.partial(force_kernel, turn),
            out_shape=outs,
            in_specs=[smem] + [vmem] * 3,
            scratch_shapes=[windows(2), line_block, windows(1), pltpu.VMEM((144, LANES), F32)],
            input_output_aliases=aliases,
            cost_estimate=cost(200000000),
            name="forces",
        )(cut, held(elem), held(flux), held(before))

    def near_force_part(turn, force, before, outs, aliases, waits=()):
        return pl.pallas_call(
            functools.partial(near_force_kernel, turn),
            out_shape=outs,
            in_specs=[smem] + [vmem] * (7 + len(waits)),
            scratch_shapes=[
                windows(2),
                line_block,
                windows(1),
                pltpu.VMEM((144, LANES), F32),
                flux_block,
                elements(2),
                windows(2),
                pltpu.VMEM((2 * 72, LANES), F32),
                pltpu.VMEM((136, LANES), F32),
            ],
            input_output_aliases=aliases,
            cost_estimate=cost(200000000),
            name="near_forces",
        )(
            cut,
            held(force),
            held(near_win),
            held(near_flux),
            held(prev),
            held(after),
            held(prev_count),
            held(before),
            *[held(block) for block in waits],
        )

    force, kern = force_part(0, kern, [point_block, kern_block], {3: 1})
    whole, kern = near_force_part(0, force, kern, [point_block, kern_block], {7: 1})
    (force,) = force_part(1, force, [point_block], {3: 0})

    if events == 2:
        other = lax.ppermute(kern, "event", [(0, 1), (1, 0)])
        other, force = lax.optimization_barrier((other, force))
        kern = kern + other
    elif events > 2:
        kern = lax.psum(kern, "event")
    kern_first = lax.ppermute(kern, "cuts", pairs_first)
    kern_second = lax.ppermute(kern, "cuts", pairs_second)

    (force,) = near_force_part(1, force, whole, [point_block], {7: 0}, [kern])
    points = jax.ShapeDtypeStruct((1, NPTS), F32)
    outs = pl.pallas_call(
        step_kernel,
        out_shape=[points] * 4,
        in_specs=[vmem] * 6,
        cost_estimate=cost(200000000),
        name="step",
    )(
        held(force),
        held(forward_displacement),
        held(forward_velocity),
        held(adjoint_displacement),
        held(adjoint_velocity),
        held(inverse_mass),
    )
    shear_kernel = pl.pallas_call(
        band_kernel,
        out_shape=jax.ShapeDtypeStruct((PXU, PYZ), F32),
        in_specs=[smem] + [vmem] * 4,
        cost_estimate=cost(20000000),
        name="band",
    )(cut, held(kern), held(kern_first), held(kern_second), held(jnp.asarray(band_table())))
    return (*outs, shear_kernel)


def solution(mesh):
    in_specs = (
        P("event", "cuts"),
        P("event", "cuts"),
        P("event", "cuts"),
        P("event", "cuts"),
        P("cuts"),
        P(None, "cuts"),
        P(None, "cuts"),
        P("cuts", None),
        P("cuts"),
    )
    out_specs = (
        P("event", "cuts"),
        P("event", "cuts"),
        P("event", "cuts"),
        P("event", "cuts"),
        P("cuts", None),
    )
    return jax.shard_map(on_device, mesh=mesh, in_specs=in_specs, out_specs=out_specs, check_vma=False)
```
